256 devices in a mesh: af: 4 (over x), gx: 16 (over y_lo, z), gy: 4 (over y_hi, core).
Axes of the slice: x: 4, y: 4 (y_hi: 2, y_lo: 2; y = y_hi * 2 + y_lo), z: 8, core: 2. Of those that a mesh axis runs over, the one named last changes fastest.
Arguments:
- fields_state: float32 [32, 6, 64, 64, 128], P('af', None, 'gx', 'gy'), may hold values from -6 to 6
- velocity: float32 [3, 64, 64, 128], P(None, 'gx', 'gy'), may hold values from -3 to 3
- diffusivity: float32 [64, 64, 128], P('gx', 'gy'), may hold values from 0.02 to 0.15
- wiener_draw: float32 [32, 3], P('af'), may hold values from -4 to 4
Outputs:
- next_state: float32 [32, 6, 64, 64, 128], P('af', None, 'gx', 'gy')
The draws below stay inside these ranges and needn't reach their ends.
All inputs are finite; a program needn't handle non-finite values.
Results may differ from the reference program's by a relative error of at most 0.00002.
Values sent between devices are 32-bit elements; how exact they have to be, the bound alone decides.
A program may use at most 64 MiB of HBM per device.

```python
import math
import jax
import jax.numpy as jnp
from jax import lax

FIELDS = 32
NS = 6
Z = 128
NX = 64
NY = 64


def shard_levels(rng, extent, split, smallest, high):
    factor_of, own = 1.0, jax.random.fold_in(rng, 6)
    for position, blocks in split:
        steps = jnp.exp(jax.random.uniform(jax.random.fold_in(own, position), (blocks,), jnp.float32, smallest / len(split), high / len(split)))
        factor_of = factor_of * jnp.repeat(steps, extent[position] // blocks).reshape([-1 if axis == position else 1 for axis in range(len(extent))])
    return factor_of


def normal_values(stream_key, shape, spread, reach, pieces=(), dtype=jnp.bfloat16):
    array = spread * jax.random.normal(stream_key, shape, jnp.float32)
    if pieces:
        array = array * shard_levels(stream_key, shape, pieces, -0.22, 0.18)
    return jnp.clip(array, -reach, reach).astype(dtype)


def setup_inputs(seed: int = 0) -> dict:
    key_of = jax.random.split(jax.random.key(seed), 5)
    return {
        "fields_state": normal_values(key_of[0], (FIELDS, NS, NX, NY, Z), 1.0, 6.0, ((0, 4), (2, 16), (3, 4)), jnp.float32),
        "velocity": normal_values(key_of[1], (3, NX, NY, Z), 0.5, 3.0, ((1, 16), (2, 4)), jnp.float32),
        "diffusivity": jnp.clip(jnp.exp(math.log(0.15) - 2.014903 * jax.random.uniform(key_of[2], (NX, NY, Z), jnp.float32) ** shard_levels(key_of[2], (NX, NY, Z), ((0, 16), (1, 4)), -0.2, 0.2)), 0.02, 0.15),
        "wiener_draw": normal_values(key_of[3], (FIELDS, 3), 1.0, 4.0, ((0, 4),), jnp.float32),
    }


time_step = 0.3
mix_rate = 4.0
radiation = 0.5
nucleation = (1.0, 0.8, 0.6, 0.5)
growth_rate = 0.5
oxidation = 0.3

def neighbours_z(values):
    edge = jnp.zeros_like(values[..., :1])
    return (jnp.concatenate([values[..., 1:], edge], -1), jnp.concatenate([edge, values[..., :-1]], -1))

def soot_sources(centre):
    mixture = centre[..., 0, :, :, :]
    enthalpy = centre[..., 1, :, :, :]
    soot_weight = jax.nn.sigmoid(3.0 * enthalpy) * mixture * mixture / (1.0 + mixture * mixture)
    moments = [centre[..., 2 + moment_index, :, :, :] for moment_index in range(4)]
    source_terms = [jnp.zeros_like(mixture), -radiation * soot_weight]
    for moment_index in range(4):
        moment_rate = nucleation[moment_index] * soot_weight - oxidation * moments[moment_index]
        if moment_index > 0:
            moment_rate = moment_rate + growth_rate * soot_weight * moments[moment_index - 1]
        source_terms.append(moment_rate)
    return jnp.stack(source_terms, axis=-4)

def direction_weight(wiener, direction):
    return wiener[..., direction][..., None, None, None, None]

def tendency(padded, coefficients, field_mean, wiener):
    centre = padded[..., 1:-1, 1:-1, :]
    east_side = padded[..., 2:, 1:-1, :]
    west_side = padded[..., :-2, 1:-1, :]
    north_side = padded[..., 1:-1, 2:, :]
    south_side = padded[..., 1:-1, :-2, :]
    upper_side, lower_side = neighbours_z(centre)
    east_speed = coefficients[0, 2:, 1:-1]
    west_speed = coefficients[0, :-2, 1:-1]
    north_speed = coefficients[1, 1:-1, 2:]
    south_speed = coefficients[1, 1:-1, :-2]
    upper_speed, lower_speed = neighbours_z(coefficients[2, 1:-1, 1:-1])
    diffusion = coefficients[3, 1:-1, 1:-1]
    transport = -0.5 * (east_speed * east_side - west_speed * west_side + (north_speed * north_side - south_speed * south_side) + (upper_speed * upper_side - lower_speed * lower_side))
    laplace_sum = east_side + west_side + north_side + south_side + upper_side + lower_side - 6.0 * centre
    stirring = 0.5 * (direction_weight(wiener, 0) * (east_side - west_side) + direction_weight(wiener, 1) * (north_side - south_side) + direction_weight(wiener, 2) * (upper_side - lower_side))
    return transport + diffusion * laplace_sum + jnp.sqrt(2.0 * diffusion / time_step) * stirring - mix_rate * diffusion * (centre - field_mean) + soot_sources(centre)

def reference(fields_state, velocity, diffusivity, wiener_draw):
    coefficients = jnp.concatenate([velocity, diffusivity[None]], 0)
    coef_pad = jnp.pad(coefficients, ((0, 0), (1, 1), (1, 1), (0, 0)))

    def advance(section_now, weight_base, weight_section):
        field_mean = lax.optimization_barrier(jnp.sum(section_now, axis=0)) / FIELDS

        def update_field(members):
            start_field, section_field, wiener = members
            padded = jnp.pad(section_field, ((0, 0), (1, 1), (1, 1), (0, 0)))
            change = tendency(padded, coef_pad, field_mean, wiener)
            return weight_base * start_field + weight_section * (section_field + time_step * change)
        return lax.map(update_field, (fields_state, section_now, wiener_draw))
    first_section = advance(fields_state, 0.0, 1.0)
    second_section = advance(first_section, 0.75, 0.25)
    return advance(second_section, 1.0 / 3.0, 2.0 / 3.0)
```

```python
import functools

import jax
import jax.numpy as jnp
from jax import lax
from jax.experimental import pallas as pl
from jax.experimental.pallas import tpu as pltpu
from jax.sharding import PartitionSpec as P

MESH = pl.DeviceIdType.MESH
F32 = jnp.float32

FIELDS = 32
NS = 6
STEP = 0.3
MIX = 4.0
RADIATION = 0.5
NUCLEATION = (1.0, 0.8, 0.6, 0.5)
GROWTH = 0.5
OXIDATION = 0.3
WEIGHTS = ((0.0, 1.0), (0.75, 0.25), (1.0 / 3.0, 2.0 / 3.0))
EAST, WEST, NORTH, SOUTH, SUM1, SUM2 = range(6)


def sum_rows(tiles):
    row = lax.broadcasted_iota(jnp.int32, (8, 128), 0)
    low = row < 4
    quads = [
        jnp.where(low, tiles[i], tiles[i + 4])
        + pltpu.roll(jnp.where(low, tiles[i + 4], tiles[i]), 4, 0)
        for i in range(4)
    ]
    even = lax.rem(row, 4) < 2
    pairs = [
        jnp.where(even, quads[i], quads[i + 2])
        + jnp.where(even, pltpu.roll(quads[i], 6, 0), pltpu.roll(quads[i + 2], 2, 0))
        for i in range(2)
    ]
    first = lax.rem(row, 2) < 1
    return jnp.where(first, pairs[0], pairs[1]) + jnp.where(
        first, pltpu.roll(pairs[0], 7, 0), pltpu.roll(pairs[1], 1, 0)
    )


def spread(rows, i):
    return jnp.broadcast_to(rows[i : i + 1, :], (8, 128))


def kernel(
    counts,
    fields_hbm,
    velocity_hbm,
    diffusivity_hbm,
    wiener_hbm,
    out_hbm,
    rows_in,
    rows_out,
    p,
    coef,
    centre,
    weight,
    mean_row,
    part,
    part_1,
    half,
    part_2,
    speed_x,
    speed_y,
    speed_z,
    diffusion,
    wiener,
    in_sem,
    out_sem,
    own_sem,
    speed_send,
    speed_recv,
    send_sem,
    recv_sem,
):
    nx, ny, na = counts
    ax, ix, iy = lax.axis_index("af"), lax.axis_index("gx"), lax.axis_index("gy")
    has = {EAST: ix < nx - 1, WEST: ix > 0, NORTH: iy < ny - 1, SOUTH: iy > 0}
    back = {EAST: WEST, WEST: EAST, NORTH: SOUTH, SOUTH: NORTH}
    pair = {SUM1: ax + 1 - 2 * lax.rem(ax, 2), SUM2: na - 1 - ax}
    target = {
        EAST: {"gx": ix + 1},
        WEST: {"gx": ix - 1},
        NORTH: {"gy": iy + 1},
        SOUTH: {"gy": iy - 1},
        SUM1: {"af": pair[SUM1]},
        SUM2: {"af": pair[SUM2]},
    }

    def load_in(s):
        return pltpu.make_async_copy(fields_hbm.at[:, s], rows_in.at[s], in_sem.at[s])

    def store_out(s):
        return pltpu.make_async_copy(rows_out.at[s], out_hbm.at[:, s], out_sem.at[s])

    own = [
        pltpu.make_async_copy(velocity_hbm.at[0], speed_x.at[pl.ds(1, 4)], own_sem.at[0]),
        pltpu.make_async_copy(velocity_hbm.at[1], speed_y.at[:, pl.ds(8, 16)], own_sem.at[1]),
        pltpu.make_async_copy(velocity_hbm.at[2], speed_z, own_sem.at[2]),
        pltpu.make_async_copy(diffusivity_hbm, diffusion, own_sem.at[3]),
        pltpu.make_async_copy(wiener_hbm, wiener, own_sem.at[4]),
    ]

    def speed_face(way):
        src, dst = {
            EAST: (velocity_hbm.at[0, 3], speed_x.at[0]),
            WEST: (velocity_hbm.at[0, 0], speed_x.at[5]),
            NORTH: (velocity_hbm.at[1, :, pl.ds(8, 8)], speed_y.at[:, pl.ds(0, 8)]),
            SOUTH: (velocity_hbm.at[1, :, pl.ds(0, 8)], speed_y.at[:, pl.ds(24, 8)]),
        }[way]
        return pltpu.make_async_remote_copy(
            src_ref=src,
            dst_ref=dst,
            send_sem=speed_send.at[way],
            recv_sem=speed_recv.at[way],
            device_id=target[way],
            device_id_type=MESH,
        )

    def face(k, s, way):
        src, dst = {
            EAST: lambda: (p.at[k, s, 4, pl.ds(1, 16)], p.at[k, s, 0, pl.ds(1, 16)]),
            WEST: lambda: (p.at[k, s, 1, pl.ds(1, 16)], p.at[k, s, 5, pl.ds(1, 16)]),
            NORTH: lambda: (p.at[k, s, pl.ds(1, 4), 16], p.at[k, s, pl.ds(1, 4), 0]),
            SOUTH: lambda: (p.at[k, s, pl.ds(1, 4), 1], p.at[k, s, pl.ds(1, 4), 17]),
            SUM1: lambda: (part.at[k, s], part_1.at[k, s]),
            SUM2: lambda: (half.at[k, s], part_2.at[k, s]),
        }[way]()
        return pltpu.make_async_remote_copy(
            src_ref=src,
            dst_ref=dst,
            send_sem=send_sem.at[k, s, way],
            recv_sem=recv_sem.at[k, s, way],
            device_id=target[way],
            device_id_type=MESH,
        )

    def send(k, s, way):
        pl.when(has[way])(lambda: face(k, s, way).start())

    def arrived(k, s, way):
        pl.when(has[back[way]])(lambda: face(k, s, way).wait_recv())

    def blocks(first, step, count, body):
        def at(i, _):
            body(first + step * (i // 2), lax.rem(i, 2))
            return 0

        lax.fori_loop(0, 2 * count, at, 0)

    load_in(0).start()
    for copy in own:
        copy.start()
    for s in range(1, NS):
        load_in(s).start()

    barrier = pltpu.get_barrier_semaphore()
    expected = 2
    for way in (EAST, WEST, NORTH, SOUTH):
        pl.when(has[way])(
            lambda way=way: pl.semaphore_signal(
                barrier, inc=1, device_id=target[way], device_id_type=MESH
            )
        )
        expected = expected + has[way].astype(jnp.int32)
    for way in (SUM1, SUM2):
        pl.semaphore_signal(barrier, inc=1, device_id=target[way], device_id_type=MESH)

    zero = jnp.zeros((8, 128), F32)

    def clear_x(x, speed):
        def at(i, _):
            for y in range(16):
                p[i // NS, lax.rem(i, NS), x, 1 + y] = zero
            return 0

        lax.fori_loop(0, 3 * NS, at, 0)
        speed_x[speed] = jnp.zeros((16, 128), F32)

    def clear_y(y, speed):
        def at(i, _):
            for x in range(4):
                p[i // NS, lax.rem(i, NS), 1 + x, y] = zero
            return 0

        lax.fori_loop(0, 3 * NS, at, 0)
        for x in range(4):
            speed_y[x, speed : speed + 8] = zero

    pl.when(ix == 0)(lambda: clear_x(0, 0))
    pl.when(ix == nx - 1)(lambda: clear_x(5, 5))
    pl.when(iy == 0)(lambda: clear_y(0, 0))
    pl.when(iy == ny - 1)(lambda: clear_y(17, 24))

    pl.semaphore_wait(barrier, expected)

    def second_exchange(k, s):
        face(k, s, SUM1).wait_recv()
        half[k, s] = part[k, s] + part_1[k, s]
        face(k, s, SUM2).start()

    def mean_term(k, s):
        face(k, s, SUM2).wait_recv()
        mean_row[...] = (STEP * MIX / FIELDS) * diffusion[...] * (half[k, s] + part_2[k, s])

    def turn(s):
        flat = rows_in.reshape(NS * 8 * 64, 128)

        def body(x, h):
            tiles = []
            for i in range(8):
                start = s * 512 + x * 16 + h * 8 + i
                tiles.append(flat[pl.ds(start, 8, stride=64), :])
                p[0, s, x + 1, h * 8 + i + 1] = tiles[-1]
            part[0, s, x, pl.ds(h * 8, 8), :] = sum_rows(tiles)

        return body

    for s in range(NS):
        load_in(s).wait()
        blocks(0, 3, 2, turn(s))
        send(0, s, EAST)
        send(0, s, WEST)
        blocks(1, 1, 2, turn(s))
        send(0, s, NORTH)
        send(0, s, SOUTH)
        face(0, s, SUM1).start()
        if s == 0:
            for way in (EAST, WEST, NORTH, SOUTH):
                pl.when(has[way])(lambda way=way: speed_face(way).start())
        else:
            second_exchange(0, s - 1)

    for copy in own:
        copy.wait()
    for way in (EAST, WEST, NORTH, SOUTH):
        pl.when(has[back[way]])(lambda way=way: speed_face(way).wait_recv())

    draws = [jnp.broadcast_to(wiener[:, d : d + 1], (8, 128)) for d in range(3)]

    def coefficients(x, _):
        g = diffusion[x]
        diffuse = STEP * g
        stir = (0.5 * STEP) * jnp.sqrt((2.0 / STEP) * g)
        lane = lax.broadcasted_iota(jnp.int32, (16, 128), 1)
        upper, lower = lane < 127, lane > 0
        half_step = 0.5 * STEP
        base = [
            diffuse - half_step * speed_x[x + 2],
            diffuse + half_step * speed_x[x],
            diffuse - half_step * speed_y[x, 9:25, :],
            diffuse + half_step * speed_y[x, 7:23, :],
            jnp.where(upper, diffuse - half_step * pltpu.roll(speed_z[x], 127, 1), 0.0),
            jnp.where(lower, diffuse + half_step * pltpu.roll(speed_z[x], 1, 1), 0.0),
        ]
        stir_up, stir_down = jnp.where(upper, stir, 0.0), jnp.where(lower, stir, 0.0)
        keep = 1.0 - (6.0 + MIX) * diffuse
        for y in range(16):
            stir_y = spread(stir, y)
            for d in range(2):
                move = stir_y * draws[d]
                coef[2 * d, x, y] = spread(base[2 * d], y) + move
                coef[2 * d + 1, x, y] = spread(base[2 * d + 1], y) - move
            coef[4, x, y] = spread(base[4], y) + spread(stir_up, y) * draws[2]
            coef[5, x, y] = spread(base[5], y) - spread(stir_down, y) * draws[2]
            keep_y = spread(keep, y)
            centre[0, x, y] = keep_y
            centre[1, x, y] = keep_y - STEP * OXIDATION
        return 0

    lax.fori_loop(0, 4, coefficients, 0)

    def advance(k, s):
        base_weight, section_weight = WEIGHTS[k - 1]
        old = k - 1
        flat = rows_out.reshape(NS * 8 * 64, 128)

        def body(x, h):
            y0 = h * 8
            column = [p[old, s, x + 1, y0 + i] for i in range(10)]
            means = mean_row[x, pl.ds(y0, 8), :]
            tiles = []
            for i in range(8):
                y = y0 + i
                here = column[i + 1]
                new = (
                    centre[int(s >= 2), x, y] * here
                    + spread(means, i)
                    + coef[0, x, y] * p[old, s, x + 2, y + 1]
                    + coef[1, x, y] * p[old, s, x, y + 1]
                    + coef[2, x, y] * column[i + 2]
                    + coef[3, x, y] * column[i]
                    + coef[4, x, y] * pltpu.roll(here, 127, 1)
                    + coef[5, x, y] * pltpu.roll(here, 1, 1)
                )
                if s == 1:
                    mixture = p[old, 0, x + 1, y + 1]
                    square = mixture * mixture
                    w = square / (1.0 + square) / (1.0 + jnp.exp(-3.0 * here))
                    weight[x, y] = w
                    new = new - (STEP * RADIATION) * w
                elif s == 2:
                    new = new + (STEP * NUCLEATION[0]) * weight[x, y]
                elif s > 2:
                    new = new + weight[x, y] * (
                        STEP * NUCLEATION[s - 2] + (STEP * GROWTH) * p[old, s - 1, x + 1, y + 1]
                    )
                if base_weight:
                    new = base_weight * p[0, s, x + 1, y + 1] + section_weight * new
                tiles.append(new)
                if k < 3:
                    p[k, s, x + 1, y + 1] = new
                else:
                    flat[pl.ds(s * 512 + x * 16 + y, 8, stride=64), :] = new
            if k < 3:
                part[k, s, x, pl.ds(y0, 8), :] = sum_rows(tiles)

        return body

    for k in range(1, 4):
        for s in range(NS):
            if s == 0:
                second_exchange(k - 1, NS - 1)
            mean_term(k - 1, s)
            arrived(k - 1, s, NORTH)
            arrived(k - 1, s, SOUTH)
            blocks(1, 1, 2, advance(k, s))
            arrived(k - 1, s, EAST)
            arrived(k - 1, s, WEST)
            blocks(0, 3, 2, advance(k, s))
            if k < 3:
                for way in (EAST, WEST, NORTH, SOUTH):
                    send(k, s, way)
                face(k, s, SUM1).start()
                if s > 0:
                    second_exchange(k, s - 1)
            else:
                store_out(s).start()

    for way in (EAST, WEST, NORTH, SOUTH):
        pl.when(has[way])(lambda way=way: speed_face(way).wait_send())
        for k in range(3):
            for s in range(NS):
                pl.when(has[way])(lambda k=k, s=s, way=way: face(k, s, way).wait_send())
    for k in range(3):
        for s in range(NS):
            face(k, s, SUM1).wait_send()
            face(k, s, SUM2).wait_send()
    for s in range(NS):
        store_out(s).wait()


def local(fields_state, velocity, diffusivity, wiener_draw):
    counts = tuple(lax.axis_size(name) for name in ("gx", "gy", "af"))
    held = fields_state.shape
    dma = pltpu.SemaphoreType.DMA
    vmem = lambda *shape: pltpu.VMEM(shape, F32)
    out = pl.pallas_call(
        functools.partial(kernel, counts),
        out_shape=jax.ShapeDtypeStruct((8, NS, 64, 128), F32),
        in_specs=[pl.BlockSpec(memory_space=pl.ANY)] * 4,
        out_specs=pl.BlockSpec(memory_space=pl.ANY),
        scratch_shapes=[
            vmem(NS, 8, 64, 128),
            vmem(NS, 8, 64, 128),
            vmem(3, NS, 6, 18, 8, 128),
            vmem(6, 4, 16, 8, 128),
            vmem(2, 4, 16, 8, 128),
            vmem(4, 16, 8, 128),
            vmem(4, 16, 128),
            vmem(3, NS, 4, 16, 128),
            vmem(3, NS, 4, 16, 128),
            vmem(3, NS, 4, 16, 128),
            vmem(3, NS, 4, 16, 128),
            vmem(6, 16, 128),
            vmem(4, 32, 128),
            vmem(4, 16, 128),
            vmem(4, 16, 128),
            vmem(8, 3),
            dma((NS,)),
            dma((NS,)),
            dma((5,)),
            dma((4,)),
            dma((4,)),
            dma((3, NS, 6)),
            dma((3, NS, 6)),
        ],
        compiler_params=pltpu.CompilerParams(
            collective_id=0, has_side_effects=True, vmem_limit_bytes=48 * 1024 * 1024
        ),
    )(fields_state.reshape(8, NS, 64, 128), velocity, diffusivity, wiener_draw)
    return out.reshape(held)


def solution(mesh):
    return jax.shard_map(
        local,
        mesh=mesh,
        in_specs=(
            P("af", None, "gx", "gy", None),
            P(None, "gx", "gy", None),
            P("gx", "gy", None),
            P("af", None),
        ),
        out_specs=P("af", None, "gx", "gy", None),
        check_vma=False,
    )
```

```python
import functools

import jax
import jax.numpy as jnp
from jax import lax
from jax.experimental import pallas as pl
from jax.experimental.pallas import tpu as pltpu
from jax.sharding import PartitionSpec as P

MESH = pl.DeviceIdType.MESH
F32 = jnp.float32

FIELDS = 32
NS = 6
PAIRS = 3
STEP = 0.3
MIX = 4.0
RADIATION = 0.5
NUCLEATION = (1.0, 0.8, 0.6, 0.5)
GROWTH = 0.5
OXIDATION = 0.3
WEIGHTS = ((0.0, 1.0), (0.75, 0.25), (1.0 / 3.0, 2.0 / 3.0))
EAST, WEST, NORTH, SOUTH, SUM1, SUM2 = range(6)


def sum_rows(tiles):
    row = lax.broadcasted_iota(jnp.int32, (8, 128), 0)
    low = row < 4
    quads = [
        jnp.where(low, tiles[i], tiles[i + 4])
        + pltpu.roll(jnp.where(low, tiles[i + 4], tiles[i]), 4, 0)
        for i in range(4)
    ]
    even = lax.rem(row, 4) < 2
    pairs = [
        jnp.where(even, quads[i], quads[i + 2])
        + jnp.where(even, pltpu.roll(quads[i], 6, 0), pltpu.roll(quads[i + 2], 2, 0))
        for i in range(2)
    ]
    first = lax.rem(row, 2) < 1
    return jnp.where(first, pairs[0], pairs[1]) + jnp.where(
        first, pltpu.roll(pairs[0], 7, 0), pltpu.roll(pairs[1], 1, 0)
    )


def spread(rows, i):
    return jnp.broadcast_to(rows[i : i + 1, :], (8, 128))


def kernel(
    counts,
    fields_hbm,
    velocity_hbm,
    diffusivity_hbm,
    wiener_hbm,
    out_hbm,
    rows_in,
    rows_out,
    p,
    coef,
    centre,
    weight,
    mean_row,
    part,
    part_1,
    half,
    part_2,
    speed_x,
    speed_y,
    speed_z,
    diffusion,
    wiener,
    in_sem,
    out_sem,
    own_sem,
    speed_send,
    speed_recv,
    send_sem,
    recv_sem,
):
    nx, ny, na = counts
    ax, ix, iy = lax.axis_index("af"), lax.axis_index("gx"), lax.axis_index("gy")
    has = {EAST: ix < nx - 1, WEST: ix > 0, NORTH: iy < ny - 1, SOUTH: iy > 0}
    back = {EAST: WEST, WEST: EAST, NORTH: SOUTH, SOUTH: NORTH}
    pair = {SUM1: ax + 1 - 2 * lax.rem(ax, 2), SUM2: na - 1 - ax}
    target = {
        EAST: {"gx": ix + 1},
        WEST: {"gx": ix - 1},
        NORTH: {"gy": iy + 1},
        SOUTH: {"gy": iy - 1},
        SUM1: {"af": pair[SUM1]},
        SUM2: {"af": pair[SUM2]},
    }

    def load_in(s):
        return pltpu.make_async_copy(fields_hbm.at[:, s], rows_in.at[s], in_sem.at[s])

    def store_out(s):
        return pltpu.make_async_copy(rows_out.at[s], out_hbm.at[:, s], out_sem.at[s])

    def two(c):
        return pl.ds(2 * c, 2)

    own = [
        pltpu.make_async_copy(velocity_hbm.at[0], speed_x.at[pl.ds(1, 4)], own_sem.at[0]),
        pltpu.make_async_copy(velocity_hbm.at[1], speed_y.at[:, pl.ds(8, 16)], own_sem.at[1]),
        pltpu.make_async_copy(velocity_hbm.at[2], speed_z, own_sem.at[2]),
        pltpu.make_async_copy(diffusivity_hbm, diffusion, own_sem.at[3]),
        pltpu.make_async_copy(wiener_hbm, wiener, own_sem.at[4]),
    ]

    def speed_face(way):
        src, dst = {
            EAST: (velocity_hbm.at[0, 3], speed_x.at[0]),
            WEST: (velocity_hbm.at[0, 0], speed_x.at[5]),
            NORTH: (velocity_hbm.at[1, :, pl.ds(8, 8)], speed_y.at[:, pl.ds(0, 8)]),
            SOUTH: (velocity_hbm.at[1, :, pl.ds(0, 8)], speed_y.at[:, pl.ds(24, 8)]),
        }[way]
        return pltpu.make_async_remote_copy(
            src_ref=src,
            dst_ref=dst,
            send_sem=speed_send.at[way],
            recv_sem=speed_recv.at[way],
            device_id=target[way],
            device_id_type=MESH,
        )

    def face(k, s, way, recv=None):
        src, dst = {
            EAST: lambda: (p.at[k, s, 4, pl.ds(1, 16)], p.at[k, s, 0, pl.ds(1, 16)]),
            WEST: lambda: (p.at[k, s, 1, pl.ds(1, 16)], p.at[k, s, 5, pl.ds(1, 16)]),
            NORTH: lambda: (p.at[k, s, pl.ds(1, 4), 16], p.at[k, s, pl.ds(1, 4), 0]),
            SOUTH: lambda: (p.at[k, s, pl.ds(1, 4), 1], p.at[k, s, pl.ds(1, 4), 17]),
            SUM1: lambda: (part.at[k, s], part_1.at[k, s]),
            SUM2: lambda: (half.at[k, s], part_2.at[k, s]),
        }[way]()
        return pltpu.make_async_remote_copy(
            src_ref=src,
            dst_ref=dst,
            send_sem=send_sem.at[way],
            recv_sem=recv,
            device_id=target[way],
            device_id_type=MESH,
        )

    def chunk(k, c, way):
        return face(k, two(c), way, recv_sem.at[k, c, way])

    def all_sent(way):
        face(pl.ds(0, 3), pl.ds(0, NS), way, recv_sem.at[0, 0, way]).wait_send()

    def send(k, c, way):
        pl.when(has[way])(lambda: chunk(k, c, way).start())

    def arrived(k, c, way):
        pl.when(has[back[way]])(lambda: chunk(k, c, way).wait_recv())

    def blocks(first, step, count, body):
        def at(i, _):
            body(first + step * (i // 2), lax.rem(i, 2))
            return 0

        lax.fori_loop(0, 2 * count, at, 0)

    load_in(0).start()
    for copy in own:
        copy.start()
    for s in range(1, NS):
        load_in(s).start()

    barrier = pltpu.get_barrier_semaphore()
    expected = 2
    for way in (EAST, WEST, NORTH, SOUTH):
        pl.when(has[way])(
            lambda way=way: pl.semaphore_signal(
                barrier, inc=1, device_id=target[way], device_id_type=MESH
            )
        )
        expected = expected + has[way].astype(jnp.int32)
    for way in (SUM1, SUM2):
        pl.semaphore_signal(barrier, inc=1, device_id=target[way], device_id_type=MESH)

    zero = jnp.zeros((8, 128), F32)

    def clear_x(x, speed):
        def at(i, _):
            for y in range(16):
                p[i // NS, lax.rem(i, NS), x, 1 + y] = zero
            return 0

        lax.fori_loop(0, 3 * NS, at, 0)
        speed_x[speed] = jnp.zeros((16, 128), F32)

    def clear_y(y, speed):
        def at(i, _):
            for x in range(4):
                p[i // NS, lax.rem(i, NS), 1 + x, y] = zero
            return 0

        lax.fori_loop(0, 3 * NS, at, 0)
        for x in range(4):
            speed_y[x, speed : speed + 8] = zero

    pl.when(ix == 0)(lambda: clear_x(0, 0))
    pl.when(ix == nx - 1)(lambda: clear_x(5, 5))
    pl.when(iy == 0)(lambda: clear_y(0, 0))
    pl.when(iy == ny - 1)(lambda: clear_y(17, 24))

    pl.semaphore_wait(barrier, expected)

    def second_exchange(k, c):
        chunk(k, c, SUM1).wait_recv()
        half[k, two(c)] = part[k, two(c)] + part_1[k, two(c)]
        chunk(k, c, SUM2).start()

    def mean_term(k, c):
        chunk(k, c, SUM2).wait_recv()
        scale = (STEP * MIX / FIELDS) * diffusion[...]
        for i in range(2):
            mean_row[i] = scale * (half[k, 2 * c + i] + part_2[k, 2 * c + i])

    def turn(s):
        flat = rows_in.reshape(NS * 8 * 64, 128)

        def body(x, h):
            tiles = []
            for i in range(8):
                start = s * 512 + x * 16 + h * 8 + i
                tiles.append(flat[pl.ds(start, 8, stride=64), :])
                p[0, s, x + 1, h * 8 + i + 1] = tiles[-1]
            part[0, s, x, pl.ds(h * 8, 8), :] = sum_rows(tiles)

        return body

    for c in range(PAIRS):
        for s in (2 * c, 2 * c + 1):
            load_in(s).wait()
            blocks(0, 3, 2, turn(s))
        send(0, c, EAST)
        send(0, c, WEST)
        for s in (2 * c, 2 * c + 1):
            blocks(1, 1, 2, turn(s))
        send(0, c, NORTH)
        send(0, c, SOUTH)
        chunk(0, c, SUM1).start()
        if c == 0:
            for way in (EAST, WEST, NORTH, SOUTH):
                pl.when(has[way])(lambda way=way: speed_face(way).start())
        else:
            second_exchange(0, c - 1)

    for copy in own:
        copy.wait()
    for way in (EAST, WEST, NORTH, SOUTH):
        pl.when(has[back[way]])(lambda way=way: speed_face(way).wait_recv())

    diagonal = lax.broadcasted_iota(jnp.int32, (8, 8), 0) == lax.broadcasted_iota(
        jnp.int32, (8, 8), 1
    )
    draws = []
    for d in range(3):
        row = jnp.broadcast_to(wiener[d : d + 1, :], (8, 8))
        column = jnp.sum(jnp.where(diagonal, row, 0.0), axis=1, keepdims=True)
        draws.append(jnp.broadcast_to(column, (8, 128)))

    def coefficients(x, _):
        g = diffusion[x]
        diffuse = STEP * g
        stir = (0.5 * STEP) * jnp.sqrt((2.0 / STEP) * g)
        lane = lax.broadcasted_iota(jnp.int32, (16, 128), 1)
        upper, lower = lane < 127, lane > 0
        half_step = 0.5 * STEP
        base = [
            diffuse - half_step * speed_x[x + 2],
            diffuse + half_step * speed_x[x],
            diffuse - half_step * speed_y[x, 9:25, :],
            diffuse + half_step * speed_y[x, 7:23, :],
            jnp.where(upper, diffuse - half_step * pltpu.roll(speed_z[x], 127, 1), 0.0),
            jnp.where(lower, diffuse + half_step * pltpu.roll(speed_z[x], 1, 1), 0.0),
        ]
        stir_up, stir_down = jnp.where(upper, stir, 0.0), jnp.where(lower, stir, 0.0)
        keep = 1.0 - (6.0 + MIX) * diffuse
        for y in range(16):
            stir_y = spread(stir, y)
            for d in range(2):
                move = stir_y * draws[d]
                coef[2 * d, x, y] = spread(base[2 * d], y) + move
                coef[2 * d + 1, x, y] = spread(base[2 * d + 1], y) - move
            coef[4, x, y] = spread(base[4], y) + spread(stir_up, y) * draws[2]
            coef[5, x, y] = spread(base[5], y) - spread(stir_down, y) * draws[2]
            keep_y = spread(keep, y)
            centre[0, x, y] = keep_y
            centre[1, x, y] = keep_y - STEP * OXIDATION
        return 0

    lax.fori_loop(0, 4, coefficients, 0)

    def advance(k, c):
        base_weight, section_weight = WEIGHTS[k - 1]
        old = k - 1
        flat = rows_out.reshape(NS * 8 * 64, 128)

        def body(x, h):
            y0 = h * 8
            tiles = [[], []]
            columns = [[p[old, 2 * c + j, x + 1, y0 + i] for i in range(10)] for j in range(2)]
            means = [mean_row[j, x, pl.ds(y0, 8), :] for j in range(2)]
            for i in range(8):
                y = y0 + i
                factor = [coef[d, x, y] for d in range(6)]
                keep = centre[int(c > 0), x, y]
                here = [columns[j][i + 1] for j in range(2)]
                new = [
                    keep * here[j]
                    + spread(means[j], i)
                    + factor[0] * p[old, 2 * c + j, x + 2, y + 1]
                    + factor[1] * p[old, 2 * c + j, x, y + 1]
                    + factor[2] * columns[j][i + 2]
                    + factor[3] * columns[j][i]
                    + factor[4] * pltpu.roll(here[j], 127, 1)
                    + factor[5] * pltpu.roll(here[j], 1, 1)
                    for j in range(2)
                ]
                if c == 0:
                    square = here[0] * here[0]
                    w = square / (1.0 + square) / (1.0 + jnp.exp(-3.0 * here[1]))
                    weight[x, y] = w
                    new[1] = new[1] - (STEP * RADIATION) * w
                else:
                    w = weight[x, y]
                    before = [p[old, 3, x + 1, y + 1] if c == 2 else None, here[0]]
                    for j in range(2):
                        gain = STEP * NUCLEATION[2 * c - 2 + j]
                        if before[j] is not None:
                            gain = gain + (STEP * GROWTH) * before[j]
                        new[j] = new[j] + w * gain
                for j in range(2):
                    s = 2 * c + j
                    if base_weight:
                        new[j] = base_weight * p[0, s, x + 1, y + 1] + section_weight * new[j]
                    tiles[j].append(new[j])
                    if k < 3:
                        p[k, s, x + 1, y + 1] = new[j]
                    else:
                        flat[pl.ds(s * 512 + x * 16 + y, 8, stride=64), :] = new[j]
            if k < 3:
                for j in range(2):
                    part[k, 2 * c + j, x, pl.ds(y0, 8), :] = sum_rows(tiles[j])

        return body

    for k in range(1, 4):
        for c in range(PAIRS):
            if c == 0:
                second_exchange(k - 1, PAIRS - 1)
            mean_term(k - 1, c)
            arrived(k - 1, c, NORTH)
            arrived(k - 1, c, SOUTH)
            blocks(1, 1, 2, advance(k, c))
            arrived(k - 1, c, EAST)
            arrived(k - 1, c, WEST)
            blocks(0, 3, 2, advance(k, c))
            if k < 3:
                for way in (EAST, WEST, NORTH, SOUTH):
                    send(k, c, way)
                chunk(k, c, SUM1).start()
                if c > 0:
                    second_exchange(k, c - 1)
            else:
                store_out(2 * c).start()
                store_out(2 * c + 1).start()

    for way in (EAST, WEST, NORTH, SOUTH):
        pl.when(has[way])(lambda way=way: speed_face(way).wait_send())
        pl.when(has[way])(lambda way=way: all_sent(way))
    all_sent(SUM1)
    all_sent(SUM2)
    for s in range(NS):
        store_out(s).wait()


def local(fields_state, velocity, diffusivity, wiener_draw):
    counts = tuple(lax.axis_size(name) for name in ("gx", "gy", "af"))
    held = fields_state.shape
    dma = pltpu.SemaphoreType.DMA
    vmem = lambda *shape: pltpu.VMEM(shape, F32)
    out = pl.pallas_call(
        functools.partial(kernel, counts),
        out_shape=jax.ShapeDtypeStruct((8, NS, 64, 128), F32),
        in_specs=[pl.BlockSpec(memory_space=pl.ANY)] * 4,
        out_specs=pl.BlockSpec(memory_space=pl.ANY),
        scratch_shapes=[
            vmem(NS, 8, 64, 128),
            vmem(NS, 8, 64, 128),
            vmem(3, NS, 6, 18, 8, 128),
            vmem(6, 4, 16, 8, 128),
            vmem(2, 4, 16, 8, 128),
            vmem(4, 16, 8, 128),
            vmem(2, 4, 16, 128),
            vmem(3, NS, 4, 16, 128),
            vmem(3, NS, 4, 16, 128),
            vmem(3, NS, 4, 16, 128),
            vmem(3, NS, 4, 16, 128),
            vmem(6, 16, 128),
            vmem(4, 32, 128),
            vmem(4, 16, 128),
            vmem(4, 16, 128),
            vmem(3, 8),
            dma((NS,)),
            dma((NS,)),
            dma((5,)),
            dma((4,)),
            dma((4,)),
            dma((6,)),
            dma((3, PAIRS, 6)),
        ],
        compiler_params=pltpu.CompilerParams(
            collective_id=0, has_side_effects=True, vmem_limit_bytes=62 * 1024 * 1024
        ),
    )(fields_state.reshape(8, NS, 64, 128), velocity, diffusivity, wiener_draw.T)
    return out.reshape(held)


def solution(mesh):
    return jax.shard_map(
        local,
        mesh=mesh,
        in_specs=(
            P("af", None, "gx", "gy", None),
            P(None, "gx", "gy", None),
            P("gx", "gy", None),
            P("af", None),
        ),
        out_specs=P("af", None, "gx", "gy", None),
        check_vma=False,
    )
```

```python
import functools

import jax
import jax.numpy as jnp
from jax import lax
from jax.experimental import pallas as pl
from jax.experimental.pallas import tpu as pltpu
from jax.sharding import PartitionSpec as P

MESH = pl.DeviceIdType.MESH
F32 = jnp.float32

FIELDS = 32
NS = 6
PAIRS = 3
STEP = 0.3
MIX = 4.0
RADIATION = 0.5
NUCLEATION = (1.0, 0.8, 0.6, 0.5)
GROWTH = 0.5
OXIDATION = 0.3
WEIGHTS = ((0.0, 1.0), (0.75, 0.25), (1.0 / 3.0, 2.0 / 3.0))
EAST, WEST, NORTH, SOUTH, SUM1, SUM2 = range(6)


def sum_rows(tiles):
    row = lax.broadcasted_iota(jnp.int32, (8, 128), 0)
    low = row < 4
    quads = [
        jnp.where(low, tiles[i], tiles[i + 4])
        + pltpu.roll(jnp.where(low, tiles[i + 4], tiles[i]), 4, 0)
        for i in range(4)
    ]
    even = lax.rem(row, 4) < 2
    pairs = [
        jnp.where(even, quads[i], quads[i + 2])
        + jnp.where(even, pltpu.roll(quads[i], 6, 0), pltpu.roll(quads[i + 2], 2, 0))
        for i in range(2)
    ]
    first = lax.rem(row, 2) < 1
    return jnp.where(first, pairs[0], pairs[1]) + jnp.where(
        first, pltpu.roll(pairs[0], 7, 0), pltpu.roll(pairs[1], 1, 0)
    )


def spread(rows, i):
    return jnp.broadcast_to(rows[i : i + 1, :], (8, 128))


def kernel(
    counts,
    fields_hbm,
    velocity_hbm,
    diffusivity_hbm,
    wiener_hbm,
    out,
    rows_in,
    p,
    coef,
    centre,
    weight,
    mean_row,
    part,
    part_1,
    half,
    part_2,
    speed_x,
    speed_y,
    speed_z,
    diffusion,
    wiener,
    relay,
    in_sem,
    own_sem,
    relay_send,
    relay_recv,
    speed_send,
    speed_recv,
    send_sem,
    recv_sem,
):
    nx, ny, na = counts
    ax, ix, iy = lax.axis_index("af"), lax.axis_index("gx"), lax.axis_index("gy")
    has = {EAST: ix < nx - 1, WEST: ix > 0, NORTH: iy < ny - 1, SOUTH: iy > 0}
    back = {EAST: WEST, WEST: EAST, NORTH: SOUTH, SOUTH: NORTH}
    pair = {SUM1: ax + 1 - 2 * lax.rem(ax, 2), SUM2: na - 1 - ax}
    target = {
        EAST: {"gx": ix + 1},
        WEST: {"gx": ix - 1},
        NORTH: {"gy": iy + 1},
        SOUTH: {"gy": iy - 1},
        SUM1: {"af": pair[SUM1]},
        SUM2: {"af": pair[SUM2]},
    }

    mid, end = nx // 2, nx - 1
    to_relay = {EAST: ix == mid - 1, WEST: ix == mid}
    is_relay = {EAST: ix == end, WEST: ix == 0}
    relay_of = {EAST: {"gx": end}, WEST: {"gx": 0}}
    relay_to = {EAST: {"gx": mid}, WEST: {"gx": mid - 1}}

    def load_in(s):
        return pltpu.make_async_copy(fields_hbm.at[:, s], rows_in.at[s], in_sem.at[s])

    def two(c):
        return pl.ds(2 * c, 2)

    own = [
        pltpu.make_async_copy(velocity_hbm.at[0], speed_x.at[pl.ds(1, 4)], own_sem.at[0]),
        pltpu.make_async_copy(velocity_hbm.at[1], speed_y.at[:, pl.ds(8, 16)], own_sem.at[1]),
        pltpu.make_async_copy(velocity_hbm.at[2], speed_z, own_sem.at[2]),
        pltpu.make_async_copy(diffusivity_hbm, diffusion, own_sem.at[3]),
        pltpu.make_async_copy(wiener_hbm, wiener, own_sem.at[4]),
    ]

    def speed_face(way):
        src, dst = {
            EAST: (velocity_hbm.at[0, 3], speed_x.at[0]),
            WEST: (velocity_hbm.at[0, 0], speed_x.at[5]),
            NORTH: (velocity_hbm.at[1, :, pl.ds(8, 8)], speed_y.at[:, pl.ds(0, 8)]),
            SOUTH: (velocity_hbm.at[1, :, pl.ds(0, 8)], speed_y.at[:, pl.ds(24, 8)]),
        }[way]
        return pltpu.make_async_remote_copy(
            src_ref=src,
            dst_ref=dst,
            send_sem=speed_send.at[way],
            recv_sem=speed_recv.at[way],
            device_id=target[way],
            device_id_type=MESH,
        )

    def face(k, s, way, recv=None):
        src, dst = {
            EAST: lambda: (p.at[k, s, 4, pl.ds(1, 16)], p.at[k, s, 0, pl.ds(1, 16)]),
            WEST: lambda: (p.at[k, s, 1, pl.ds(1, 16)], p.at[k, s, 5, pl.ds(1, 16)]),
            NORTH: lambda: (p.at[k, s, pl.ds(1, 4), 16], p.at[k, s, pl.ds(1, 4), 0]),
            SOUTH: lambda: (p.at[k, s, pl.ds(1, 4), 1], p.at[k, s, pl.ds(1, 4), 17]),
            SUM1: lambda: (part.at[k, s], part_1.at[k, s]),
            SUM2: lambda: (half.at[k, s], part_2.at[k, s]),
        }[way]()
        return pltpu.make_async_remote_copy(
            src_ref=src,
            dst_ref=dst,
            send_sem=send_sem.at[way],
            recv_sem=recv,
            device_id=target[way],
            device_id_type=MESH,
        )

    def chunk(k, c, way):
        return face(k, two(c), way, recv_sem.at[k, c, way])

    def all_sent(way):
        face(pl.ds(0, 3), pl.ds(0, NS), way, recv_sem.at[0, 0, way]).wait_send()

    def send(k, c, way):
        if way not in to_relay:
            pl.when(has[way])(lambda: chunk(k, c, way).start())
            return

        @pl.when(has[way] & jnp.logical_not(to_relay[way]))
        def _():
            chunk(k, c, way).start()

        @pl.when(to_relay[way])
        def _():
            pltpu.make_async_remote_copy(
                src_ref=p.at[k, 2 * c + 1, 4 if way == EAST else 1, pl.ds(1, 16)],
                dst_ref=relay.at[k, c],
                send_sem=send_sem.at[way],
                recv_sem=relay_recv.at[k, c],
                device_id=relay_of[way],
                device_id_type=MESH,
            ).start()
            face(k, pl.ds(2 * c, 1), way, recv_sem.at[k, c, way]).start()

    def passed_on(k, c, way):
        return pltpu.make_async_remote_copy(
            src_ref=relay.at[k, c],
            dst_ref=p.at[k, 2 * c + 1, 0 if way == EAST else 5, pl.ds(1, 16)],
            send_sem=relay_send,
            recv_sem=recv_sem.at[k, c, way],
            device_id=relay_to[way],
            device_id_type=MESH,
        )

    def pass_on(k, c):
        for way in (EAST, WEST):

            @pl.when(is_relay[way])
            def _():
                pltpu.make_async_copy(relay.at[k, c], relay.at[k, c], relay_recv.at[k, c]).wait()
                passed_on(k, c, way).start()

    def all_passed_on():
        for way in (EAST, WEST):

            @pl.when(is_relay[way])
            def _():
                pltpu.make_async_copy(relay, relay, relay_send).wait()

    def arrived(k, c, way):
        pl.when(has[back[way]])(lambda: chunk(k, c, way).wait_recv())

    def blocks(first, step, count, body):
        def at(i, _):
            body(first + step * (i // 2), lax.rem(i, 2))
            return 0

        lax.fori_loop(0, 2 * count, at, 0)

    load_in(0).start()
    for copy in own:
        copy.start()
    for s in range(1, NS):
        load_in(s).start()

    barrier = pltpu.get_barrier_semaphore()
    expected = 2
    for way in (EAST, WEST, NORTH, SOUTH):
        pl.when(has[way])(
            lambda way=way: pl.semaphore_signal(
                barrier, inc=1, device_id=target[way], device_id_type=MESH
            )
        )
        expected = expected + has[way].astype(jnp.int32)
    for way in (EAST, WEST):
        for near, partners in (
            (to_relay[way], ({"gx": 0}, {"gx": end})),
            (is_relay[way], ({"gx": mid - 1}, {"gx": mid})),
        ):
            expected = expected + 2 * near.astype(jnp.int32)

            @pl.when(near)
            def _(partners=partners):
                for partner in partners:
                    pl.semaphore_signal(barrier, inc=1, device_id=partner, device_id_type=MESH)

    for way in (SUM1, SUM2):
        pl.semaphore_signal(barrier, inc=1, device_id=target[way], device_id_type=MESH)

    zero = jnp.zeros((8, 128), F32)

    def clear_x(x, speed):
        def at(i, _):
            for y in range(16):
                p[i // NS, lax.rem(i, NS), x, 1 + y] = zero
            return 0

        lax.fori_loop(0, 3 * NS, at, 0)
        speed_x[speed] = jnp.zeros((16, 128), F32)

    def clear_y(y, speed):
        def at(i, _):
            for x in range(4):
                p[i // NS, lax.rem(i, NS), 1 + x, y] = zero
            return 0

        lax.fori_loop(0, 3 * NS, at, 0)
        for x in range(4):
            speed_y[x, speed : speed + 8] = zero

    pl.when(ix == 0)(lambda: clear_x(0, 0))
    pl.when(ix == nx - 1)(lambda: clear_x(5, 5))
    pl.when(iy == 0)(lambda: clear_y(0, 0))
    pl.when(iy == ny - 1)(lambda: clear_y(17, 24))

    pl.semaphore_wait(barrier, expected)

    def second_exchange(k, c):
        chunk(k, c, SUM1).wait_recv()
        half[k, two(c)] = part[k, two(c)] + part_1[k, two(c)]
        chunk(k, c, SUM2).start()

    def mean_term(k, c):
        chunk(k, c, SUM2).wait_recv()
        scale = (STEP * MIX / FIELDS) * diffusion[...]
        for i in range(2):
            mean_row[i] = scale * (half[k, 2 * c + i] + part_2[k, 2 * c + i])

    def turn(s):
        flat = rows_in.reshape(NS * 8 * 64, 128)

        def body(x, h):
            tiles = []
            for i in range(8):
                start = s * 512 + x * 16 + h * 8 + i
                tiles.append(flat[pl.ds(start, 8, stride=64), :])
                p[0, s, x + 1, h * 8 + i + 1] = tiles[-1]
            part[0, s, x, pl.ds(h * 8, 8), :] = sum_rows(tiles)

        return body

    for c in range(PAIRS):
        for s in (2 * c, 2 * c + 1):
            load_in(s).wait()
            blocks(0, 3, 2, turn(s))
        send(0, c, EAST)
        send(0, c, WEST)
        for s in (2 * c, 2 * c + 1):
            blocks(1, 1, 2, turn(s))
        send(0, c, NORTH)
        send(0, c, SOUTH)
        chunk(0, c, SUM1).start()
        if c == 0:
            for way in (EAST, WEST, NORTH, SOUTH):
                pl.when(has[way])(lambda way=way: speed_face(way).start())
        else:
            pass_on(0, c - 1)
            second_exchange(0, c - 1)

    for copy in own:
        copy.wait()
    for way in (EAST, WEST, NORTH, SOUTH):
        pl.when(has[back[way]])(lambda way=way: speed_face(way).wait_recv())

    diagonal = lax.broadcasted_iota(jnp.int32, (8, 8), 0) == lax.broadcasted_iota(
        jnp.int32, (8, 8), 1
    )
    draws = []
    for d in range(3):
        row = jnp.broadcast_to(wiener[d : d + 1, :], (8, 8))
        column = jnp.sum(jnp.where(diagonal, row, 0.0), axis=1, keepdims=True)
        draws.append(jnp.broadcast_to(column, (8, 128)))

    def coefficients(x, _):
        g = diffusion[x]
        diffuse = STEP * g
        stir = (0.5 * STEP) * jnp.sqrt((2.0 / STEP) * g)
        lane = lax.broadcasted_iota(jnp.int32, (16, 128), 1)
        upper, lower = lane < 127, lane > 0
        half_step = 0.5 * STEP
        base = [
            diffuse - half_step * speed_x[x + 2],
            diffuse + half_step * speed_x[x],
            diffuse - half_step * speed_y[x, 9:25, :],
            diffuse + half_step * speed_y[x, 7:23, :],
            jnp.where(upper, diffuse - half_step * pltpu.roll(speed_z[x], 127, 1), 0.0),
            jnp.where(lower, diffuse + half_step * pltpu.roll(speed_z[x], 1, 1), 0.0),
        ]
        stir_up, stir_down = jnp.where(upper, stir, 0.0), jnp.where(lower, stir, 0.0)
        keep = 1.0 - (6.0 + MIX) * diffuse
        for y in range(16):
            stir_y = spread(stir, y)
            for d in range(2):
                move = stir_y * draws[d]
                coef[2 * d, x, y] = spread(base[2 * d], y) + move
                coef[2 * d + 1, x, y] = spread(base[2 * d + 1], y) - move
            coef[4, x, y] = spread(base[4], y) + spread(stir_up, y) * draws[2]
            coef[5, x, y] = spread(base[5], y) - spread(stir_down, y) * draws[2]
            keep_y = spread(keep, y)
            centre[0, x, y] = keep_y
            centre[1, x, y] = keep_y - STEP * OXIDATION
        return 0

    lax.fori_loop(0, 4, coefficients, 0)

    def advance(k, c):
        base_weight, section_weight = WEIGHTS[k - 1]
        old = k - 1
        flat = out.reshape(8 * NS * 64, 128)

        def body(x, h):
            y0 = h * 8
            tiles = [[], []]
            columns = [[p[old, 2 * c + j, x + 1, y0 + i] for i in range(10)] for j in range(2)]
            means = [mean_row[j, x, pl.ds(y0, 8), :] for j in range(2)]
            for i in range(8):
                y = y0 + i
                factor = [coef[d, x, y] for d in range(6)]
                keep = centre[int(c > 0), x, y]
                here = [columns[j][i + 1] for j in range(2)]
                new = [
                    keep * here[j]
                    + spread(means[j], i)
                    + factor[0] * p[old, 2 * c + j, x + 2, y + 1]
                    + factor[1] * p[old, 2 * c + j, x, y + 1]
                    + factor[2] * columns[j][i + 2]
                    + factor[3] * columns[j][i]
                    + factor[4] * pltpu.roll(here[j], 127, 1)
                    + factor[5] * pltpu.roll(here[j], 1, 1)
                    for j in range(2)
                ]
                if c == 0:
                    square = here[0] * here[0]
                    w = square / (1.0 + square) / (1.0 + jnp.exp(-3.0 * here[1]))
                    weight[x, y] = w
                    new[1] = new[1] - (STEP * RADIATION) * w
                else:
                    w = weight[x, y]
                    before = [p[old, 3, x + 1, y + 1] if c == 2 else None, here[0]]
                    for j in range(2):
                        gain = STEP * NUCLEATION[2 * c - 2 + j]
                        if before[j] is not None:
                            gain = gain + (STEP * GROWTH) * before[j]
                        new[j] = new[j] + w * gain
                for j in range(2):
                    s = 2 * c + j
                    if base_weight:
                        new[j] = base_weight * p[0, s, x + 1, y + 1] + section_weight * new[j]
                    tiles[j].append(new[j])
                    if k < 3:
                        p[k, s, x + 1, y + 1] = new[j]
                    else:
                        flat[pl.ds(s * 64 + x * 16 + y, 8, stride=NS * 64), :] = new[j]
            if k < 3:
                for j in range(2):
                    part[k, 2 * c + j, x, pl.ds(y0, 8), :] = sum_rows(tiles[j])

        return body

    for k in range(1, 4):
        for c in range(PAIRS):
            if c == 0:
                pass_on(k - 1, PAIRS - 1)
                second_exchange(k - 1, PAIRS - 1)
            mean_term(k - 1, c)
            arrived(k - 1, c, NORTH)
            arrived(k - 1, c, SOUTH)
            blocks(1, 1, 2, advance(k, c))
            arrived(k - 1, c, EAST)
            arrived(k - 1, c, WEST)
            blocks(0, 3, 2, advance(k, c))
            if k < 3:
                for way in (EAST, WEST, NORTH, SOUTH):
                    send(k, c, way)
                chunk(k, c, SUM1).start()
                if c > 0:
                    pass_on(k, c - 1)
                    second_exchange(k, c - 1)

    for way in (EAST, WEST, NORTH, SOUTH):
        pl.when(has[way])(lambda way=way: speed_face(way).wait_send())
        pl.when(has[way])(lambda way=way: all_sent(way))
    all_passed_on()
    all_sent(SUM1)
    all_sent(SUM2)


def local(fields_state, velocity, diffusivity, wiener_draw):
    counts = tuple(lax.axis_size(name) for name in ("gx", "gy", "af"))
    held = fields_state.shape
    dma = pltpu.SemaphoreType.DMA
    vmem = lambda *shape: pltpu.VMEM(shape, F32)
    held_in_hbm = (fields_state.reshape(8, NS, 64, 128), velocity, diffusivity, wiener_draw.T)
    out = pl.pallas_call(
        functools.partial(kernel, counts),
        out_shape=pltpu.VMEM((8, NS, 64, 128), F32),
        in_specs=[pl.BlockSpec(memory_space=pltpu.HBM)] * 4,
        out_specs=pl.BlockSpec(memory_space=pltpu.VMEM),
        scratch_shapes=[
            vmem(NS, 8, 64, 128),
            vmem(3, NS, 6, 18, 8, 128),
            vmem(6, 4, 16, 8, 128),
            vmem(2, 4, 16, 8, 128),
            vmem(4, 16, 8, 128),
            vmem(2, 4, 16, 128),
            vmem(3, NS, 4, 16, 128),
            vmem(3, NS, 4, 16, 128),
            vmem(3, NS, 4, 16, 128),
            vmem(3, NS, 4, 16, 128),
            vmem(6, 16, 128),
            vmem(4, 32, 128),
            vmem(4, 16, 128),
            vmem(4, 16, 128),
            vmem(3, 8),
            vmem(3, PAIRS, 16, 8, 128),
            dma((NS,)),
            dma((5,)),
            dma,
            dma((3, PAIRS)),
            dma((4,)),
            dma((4,)),
            dma((6,)),
            dma((3, PAIRS, 6)),
        ],
        compiler_params=pltpu.CompilerParams(
            collective_id=0, has_side_effects=True, vmem_limit_bytes=48 * 1024 * 1024
        ),
    )(*(pltpu.with_memory_space_constraint(x, pltpu.HBM) for x in held_in_hbm))
    return out.reshape(held)


def solution(mesh):
    return jax.shard_map(
        local,
        mesh=mesh,
        in_specs=(
            P("af", None, "gx", "gy", None),
            P(None, "gx", "gy", None),
            P("gx", "gy", None),
            P("af", None),
        ),
        out_specs=P("af", None, "gx", "gy", None),
        check_vma=False,
    )
```

```python
import functools

import jax
import jax.numpy as jnp
from jax import lax
from jax.experimental import pallas as pl
from jax.experimental.pallas import tpu as pltpu
from jax.sharding import PartitionSpec as P

MESH = pl.DeviceIdType.MESH
F32 = jnp.float32

FIELDS = 32
NS = 6
PAIRS = 3
STEP = 0.3
MIX = 4.0
RADIATION = 0.5
NUCLEATION = (1.0, 0.8, 0.6, 0.5)
GROWTH = 0.5
OXIDATION = 0.3
WEIGHTS = ((0.0, 1.0), (0.75, 0.25), (1.0 / 3.0, 2.0 / 3.0))
EAST, WEST, NORTH, SOUTH, SUM1, SUM2 = range(6)


def sum_rows(tiles):
    row = lax.broadcasted_iota(jnp.int32, (8, 128), 0)
    low = row < 4
    quads = [
        jnp.where(low, tiles[i], tiles[i + 4])
        + pltpu.roll(jnp.where(low, tiles[i + 4], tiles[i]), 4, 0)
        for i in range(4)
    ]
    even = lax.rem(row, 4) < 2
    pairs = [
        jnp.where(even, quads[i], quads[i + 2])
        + jnp.where(even, pltpu.roll(quads[i], 6, 0), pltpu.roll(quads[i + 2], 2, 0))
        for i in range(2)
    ]
    first = lax.rem(row, 2) < 1
    return jnp.where(first, pairs[0], pairs[1]) + jnp.where(
        first, pltpu.roll(pairs[0], 7, 0), pltpu.roll(pairs[1], 1, 0)
    )


def spread(rows, i):
    return jnp.broadcast_to(rows[i : i + 1, :], (8, 128))


def kernel(
    counts,
    fields_hbm,
    velocity_hbm,
    diffusivity_hbm,
    wiener_hbm,
    out,
    rows_in,
    p,
    coef,
    centre,
    weight,
    mean_row,
    part,
    part_1,
    half,
    part_2,
    speed_x,
    speed_y,
    speed_z,
    diffusion,
    wiener,
    relay,
    in_sem,
    own_sem,
    relay_send,
    relay_recv,
    speed_send,
    speed_recv,
    send_sem,
    recv_sem,
):
    nx, ny, na = counts
    ax, ix, iy = lax.axis_index("af"), lax.axis_index("gx"), lax.axis_index("gy")
    has = {EAST: ix < nx - 1, WEST: ix > 0, NORTH: iy < ny - 1, SOUTH: iy > 0}
    back = {EAST: WEST, WEST: EAST, NORTH: SOUTH, SOUTH: NORTH}
    pair = {SUM1: ax + 1 - 2 * lax.rem(ax, 2), SUM2: na - 1 - ax}
    target = {
        EAST: {"gx": ix + 1},
        WEST: {"gx": ix - 1},
        NORTH: {"gy": iy + 1},
        SOUTH: {"gy": iy - 1},
        SUM1: {"af": pair[SUM1]},
        SUM2: {"af": pair[SUM2]},
    }

    mid, end = nx // 2, nx - 1
    to_relay = {EAST: ix == mid - 1, WEST: ix == mid}
    is_relay = {EAST: ix == end, WEST: ix == 0}
    relay_of = {EAST: {"gx": end}, WEST: {"gx": 0}}
    relay_to = {EAST: {"gx": mid}, WEST: {"gx": mid - 1}}

    def load_in(s):
        return pltpu.make_async_copy(fields_hbm.at[:, s], rows_in.at[s], in_sem.at[s])

    def two(c):
        return pl.ds(2 * c, 2)

    own = [
        pltpu.make_async_copy(velocity_hbm.at[0], speed_x.at[pl.ds(1, 4)], own_sem.at[0]),
        pltpu.make_async_copy(velocity_hbm.at[1], speed_y.at[:, pl.ds(8, 16)], own_sem.at[1]),
        pltpu.make_async_copy(velocity_hbm.at[2], speed_z, own_sem.at[2]),
        pltpu.make_async_copy(diffusivity_hbm, diffusion, own_sem.at[3]),
        pltpu.make_async_copy(wiener_hbm, wiener, own_sem.at[4]),
    ]

    def speed_face(way):
        src, dst = {
            EAST: (velocity_hbm.at[0, 3], speed_x.at[0]),
            WEST: (velocity_hbm.at[0, 0], speed_x.at[5]),
            NORTH: (velocity_hbm.at[1, :, pl.ds(8, 8)], speed_y.at[:, pl.ds(0, 8)]),
            SOUTH: (velocity_hbm.at[1, :, pl.ds(0, 8)], speed_y.at[:, pl.ds(24, 8)]),
        }[way]
        return pltpu.make_async_remote_copy(
            src_ref=src,
            dst_ref=dst,
            send_sem=speed_send.at[way],
            recv_sem=speed_recv.at[way],
            device_id=target[way],
            device_id_type=MESH,
        )

    def face(k, s, way, recv=None):
        src, dst = {
            EAST: lambda: (p.at[k, s, 4, pl.ds(1, 16)], p.at[k, s, 0, pl.ds(1, 16)]),
            WEST: lambda: (p.at[k, s, 1, pl.ds(1, 16)], p.at[k, s, 5, pl.ds(1, 16)]),
            NORTH: lambda: (p.at[k, s, pl.ds(1, 4), 16], p.at[k, s, pl.ds(1, 4), 0]),
            SOUTH: lambda: (p.at[k, s, pl.ds(1, 4), 1], p.at[k, s, pl.ds(1, 4), 17]),
            SUM1: lambda: (part.at[k, s], part_1.at[k, s]),
            SUM2: lambda: (half.at[k, s], part_2.at[k, s]),
        }[way]()
        return pltpu.make_async_remote_copy(
            src_ref=src,
            dst_ref=dst,
            send_sem=send_sem.at[way],
            recv_sem=recv,
            device_id=target[way],
            device_id_type=MESH,
        )

    def chunk(k, c, way):
        return face(k, two(c), way, recv_sem.at[k, c, way])

    def all_sent(way):
        face(pl.ds(0, 3), pl.ds(0, NS), way, recv_sem.at[0, 0, way]).wait_send()

    def send(k, c, way):
        if way not in to_relay:
            pl.when(has[way])(lambda: chunk(k, c, way).start())
            return

        @pl.when(has[way] & jnp.logical_not(to_relay[way]))
        def _():
            chunk(k, c, way).start()

        @pl.when(to_relay[way])
        def _():
            pltpu.make_async_remote_copy(
                src_ref=p.at[k, 2 * c + 1, 4 if way == EAST else 1, pl.ds(1, 16)],
                dst_ref=relay.at[k, c],
                send_sem=send_sem.at[way],
                recv_sem=relay_recv.at[k, c],
                device_id=relay_of[way],
                device_id_type=MESH,
            ).start()
            face(k, pl.ds(2 * c, 1), way, recv_sem.at[k, c, way]).start()

    def passed_on(k, c, way):
        return pltpu.make_async_remote_copy(
            src_ref=relay.at[k, c],
            dst_ref=p.at[k, 2 * c + 1, 0 if way == EAST else 5, pl.ds(1, 16)],
            send_sem=relay_send,
            recv_sem=recv_sem.at[k, c, way],
            device_id=relay_to[way],
            device_id_type=MESH,
        )

    def pass_on(k, c):
        for way in (EAST, WEST):

            @pl.when(is_relay[way])
            def _():
                pltpu.make_async_copy(relay.at[k, c], relay.at[k, c], relay_recv.at[k, c]).wait()
                passed_on(k, c, way).start()

    def all_passed_on():
        for way in (EAST, WEST):

            @pl.when(is_relay[way])
            def _():
                pltpu.make_async_copy(relay, relay, relay_send).wait()

    def arrived(k, c, way):
        pl.when(has[back[way]])(lambda: chunk(k, c, way).wait_recv())

    def blocks(first, step, count, body):
        def at(i, _):
            body(first + step * (i // 2), lax.rem(i, 2))
            return 0

        lax.fori_loop(0, 2 * count, at, 0)

    load_in(0).start()
    for copy in own:
        copy.start()
    for s in range(1, NS):
        load_in(s).start()

    barrier = pltpu.get_barrier_semaphore()
    expected = 2
    for way in (EAST, WEST, NORTH, SOUTH):
        pl.when(has[way])(
            lambda way=way: pl.semaphore_signal(
                barrier, inc=1, device_id=target[way], device_id_type=MESH
            )
        )
        expected = expected + has[way].astype(jnp.int32)
    for way in (EAST, WEST):
        for near, partners in (
            (to_relay[way], ({"gx": 0}, {"gx": end})),
            (is_relay[way], ({"gx": mid - 1}, {"gx": mid})),
        ):
            expected = expected + 2 * near.astype(jnp.int32)

            @pl.when(near)
            def _(partners=partners):
                for partner in partners:
                    pl.semaphore_signal(barrier, inc=1, device_id=partner, device_id_type=MESH)

    for way in (SUM1, SUM2):
        pl.semaphore_signal(barrier, inc=1, device_id=target[way], device_id_type=MESH)

    zero = jnp.zeros((8, 128), F32)

    def clear_x(x, speed):
        def at(i, _):
            for y in range(16):
                p[i // NS, lax.rem(i, NS), x, 1 + y] = zero
            return 0

        lax.fori_loop(0, 3 * NS, at, 0)
        speed_x[speed] = jnp.zeros((16, 128), F32)

    def clear_y(y, speed):
        def at(i, _):
            for x in range(4):
                p[i // NS, lax.rem(i, NS), 1 + x, y] = zero
            return 0

        lax.fori_loop(0, 3 * NS, at, 0)
        for x in range(4):
            speed_y[x, speed : speed + 8] = zero

    pl.when(ix == 0)(lambda: clear_x(0, 0))
    pl.when(ix == nx - 1)(lambda: clear_x(5, 5))
    pl.when(iy == 0)(lambda: clear_y(0, 0))
    pl.when(iy == ny - 1)(lambda: clear_y(17, 24))

    pl.semaphore_wait(barrier, expected)

    def second_exchange(k, c):
        chunk(k, c, SUM1).wait_recv()
        half[k, two(c)] = part[k, two(c)] + part_1[k, two(c)]
        chunk(k, c, SUM2).start()

    def mean_term(k, c):
        chunk(k, c, SUM2).wait_recv()
        scale = (STEP * MIX / FIELDS) * diffusion[...]
        for i in range(2):
            mean_row[i] = scale * (half[k, 2 * c + i] + part_2[k, 2 * c + i])

    def turn(s):
        flat = rows_in.reshape(NS * 8 * 64, 128)

        def body(x, h):
            start = s * 512 + x * 16 + h * 8
            tiles = [flat[pl.ds(start + i, 8, stride=64), :] for i in range(8)]
            for i in range(8):
                p[0, s, x + 1, h * 8 + i + 1] = tiles[i]
            part[0, s, x, pl.ds(h * 8, 8), :] = sum_rows(tiles)

        return body

    for c in range(PAIRS):
        for s in (2 * c, 2 * c + 1):
            load_in(s).wait()
            blocks(0, 3, 2, turn(s))
        send(0, c, EAST)
        send(0, c, WEST)
        for s in (2 * c, 2 * c + 1):
            blocks(1, 1, 2, turn(s))
        send(0, c, NORTH)
        send(0, c, SOUTH)
        chunk(0, c, SUM1).start()
        if c == 0:
            for way in (EAST, WEST, NORTH, SOUTH):
                pl.when(has[way])(lambda way=way: speed_face(way).start())
        else:
            pass_on(0, c - 1)
            second_exchange(0, c - 1)

    for copy in own:
        copy.wait()
    for way in (EAST, WEST, NORTH, SOUTH):
        pl.when(has[back[way]])(lambda way=way: speed_face(way).wait_recv())

    diagonal = lax.broadcasted_iota(jnp.int32, (8, 8), 0) == lax.broadcasted_iota(
        jnp.int32, (8, 8), 1
    )
    draws = []
    for d in range(3):
        row = jnp.broadcast_to(wiener[d : d + 1, :], (8, 8))
        column = jnp.sum(jnp.where(diagonal, row, 0.0), axis=1, keepdims=True)
        draws.append(jnp.broadcast_to(column, (8, 128)))

    def coefficients(x, _):
        g = diffusion[x]
        diffuse = STEP * g
        stir = (0.5 * STEP) * jnp.sqrt((2.0 / STEP) * g)
        lane = lax.broadcasted_iota(jnp.int32, (16, 128), 1)
        upper, lower = lane < 127, lane > 0
        half_step = 0.5 * STEP
        base = [
            diffuse - half_step * speed_x[x + 2],
            diffuse + half_step * speed_x[x],
            diffuse - half_step * speed_y[x, 9:25, :],
            diffuse + half_step * speed_y[x, 7:23, :],
            jnp.where(upper, diffuse - half_step * pltpu.roll(speed_z[x], 127, 1), 0.0),
            jnp.where(lower, diffuse + half_step * pltpu.roll(speed_z[x], 1, 1), 0.0),
        ]
        stir_up, stir_down = jnp.where(upper, stir, 0.0), jnp.where(lower, stir, 0.0)
        keep = 1.0 - (6.0 + MIX) * diffuse
        for y in range(16):
            stir_y = spread(stir, y)
            for d in range(2):
                move = stir_y * draws[d]
                coef[2 * d, x, y] = spread(base[2 * d], y) + move
                coef[2 * d + 1, x, y] = spread(base[2 * d + 1], y) - move
            coef[4, x, y] = spread(base[4], y) + spread(stir_up, y) * draws[2]
            coef[5, x, y] = spread(base[5], y) - spread(stir_down, y) * draws[2]
            keep_y = spread(keep, y)
            centre[0, x, y] = keep_y
            centre[1, x, y] = keep_y - STEP * OXIDATION
        return 0

    lax.fori_loop(0, 4, coefficients, 0)

    def advance(k, c):
        base_weight, section_weight = WEIGHTS[k - 1]
        old = k - 1
        flat = out.reshape(8 * NS * 64, 128)

        def body(x, h):
            y0 = h * 8
            tiles, weights = [[], []], []
            columns = [[p[old, 2 * c + j, x + 1, y0 + i] for i in range(10)] for j in range(2)]
            means = [mean_row[j, x, pl.ds(y0, 8), :] for j in range(2)]
            for i in range(8):
                y = y0 + i
                factor = [coef[d, x, y] for d in range(6)]
                keep = centre[int(c > 0), x, y]
                here = [columns[j][i + 1] for j in range(2)]
                new = [
                    keep * here[j]
                    + spread(means[j], i)
                    + factor[0] * p[old, 2 * c + j, x + 2, y + 1]
                    + factor[1] * p[old, 2 * c + j, x, y + 1]
                    + factor[2] * columns[j][i + 2]
                    + factor[3] * columns[j][i]
                    + factor[4] * pltpu.roll(here[j], 127, 1)
                    + factor[5] * pltpu.roll(here[j], 1, 1)
                    for j in range(2)
                ]
                if c == 0:
                    square = here[0] * here[0]
                    w = square / (1.0 + square) / (1.0 + jnp.exp(-3.0 * here[1]))
                    weights.append(w)
                    new[1] = new[1] - (STEP * RADIATION) * w
                else:
                    w = weight[x, y]
                    before = [p[old, 3, x + 1, y + 1] if c == 2 else None, here[0]]
                    for j in range(2):
                        gain = STEP * NUCLEATION[2 * c - 2 + j]
                        if before[j] is not None:
                            gain = gain + (STEP * GROWTH) * before[j]
                        new[j] = new[j] + w * gain
                for j in range(2):
                    s = 2 * c + j
                    if base_weight:
                        new[j] = base_weight * p[0, s, x + 1, y + 1] + section_weight * new[j]
                    tiles[j].append(new[j])
            for i, w in enumerate(weights):
                weight[x, y0 + i] = w
            for j in range(2):
                s = 2 * c + j
                for i in range(8):
                    if k < 3:
                        p[k, s, x + 1, y0 + i + 1] = tiles[j][i]
                    else:
                        flat[pl.ds(s * 64 + x * 16 + y0 + i, 8, stride=NS * 64), :] = tiles[j][i]
            if k < 3:
                for j in range(2):
                    part[k, 2 * c + j, x, pl.ds(y0, 8), :] = sum_rows(tiles[j])

        return body

    for k in range(1, 4):
        for c in range(PAIRS):
            if c == 0:
                pass_on(k - 1, PAIRS - 1)
                second_exchange(k - 1, PAIRS - 1)
            mean_term(k - 1, c)
            arrived(k - 1, c, NORTH)
            arrived(k - 1, c, SOUTH)
            blocks(1, 1, 2, advance(k, c))
            arrived(k - 1, c, EAST)
            arrived(k - 1, c, WEST)
            blocks(0, 3, 2, advance(k, c))
            if k < 3:
                for way in (EAST, WEST, NORTH, SOUTH):
                    send(k, c, way)
                chunk(k, c, SUM1).start()
                if c > 0:
                    pass_on(k, c - 1)
                    second_exchange(k, c - 1)

    for way in (EAST, WEST, NORTH, SOUTH):
        pl.when(has[way])(lambda way=way: speed_face(way).wait_send())
        pl.when(has[way])(lambda way=way: all_sent(way))
    all_passed_on()
    all_sent(SUM1)
    all_sent(SUM2)


def local(fields_state, velocity, diffusivity, wiener_draw):
    counts = tuple(lax.axis_size(name) for name in ("gx", "gy", "af"))
    held = fields_state.shape
    dma = pltpu.SemaphoreType.DMA
    vmem = lambda *shape: pltpu.VMEM(shape, F32)
    held_in_hbm = (fields_state.reshape(8, NS, 64, 128), velocity, diffusivity, wiener_draw.T)
    out = pl.pallas_call(
        functools.partial(kernel, counts),
        out_shape=pltpu.VMEM((8, NS, 64, 128), F32),
        in_specs=[pl.BlockSpec(memory_space=pltpu.HBM)] * 4,
        out_specs=pl.BlockSpec(memory_space=pltpu.VMEM),
        scratch_shapes=[
            vmem(NS, 8, 64, 128),
            vmem(3, NS, 6, 18, 8, 128),
            vmem(6, 4, 16, 8, 128),
            vmem(2, 4, 16, 8, 128),
            vmem(4, 16, 8, 128),
            vmem(2, 4, 16, 128),
            vmem(3, NS, 4, 16, 128),
            vmem(3, NS, 4, 16, 128),
            vmem(3, NS, 4, 16, 128),
            vmem(3, NS, 4, 16, 128),
            vmem(6, 16, 128),
            vmem(4, 32, 128),
            vmem(4, 16, 128),
            vmem(4, 16, 128),
            vmem(3, 8),
            vmem(3, PAIRS, 16, 8, 128),
            dma((NS,)),
            dma((5,)),
            dma,
            dma((3, PAIRS)),
            dma((4,)),
            dma((4,)),
            dma((6,)),
            dma((3, PAIRS, 6)),
        ],
        compiler_params=pltpu.CompilerParams(
            collective_id=0, has_side_effects=True, vmem_limit_bytes=48 * 1024 * 1024
        ),
    )(*(pltpu.with_memory_space_constraint(x, pltpu.HBM) for x in held_in_hbm))
    return out.reshape(held)


def solution(mesh):
    return jax.shard_map(
        local,
        mesh=mesh,
        in_specs=(
            P("af", None, "gx", "gy", None),
            P(None, "gx", "gy", None),
            P("gx", "gy", None),
            P("af", None),
        ),
        out_specs=P("af", None, "gx", "gy", None),
        check_vma=False,
    )
```

```python
import functools

import jax
import jax.numpy as jnp
from jax import lax
from jax.experimental import pallas as pl
from jax.experimental.pallas import tpu as pltpu
from jax.sharding import PartitionSpec as P

MESH = pl.DeviceIdType.MESH
F32 = jnp.float32

FIELDS = 32
NS = 6
PAIRS = 3
STEP = 0.3
MIX = 4.0
RADIATION = 0.5
NUCLEATION = (1.0, 0.8, 0.6, 0.5)
GROWTH = 0.5
OXIDATION = 0.3
WEIGHTS = ((0.0, 1.0), (0.75, 0.25), (1.0 / 3.0, 2.0 / 3.0))
EAST, WEST, NORTH, SOUTH, SUM1, SUM2 = range(6)


def sum_rows(tiles):
    row = lax.broadcasted_iota(jnp.int32, (8, 128), 0)
    low = row < 4
    quads = [
        jnp.where(low, tiles[i], tiles[i + 4])
        + pltpu.roll(jnp.where(low, tiles[i + 4], tiles[i]), 4, 0)
        for i in range(4)
    ]
    even = lax.rem(row, 4) < 2
    pairs = [
        jnp.where(even, quads[i], quads[i + 2])
        + jnp.where(even, pltpu.roll(quads[i], 6, 0), pltpu.roll(quads[i + 2], 2, 0))
        for i in range(2)
    ]
    first = lax.rem(row, 2) < 1
    return jnp.where(first, pairs[0], pairs[1]) + jnp.where(
        first, pltpu.roll(pairs[0], 7, 0), pltpu.roll(pairs[1], 1, 0)
    )


def spread(rows, i):
    return jnp.broadcast_to(rows[i : i + 1, :], (8, 128))


def kernel(
    counts,
    fields_hbm,
    velocity_hbm,
    diffusivity_hbm,
    wiener_hbm,
    out,
    rows_in,
    p,
    coef,
    centre,
    weight,
    mean_row,
    part,
    part_1,
    half,
    part_2,
    speed_x,
    speed_y,
    speed_z,
    diffusion,
    wiener,
    relay,
    in_sem,
    own_sem,
    relay_send,
    relay_recv,
    x_sem,
    speed_send,
    speed_recv,
    send_sem,
    recv_sem,
):
    nx, ny, na = counts
    ax, ix, iy = lax.axis_index("af"), lax.axis_index("gx"), lax.axis_index("gy")
    has = {EAST: ix < nx - 1, WEST: ix > 0, NORTH: iy < ny - 1, SOUTH: iy > 0}
    back = {EAST: WEST, WEST: EAST, NORTH: SOUTH, SOUTH: NORTH}
    pair = {SUM1: ax + 1 - 2 * lax.rem(ax, 2), SUM2: na - 1 - ax}
    target = {
        EAST: {"gx": ix + 1},
        WEST: {"gx": ix - 1},
        NORTH: {"gy": iy + 1},
        SOUTH: {"gy": iy - 1},
        SUM1: {"af": pair[SUM1]},
        SUM2: {"af": pair[SUM2]},
    }

    mid, end = nx // 2, nx - 1
    to_relay = {EAST: ix == mid - 1, WEST: ix == mid}
    is_relay = {EAST: ix == end, WEST: ix == 0}
    relay_of = {EAST: {"gx": end}, WEST: {"gx": 0}}
    relay_to = {EAST: {"gx": mid}, WEST: {"gx": mid - 1}}

    def load_in(s):
        return pltpu.make_async_copy(fields_hbm.at[:, s], rows_in.at[s], in_sem.at[s])

    def two(c):
        return pl.ds(2 * c, 2)

    own = [
        pltpu.make_async_copy(velocity_hbm.at[0], speed_x.at[pl.ds(1, 4)], own_sem.at[0]),
        pltpu.make_async_copy(velocity_hbm.at[1], speed_y.at[:, pl.ds(8, 16)], own_sem.at[1]),
        pltpu.make_async_copy(velocity_hbm.at[2], speed_z, own_sem.at[2]),
        pltpu.make_async_copy(diffusivity_hbm, diffusion, own_sem.at[3]),
        pltpu.make_async_copy(wiener_hbm, wiener, own_sem.at[4]),
    ]

    def speed_face(way):
        src, dst = {
            EAST: (velocity_hbm.at[0, 3], speed_x.at[0]),
            WEST: (velocity_hbm.at[0, 0], speed_x.at[5]),
            NORTH: (velocity_hbm.at[1, :, pl.ds(8, 8)], speed_y.at[:, pl.ds(0, 8)]),
            SOUTH: (velocity_hbm.at[1, :, pl.ds(0, 8)], speed_y.at[:, pl.ds(24, 8)]),
        }[way]
        return pltpu.make_async_remote_copy(
            src_ref=src,
            dst_ref=dst,
            send_sem=speed_send.at[way],
            recv_sem=speed_recv.at[way],
            device_id=target[way],
            device_id_type=MESH,
        )

    def face_x(k, s, way):
        src, dst = {EAST: (4, 0), WEST: (1, 5)}[way]
        return p.at[k, s, src, pl.ds(1, 16)], p.at[k, s, dst, pl.ds(1, 16)]

    def face(k, s, way, recv=None):
        src, dst = {
            EAST: lambda: face_x(k, s, EAST),
            WEST: lambda: face_x(k, s, WEST),
            NORTH: lambda: (p.at[k, s, pl.ds(1, 4), 16], p.at[k, s, pl.ds(1, 4), 0]),
            SOUTH: lambda: (p.at[k, s, pl.ds(1, 4), 1], p.at[k, s, pl.ds(1, 4), 17]),
            SUM1: lambda: (part.at[k, s], part_1.at[k, s]),
            SUM2: lambda: (half.at[k, s], part_2.at[k, s]),
        }[way]()
        return pltpu.make_async_remote_copy(
            src_ref=src,
            dst_ref=dst,
            send_sem=send_sem.at[way],
            recv_sem=recv,
            device_id=target[way],
            device_id_type=MESH,
        )

    def chunk(k, c, way):
        return face(k, two(c), way, recv_sem.at[k, c, way])

    def all_sent(way):
        face(pl.ds(0, 3), pl.ds(0, NS), way, recv_sem.at[0, 0, way]).wait_send()

    def send(k, c, way):
        pl.when(has[way])(lambda: chunk(k, c, way).start())

    def x_face(k, s, way, by_relay=False):
        src, dst = face_x(k, s, way)
        return pltpu.make_async_remote_copy(
            src_ref=src,
            dst_ref=relay.at[k, s // 2] if by_relay else dst,
            send_sem=x_sem.at[way, s % 2],
            recv_sem=relay_recv.at[k, s // 2] if by_relay else recv_sem.at[k, s // 2, way],
            device_id=relay_of[way] if by_relay else target[way],
            device_id_type=MESH,
        )

    def left(k, s, way):
        pl.when(has[way])(lambda: x_face(k, s, way).wait_send())

    def send_x(k, c):
        for s in (2 * c, 2 * c + 1):
            for way in (EAST, WEST):
                if k or c:
                    left(k, s, way)
                if s % 2 == 0:
                    pl.when(has[way])(lambda: x_face(k, s, way).start())
                else:
                    pl.when(has[way] & jnp.logical_not(to_relay[way]))(
                        lambda: x_face(k, s, way).start()
                    )
                    pl.when(to_relay[way])(lambda: x_face(k, s, way, by_relay=True).start())

    def passed_on(k, c, way):
        return pltpu.make_async_remote_copy(
            src_ref=relay.at[k, c],
            dst_ref=p.at[k, 2 * c + 1, 0 if way == EAST else 5, pl.ds(1, 16)],
            send_sem=relay_send,
            recv_sem=recv_sem.at[k, c, way],
            device_id=relay_to[way],
            device_id_type=MESH,
        )

    def pass_on(k, c):
        for way in (EAST, WEST):

            @pl.when(is_relay[way])
            def _():
                pltpu.make_async_copy(relay.at[k, c], relay.at[k, c], relay_recv.at[k, c]).wait()
                passed_on(k, c, way).start()

    def all_passed_on():
        for way in (EAST, WEST):

            @pl.when(is_relay[way])
            def _():
                pltpu.make_async_copy(relay, relay, relay_send).wait()

    def arrived(k, c, way):
        pl.when(has[back[way]])(lambda: chunk(k, c, way).wait_recv())

    def blocks(first, step, count, body):
        def at(i, _):
            body(first + step * (i // 2), lax.rem(i, 2))
            return 0

        lax.fori_loop(0, 2 * count, at, 0)

    load_in(0).start()
    for copy in own:
        copy.start()
    for s in range(1, NS):
        load_in(s).start()

    barrier = pltpu.get_barrier_semaphore()
    expected = 2
    for way in (EAST, WEST, NORTH, SOUTH):
        pl.when(has[way])(
            lambda way=way: pl.semaphore_signal(
                barrier, inc=1, device_id=target[way], device_id_type=MESH
            )
        )
        expected = expected + has[way].astype(jnp.int32)
    for way in (EAST, WEST):
        for near, partners in (
            (to_relay[way], ({"gx": 0}, {"gx": end})),
            (is_relay[way], ({"gx": mid - 1}, {"gx": mid})),
        ):
            expected = expected + 2 * near.astype(jnp.int32)

            @pl.when(near)
            def _(partners=partners):
                for partner in partners:
                    pl.semaphore_signal(barrier, inc=1, device_id=partner, device_id_type=MESH)

    for way in (SUM1, SUM2):
        pl.semaphore_signal(barrier, inc=1, device_id=target[way], device_id_type=MESH)

    zero = jnp.zeros((8, 128), F32)

    def clear_x(x, speed):
        def at(i, _):
            for y in range(16):
                p[i // NS, lax.rem(i, NS), x, 1 + y] = zero
            return 0

        lax.fori_loop(0, 3 * NS, at, 0)
        speed_x[speed] = jnp.zeros((16, 128), F32)

    def clear_y(y, speed):
        def at(i, _):
            for x in range(4):
                p[i // NS, lax.rem(i, NS), 1 + x, y] = zero
            return 0

        lax.fori_loop(0, 3 * NS, at, 0)
        for x in range(4):
            speed_y[x, speed : speed + 8] = zero

    pl.when(ix == 0)(lambda: clear_x(0, 0))
    pl.when(ix == nx - 1)(lambda: clear_x(5, 5))
    pl.when(iy == 0)(lambda: clear_y(0, 0))
    pl.when(iy == ny - 1)(lambda: clear_y(17, 24))

    pl.semaphore_wait(barrier, expected)

    def second_exchange(k, c):
        chunk(k, c, SUM1).wait_recv()
        half[k, two(c)] = part[k, two(c)] + part_1[k, two(c)]
        chunk(k, c, SUM2).start()

    def mean_term(k, c):
        chunk(k, c, SUM2).wait_recv()
        scale = (STEP * MIX / FIELDS) * diffusion[...]
        for i in range(2):
            mean_row[i] = scale * (half[k, 2 * c + i] + part_2[k, 2 * c + i])

    def turn(s):
        flat = rows_in.reshape(NS * 8 * 64, 128)

        def body(x, h):
            start = s * 512 + x * 16 + h * 8
            tiles = [flat[pl.ds(start + i, 8, stride=64), :] for i in range(8)]
            for i in range(8):
                p[0, s, x + 1, h * 8 + i + 1] = tiles[i]
            part[0, s, x, pl.ds(h * 8, 8), :] = sum_rows(tiles)

        return body

    for c in range(PAIRS):
        for s in (2 * c, 2 * c + 1):
            load_in(s).wait()
            blocks(0, 3, 2, turn(s))
        if c == 0:
            send_x(0, 0)
        for s in (2 * c, 2 * c + 1):
            blocks(1, 1, 2, turn(s))
        send(0, c, NORTH)
        send(0, c, SOUTH)
        chunk(0, c, SUM1).start()
        if c == 0:
            for way in (EAST, WEST, NORTH, SOUTH):
                pl.when(has[way])(lambda way=way: speed_face(way).start())
        else:
            pass_on(0, c - 1)
            second_exchange(0, c - 1)

    for copy in own:
        copy.wait()
    for way in (EAST, WEST, NORTH, SOUTH):
        pl.when(has[back[way]])(lambda way=way: speed_face(way).wait_recv())

    diagonal = lax.broadcasted_iota(jnp.int32, (8, 8), 0) == lax.broadcasted_iota(
        jnp.int32, (8, 8), 1
    )
    draws = []
    for d in range(3):
        row = jnp.broadcast_to(wiener[d : d + 1, :], (8, 8))
        column = jnp.sum(jnp.where(diagonal, row, 0.0), axis=1, keepdims=True)
        draws.append(jnp.broadcast_to(column, (8, 128)))

    def coefficients(x, _):
        g = diffusion[x]
        diffuse = STEP * g
        stir = (0.5 * STEP) * jnp.sqrt((2.0 / STEP) * g)
        lane = lax.broadcasted_iota(jnp.int32, (16, 128), 1)
        upper, lower = lane < 127, lane > 0
        half_step = 0.5 * STEP
        base = [
            diffuse - half_step * speed_x[x + 2],
            diffuse + half_step * speed_x[x],
            diffuse - half_step * speed_y[x, 9:25, :],
            diffuse + half_step * speed_y[x, 7:23, :],
            jnp.where(upper, diffuse - half_step * pltpu.roll(speed_z[x], 127, 1), 0.0),
            jnp.where(lower, diffuse + half_step * pltpu.roll(speed_z[x], 1, 1), 0.0),
        ]
        stir_up, stir_down = jnp.where(upper, stir, 0.0), jnp.where(lower, stir, 0.0)
        keep = 1.0 - (6.0 + MIX) * diffuse
        for y in range(16):
            stir_y = spread(stir, y)
            for d in range(2):
                move = stir_y * draws[d]
                coef[2 * d, x, y] = spread(base[2 * d], y) + move
                coef[2 * d + 1, x, y] = spread(base[2 * d + 1], y) - move
            coef[4, x, y] = spread(base[4], y) + spread(stir_up, y) * draws[2]
            coef[5, x, y] = spread(base[5], y) - spread(stir_down, y) * draws[2]
            keep_y = spread(keep, y)
            centre[0, x, y] = keep_y
            centre[1, x, y] = keep_y - STEP * OXIDATION
        return 0

    lax.fori_loop(0, 4, coefficients, 0)
    for c in range(1, PAIRS):
        send_x(0, c)

    def advance(k, c):
        base_weight, section_weight = WEIGHTS[k - 1]
        old = k - 1
        flat = out.reshape(8 * NS * 64, 128)

        def body(x, h):
            y0 = h * 8
            tiles, weights = [[], []], []
            columns = [[p[old, 2 * c + j, x + 1, y0 + i] for i in range(10)] for j in range(2)]
            means = [mean_row[j, x, pl.ds(y0, 8), :] for j in range(2)]
            for i in range(8):
                y = y0 + i
                factor = [coef[d, x, y] for d in range(6)]
                keep = centre[int(c > 0), x, y]
                here = [columns[j][i + 1] for j in range(2)]
                new = [
                    keep * here[j]
                    + spread(means[j], i)
                    + factor[0] * p[old, 2 * c + j, x + 2, y + 1]
                    + factor[1] * p[old, 2 * c + j, x, y + 1]
                    + factor[2] * columns[j][i + 2]
                    + factor[3] * columns[j][i]
                    + factor[4] * pltpu.roll(here[j], 127, 1)
                    + factor[5] * pltpu.roll(here[j], 1, 1)
                    for j in range(2)
                ]
                if c == 0:
                    square = here[0] * here[0]
                    w = square / (1.0 + square) / (1.0 + jnp.exp(-3.0 * here[1]))
                    weights.append(w)
                    new[1] = new[1] - (STEP * RADIATION) * w
                else:
                    w = weight[x, y]
                    before = [p[old, 3, x + 1, y + 1] if c == 2 else None, here[0]]
                    for j in range(2):
                        gain = STEP * NUCLEATION[2 * c - 2 + j]
                        if before[j] is not None:
                            gain = gain + (STEP * GROWTH) * before[j]
                        new[j] = new[j] + w * gain
                for j in range(2):
                    s = 2 * c + j
                    if base_weight:
                        new[j] = base_weight * p[0, s, x + 1, y + 1] + section_weight * new[j]
                    tiles[j].append(new[j])
            for i, w in enumerate(weights):
                weight[x, y0 + i] = w
            for j in range(2):
                s = 2 * c + j
                for i in range(8):
                    if k < 3:
                        p[k, s, x + 1, y0 + i + 1] = tiles[j][i]
                    else:
                        flat[pl.ds(s * 64 + x * 16 + y0 + i, 8, stride=NS * 64), :] = tiles[j][i]
            if k < 3:
                for j in range(2):
                    part[k, 2 * c + j, x, pl.ds(y0, 8), :] = sum_rows(tiles[j])

        return body

    for k in range(1, 4):
        for c in range(PAIRS):
            if c == 0:
                pass_on(k - 1, PAIRS - 1)
                second_exchange(k - 1, PAIRS - 1)
            mean_term(k - 1, c)
            arrived(k - 1, c, NORTH)
            arrived(k - 1, c, SOUTH)
            blocks(1, 1, 2, advance(k, c))
            arrived(k - 1, c, EAST)
            arrived(k - 1, c, WEST)
            blocks(0, 3, 2, advance(k, c))
            if k < 3:
                for way in (NORTH, SOUTH):
                    send(k, c, way)
                chunk(k, c, SUM1).start()
                if c > 0:
                    pass_on(k, c - 1)
                    second_exchange(k, c - 1)
                send_x(k, c)

    for way in (EAST, WEST, NORTH, SOUTH):
        pl.when(has[way])(lambda way=way: speed_face(way).wait_send())
        if way in to_relay:
            left(2, NS - 2, way)
            left(2, NS - 1, way)
        else:
            pl.when(has[way])(lambda way=way: all_sent(way))
    all_passed_on()
    all_sent(SUM1)
    all_sent(SUM2)


def local(fields_state, velocity, diffusivity, wiener_draw):
    counts = tuple(lax.axis_size(name) for name in ("gx", "gy", "af"))
    held = fields_state.shape
    dma = pltpu.SemaphoreType.DMA
    vmem = lambda *shape: pltpu.VMEM(shape, F32)
    held_in_hbm = (fields_state.reshape(8, NS, 64, 128), velocity, diffusivity, wiener_draw.T)
    out = pl.pallas_call(
        functools.partial(kernel, counts),
        out_shape=pltpu.VMEM((8, NS, 64, 128), F32),
        in_specs=[pl.BlockSpec(memory_space=pltpu.HBM)] * 4,
        out_specs=pl.BlockSpec(memory_space=pltpu.VMEM),
        scratch_shapes=[
            vmem(NS, 8, 64, 128),
            vmem(3, NS, 6, 18, 8, 128),
            vmem(6, 4, 16, 8, 128),
            vmem(2, 4, 16, 8, 128),
            vmem(4, 16, 8, 128),
            vmem(2, 4, 16, 128),
            vmem(3, NS, 4, 16, 128),
            vmem(3, NS, 4, 16, 128),
            vmem(3, NS, 4, 16, 128),
            vmem(3, NS, 4, 16, 128),
            vmem(6, 16, 128),
            vmem(4, 32, 128),
            vmem(4, 16, 128),
            vmem(4, 16, 128),
            vmem(3, 8),
            vmem(3, PAIRS, 16, 8, 128),
            dma((NS,)),
            dma((5,)),
            dma,
            dma((3, PAIRS)),
            dma((2, 2)),
            dma((4,)),
            dma((4,)),
            dma((6,)),
            dma((3, PAIRS, 6)),
        ],
        compiler_params=pltpu.CompilerParams(
            collective_id=0, has_side_effects=True, vmem_limit_bytes=48 * 1024 * 1024
        ),
    )(*(pltpu.with_memory_space_constraint(x, pltpu.HBM) for x in held_in_hbm))
    return out.reshape(held)


def solution(mesh):
    return jax.shard_map(
        local,
        mesh=mesh,
        in_specs=(
            P("af", None, "gx", "gy", None),
            P(None, "gx", "gy", None),
            P("gx", "gy", None),
            P("af", None),
        ),
        out_specs=P("af", None, "gx", "gy", None),
        check_vma=False,
    )
```

```python
import functools

import jax
import jax.numpy as jnp
from jax import lax
from jax.experimental import pallas as pl
from jax.experimental.pallas import tpu as pltpu
from jax.sharding import PartitionSpec as P

MESH = pl.DeviceIdType.MESH
F32 = jnp.float32

FIELDS = 32
NS = 6
PAIRS = 3
STEP = 0.3
MIX = 4.0
RADIATION = 0.5
NUCLEATION = (1.0, 0.8, 0.6, 0.5)
GROWTH = 0.5
OXIDATION = 0.3
EAST, WEST, NORTH, SOUTH, SUM1, SUM2 = range(6)


def sum_rows(tiles):
    row = lax.broadcasted_iota(jnp.int32, (8, 128), 0)
    low = row < 4
    quads = [
        jnp.where(low, tiles[i], tiles[i + 4])
        + pltpu.roll(jnp.where(low, tiles[i + 4], tiles[i]), 4, 0)
        for i in range(4)
    ]
    even = lax.rem(row, 4) < 2
    pairs = [
        jnp.where(even, quads[i], quads[i + 2])
        + jnp.where(even, pltpu.roll(quads[i], 6, 0), pltpu.roll(quads[i + 2], 2, 0))
        for i in range(2)
    ]
    first = lax.rem(row, 2) < 1
    return jnp.where(first, pairs[0], pairs[1]) + jnp.where(
        first, pltpu.roll(pairs[0], 7, 0), pltpu.roll(pairs[1], 1, 0)
    )


def spread(rows, i):
    return jnp.broadcast_to(rows[i : i + 1, :], (8, 128))


def kernel(
    counts,
    fields_hbm,
    velocity_hbm,
    diffusivity_hbm,
    wiener_hbm,
    out,
    rows_in,
    p,
    coef,
    centre,
    weight,
    mean_row,
    part,
    part_1,
    half,
    part_2,
    speed_x,
    speed_y,
    speed_z,
    diffusion,
    wiener,
    relay,
    in_sem,
    own_sem,
    relay_send,
    relay_recv,
    speed_send,
    speed_recv,
    send_sem,
    recv_sem,
):
    nx, ny, na = counts
    ax, ix, iy = lax.axis_index("af"), lax.axis_index("gx"), lax.axis_index("gy")
    has = {EAST: ix < nx - 1, WEST: ix > 0, NORTH: iy < ny - 1, SOUTH: iy > 0}
    back = {EAST: WEST, WEST: EAST, NORTH: SOUTH, SOUTH: NORTH}
    pair = {SUM1: ax + 1 - 2 * lax.rem(ax, 2), SUM2: na - 1 - ax}
    target = {
        EAST: {"gx": ix + 1},
        WEST: {"gx": ix - 1},
        NORTH: {"gy": iy + 1},
        SOUTH: {"gy": iy - 1},
        SUM1: {"af": pair[SUM1]},
        SUM2: {"af": pair[SUM2]},
    }

    mid, end = nx // 2, nx - 1
    to_relay = {EAST: ix == mid - 1, WEST: ix == mid}
    is_relay = {EAST: ix == end, WEST: ix == 0}
    relay_of = {EAST: {"gx": end}, WEST: {"gx": 0}}
    relay_to = {EAST: {"gx": mid}, WEST: {"gx": mid - 1}}

    def load_in(s):
        return pltpu.make_async_copy(fields_hbm.at[:, s], rows_in.at[s], in_sem.at[s])

    def two(c):
        return pl.ds(2 * c, 2)

    own = [
        pltpu.make_async_copy(velocity_hbm.at[0], speed_x.at[pl.ds(1, 4)], own_sem.at[0]),
        pltpu.make_async_copy(velocity_hbm.at[1], speed_y.at[:, pl.ds(8, 16)], own_sem.at[1]),
        pltpu.make_async_copy(velocity_hbm.at[2], speed_z, own_sem.at[2]),
        pltpu.make_async_copy(diffusivity_hbm, diffusion, own_sem.at[3]),
        pltpu.make_async_copy(wiener_hbm, wiener, own_sem.at[4]),
    ]

    def speed_face(way):
        src, dst = {
            EAST: (velocity_hbm.at[0, 3], speed_x.at[0]),
            WEST: (velocity_hbm.at[0, 0], speed_x.at[5]),
            NORTH: (velocity_hbm.at[1, :, pl.ds(8, 8)], speed_y.at[:, pl.ds(0, 8)]),
            SOUTH: (velocity_hbm.at[1, :, pl.ds(0, 8)], speed_y.at[:, pl.ds(24, 8)]),
        }[way]
        return pltpu.make_async_remote_copy(
            src_ref=src,
            dst_ref=dst,
            send_sem=speed_send.at[way],
            recv_sem=speed_recv.at[way],
            device_id=target[way],
            device_id_type=MESH,
        )

    def face(k, s, way, recv=None):
        src, dst = {
            EAST: lambda: (p.at[k, s, 4, pl.ds(1, 16)], p.at[k, s, 0, pl.ds(1, 16)]),
            WEST: lambda: (p.at[k, s, 1, pl.ds(1, 16)], p.at[k, s, 5, pl.ds(1, 16)]),
            NORTH: lambda: (p.at[k, s, pl.ds(1, 4), 16], p.at[k, s, pl.ds(1, 4), 0]),
            SOUTH: lambda: (p.at[k, s, pl.ds(1, 4), 1], p.at[k, s, pl.ds(1, 4), 17]),
            SUM1: lambda: (part.at[k, s], part_1.at[k, s]),
            SUM2: lambda: (half.at[k, s], part_2.at[k, s]),
        }[way]()
        return pltpu.make_async_remote_copy(
            src_ref=src,
            dst_ref=dst,
            send_sem=send_sem.at[way],
            recv_sem=recv,
            device_id=target[way],
            device_id_type=MESH,
        )

    def chunk(k, c, way):
        return face(k, two(c), way, recv_sem.at[k, c, way])

    def all_sent(way):
        face(pl.ds(0, 3), pl.ds(0, NS), way, recv_sem.at[0, 0, way]).wait_send()

    def send(k, c, way):
        if way not in to_relay:
            pl.when(has[way])(lambda: chunk(k, c, way).start())
            return

        @pl.when(has[way] & jnp.logical_not(to_relay[way]))
        def _():
            chunk(k, c, way).start()

        @pl.when(to_relay[way])
        def _():
            pltpu.make_async_remote_copy(
                src_ref=p.at[k, 2 * c + 1, 4 if way == EAST else 1, pl.ds(1, 16)],
                dst_ref=relay.at[k, c],
                send_sem=send_sem.at[way],
                recv_sem=relay_recv.at[k, c],
                device_id=relay_of[way],
                device_id_type=MESH,
            ).start()
            face(k, pl.ds(2 * c, 1), way, recv_sem.at[k, c, way]).start()

    def passed_on(k, c, way):
        return pltpu.make_async_remote_copy(
            src_ref=relay.at[k, c],
            dst_ref=p.at[k, 2 * c + 1, 0 if way == EAST else 5, pl.ds(1, 16)],
            send_sem=relay_send,
            recv_sem=recv_sem.at[k, c, way],
            device_id=relay_to[way],
            device_id_type=MESH,
        )

    def pass_on(k, c):
        for way in (EAST, WEST):

            @pl.when(is_relay[way])
            def _():
                pltpu.make_async_copy(relay.at[k, c], relay.at[k, c], relay_recv.at[k, c]).wait()
                passed_on(k, c, way).start()

    def all_passed_on():
        for way in (EAST, WEST):

            @pl.when(is_relay[way])
            def _():
                pltpu.make_async_copy(relay, relay, relay_send).wait()

    def arrived(k, c, way):
        pl.when(has[back[way]])(lambda: chunk(k, c, way).wait_recv())

    def blocks(count, body):
        lax.fori_loop(0, count, lambda i, _: (body(i), 0)[1], 0)

    load_in(0).start()
    for copy in own:
        copy.start()
    for s in range(1, NS):
        load_in(s).start()

    barrier = pltpu.get_barrier_semaphore()
    expected = 2
    for way in (EAST, WEST, NORTH, SOUTH):
        pl.when(has[way])(
            lambda way=way: pl.semaphore_signal(
                barrier, inc=1, device_id=target[way], device_id_type=MESH
            )
        )
        expected = expected + has[way].astype(jnp.int32)
    for way in (EAST, WEST):
        for near, partners in (
            (to_relay[way], ({"gx": 0}, {"gx": end})),
            (is_relay[way], ({"gx": mid - 1}, {"gx": mid})),
        ):
            expected = expected + 2 * near.astype(jnp.int32)

            @pl.when(near)
            def _(partners=partners):
                for partner in partners:
                    pl.semaphore_signal(barrier, inc=1, device_id=partner, device_id_type=MESH)

    for way in (SUM1, SUM2):
        pl.semaphore_signal(barrier, inc=1, device_id=target[way], device_id_type=MESH)

    zero = jnp.zeros((8, 128), F32)

    def clear_x(x, speed):
        def at(i, _):
            for y in range(16):
                p[i // NS, lax.rem(i, NS), x, 1 + y] = zero
            return 0

        lax.fori_loop(0, 3 * NS, at, 0)
        speed_x[speed] = jnp.zeros((16, 128), F32)

    def clear_y(y, speed):
        def at(i, _):
            for x in range(4):
                p[i // NS, lax.rem(i, NS), 1 + x, y] = zero
            return 0

        lax.fori_loop(0, 3 * NS, at, 0)
        for x in range(4):
            speed_y[x, speed : speed + 8] = zero

    pl.when(ix == 0)(lambda: clear_x(0, 0))
    pl.when(ix == nx - 1)(lambda: clear_x(5, 5))
    pl.when(iy == 0)(lambda: clear_y(0, 0))
    pl.when(iy == ny - 1)(lambda: clear_y(17, 24))

    pl.semaphore_wait(barrier, expected)

    def second_exchange(k, c):
        chunk(k, c, SUM1).wait_recv()
        half[k, two(c)] = part[k, two(c)] + part_1[k, two(c)]
        chunk(k, c, SUM2).start()

    def mean_term(k, c):
        chunk(k, c, SUM2).wait_recv()
        scale = (STEP * MIX / FIELDS) * diffusion[...]
        for i in range(2):
            mean_row[i] = scale * (half[k, 2 * c + i] + part_2[k, 2 * c + i])

    flat_in = rows_in.reshape(NS * 8 * 64, 128)

    def turn(c, planes):
        def body(i):
            s, x, h = 2 * c + i // 4, planes(lax.rem(i // 2, 2)), lax.rem(i, 2)
            start = s * 512 + x * 16 + h * 8
            tiles = [flat_in[pl.ds(start + y, 8, stride=64), :] for y in range(8)]
            for y in range(8):
                p[0, s, x + 1, h * 8 + y + 1] = tiles[y]
            part[0, s, x, pl.ds(h * 8, 8), :] = sum_rows(tiles)

        return body

    def section_0(c, _):
        load_in(2 * c).wait()
        load_in(2 * c + 1).wait()
        blocks(8, turn(c, lambda i: 3 * i))
        send(0, c, EAST)
        send(0, c, WEST)
        blocks(8, turn(c, lambda i: 1 + i))
        send(0, c, NORTH)
        send(0, c, SOUTH)
        chunk(0, c, SUM1).start()

        @pl.when(c == 0)
        def _():
            for way in (EAST, WEST, NORTH, SOUTH):
                pl.when(has[way])(lambda way=way: speed_face(way).start())

        @pl.when(c > 0)
        def _():
            pass_on(0, c - 1)
            second_exchange(0, c - 1)

        return 0

    lax.fori_loop(0, PAIRS, section_0, 0)

    for copy in own:
        copy.wait()
    for way in (EAST, WEST, NORTH, SOUTH):
        pl.when(has[back[way]])(lambda way=way: speed_face(way).wait_recv())

    diagonal = lax.broadcasted_iota(jnp.int32, (8, 8), 0) == lax.broadcasted_iota(
        jnp.int32, (8, 8), 1
    )
    draws = []
    for d in range(3):
        row = jnp.broadcast_to(wiener[d : d + 1, :], (8, 8))
        column = jnp.sum(jnp.where(diagonal, row, 0.0), axis=1, keepdims=True)
        draws.append(jnp.broadcast_to(column, (8, 128)))

    def coefficients(x, _):
        g = diffusion[x]
        diffuse = STEP * g
        stir = (0.5 * STEP) * jnp.sqrt((2.0 / STEP) * g)
        lane = lax.broadcasted_iota(jnp.int32, (16, 128), 1)
        upper, lower = lane < 127, lane > 0
        half_step = 0.5 * STEP
        base = [
            diffuse - half_step * speed_x[x + 2],
            diffuse + half_step * speed_x[x],
            diffuse - half_step * speed_y[x, 9:25, :],
            diffuse + half_step * speed_y[x, 7:23, :],
            jnp.where(upper, diffuse - half_step * pltpu.roll(speed_z[x], 127, 1), 0.0),
            jnp.where(lower, diffuse + half_step * pltpu.roll(speed_z[x], 1, 1), 0.0),
        ]
        stir_up, stir_down = jnp.where(upper, stir, 0.0), jnp.where(lower, stir, 0.0)
        keep = 1.0 - (6.0 + MIX) * diffuse
        for y in range(16):
            stir_y = spread(stir, y)
            for d in range(2):
                move = stir_y * draws[d]
                coef[2 * d, x, y] = spread(base[2 * d], y) + move
                coef[2 * d + 1, x, y] = spread(base[2 * d + 1], y) - move
            coef[4, x, y] = spread(base[4], y) + spread(stir_up, y) * draws[2]
            coef[5, x, y] = spread(base[5], y) - spread(stir_down, y) * draws[2]
            keep_y = spread(keep, y)
            centre[0, x, y] = keep_y
            centre[1, x, y] = keep_y - STEP * OXIDATION
        return 0

    lax.fori_loop(0, 4, coefficients, 0)

    flat_out = out.reshape(8 * NS * 64, 128)

    def advance(k, c):
        old = k - 1
        base_weight = jnp.where(k == 1, 0.0, jnp.where(k == 2, 0.75, 1.0 / 3.0))
        section_weight = jnp.where(k == 1, 1.0, jnp.where(k == 2, 0.25, 2.0 / 3.0))

        def body(turn):
            x, y0 = jnp.where(turn < 4, 1 + turn // 2, 3 * (turn // 2) - 6), 8 * lax.rem(turn, 2)

            @pl.when(turn == 4)
            def _():
                arrived(old, c, EAST)
                arrived(old, c, WEST)

            tiles, weights = [[], []], []
            columns = [[p[old, 2 * c + j, x + 1, y0 + i] for i in range(10)] for j in range(2)]
            means = [mean_row[j, x, pl.ds(y0, 8), :] for j in range(2)]
            for i in range(8):
                y = y0 + i
                factor = [coef[d, x, y] for d in range(6)]
                keep = centre[int(c > 0), x, y]
                here = [columns[j][i + 1] for j in range(2)]
                new = [
                    keep * here[j]
                    + spread(means[j], i)
                    + factor[0] * p[old, 2 * c + j, x + 2, y + 1]
                    + factor[1] * p[old, 2 * c + j, x, y + 1]
                    + factor[2] * columns[j][i + 2]
                    + factor[3] * columns[j][i]
                    + factor[4] * pltpu.roll(here[j], 127, 1)
                    + factor[5] * pltpu.roll(here[j], 1, 1)
                    for j in range(2)
                ]
                if c == 0:
                    square = here[0] * here[0]
                    w = square / (1.0 + square) / (1.0 + jnp.exp(-3.0 * here[1]))
                    weights.append(w)
                    new[1] = new[1] - (STEP * RADIATION) * w
                else:
                    w = weight[x, y]
                    before = [p[old, 3, x + 1, y + 1] if c == 2 else None, here[0]]
                    for j in range(2):
                        gain = STEP * NUCLEATION[2 * c - 2 + j]
                        if before[j] is not None:
                            gain = gain + (STEP * GROWTH) * before[j]
                        new[j] = new[j] + w * gain
                for j in range(2):
                    start = p[0, 2 * c + j, x + 1, y + 1]
                    tiles[j].append(base_weight * start + section_weight * new[j])
            for i, w in enumerate(weights):
                weight[x, y0 + i] = w

            @pl.when(k < 3)
            def _():
                for j in range(2):
                    for i in range(8):
                        p[k, 2 * c + j, x + 1, y0 + i + 1] = tiles[j][i]
                    part[k, 2 * c + j, x, pl.ds(y0, 8), :] = sum_rows(tiles[j])

            @pl.when(k == 3)
            def _():
                for j in range(2):
                    row = (2 * c + j) * 64 + x * 16 + y0
                    for i in range(8):
                        flat_out[pl.ds(row + i, 8, stride=NS * 64), :] = tiles[j][i]

        return body

    def section(k, _):
        pass_on(k - 1, PAIRS - 1)
        second_exchange(k - 1, PAIRS - 1)
        for c in range(PAIRS):
            mean_term(k - 1, c)
            arrived(k - 1, c, NORTH)
            arrived(k - 1, c, SOUTH)
            blocks(8, advance(k, c))

            @pl.when(k < 3)
            def _():
                for way in (EAST, WEST, NORTH, SOUTH):
                    send(k, c, way)
                chunk(k, c, SUM1).start()
                if c > 0:
                    pass_on(k, c - 1)
                    second_exchange(k, c - 1)

        return 0

    lax.fori_loop(1, 4, section, 0)

    for way in (EAST, WEST, NORTH, SOUTH):
        pl.when(has[way])(lambda way=way: speed_face(way).wait_send())
        pl.when(has[way])(lambda way=way: all_sent(way))
    all_passed_on()
    all_sent(SUM1)
    all_sent(SUM2)


def local(fields_state, velocity, diffusivity, wiener_draw):
    counts = tuple(lax.axis_size(name) for name in ("gx", "gy", "af"))
    held = fields_state.shape
    dma = pltpu.SemaphoreType.DMA
    vmem = lambda *shape: pltpu.VMEM(shape, F32)
    held_in_hbm = (fields_state.reshape(8, NS, 64, 128), velocity, diffusivity, wiener_draw.T)
    out = pl.pallas_call(
        functools.partial(kernel, counts),
        out_shape=pltpu.VMEM((8, NS, 64, 128), F32),
        in_specs=[pl.BlockSpec(memory_space=pltpu.HBM)] * 4,
        out_specs=pl.BlockSpec(memory_space=pltpu.VMEM),
        scratch_shapes=[
            vmem(NS, 8, 64, 128),
            vmem(3, NS, 6, 18, 8, 128),
            vmem(6, 4, 16, 8, 128),
            vmem(2, 4, 16, 8, 128),
            vmem(4, 16, 8, 128),
            vmem(2, 4, 16, 128),
            vmem(3, NS, 4, 16, 128),
            vmem(3, NS, 4, 16, 128),
            vmem(3, NS, 4, 16, 128),
            vmem(3, NS, 4, 16, 128),
            vmem(6, 16, 128),
            vmem(4, 32, 128),
            vmem(4, 16, 128),
            vmem(4, 16, 128),
            vmem(3, 8),
            vmem(3, PAIRS, 16, 8, 128),
            dma((NS,)),
            dma((5,)),
            dma,
            dma((3, PAIRS)),
            dma((4,)),
            dma((4,)),
            dma((6,)),
            dma((3, PAIRS, 6)),
        ],
        compiler_params=pltpu.CompilerParams(
            collective_id=0, has_side_effects=True, vmem_limit_bytes=48 * 1024 * 1024
        ),
    )(*(pltpu.with_memory_space_constraint(x, pltpu.HBM) for x in held_in_hbm))
    return out.reshape(held)


def solution(mesh):
    return jax.shard_map(
        local,
        mesh=mesh,
        in_specs=(
            P("af", None, "gx", "gy", None),
            P(None, "gx", "gy", None),
            P("gx", "gy", None),
            P("af", None),
        ),
        out_specs=P("af", None, "gx", "gy", None),
        check_vma=False,
    )
```

```python
import functools

import jax
import jax.numpy as jnp
from jax import lax
from jax.experimental import pallas as pl
from jax.experimental.pallas import tpu as pltpu
from jax.sharding import PartitionSpec as P

MESH = pl.DeviceIdType.MESH
F32 = jnp.float32

FIELDS = 32
NS = 6
PAIRS = 3
STEP = 0.3
MIX = 4.0
RADIATION = 0.5
NUCLEATION = (1.0, 0.8, 0.6, 0.5)
GROWTH = 0.5
OXIDATION = 0.3
WEIGHTS = ((0.0, 1.0), (0.75, 0.25), (1.0 / 3.0, 2.0 / 3.0))
EAST, WEST, NORTH, SOUTH, SUM1, SUM2 = range(6)


def sum_rows(tiles):
    row = lax.broadcasted_iota(jnp.int32, (8, 128), 0)
    low = row < 4
    quads = [
        jnp.where(low, tiles[i], tiles[i + 4])
        + pltpu.roll(jnp.where(low, tiles[i + 4], tiles[i]), 4, 0)
        for i in range(4)
    ]
    even = lax.rem(row, 4) < 2
    pairs = [
        jnp.where(even, quads[i], quads[i + 2])
        + jnp.where(even, pltpu.roll(quads[i], 6, 0), pltpu.roll(quads[i + 2], 2, 0))
        for i in range(2)
    ]
    first = lax.rem(row, 2) < 1
    return jnp.where(first, pairs[0], pairs[1]) + jnp.where(
        first, pltpu.roll(pairs[0], 7, 0), pltpu.roll(pairs[1], 1, 0)
    )


def spread(rows, i):
    return jnp.broadcast_to(rows[i : i + 1, :], (8, 128))


def kernel(
    counts,
    fields_hbm,
    velocity_hbm,
    diffusivity_hbm,
    wiener_hbm,
    out,
    rows_in,
    p,
    coef,
    centre,
    weight,
    mean_row,
    part,
    part_1,
    half,
    part_2,
    speed_x,
    speed_y,
    speed_z,
    diffusion,
    wiener,
    relay,
    raw,
    raw_relay,
    in_sem,
    own_sem,
    relay_send,
    relay_recv,
    speed_send,
    speed_recv,
    send_sem,
    recv_sem,
):
    nx, ny, na = counts
    ax, ix, iy = lax.axis_index("af"), lax.axis_index("gx"), lax.axis_index("gy")
    has = {EAST: ix < nx - 1, WEST: ix > 0, NORTH: iy < ny - 1, SOUTH: iy > 0}
    back = {EAST: WEST, WEST: EAST, NORTH: SOUTH, SOUTH: NORTH}
    pair = {SUM1: ax + 1 - 2 * lax.rem(ax, 2), SUM2: na - 1 - ax}
    target = {
        EAST: {"gx": ix + 1},
        WEST: {"gx": ix - 1},
        NORTH: {"gy": iy + 1},
        SOUTH: {"gy": iy - 1},
        SUM1: {"af": pair[SUM1]},
        SUM2: {"af": pair[SUM2]},
    }

    mid, end = nx // 2, nx - 1
    to_relay = {EAST: ix == mid - 1, WEST: ix == mid}
    is_relay = {EAST: ix == end, WEST: ix == 0}
    relay_of = {EAST: {"gx": end}, WEST: {"gx": 0}}
    relay_to = {EAST: {"gx": mid}, WEST: {"gx": mid - 1}}

    def load_in(s):
        return pltpu.make_async_copy(fields_hbm.at[:, s], rows_in.at[s], in_sem.at[s])

    def two(c):
        return pl.ds(2 * c, 2)

    own = [
        pltpu.make_async_copy(velocity_hbm.at[0], speed_x.at[pl.ds(1, 4)], own_sem.at[0]),
        pltpu.make_async_copy(velocity_hbm.at[1], speed_y.at[:, pl.ds(8, 16)], own_sem.at[1]),
        pltpu.make_async_copy(velocity_hbm.at[2], speed_z, own_sem.at[2]),
        pltpu.make_async_copy(diffusivity_hbm, diffusion, own_sem.at[3]),
        pltpu.make_async_copy(wiener_hbm, wiener, own_sem.at[4]),
    ]

    def speed_face(way):
        src, dst = {
            EAST: (velocity_hbm.at[0, 3], speed_x.at[0]),
            WEST: (velocity_hbm.at[0, 0], speed_x.at[5]),
            NORTH: (velocity_hbm.at[1, :, pl.ds(8, 8)], speed_y.at[:, pl.ds(0, 8)]),
            SOUTH: (velocity_hbm.at[1, :, pl.ds(0, 8)], speed_y.at[:, pl.ds(24, 8)]),
        }[way]
        return pltpu.make_async_remote_copy(
            src_ref=src,
            dst_ref=dst,
            send_sem=speed_send.at[way],
            recv_sem=speed_recv.at[way],
            device_id=target[way],
            device_id_type=MESH,
        )

    def face(k, s, way, recv=None):
        src, dst = {
            NORTH: lambda: (p.at[k, s, pl.ds(1, 4), 16], p.at[k, s, pl.ds(1, 4), 0]),
            SOUTH: lambda: (p.at[k, s, pl.ds(1, 4), 1], p.at[k, s, pl.ds(1, 4), 17]),
            SUM1: lambda: (part.at[k, s], part_1.at[k, s]),
            SUM2: lambda: (half.at[k, s], part_2.at[k, s]),
        }[way]()
        return pltpu.make_async_remote_copy(
            src_ref=src,
            dst_ref=dst,
            send_sem=send_sem.at[way],
            recv_sem=recv,
            device_id=target[way],
            device_id_type=MESH,
        )

    def chunk(k, c, way):
        return face(k, two(c), way, recv_sem.at[k, c, way])

    def all_sent(way):
        if way in to_relay:
            all_x = p.at[:, :, 1, pl.ds(1, 16)]
            copy_x((all_x, all_x), way, recv_sem.at[0, 0, way], target[way]).wait_send()
        else:
            face(pl.ds(0, 3), pl.ds(0, NS), way, recv_sem.at[0, 0, way]).wait_send()

    def x_face(k, c, way, s=None):
        src, dst = {EAST: (4, 0), WEST: (1, 5)}[way]
        side = way
        which = pl.ds(2 * c, 2) if s is None else pl.ds(2 * c + s, 1)
        to = pl.ds(0, 2) if s is None else pl.ds(s, 1)
        if k == 0:
            refs = fields_hbm.at[:, which, pl.ds(16 * (src - 1), 16)], raw.at[side, c, :, to]
        else:
            refs = p.at[k, which, src, pl.ds(1, 16)], p.at[k, which, dst, pl.ds(1, 16)]
        return refs

    def copy_x(refs, way, recv, to):
        return pltpu.make_async_remote_copy(
            src_ref=refs[0],
            dst_ref=refs[1],
            send_sem=send_sem.at[way],
            recv_sem=recv,
            device_id=to,
            device_id_type=MESH,
        )

    def relay_at(k, c):
        return raw_relay.at[c] if k == 0 else relay.at[k - 1, c]

    def send_x(k, c):
        for way in (EAST, WEST):
            recv = recv_sem.at[k, c, way]

            @pl.when(has[way] & jnp.logical_not(to_relay[way]))
            def _():
                copy_x(x_face(k, c, way), way, recv, target[way]).start()

            @pl.when(to_relay[way])
            def _():
                src = x_face(k, c, way, 1)[0]
                copy_x(
                    (src, relay_at(k, c)), way, relay_recv.at[k, c], relay_of[way]
                ).start()
                copy_x(x_face(k, c, way, 0), way, recv, target[way]).start()

    def send(k, c, way):
        pl.when(has[way])(lambda: chunk(k, c, way).start())

    def arrived_x(k, c):
        for way in (EAST, WEST):

            @pl.when(has[back[way]])
            def _():
                copy_x(x_face(k, c, way), way, recv_sem.at[k, c, way], target[way]).wait_recv()

    def pass_on(k, c):
        for way in (EAST, WEST):

            @pl.when(is_relay[way])
            def _():
                here = relay_at(k, c)
                pltpu.make_async_copy(here, here, relay_recv.at[k, c]).wait()
                pltpu.make_async_remote_copy(
                    src_ref=here,
                    dst_ref=x_face(k, c, way, 1)[1],
                    send_sem=relay_send,
                    recv_sem=recv_sem.at[k, c, way],
                    device_id=relay_to[way],
                    device_id_type=MESH,
                ).start()

    def all_passed_on():
        for way in (EAST, WEST):

            @pl.when(is_relay[way])
            def _():
                pltpu.make_async_copy(relay, relay, relay_send).wait()
                pltpu.make_async_copy(raw_relay, raw_relay, relay_send).wait()

    def arrived(k, c, way):
        pl.when(has[back[way]])(lambda: chunk(k, c, way).wait_recv())

    def blocks(first, step, count, body):
        def at(i, _):
            body(first + step * (i // 2), lax.rem(i, 2))
            return 0

        lax.fori_loop(0, 2 * count, at, 0)

    load_in(0).start()
    for copy in own:
        copy.start()
    for s in range(1, NS):
        load_in(s).start()

    barrier = pltpu.get_barrier_semaphore()
    expected = 2
    for way in (EAST, WEST, NORTH, SOUTH):
        pl.when(has[way])(
            lambda way=way: pl.semaphore_signal(
                barrier, inc=1, device_id=target[way], device_id_type=MESH
            )
        )
        expected = expected + has[way].astype(jnp.int32)
    for way in (EAST, WEST):
        for near, partners in (
            (to_relay[way], ({"gx": 0}, {"gx": end})),
            (is_relay[way], ({"gx": mid - 1}, {"gx": mid})),
        ):
            expected = expected + 2 * near.astype(jnp.int32)

            @pl.when(near)
            def _(partners=partners):
                for partner in partners:
                    pl.semaphore_signal(barrier, inc=1, device_id=partner, device_id_type=MESH)

    for way in (SUM1, SUM2):
        pl.semaphore_signal(barrier, inc=1, device_id=target[way], device_id_type=MESH)

    zero = jnp.zeros((8, 128), F32)

    def clear_x(x, speed):
        def at(i, _):
            for y in range(16):
                p[i // NS, lax.rem(i, NS), x, 1 + y] = zero
            return 0

        lax.fori_loop(0, 3 * NS, at, 0)
        speed_x[speed] = jnp.zeros((16, 128), F32)

    def clear_y(y, speed):
        def at(i, _):
            for x in range(4):
                p[i // NS, lax.rem(i, NS), 1 + x, y] = zero
            return 0

        lax.fori_loop(0, 3 * NS, at, 0)
        for x in range(4):
            speed_y[x, speed : speed + 8] = zero

    pl.when(ix == 0)(lambda: clear_x(0, 0))
    pl.when(ix == nx - 1)(lambda: clear_x(5, 5))
    pl.when(iy == 0)(lambda: clear_y(0, 0))
    pl.when(iy == ny - 1)(lambda: clear_y(17, 24))

    pl.semaphore_wait(barrier, expected)
    send_x(0, 0)
    for way in (EAST, WEST, NORTH, SOUTH):
        pl.when(has[way])(lambda way=way: speed_face(way).start())
    for c in range(1, PAIRS):
        send_x(0, c)

    def second_exchange(k, c):
        chunk(k, c, SUM1).wait_recv()
        half[k, two(c)] = part[k, two(c)] + part_1[k, two(c)]
        chunk(k, c, SUM2).start()

    def mean_term(k, c):
        chunk(k, c, SUM2).wait_recv()
        scale = (STEP * MIX / FIELDS) * diffusion[...]
        for i in range(2):
            mean_row[i] = scale * (half[k, 2 * c + i] + part_2[k, 2 * c + i])

    def turn(s):
        flat = rows_in.reshape(NS * 8 * 64, 128)

        def body(x, h):
            start = s * 512 + x * 16 + h * 8
            tiles = [flat[pl.ds(start + i, 8, stride=64), :] for i in range(8)]
            for i in range(8):
                p[0, s, x + 1, h * 8 + i + 1] = tiles[i]
            part[0, s, x, pl.ds(h * 8, 8), :] = sum_rows(tiles)

        return body

    raw_rows = raw.reshape(2 * PAIRS * 8 * 32, 128)

    def turn_face(c, way):
        def at(i, _):
            j, h = i // 2, lax.rem(i, 2)
            start = (way * PAIRS + c) * 256 + i * 8
            tiles = [raw_rows[pl.ds(start + y, 8, stride=32), :] for y in range(8)]
            for y in range(8):
                p[0, 2 * c + j, 0 if way == EAST else 5, h * 8 + y + 1] = tiles[y]
            return 0

        lax.fori_loop(0, 4, at, 0)

    for c in range(PAIRS):
        for s in (2 * c, 2 * c + 1):
            load_in(s).wait()
            blocks(0, 1, 4, turn(s))
        send(0, c, NORTH)
        send(0, c, SOUTH)
        chunk(0, c, SUM1).start()
        if c > 0:
            pass_on(0, c - 1)
            second_exchange(0, c - 1)

    for copy in own:
        copy.wait()
    for way in (EAST, WEST, NORTH, SOUTH):
        pl.when(has[back[way]])(lambda way=way: speed_face(way).wait_recv())

    diagonal = lax.broadcasted_iota(jnp.int32, (8, 8), 0) == lax.broadcasted_iota(
        jnp.int32, (8, 8), 1
    )
    draws = []
    for d in range(3):
        row = jnp.broadcast_to(wiener[d : d + 1, :], (8, 8))
        column = jnp.sum(jnp.where(diagonal, row, 0.0), axis=1, keepdims=True)
        draws.append(jnp.broadcast_to(column, (8, 128)))

    def coefficients(x, _):
        g = diffusion[x]
        diffuse = STEP * g
        stir = (0.5 * STEP) * jnp.sqrt((2.0 / STEP) * g)
        lane = lax.broadcasted_iota(jnp.int32, (16, 128), 1)
        upper, lower = lane < 127, lane > 0
        half_step = 0.5 * STEP
        base = [
            diffuse - half_step * speed_x[x + 2],
            diffuse + half_step * speed_x[x],
            diffuse - half_step * speed_y[x, 9:25, :],
            diffuse + half_step * speed_y[x, 7:23, :],
            jnp.where(upper, diffuse - half_step * pltpu.roll(speed_z[x], 127, 1), 0.0),
            jnp.where(lower, diffuse + half_step * pltpu.roll(speed_z[x], 1, 1), 0.0),
        ]
        stir_up, stir_down = jnp.where(upper, stir, 0.0), jnp.where(lower, stir, 0.0)
        keep = 1.0 - (6.0 + MIX) * diffuse
        for y in range(16):
            stir_y = spread(stir, y)
            for d in range(2):
                move = stir_y * draws[d]
                coef[2 * d, x, y] = spread(base[2 * d], y) + move
                coef[2 * d + 1, x, y] = spread(base[2 * d + 1], y) - move
            coef[4, x, y] = spread(base[4], y) + spread(stir_up, y) * draws[2]
            coef[5, x, y] = spread(base[5], y) - spread(stir_down, y) * draws[2]
            keep_y = spread(keep, y)
            centre[0, x, y] = keep_y
            centre[1, x, y] = keep_y - STEP * OXIDATION
        return 0

    lax.fori_loop(0, 4, coefficients, 0)

    def advance(k, c):
        base_weight, section_weight = WEIGHTS[k - 1]
        old = k - 1
        flat = out.reshape(8 * NS * 64, 128)

        def body(x, h):
            y0 = h * 8
            tiles, weights = [[], []], []
            columns = [[p[old, 2 * c + j, x + 1, y0 + i] for i in range(10)] for j in range(2)]
            means = [mean_row[j, x, pl.ds(y0, 8), :] for j in range(2)]
            for i in range(8):
                y = y0 + i
                factor = [coef[d, x, y] for d in range(6)]
                keep = centre[int(c > 0), x, y]
                here = [columns[j][i + 1] for j in range(2)]
                new = [
                    keep * here[j]
                    + spread(means[j], i)
                    + factor[0] * p[old, 2 * c + j, x + 2, y + 1]
                    + factor[1] * p[old, 2 * c + j, x, y + 1]
                    + factor[2] * columns[j][i + 2]
                    + factor[3] * columns[j][i]
                    + factor[4] * pltpu.roll(here[j], 127, 1)
                    + factor[5] * pltpu.roll(here[j], 1, 1)
                    for j in range(2)
                ]
                if c == 0:
                    square = here[0] * here[0]
                    w = square / (1.0 + square) / (1.0 + jnp.exp(-3.0 * here[1]))
                    weights.append(w)
                    new[1] = new[1] - (STEP * RADIATION) * w
                else:
                    w = weight[x, y]
                    before = [p[old, 3, x + 1, y + 1] if c == 2 else None, here[0]]
                    for j in range(2):
                        gain = STEP * NUCLEATION[2 * c - 2 + j]
                        if before[j] is not None:
                            gain = gain + (STEP * GROWTH) * before[j]
                        new[j] = new[j] + w * gain
                for j in range(2):
                    s = 2 * c + j
                    if base_weight:
                        new[j] = base_weight * p[0, s, x + 1, y + 1] + section_weight * new[j]
                    tiles[j].append(new[j])
            for i, w in enumerate(weights):
                weight[x, y0 + i] = w
            for j in range(2):
                s = 2 * c + j
                for i in range(8):
                    if k < 3:
                        p[k, s, x + 1, y0 + i + 1] = tiles[j][i]
                    else:
                        flat[pl.ds(s * 64 + x * 16 + y0 + i, 8, stride=NS * 64), :] = tiles[j][i]
            if k < 3:
                for j in range(2):
                    part[k, 2 * c + j, x, pl.ds(y0, 8), :] = sum_rows(tiles[j])

        return body

    for k in range(1, 4):
        for c in range(PAIRS):
            mean_term(k - 1, c)
            arrived(k - 1, c, NORTH)
            arrived(k - 1, c, SOUTH)
            blocks(1, 1, 2, advance(k, c))
            arrived_x(k - 1, c)
            if k == 1:
                for way in (EAST, WEST):
                    pl.when(has[back[way]])(lambda way=way: turn_face(c, way))
            blocks(0, 3, 2, advance(k, c))
            if k < 3:
                send_x(k, c)
                for way in (NORTH, SOUTH):
                    send(k, c, way)
                chunk(k, c, SUM1).start()
            if c == 0:
                pass_on(k - 1, PAIRS - 1)
                second_exchange(k - 1, PAIRS - 1)
            elif k < 3:
                pass_on(k, c - 1)
                second_exchange(k, c - 1)

    for way in (EAST, WEST, NORTH, SOUTH):
        pl.when(has[way])(lambda way=way: speed_face(way).wait_send())
        pl.when(has[way])(lambda way=way: all_sent(way))
    all_passed_on()
    all_sent(SUM1)
    all_sent(SUM2)


def local(fields_state, velocity, diffusivity, wiener_draw):
    counts = tuple(lax.axis_size(name) for name in ("gx", "gy", "af"))
    held = fields_state.shape
    dma = pltpu.SemaphoreType.DMA
    vmem = lambda *shape: pltpu.VMEM(shape, F32)
    held_in_hbm = (fields_state.reshape(8, NS, 64, 128), velocity, diffusivity, wiener_draw.T)
    out = pl.pallas_call(
        functools.partial(kernel, counts),
        out_shape=pltpu.VMEM((8, NS, 64, 128), F32),
        in_specs=[pl.BlockSpec(memory_space=pltpu.HBM)] * 4,
        out_specs=pl.BlockSpec(memory_space=pltpu.VMEM),
        scratch_shapes=[
            vmem(NS, 8, 64, 128),
            vmem(3, NS, 6, 18, 8, 128),
            vmem(6, 4, 16, 8, 128),
            vmem(2, 4, 16, 8, 128),
            vmem(4, 16, 8, 128),
            vmem(2, 4, 16, 128),
            vmem(3, NS, 4, 16, 128),
            vmem(3, NS, 4, 16, 128),
            vmem(3, NS, 4, 16, 128),
            vmem(3, NS, 4, 16, 128),
            vmem(6, 16, 128),
            vmem(4, 32, 128),
            vmem(4, 16, 128),
            vmem(4, 16, 128),
            vmem(3, 8),
            vmem(2, PAIRS, 1, 16, 8, 128),
            vmem(2, PAIRS, 8, 2, 16, 128),
            vmem(PAIRS, 8, 1, 16, 128),
            dma((NS,)),
            dma((5,)),
            dma,
            dma((3, PAIRS)),
            dma((4,)),
            dma((4,)),
            dma((6,)),
            dma((3, PAIRS, 6)),
        ],
        compiler_params=pltpu.CompilerParams(
            collective_id=0, has_side_effects=True, vmem_limit_bytes=48 * 1024 * 1024
        ),
    )(*(pltpu.with_memory_space_constraint(x, pltpu.HBM) for x in held_in_hbm))
    return out.reshape(held)


def solution(mesh):
    return jax.shard_map(
        local,
        mesh=mesh,
        in_specs=(
            P("af", None, "gx", "gy", None),
            P(None, "gx", "gy", None),
            P("gx", "gy", None),
            P("af", None),
        ),
        out_specs=P("af", None, "gx", "gy", None),
        check_vma=False,
    )
```

```python
import functools

import jax
import jax.numpy as jnp
from jax import lax
from jax.experimental import pallas as pl
from jax.experimental.pallas import tpu as pltpu
from jax.sharding import PartitionSpec as P

MESH = pl.DeviceIdType.MESH
F32 = jnp.float32

FIELDS = 32
NS = 6
PAIRS = 3
STEP = 0.3
MIX = 4.0
RADIATION = 0.5
NUCLEATION = (1.0, 0.8, 0.6, 0.5)
GROWTH = 0.5
OXIDATION = 0.3
WEIGHTS = ((0.0, 1.0), (0.75, 0.25), (1.0 / 3.0, 2.0 / 3.0))
EAST, WEST, NORTH, SOUTH, SUM1, SUM2 = range(6)


def sum_rows(tiles):
    row = lax.broadcasted_iota(jnp.int32, (8, 128), 0)
    low = row < 4
    quads = [
        jnp.where(low, tiles[i], tiles[i + 4])
        + pltpu.roll(jnp.where(low, tiles[i + 4], tiles[i]), 4, 0)
        for i in range(4)
    ]
    even = lax.rem(row, 4) < 2
    pairs = [
        jnp.where(even, quads[i], quads[i + 2])
        + jnp.where(even, pltpu.roll(quads[i], 6, 0), pltpu.roll(quads[i + 2], 2, 0))
        for i in range(2)
    ]
    first = lax.rem(row, 2) < 1
    return jnp.where(first, pairs[0], pairs[1]) + jnp.where(
        first, pltpu.roll(pairs[0], 7, 0), pltpu.roll(pairs[1], 1, 0)
    )


def spread(rows, i):
    return jnp.broadcast_to(rows[i : i + 1, :], (8, 128))


def kernel(
    counts,
    fields_hbm,
    velocity_hbm,
    diffusivity_hbm,
    wiener_hbm,
    out,
    rows_in,
    p,
    coef,
    centre,
    weight,
    mean_row,
    part,
    part_1,
    half,
    part_2,
    speed_x,
    speed_y,
    speed_z,
    diffusion,
    wiener,
    relay,
    raw,
    raw_relay,
    in_sem,
    own_sem,
    relay_send,
    relay_recv,
    x_sem,
    speed_send,
    speed_recv,
    send_sem,
    recv_sem,
):
    nx, ny, na = counts
    ax, ix, iy = lax.axis_index("af"), lax.axis_index("gx"), lax.axis_index("gy")
    has = {EAST: ix < nx - 1, WEST: ix > 0, NORTH: iy < ny - 1, SOUTH: iy > 0}
    back = {EAST: WEST, WEST: EAST, NORTH: SOUTH, SOUTH: NORTH}
    pair = {SUM1: ax + 1 - 2 * lax.rem(ax, 2), SUM2: na - 1 - ax}
    target = {
        EAST: {"gx": ix + 1},
        WEST: {"gx": ix - 1},
        NORTH: {"gy": iy + 1},
        SOUTH: {"gy": iy - 1},
        SUM1: {"af": pair[SUM1]},
        SUM2: {"af": pair[SUM2]},
    }

    mid, end = nx // 2, nx - 1
    to_relay = {EAST: ix == mid - 1, WEST: ix == mid}
    is_relay = {EAST: ix == end, WEST: ix == 0}
    relay_of = {EAST: {"gx": end}, WEST: {"gx": 0}}
    relay_to = {EAST: {"gx": mid}, WEST: {"gx": mid - 1}}

    def load_in(s):
        return pltpu.make_async_copy(fields_hbm.at[:, s], rows_in.at[s], in_sem.at[s])

    def two(c):
        return pl.ds(2 * c, 2)

    own = [
        pltpu.make_async_copy(velocity_hbm.at[0], speed_x.at[pl.ds(1, 4)], own_sem.at[0]),
        pltpu.make_async_copy(velocity_hbm.at[1], speed_y.at[:, pl.ds(8, 16)], own_sem.at[1]),
        pltpu.make_async_copy(velocity_hbm.at[2], speed_z, own_sem.at[2]),
        pltpu.make_async_copy(diffusivity_hbm, diffusion, own_sem.at[3]),
        pltpu.make_async_copy(wiener_hbm, wiener, own_sem.at[4]),
    ]

    def speed_face(way):
        src, dst = {
            EAST: (velocity_hbm.at[0, 3], speed_x.at[0]),
            WEST: (velocity_hbm.at[0, 0], speed_x.at[5]),
            NORTH: (velocity_hbm.at[1, :, pl.ds(8, 8)], speed_y.at[:, pl.ds(0, 8)]),
            SOUTH: (velocity_hbm.at[1, :, pl.ds(0, 8)], speed_y.at[:, pl.ds(24, 8)]),
        }[way]
        return pltpu.make_async_remote_copy(
            src_ref=src,
            dst_ref=dst,
            send_sem=speed_send.at[way],
            recv_sem=speed_recv.at[way],
            device_id=target[way],
            device_id_type=MESH,
        )

    def face(k, s, way, recv=None):
        src, dst = {
            NORTH: lambda: (p.at[k, s, pl.ds(1, 4), 16], p.at[k, s, pl.ds(1, 4), 0]),
            SOUTH: lambda: (p.at[k, s, pl.ds(1, 4), 1], p.at[k, s, pl.ds(1, 4), 17]),
            SUM1: lambda: (part.at[k, s], part_1.at[k, s]),
            SUM2: lambda: (half.at[k, s], part_2.at[k, s]),
        }[way]()
        return pltpu.make_async_remote_copy(
            src_ref=src,
            dst_ref=dst,
            send_sem=send_sem.at[way],
            recv_sem=recv,
            device_id=target[way],
            device_id_type=MESH,
        )

    def chunk(k, c, way):
        return face(k, two(c), way, recv_sem.at[k, c, way])

    def all_sent(way):
        face(pl.ds(0, 3), pl.ds(0, NS), way, recv_sem.at[0, 0, way]).wait_send()

    def x_face(k, c, way, s=None):
        src, dst = {EAST: (4, 0), WEST: (1, 5)}[way]
        side = way
        which = pl.ds(2 * c, 2) if s is None else pl.ds(2 * c + s, 1)
        to = pl.ds(0, 2) if s is None else pl.ds(s, 1)
        if k == 0:
            refs = fields_hbm.at[:, which, pl.ds(16 * (src - 1), 16)], raw.at[side, c, :, to]
        else:
            refs = p.at[k, which, src, pl.ds(1, 16)], p.at[k, which, dst, pl.ds(1, 16)]
        return refs

    def copy_x(refs, way, k, c, recv, to):
        return pltpu.make_async_remote_copy(
            src_ref=refs[0],
            dst_ref=refs[1],
            send_sem=x_sem.at[way, (3 * k + c) % 2],
            recv_sem=recv,
            device_id=to,
            device_id_type=MESH,
        )

    def relay_at(k, c):
        return raw_relay.at[c] if k == 0 else relay.at[k - 1, c]

    def left_x(k, c):
        for way in (EAST, WEST):

            @pl.when(has[way])
            def _():
                copy_x(
                    x_face(k, c, way), way, k, c, recv_sem.at[k, c, way], target[way]
                ).wait_send()

    def send_x(k, c):
        if 3 * k + c >= 2:
            left_x(*divmod(3 * k + c - 2, 3))
        for way in (EAST, WEST):
            recv = recv_sem.at[k, c, way]

            @pl.when(has[way] & jnp.logical_not(to_relay[way]))
            def _():
                copy_x(x_face(k, c, way), way, k, c, recv, target[way]).start()

            @pl.when(to_relay[way])
            def _():
                src = x_face(k, c, way, 1)[0]
                copy_x(
                    (src, relay_at(k, c)), way, k, c, relay_recv.at[k, c], relay_of[way]
                ).start()
                copy_x(x_face(k, c, way, 0), way, k, c, recv, target[way]).start()

    def send(k, c, way):
        pl.when(has[way])(lambda: chunk(k, c, way).start())

    def arrived_x(k, c):
        for way in (EAST, WEST):

            @pl.when(has[back[way]])
            def _():
                copy_x(
                    x_face(k, c, way), way, k, c, recv_sem.at[k, c, way], target[way]
                ).wait_recv()

    def pass_on(k, c):
        for way in (EAST, WEST):

            @pl.when(is_relay[way])
            def _():
                here = relay_at(k, c)
                pltpu.make_async_copy(here, here, relay_recv.at[k, c]).wait()
                pltpu.make_async_remote_copy(
                    src_ref=here,
                    dst_ref=x_face(k, c, way, 1)[1],
                    send_sem=relay_send,
                    recv_sem=recv_sem.at[k, c, way],
                    device_id=relay_to[way],
                    device_id_type=MESH,
                ).start()

    def all_passed_on():
        for way in (EAST, WEST):

            @pl.when(is_relay[way])
            def _():
                pltpu.make_async_copy(relay, relay, relay_send).wait()
                pltpu.make_async_copy(raw_relay, raw_relay, relay_send).wait()

    def arrived(k, c, way):
        pl.when(has[back[way]])(lambda: chunk(k, c, way).wait_recv())

    def blocks(first, step, count, body):
        def at(i, _):
            body(first + step * (i // 2), lax.rem(i, 2))
            return 0

        lax.fori_loop(0, 2 * count, at, 0)

    load_in(0).start()
    for copy in own:
        copy.start()
    for s in range(1, NS):
        load_in(s).start()

    barrier = pltpu.get_barrier_semaphore()
    expected = 2
    for way in (EAST, WEST, NORTH, SOUTH):
        pl.when(has[way])(
            lambda way=way: pl.semaphore_signal(
                barrier, inc=1, device_id=target[way], device_id_type=MESH
            )
        )
        expected = expected + has[way].astype(jnp.int32)
    for way in (EAST, WEST):
        for near, partners in (
            (to_relay[way], ({"gx": 0}, {"gx": end})),
            (is_relay[way], ({"gx": mid - 1}, {"gx": mid})),
        ):
            expected = expected + 2 * near.astype(jnp.int32)

            @pl.when(near)
            def _(partners=partners):
                for partner in partners:
                    pl.semaphore_signal(barrier, inc=1, device_id=partner, device_id_type=MESH)

    for way in (SUM1, SUM2):
        pl.semaphore_signal(barrier, inc=1, device_id=target[way], device_id_type=MESH)

    zero = jnp.zeros((8, 128), F32)

    def clear_x(x, speed):
        def at(i, _):
            for y in range(16):
                p[i // NS, lax.rem(i, NS), x, 1 + y] = zero
            return 0

        lax.fori_loop(0, 3 * NS, at, 0)
        speed_x[speed] = jnp.zeros((16, 128), F32)

    def clear_y(y, speed):
        def at(i, _):
            for x in range(4):
                p[i // NS, lax.rem(i, NS), 1 + x, y] = zero
            return 0

        lax.fori_loop(0, 3 * NS, at, 0)
        for x in range(4):
            speed_y[x, speed : speed + 8] = zero

    pl.when(ix == 0)(lambda: clear_x(0, 0))
    pl.when(ix == nx - 1)(lambda: clear_x(5, 5))
    pl.when(iy == 0)(lambda: clear_y(0, 0))
    pl.when(iy == ny - 1)(lambda: clear_y(17, 24))

    pl.semaphore_wait(barrier, expected)
    send_x(0, 0)
    for way in (EAST, WEST, NORTH, SOUTH):
        pl.when(has[way])(lambda way=way: speed_face(way).start())
    send_x(0, 1)

    def second_exchange(k, c):
        chunk(k, c, SUM1).wait_recv()
        half[k, two(c)] = part[k, two(c)] + part_1[k, two(c)]
        chunk(k, c, SUM2).start()

    def mean_term(k, c):
        chunk(k, c, SUM2).wait_recv()
        scale = (STEP * MIX / FIELDS) * diffusion[...]
        for i in range(2):
            mean_row[i] = scale * (half[k, 2 * c + i] + part_2[k, 2 * c + i])

    def turn(s):
        flat = rows_in.reshape(NS * 8 * 64, 128)

        def body(x, h):
            start = s * 512 + x * 16 + h * 8
            tiles = [flat[pl.ds(start + i, 8, stride=64), :] for i in range(8)]
            for i in range(8):
                p[0, s, x + 1, h * 8 + i + 1] = tiles[i]
            part[0, s, x, pl.ds(h * 8, 8), :] = sum_rows(tiles)

        return body

    raw_rows = raw.reshape(2 * PAIRS * 8 * 32, 128)

    def turn_face(c, way):
        def at(i, _):
            j, h = i // 2, lax.rem(i, 2)
            start = (way * PAIRS + c) * 256 + i * 8
            tiles = [raw_rows[pl.ds(start + y, 8, stride=32), :] for y in range(8)]
            for y in range(8):
                p[0, 2 * c + j, 0 if way == EAST else 5, h * 8 + y + 1] = tiles[y]
            return 0

        lax.fori_loop(0, 4, at, 0)

    for c in range(PAIRS):
        for s in (2 * c, 2 * c + 1):
            load_in(s).wait()
            blocks(0, 1, 4, turn(s))
        send(0, c, NORTH)
        send(0, c, SOUTH)
        chunk(0, c, SUM1).start()
        if c > 0:
            pass_on(0, c - 1)
            second_exchange(0, c - 1)

    for copy in own:
        copy.wait()
    for way in (EAST, WEST, NORTH, SOUTH):
        pl.when(has[back[way]])(lambda way=way: speed_face(way).wait_recv())

    diagonal = lax.broadcasted_iota(jnp.int32, (8, 8), 0) == lax.broadcasted_iota(
        jnp.int32, (8, 8), 1
    )
    draws = []
    for d in range(3):
        row = jnp.broadcast_to(wiener[d : d + 1, :], (8, 8))
        column = jnp.sum(jnp.where(diagonal, row, 0.0), axis=1, keepdims=True)
        draws.append(jnp.broadcast_to(column, (8, 128)))

    def coefficients(x, _):
        g = diffusion[x]
        diffuse = STEP * g
        stir = (0.5 * STEP) * jnp.sqrt((2.0 / STEP) * g)
        lane = lax.broadcasted_iota(jnp.int32, (16, 128), 1)
        upper, lower = lane < 127, lane > 0
        half_step = 0.5 * STEP
        base = [
            diffuse - half_step * speed_x[x + 2],
            diffuse + half_step * speed_x[x],
            diffuse - half_step * speed_y[x, 9:25, :],
            diffuse + half_step * speed_y[x, 7:23, :],
            jnp.where(upper, diffuse - half_step * pltpu.roll(speed_z[x], 127, 1), 0.0),
            jnp.where(lower, diffuse + half_step * pltpu.roll(speed_z[x], 1, 1), 0.0),
        ]
        stir_up, stir_down = jnp.where(upper, stir, 0.0), jnp.where(lower, stir, 0.0)
        keep = 1.0 - (6.0 + MIX) * diffuse
        for y in range(16):
            stir_y = spread(stir, y)
            for d in range(2):
                move = stir_y * draws[d]
                coef[2 * d, x, y] = spread(base[2 * d], y) + move
                coef[2 * d + 1, x, y] = spread(base[2 * d + 1], y) - move
            coef[4, x, y] = spread(base[4], y) + spread(stir_up, y) * draws[2]
            coef[5, x, y] = spread(base[5], y) - spread(stir_down, y) * draws[2]
            keep_y = spread(keep, y)
            centre[0, x, y] = keep_y
            centre[1, x, y] = keep_y - STEP * OXIDATION
        return 0

    lax.fori_loop(0, 4, coefficients, 0)
    send_x(0, 2)

    def advance(k, c):
        base_weight, section_weight = WEIGHTS[k - 1]
        old = k - 1
        flat = out.reshape(8 * NS * 64, 128)

        def body(x, h):
            y0 = h * 8
            tiles, weights = [[], []], []
            columns = [[p[old, 2 * c + j, x + 1, y0 + i] for i in range(10)] for j in range(2)]
            means = [mean_row[j, x, pl.ds(y0, 8), :] for j in range(2)]
            for i in range(8):
                y = y0 + i
                factor = [coef[d, x, y] for d in range(6)]
                keep = centre[int(c > 0), x, y]
                here = [columns[j][i + 1] for j in range(2)]
                new = [
                    keep * here[j]
                    + spread(means[j], i)
                    + factor[0] * p[old, 2 * c + j, x + 2, y + 1]
                    + factor[1] * p[old, 2 * c + j, x, y + 1]
                    + factor[2] * columns[j][i + 2]
                    + factor[3] * columns[j][i]
                    + factor[4] * pltpu.roll(here[j], 127, 1)
                    + factor[5] * pltpu.roll(here[j], 1, 1)
                    for j in range(2)
                ]
                if c == 0:
                    square = here[0] * here[0]
                    w = square / (1.0 + square) / (1.0 + jnp.exp(-3.0 * here[1]))
                    weights.append(w)
                    new[1] = new[1] - (STEP * RADIATION) * w
                else:
                    w = weight[x, y]
                    before = [p[old, 3, x + 1, y + 1] if c == 2 else None, here[0]]
                    for j in range(2):
                        gain = STEP * NUCLEATION[2 * c - 2 + j]
                        if before[j] is not None:
                            gain = gain + (STEP * GROWTH) * before[j]
                        new[j] = new[j] + w * gain
                for j in range(2):
                    s = 2 * c + j
                    if base_weight:
                        new[j] = base_weight * p[0, s, x + 1, y + 1] + section_weight * new[j]
                    tiles[j].append(new[j])
            for i, w in enumerate(weights):
                weight[x, y0 + i] = w
            for j in range(2):
                s = 2 * c + j
                for i in range(8):
                    if k < 3:
                        p[k, s, x + 1, y0 + i + 1] = tiles[j][i]
                    else:
                        flat[pl.ds(s * 64 + x * 16 + y0 + i, 8, stride=NS * 64), :] = tiles[j][i]
            if k < 3:
                for j in range(2):
                    part[k, 2 * c + j, x, pl.ds(y0, 8), :] = sum_rows(tiles[j])

        return body

    for k in range(1, 4):
        for c in range(PAIRS):
            mean_term(k - 1, c)
            arrived(k - 1, c, NORTH)
            arrived(k - 1, c, SOUTH)
            blocks(1, 1, 2, advance(k, c))
            arrived_x(k - 1, c)
            if k == 1:
                for way in (EAST, WEST):
                    pl.when(has[back[way]])(lambda way=way: turn_face(c, way))
            blocks(0, 3, 2, advance(k, c))
            if k < 3:
                for way in (NORTH, SOUTH):
                    send(k, c, way)
                chunk(k, c, SUM1).start()
                send_x(k, c)
            if c == 0:
                pass_on(k - 1, PAIRS - 1)
                second_exchange(k - 1, PAIRS - 1)
            elif k < 3:
                pass_on(k, c - 1)
                second_exchange(k, c - 1)

    for way in (EAST, WEST, NORTH, SOUTH):
        pl.when(has[way])(lambda way=way: speed_face(way).wait_send())
        if way not in to_relay:
            pl.when(has[way])(lambda way=way: all_sent(way))
    left_x(2, 1)
    left_x(2, 2)
    all_passed_on()
    all_sent(SUM1)
    all_sent(SUM2)


def local(fields_state, velocity, diffusivity, wiener_draw):
    counts = tuple(lax.axis_size(name) for name in ("gx", "gy", "af"))
    held = fields_state.shape
    dma = pltpu.SemaphoreType.DMA
    vmem = lambda *shape: pltpu.VMEM(shape, F32)
    held_in_hbm = (fields_state.reshape(8, NS, 64, 128), velocity, diffusivity, wiener_draw.T)
    out = pl.pallas_call(
        functools.partial(kernel, counts),
        out_shape=pltpu.VMEM((8, NS, 64, 128), F32),
        in_specs=[pl.BlockSpec(memory_space=pltpu.HBM)] * 4,
        out_specs=pl.BlockSpec(memory_space=pltpu.VMEM),
        scratch_shapes=[
            vmem(NS, 8, 64, 128),
            vmem(3, NS, 6, 18, 8, 128),
            vmem(6, 4, 16, 8, 128),
            vmem(2, 4, 16, 8, 128),
            vmem(4, 16, 8, 128),
            vmem(2, 4, 16, 128),
            vmem(3, NS, 4, 16, 128),
            vmem(3, NS, 4, 16, 128),
            vmem(3, NS, 4, 16, 128),
            vmem(3, NS, 4, 16, 128),
            vmem(6, 16, 128),
            vmem(4, 32, 128),
            vmem(4, 16, 128),
            vmem(4, 16, 128),
            vmem(3, 8),
            vmem(2, PAIRS, 1, 16, 8, 128),
            vmem(2, PAIRS, 8, 2, 16, 128),
            vmem(PAIRS, 8, 1, 16, 128),
            dma((NS,)),
            dma((5,)),
            dma,
            dma((3, PAIRS)),
            dma((2, 2)),
            dma((4,)),
            dma((4,)),
            dma((6,)),
            dma((3, PAIRS, 6)),
        ],
        compiler_params=pltpu.CompilerParams(
            collective_id=0, has_side_effects=True, vmem_limit_bytes=48 * 1024 * 1024
        ),
    )(*(pltpu.with_memory_space_constraint(x, pltpu.HBM) for x in held_in_hbm))
    return out.reshape(held)


def solution(mesh):
    return jax.shard_map(
        local,
        mesh=mesh,
        in_specs=(
            P("af", None, "gx", "gy", None),
            P(None, "gx", "gy", None),
            P("gx", "gy", None),
            P("af", None),
        ),
        out_specs=P("af", None, "gx", "gy", None),
        check_vma=False,
    )
```

```python
import functools

import jax
import jax.numpy as jnp
from jax import lax
from jax.experimental import pallas as pl
from jax.experimental.pallas import tpu as pltpu
from jax.sharding import PartitionSpec as P

MESH = pl.DeviceIdType.MESH
F32 = jnp.float32

FIELDS = 32
NS = 6
PAIRS = 3
STEP = 0.3
MIX = 4.0
RADIATION = 0.5
NUCLEATION = (1.0, 0.8, 0.6, 0.5)
GROWTH = 0.5
OXIDATION = 0.3
WEIGHTS = ((0.0, 1.0), (0.75, 0.25), (1.0 / 3.0, 2.0 / 3.0))
EAST, WEST, NORTH, SOUTH, SUM1, SUM2 = range(6)


def sum_rows(tiles):
    row = lax.broadcasted_iota(jnp.int32, (8, 128), 0)
    low = row < 4
    quads = [
        jnp.where(low, tiles[i], tiles[i + 4])
        + pltpu.roll(jnp.where(low, tiles[i + 4], tiles[i]), 4, 0)
        for i in range(4)
    ]
    even = (row & 2) == 0
    pairs = [
        jnp.where(even, quads[i], quads[i + 2])
        + jnp.where(even, pltpu.roll(quads[i], 6, 0), pltpu.roll(quads[i + 2], 2, 0))
        for i in range(2)
    ]
    first = (row & 1) == 0
    return jnp.where(first, pairs[0], pairs[1]) + jnp.where(
        first, pltpu.roll(pairs[0], 7, 0), pltpu.roll(pairs[1], 1, 0)
    )


def spread(rows, i):
    return jnp.broadcast_to(rows[i : i + 1, :], (8, 128))


def kernel(
    counts,
    fields_hbm,
    velocity_hbm,
    diffusivity_hbm,
    wiener_hbm,
    out,
    rows_in,
    p,
    coef,
    centre,
    weight,
    mean_row,
    part,
    part_1,
    half,
    part_2,
    speed_x,
    speed_y,
    speed_z,
    diffusion,
    wiener,
    relay,
    raw,
    raw_relay,
    in_sem,
    own_sem,
    relay_send,
    relay_recv,
    speed_send,
    speed_recv,
    send_sem,
    recv_sem,
):
    nx, ny, na = counts
    ax, ix, iy = lax.axis_index("af"), lax.axis_index("gx"), lax.axis_index("gy")
    has = {EAST: ix < nx - 1, WEST: ix > 0, NORTH: iy < ny - 1, SOUTH: iy > 0}
    back = {EAST: WEST, WEST: EAST, NORTH: SOUTH, SOUTH: NORTH}
    pair = {SUM1: ax + 1 - 2 * lax.rem(ax, 2), SUM2: na - 1 - ax}
    target = {
        EAST: {"gx": ix + 1},
        WEST: {"gx": ix - 1},
        NORTH: {"gy": iy + 1},
        SOUTH: {"gy": iy - 1},
        SUM1: {"af": pair[SUM1]},
        SUM2: {"af": pair[SUM2]},
    }

    mid, end = nx // 2, nx - 1
    to_relay = {EAST: ix == mid - 1, WEST: ix == mid}
    is_relay = {EAST: ix == end, WEST: ix == 0}
    relay_of = {EAST: {"gx": end}, WEST: {"gx": 0}}
    relay_to = {EAST: {"gx": mid}, WEST: {"gx": mid - 1}}

    def load_in(s):
        return pltpu.make_async_copy(fields_hbm.at[:, s], rows_in.at[s], in_sem.at[s])

    def two(c):
        return pl.ds(2 * c, 2)

    own = [
        pltpu.make_async_copy(velocity_hbm.at[0], speed_x.at[pl.ds(1, 4)], own_sem.at[0]),
        pltpu.make_async_copy(velocity_hbm.at[1], speed_y.at[:, pl.ds(8, 16)], own_sem.at[1]),
        pltpu.make_async_copy(velocity_hbm.at[2], speed_z, own_sem.at[2]),
        pltpu.make_async_copy(diffusivity_hbm, diffusion, own_sem.at[3]),
        pltpu.make_async_copy(wiener_hbm, wiener, own_sem.at[4]),
    ]

    def speed_face(way):
        src, dst = {
            EAST: (velocity_hbm.at[0, 3], speed_x.at[0]),
            WEST: (velocity_hbm.at[0, 0], speed_x.at[5]),
            NORTH: (velocity_hbm.at[1, :, pl.ds(8, 8)], speed_y.at[:, pl.ds(0, 8)]),
            SOUTH: (velocity_hbm.at[1, :, pl.ds(0, 8)], speed_y.at[:, pl.ds(24, 8)]),
        }[way]
        return pltpu.make_async_remote_copy(
            src_ref=src,
            dst_ref=dst,
            send_sem=speed_send.at[way],
            recv_sem=speed_recv.at[way],
            device_id=target[way],
            device_id_type=MESH,
        )

    def face(k, s, way, recv=None):
        src, dst = {
            NORTH: lambda: (p.at[k, s, pl.ds(1, 4), 16], p.at[k, s, pl.ds(1, 4), 0]),
            SOUTH: lambda: (p.at[k, s, pl.ds(1, 4), 1], p.at[k, s, pl.ds(1, 4), 17]),
            SUM1: lambda: (part.at[k, s], part_1.at[k, s]),
            SUM2: lambda: (half.at[k, s], part_2.at[k, s]),
        }[way]()
        return pltpu.make_async_remote_copy(
            src_ref=src,
            dst_ref=dst,
            send_sem=send_sem.at[way],
            recv_sem=recv,
            device_id=target[way],
            device_id_type=MESH,
        )

    def chunk(k, c, way):
        return face(k, two(c), way, recv_sem.at[k, c, way])

    def all_sent(way):
        if way in to_relay:
            all_x = p.at[:, :, 1, pl.ds(1, 16)]
            copy_x((all_x, all_x), way, recv_sem.at[0, 0, way], target[way]).wait_send()
        else:
            face(pl.ds(0, 3), pl.ds(0, NS), way, recv_sem.at[0, 0, way]).wait_send()

    def x_face(k, c, way, s=None):
        src, dst = {EAST: (4, 0), WEST: (1, 5)}[way]
        side = way
        which = pl.ds(2 * c, 2) if s is None else pl.ds(2 * c + s, 1)
        to = pl.ds(0, 2) if s is None else pl.ds(s, 1)
        if k == 0:
            refs = fields_hbm.at[:, which, pl.ds(16 * (src - 1), 16)], raw.at[side, c, :, to]
        else:
            refs = p.at[k, which, src, pl.ds(1, 16)], p.at[k, which, dst, pl.ds(1, 16)]
        return refs

    def copy_x(refs, way, recv, to):
        return pltpu.make_async_remote_copy(
            src_ref=refs[0],
            dst_ref=refs[1],
            send_sem=send_sem.at[way],
            recv_sem=recv,
            device_id=to,
            device_id_type=MESH,
        )

    def relay_at(k, c):
        return raw_relay.at[c] if k == 0 else relay.at[k - 1, c]

    def send_x(k, c):
        for way in (EAST, WEST):
            recv = recv_sem.at[k, c, way]

            @pl.when(has[way] & jnp.logical_not(to_relay[way]))
            def _():
                copy_x(x_face(k, c, way), way, recv, target[way]).start()

            @pl.when(to_relay[way])
            def _():
                src = x_face(k, c, way, 1)[0]
                copy_x(
                    (src, relay_at(k, c)), way, relay_recv.at[k, c], relay_of[way]
                ).start()
                copy_x(x_face(k, c, way, 0), way, recv, target[way]).start()

    def send(k, c, way):
        pl.when(has[way])(lambda: chunk(k, c, way).start())

    def arrived_x(k, c):
        for way in (EAST, WEST):

            @pl.when(has[back[way]])
            def _():
                copy_x(x_face(k, c, way), way, recv_sem.at[k, c, way], target[way]).wait_recv()

    def pass_on(k, c):
        for way in (EAST, WEST):

            @pl.when(is_relay[way])
            def _():
                here = relay_at(k, c)
                pltpu.make_async_copy(here, here, relay_recv.at[k, c]).wait()
                pltpu.make_async_remote_copy(
                    src_ref=here,
                    dst_ref=x_face(k, c, way, 1)[1],
                    send_sem=relay_send,
                    recv_sem=recv_sem.at[k, c, way],
                    device_id=relay_to[way],
                    device_id_type=MESH,
                ).start()

    def all_passed_on():
        for way in (EAST, WEST):

            @pl.when(is_relay[way])
            def _():
                pltpu.make_async_copy(relay, relay, relay_send).wait()
                pltpu.make_async_copy(raw_relay, raw_relay, relay_send).wait()

    def arrived(k, c, way):
        pl.when(has[back[way]])(lambda: chunk(k, c, way).wait_recv())

    def planes(first, step, count, body):
        def at(i, _):
            for h in range(2):
                body(first + step * i, h)
            return 0

        lax.fori_loop(0, count, at, 0)

    load_in(0).start()
    for copy in own:
        copy.start()
    for s in range(1, NS):
        load_in(s).start()

    barrier = pltpu.get_barrier_semaphore()
    expected = 2
    for way in (EAST, WEST, NORTH, SOUTH):
        pl.when(has[way])(
            lambda way=way: pl.semaphore_signal(
                barrier, inc=1, device_id=target[way], device_id_type=MESH
            )
        )
        expected = expected + has[way].astype(jnp.int32)
    for way in (EAST, WEST):
        for near, partners in (
            (to_relay[way], ({"gx": 0}, {"gx": end})),
            (is_relay[way], ({"gx": mid - 1}, {"gx": mid})),
        ):
            expected = expected + 2 * near.astype(jnp.int32)

            @pl.when(near)
            def _(partners=partners):
                for partner in partners:
                    pl.semaphore_signal(barrier, inc=1, device_id=partner, device_id_type=MESH)

    for way in (SUM1, SUM2):
        pl.semaphore_signal(barrier, inc=1, device_id=target[way], device_id_type=MESH)

    zero = jnp.zeros((8, 128), F32)

    def clear_x(x, speed):
        def at(s, _):
            for k in range(3):
                for y in range(16):
                    p[k, s, x, 1 + y] = zero
            return 0

        lax.fori_loop(0, NS, at, 0)
        speed_x[speed] = jnp.zeros((16, 128), F32)

    def clear_y(y, speed):
        def at(s, _):
            for k in range(3):
                for x in range(4):
                    p[k, s, 1 + x, y] = zero
            return 0

        lax.fori_loop(0, NS, at, 0)
        for x in range(4):
            speed_y[x, speed : speed + 8] = zero

    pl.when(ix == 0)(lambda: clear_x(0, 0))
    pl.when(ix == nx - 1)(lambda: clear_x(5, 5))
    pl.when(iy == 0)(lambda: clear_y(0, 0))
    pl.when(iy == ny - 1)(lambda: clear_y(17, 24))

    pl.semaphore_wait(barrier, expected)
    send_x(0, 0)
    for way in (EAST, WEST, NORTH, SOUTH):
        pl.when(has[way])(lambda way=way: speed_face(way).start())
    for c in range(1, PAIRS):
        send_x(0, c)

    def second_exchange(k, c):
        chunk(k, c, SUM1).wait_recv()
        half[k, two(c)] = part[k, two(c)] + part_1[k, two(c)]
        chunk(k, c, SUM2).start()

    def mean_term(k, c):
        chunk(k, c, SUM2).wait_recv()
        scale = (STEP * MIX / FIELDS) * diffusion[...]
        for i in range(2):
            mean_row[i] = scale * (half[k, 2 * c + i] + part_2[k, 2 * c + i])

    def turn(s):
        flat = rows_in.reshape(NS * 8 * 64, 128)

        def body(x, h):
            start = s * 512 + x * 16 + h * 8
            tiles = [flat[pl.ds(start + i, 8, stride=64), :] for i in range(8)]
            for i in range(8):
                p[0, s, x + 1, h * 8 + i + 1] = tiles[i]
            part[0, s, x, pl.ds(h * 8, 8), :] = sum_rows(tiles)

        return body

    raw_rows = raw.reshape(2 * PAIRS * 8 * 32, 128)

    def turn_face(c, way):
        for j in range(2):
            start = (way * PAIRS + c) * 256 + j * 16
            for y in range(16):
                tile = raw_rows[pl.ds(start + y, 8, stride=32), :]
                p[0, 2 * c + j, 0 if way == EAST else 5, y + 1] = tile

    for c in range(PAIRS):
        for s in (2 * c, 2 * c + 1):
            load_in(s).wait()
            planes(0, 1, 4, turn(s))
        send(0, c, NORTH)
        send(0, c, SOUTH)
        chunk(0, c, SUM1).start()
        if c > 0:
            pass_on(0, c - 1)
            second_exchange(0, c - 1)

    for copy in own:
        copy.wait()
    for way in (EAST, WEST, NORTH, SOUTH):
        pl.when(has[back[way]])(lambda way=way: speed_face(way).wait_recv())

    diagonal = lax.broadcasted_iota(jnp.int32, (8, 8), 0) == lax.broadcasted_iota(
        jnp.int32, (8, 8), 1
    )
    draws = []
    for d in range(3):
        row = jnp.broadcast_to(wiener[d : d + 1, :], (8, 8))
        column = jnp.sum(jnp.where(diagonal, row, 0.0), axis=1, keepdims=True)
        draws.append(jnp.broadcast_to(column, (8, 128)))

    def coefficients(x, _):
        g = diffusion[x]
        diffuse = STEP * g
        stir = (0.5 * STEP) * jnp.sqrt((2.0 / STEP) * g)
        lane = lax.broadcasted_iota(jnp.int32, (16, 128), 1)
        upper, lower = lane < 127, lane > 0
        half_step = 0.5 * STEP
        base = [
            diffuse - half_step * speed_x[x + 2],
            diffuse + half_step * speed_x[x],
            diffuse - half_step * speed_y[x, 9:25, :],
            diffuse + half_step * speed_y[x, 7:23, :],
            jnp.where(upper, diffuse - half_step * pltpu.roll(speed_z[x], 127, 1), 0.0),
            jnp.where(lower, diffuse + half_step * pltpu.roll(speed_z[x], 1, 1), 0.0),
        ]
        stir_up, stir_down = jnp.where(upper, stir, 0.0), jnp.where(lower, stir, 0.0)
        keep = 1.0 - (6.0 + MIX) * diffuse
        for y in range(16):
            stir_y = spread(stir, y)
            for d in range(2):
                move = stir_y * draws[d]
                coef[2 * d, x, y] = spread(base[2 * d], y) + move
                coef[2 * d + 1, x, y] = spread(base[2 * d + 1], y) - move
            coef[4, x, y] = spread(base[4], y) + spread(stir_up, y) * draws[2]
            coef[5, x, y] = spread(base[5], y) - spread(stir_down, y) * draws[2]
            keep_y = spread(keep, y)
            centre[0, x, y] = keep_y
            centre[1, x, y] = keep_y - STEP * OXIDATION
        return 0

    lax.fori_loop(0, 4, coefficients, 0)

    def advance(k, c):
        base_weight, section_weight = WEIGHTS[k - 1]
        old = k - 1
        flat = out.reshape(8 * NS * 64, 128)

        def body(x, h):
            y0 = h * 8
            tiles, weights = [[], []], []
            columns = [[p[old, 2 * c + j, x + 1, y0 + i] for i in range(10)] for j in range(2)]
            means = [mean_row[j, x, pl.ds(y0, 8), :] for j in range(2)]
            for i in range(8):
                y = y0 + i
                factor = [coef[d, x, y] for d in range(6)]
                keep = centre[int(c > 0), x, y]
                here = [columns[j][i + 1] for j in range(2)]
                new = [
                    keep * here[j]
                    + spread(means[j], i)
                    + factor[0] * p[old, 2 * c + j, x + 2, y + 1]
                    + factor[1] * p[old, 2 * c + j, x, y + 1]
                    + factor[2] * columns[j][i + 2]
                    + factor[3] * columns[j][i]
                    + factor[4] * pltpu.roll(here[j], 127, 1)
                    + factor[5] * pltpu.roll(here[j], 1, 1)
                    for j in range(2)
                ]
                if c == 0:
                    square = here[0] * here[0]
                    w = square / (1.0 + square) / (1.0 + jnp.exp(-3.0 * here[1]))
                    weights.append(w)
                    new[1] = new[1] - (STEP * RADIATION) * w
                else:
                    w = weight[x, y]
                    before = [p[old, 3, x + 1, y + 1] if c == 2 else None, here[0]]
                    for j in range(2):
                        gain = STEP * NUCLEATION[2 * c - 2 + j]
                        if before[j] is not None:
                            gain = gain + (STEP * GROWTH) * before[j]
                        new[j] = new[j] + w * gain
                for j in range(2):
                    s = 2 * c + j
                    if base_weight:
                        new[j] = base_weight * p[0, s, x + 1, y + 1] + section_weight * new[j]
                    tiles[j].append(new[j])
            for i, w in enumerate(weights):
                weight[x, y0 + i] = w
            for j in range(2):
                s = 2 * c + j
                for i in range(8):
                    if k < 3:
                        p[k, s, x + 1, y0 + i + 1] = tiles[j][i]
                    else:
                        flat[pl.ds(s * 64 + x * 16 + y0 + i, 8, stride=NS * 64), :] = tiles[j][i]
            if k < 3:
                for j in range(2):
                    part[k, 2 * c + j, x, pl.ds(y0, 8), :] = sum_rows(tiles[j])

        return body

    for k in range(1, 4):
        for c in range(PAIRS):
            mean_term(k - 1, c)
            arrived(k - 1, c, NORTH)
            arrived(k - 1, c, SOUTH)
            planes(1, 1, 2, advance(k, c))
            arrived_x(k - 1, c)
            if k == 1:
                for way in (EAST, WEST):
                    pl.when(has[back[way]])(lambda way=way: turn_face(c, way))
            planes(0, 3, 2, advance(k, c))
            if k < 3:
                send_x(k, c)
                for way in (NORTH, SOUTH):
                    send(k, c, way)
                chunk(k, c, SUM1).start()
            if c == 0:
                pass_on(k - 1, PAIRS - 1)
                second_exchange(k - 1, PAIRS - 1)
            elif k < 3:
                pass_on(k, c - 1)
                second_exchange(k, c - 1)

    for way in (EAST, WEST, NORTH, SOUTH):
        pl.when(has[way])(lambda way=way: speed_face(way).wait_send())
        pl.when(has[way])(lambda way=way: all_sent(way))
    all_passed_on()
    all_sent(SUM1)
    all_sent(SUM2)


def local(fields_state, velocity, diffusivity, wiener_draw):
    counts = tuple(lax.axis_size(name) for name in ("gx", "gy", "af"))
    held = fields_state.shape
    dma = pltpu.SemaphoreType.DMA
    vmem = lambda *shape: pltpu.VMEM(shape, F32)
    held_in_hbm = (fields_state.reshape(8, NS, 64, 128), velocity, diffusivity, wiener_draw.T)
    out = pl.pallas_call(
        functools.partial(kernel, counts),
        out_shape=pltpu.VMEM((8, NS, 64, 128), F32),
        in_specs=[pl.BlockSpec(memory_space=pltpu.HBM)] * 4,
        out_specs=pl.BlockSpec(memory_space=pltpu.VMEM),
        scratch_shapes=[
            vmem(NS, 8, 64, 128),
            vmem(3, NS, 6, 18, 8, 128),
            vmem(6, 4, 16, 8, 128),
            vmem(2, 4, 16, 8, 128),
            vmem(4, 16, 8, 128),
            vmem(2, 4, 16, 128),
            vmem(3, NS, 4, 16, 128),
            vmem(3, NS, 4, 16, 128),
            vmem(3, NS, 4, 16, 128),
            vmem(3, NS, 4, 16, 128),
            vmem(6, 16, 128),
            vmem(4, 32, 128),
            vmem(4, 16, 128),
            vmem(4, 16, 128),
            vmem(3, 8),
            vmem(2, PAIRS, 1, 16, 8, 128),
            vmem(2, PAIRS, 8, 2, 16, 128),
            vmem(PAIRS, 8, 1, 16, 128),
            dma((NS,)),
            dma((5,)),
            dma,
            dma((3, PAIRS)),
            dma((4,)),
            dma((4,)),
            dma((6,)),
            dma((3, PAIRS, 6)),
        ],
        compiler_params=pltpu.CompilerParams(
            collective_id=0, has_side_effects=True, vmem_limit_bytes=48 * 1024 * 1024
        ),
    )(*(pltpu.with_memory_space_constraint(x, pltpu.HBM) for x in held_in_hbm))
    return out.reshape(held)


def solution(mesh):
    return jax.shard_map(
        local,
        mesh=mesh,
        in_specs=(
            P("af", None, "gx", "gy", None),
            P(None, "gx", "gy", None),
            P("gx", "gy", None),
            P("af", None),
        ),
        out_specs=P("af", None, "gx", "gy", None),
        check_vma=False,
    )
```

```python
import functools

import jax
import jax.numpy as jnp
from jax import lax
from jax.experimental import pallas as pl
from jax.experimental.pallas import tpu as pltpu
from jax.sharding import PartitionSpec as P

MESH = pl.DeviceIdType.MESH
F32 = jnp.float32

FIELDS = 32
NS = 6
PAIRS = 3
STEP = 0.3
MIX = 4.0
RADIATION = 0.5
NUCLEATION = (1.0, 0.8, 0.6, 0.5)
GROWTH = 0.5
OXIDATION = 0.3
WEIGHTS = ((0.0, 1.0), (0.75, 0.25), (1.0 / 3.0, 2.0 / 3.0))
EAST, WEST, NORTH, SOUTH, SUM1, SUM2 = range(6)


def sum_rows(tiles):
    row = lax.broadcasted_iota(jnp.int32, (8, 128), 0)
    low = row < 4
    quads = [
        jnp.where(low, tiles[i], tiles[i + 4])
        + pltpu.roll(jnp.where(low, tiles[i + 4], tiles[i]), 4, 0)
        for i in range(4)
    ]
    even = (row & 2) == 0
    pairs = [
        jnp.where(even, quads[i], quads[i + 2])
        + jnp.where(even, pltpu.roll(quads[i], 6, 0), pltpu.roll(quads[i + 2], 2, 0))
        for i in range(2)
    ]
    first = (row & 1) == 0
    return jnp.where(first, pairs[0], pairs[1]) + jnp.where(
        first, pltpu.roll(pairs[0], 7, 0), pltpu.roll(pairs[1], 1, 0)
    )


def spread(rows, i):
    return jnp.broadcast_to(rows[i : i + 1, :], (8, 128))


def kernel(
    counts,
    fields_hbm,
    velocity_hbm,
    diffusivity_hbm,
    wiener_hbm,
    out,
    rows_in,
    p,
    coef,
    centre,
    weight,
    mean_row,
    part,
    part_in,
    total,
    speed_x,
    speed_y,
    speed_z,
    diffusion,
    wiener,
    relay,
    raw,
    raw_relay,
    in_sem,
    own_sem,
    relay_send,
    relay_recv,
    speed_send,
    speed_recv,
    send_sem,
    recv_sem,
):
    nx, ny, na = counts
    ax, ix, iy = lax.axis_index("af"), lax.axis_index("gx"), lax.axis_index("gy")
    has = {EAST: ix < nx - 1, WEST: ix > 0, NORTH: iy < ny - 1, SOUTH: iy > 0}
    back = {EAST: WEST, WEST: EAST, NORTH: SOUTH, SOUTH: NORTH}
    target = {
        EAST: {"gx": ix + 1},
        WEST: {"gx": ix - 1},
        NORTH: {"gy": iy + 1},
        SOUTH: {"gy": iy - 1},
    }

    mid, end = nx // 2, nx - 1
    to_relay = {EAST: ix == mid - 1, WEST: ix == mid}
    is_relay = {EAST: ix == end, WEST: ix == 0}
    relay_of = {EAST: {"gx": end}, WEST: {"gx": 0}}
    relay_to = {EAST: {"gx": mid}, WEST: {"gx": mid - 1}}

    def load_in(s):
        return pltpu.make_async_copy(fields_hbm.at[:, s], rows_in.at[s], in_sem.at[s])

    def two(c):
        return pl.ds(2 * c, 2)

    own = [
        pltpu.make_async_copy(velocity_hbm.at[0], speed_x.at[pl.ds(1, 4)], own_sem.at[0]),
        pltpu.make_async_copy(velocity_hbm.at[1], speed_y.at[:, pl.ds(8, 16)], own_sem.at[1]),
        pltpu.make_async_copy(velocity_hbm.at[2], speed_z, own_sem.at[2]),
        pltpu.make_async_copy(diffusivity_hbm, diffusion, own_sem.at[3]),
        pltpu.make_async_copy(wiener_hbm, wiener, own_sem.at[4]),
    ]

    def speed_face(way):
        src, dst = {
            EAST: (velocity_hbm.at[0, 3], speed_x.at[0]),
            WEST: (velocity_hbm.at[0, 0], speed_x.at[5]),
            NORTH: (velocity_hbm.at[1, :, pl.ds(8, 8)], speed_y.at[:, pl.ds(0, 8)]),
            SOUTH: (velocity_hbm.at[1, :, pl.ds(0, 8)], speed_y.at[:, pl.ds(24, 8)]),
        }[way]
        return pltpu.make_async_remote_copy(
            src_ref=src,
            dst_ref=dst,
            send_sem=speed_send.at[way],
            recv_sem=speed_recv.at[way],
            device_id=target[way],
            device_id_type=MESH,
        )

    def face(k, s, way, recv=None):
        src, dst = {
            NORTH: lambda: (p.at[k, s, pl.ds(1, 4), 16], p.at[k, s, pl.ds(1, 4), 0]),
            SOUTH: lambda: (p.at[k, s, pl.ds(1, 4), 1], p.at[k, s, pl.ds(1, 4), 17]),
        }[way]()
        return pltpu.make_async_remote_copy(
            src_ref=src,
            dst_ref=dst,
            send_sem=send_sem.at[way],
            recv_sem=recv,
            device_id=target[way],
            device_id_type=MESH,
        )

    def chunk(k, c, way):
        return face(k, two(c), way, recv_sem.at[k, c, way])

    def all_sent(way):
        if way in to_relay:
            all_x = p.at[:, :, 1, pl.ds(1, 16)]
            copy_x((all_x, all_x), way, recv_sem.at[0, 0, way], target[way]).wait_send()
        else:
            face(pl.ds(0, 3), pl.ds(0, NS), way, recv_sem.at[0, 0, way]).wait_send()

    def x_face(k, c, way, s=None):
        src, dst = {EAST: (4, 0), WEST: (1, 5)}[way]
        side = way
        which = pl.ds(2 * c, 2) if s is None else pl.ds(2 * c + s, 1)
        to = pl.ds(0, 2) if s is None else pl.ds(s, 1)
        if k == 0:
            refs = fields_hbm.at[:, which, pl.ds(16 * (src - 1), 16)], raw.at[side, c, :, to]
        else:
            refs = p.at[k, which, src, pl.ds(1, 16)], p.at[k, which, dst, pl.ds(1, 16)]
        return refs

    def copy_x(refs, way, recv, to):
        return pltpu.make_async_remote_copy(
            src_ref=refs[0],
            dst_ref=refs[1],
            send_sem=send_sem.at[way],
            recv_sem=recv,
            device_id=to,
            device_id_type=MESH,
        )

    def relay_at(k, c):
        return raw_relay.at[c] if k == 0 else relay.at[k - 1, c]

    def send_x(k, c):
        for way in (EAST, WEST):
            recv = recv_sem.at[k, c, way]

            @pl.when(has[way] & jnp.logical_not(to_relay[way]))
            def _():
                copy_x(x_face(k, c, way), way, recv, target[way]).start()

            @pl.when(to_relay[way])
            def _():
                src = x_face(k, c, way, 1)[0]
                copy_x(
                    (src, relay_at(k, c)), way, relay_recv.at[k, c], relay_of[way]
                ).start()
                copy_x(x_face(k, c, way, 0), way, recv, target[way]).start()

    def send(k, c, way):
        pl.when(has[way])(lambda: chunk(k, c, way).start())

    def arrived_x(k, c):
        for way in (EAST, WEST):

            @pl.when(has[back[way]])
            def _():
                copy_x(x_face(k, c, way), way, recv_sem.at[k, c, way], target[way]).wait_recv()

    def pass_on(k, c):
        for way in (EAST, WEST):

            @pl.when(is_relay[way])
            def _():
                here = relay_at(k, c)
                pltpu.make_async_copy(here, here, relay_recv.at[k, c]).wait()
                pltpu.make_async_remote_copy(
                    src_ref=here,
                    dst_ref=x_face(k, c, way, 1)[1],
                    send_sem=relay_send,
                    recv_sem=recv_sem.at[k, c, way],
                    device_id=relay_to[way],
                    device_id_type=MESH,
                ).start()

    def all_passed_on():
        for way in (EAST, WEST):

            @pl.when(is_relay[way])
            def _():
                pltpu.make_async_copy(relay, relay, relay_send).wait()
                pltpu.make_async_copy(raw_relay, raw_relay, relay_send).wait()

    def arrived(k, c, way):
        pl.when(has[back[way]])(lambda: chunk(k, c, way).wait_recv())

    def planes(first, step, count, body):
        def at(i, _):
            for h in range(2):
                body(first + step * i, h)
            return 0

        lax.fori_loop(0, count, at, 0)

    load_in(0).start()
    for copy in own:
        copy.start()
    for s in range(1, NS):
        load_in(s).start()

    barrier = pltpu.get_barrier_semaphore()
    expected = na - 1
    for way in (EAST, WEST, NORTH, SOUTH):
        pl.when(has[way])(
            lambda way=way: pl.semaphore_signal(
                barrier, inc=1, device_id=target[way], device_id_type=MESH
            )
        )
        expected = expected + has[way].astype(jnp.int32)
    for way in (EAST, WEST):
        for near, partners in (
            (to_relay[way], ({"gx": 0}, {"gx": end})),
            (is_relay[way], ({"gx": mid - 1}, {"gx": mid})),
        ):
            expected = expected + 2 * near.astype(jnp.int32)

            @pl.when(near)
            def _(partners=partners):
                for partner in partners:
                    pl.semaphore_signal(barrier, inc=1, device_id=partner, device_id_type=MESH)

    for step in range(1, na):
        other = {"af": lax.rem(ax + step, na)}
        pl.semaphore_signal(barrier, inc=1, device_id=other, device_id_type=MESH)

    zero = jnp.zeros((8, 128), F32)

    def clear_x(x, speed):
        def at(s, _):
            for k in range(3):
                for y in range(16):
                    p[k, s, x, 1 + y] = zero
            return 0

        lax.fori_loop(0, NS, at, 0)
        speed_x[speed] = jnp.zeros((16, 128), F32)

    def clear_y(y, speed):
        def at(s, _):
            for k in range(3):
                for x in range(4):
                    p[k, s, 1 + x, y] = zero
            return 0

        lax.fori_loop(0, NS, at, 0)
        for x in range(4):
            speed_y[x, speed : speed + 8] = zero

    pl.when(ix == 0)(lambda: clear_x(0, 0))
    pl.when(ix == nx - 1)(lambda: clear_x(5, 5))
    pl.when(iy == 0)(lambda: clear_y(0, 0))
    pl.when(iy == ny - 1)(lambda: clear_y(17, 24))

    pl.semaphore_wait(barrier, expected)
    send_x(0, 0)
    for way in (EAST, WEST, NORTH, SOUTH):
        pl.when(has[way])(lambda way=way: speed_face(way).start())
    for c in range(1, PAIRS):
        send_x(0, c)

    def scatter(k, c, owner):
        @pl.when(ax != owner)
        def _():
            pltpu.make_async_remote_copy(
                src_ref=part.at[k, two(c), owner],
                dst_ref=part_in.at[k, c, lax.rem(owner - ax + na, na) - 1],
                send_sem=send_sem.at[SUM1],
                recv_sem=recv_sem.at[k, c, SUM1],
                device_id={"af": owner},
                device_id_type=MESH,
            ).start()

    def wait_bytes(ref, sem):
        pltpu.make_async_copy(ref, ref, sem).wait()

    def second_exchange(k, c):
        wait_bytes(part_in.at[k, c], recv_sem.at[k, c, SUM1])
        for i in range(2):
            total[k, 2 * c + i, ax] = (part[k, 2 * c + i, ax] + part_in[k, c, 0, i]) + (
                part_in[k, c, 1, i] + part_in[k, c, 2, i]
            )
        for member in range(na):

            @pl.when(ax != member)
            def _():
                mine = total.at[k, two(c), ax]
                pltpu.make_async_remote_copy(
                    src_ref=mine,
                    dst_ref=mine,
                    send_sem=send_sem.at[SUM2],
                    recv_sem=recv_sem.at[k, c, SUM2],
                    device_id={"af": member},
                    device_id_type=MESH,
                ).start()

    def mean_term(k, c):
        wait_bytes(total.at[k, two(c), pl.ds(0, na - 1)], recv_sem.at[k, c, SUM2])
        scale = (STEP * MIX / FIELDS) * diffusion[...]
        for i in range(2):
            mean_row[i] = scale * total[k, 2 * c + i]

    def turn(s):
        flat = rows_in.reshape(NS * 8 * 64, 128)

        def body(x, h):
            start = s * 512 + x * 16 + h * 8
            tiles = [flat[pl.ds(start + i, 8, stride=64), :] for i in range(8)]
            for i in range(8):
                p[0, s, x + 1, h * 8 + i + 1] = tiles[i]
            part[0, s, x, pl.ds(h * 8, 8), :] = sum_rows(tiles)

        return body

    raw_rows = raw.reshape(2 * PAIRS * 8 * 32, 128)

    def turn_face(c, way):
        for j in range(2):
            start = (way * PAIRS + c) * 256 + j * 16
            for y in range(16):
                tile = raw_rows[pl.ds(start + y, 8, stride=32), :]
                p[0, 2 * c + j, 0 if way == EAST else 5, y + 1] = tile

    for c in range(PAIRS):
        for s in (2 * c, 2 * c + 1):
            load_in(s).wait()
            planes(0, 1, 4, turn(s))
        send(0, c, NORTH)
        send(0, c, SOUTH)
        for owner in range(na):
            scatter(0, c, owner)
        if c > 0:
            pass_on(0, c - 1)
            second_exchange(0, c - 1)

    for copy in own:
        copy.wait()
    for way in (EAST, WEST, NORTH, SOUTH):
        pl.when(has[back[way]])(lambda way=way: speed_face(way).wait_recv())

    diagonal = lax.broadcasted_iota(jnp.int32, (8, 8), 0) == lax.broadcasted_iota(
        jnp.int32, (8, 8), 1
    )
    draws = []
    for d in range(3):
        row = jnp.broadcast_to(wiener[d : d + 1, :], (8, 8))
        column = jnp.sum(jnp.where(diagonal, row, 0.0), axis=1, keepdims=True)
        draws.append(jnp.broadcast_to(column, (8, 128)))

    def coefficients(x, _):
        g = diffusion[x]
        diffuse = STEP * g
        stir = (0.5 * STEP) * jnp.sqrt((2.0 / STEP) * g)
        lane = lax.broadcasted_iota(jnp.int32, (16, 128), 1)
        upper, lower = lane < 127, lane > 0
        half_step = 0.5 * STEP
        base = [
            diffuse - half_step * speed_x[x + 2],
            diffuse + half_step * speed_x[x],
            diffuse - half_step * speed_y[x, 9:25, :],
            diffuse + half_step * speed_y[x, 7:23, :],
            jnp.where(upper, diffuse - half_step * pltpu.roll(speed_z[x], 127, 1), 0.0),
            jnp.where(lower, diffuse + half_step * pltpu.roll(speed_z[x], 1, 1), 0.0),
        ]
        stir_up, stir_down = jnp.where(upper, stir, 0.0), jnp.where(lower, stir, 0.0)
        keep = 1.0 - (6.0 + MIX) * diffuse
        for y in range(16):
            stir_y = spread(stir, y)
            for d in range(2):
                move = stir_y * draws[d]
                coef[2 * d, x, y] = spread(base[2 * d], y) + move
                coef[2 * d + 1, x, y] = spread(base[2 * d + 1], y) - move
            coef[4, x, y] = spread(base[4], y) + spread(stir_up, y) * draws[2]
            coef[5, x, y] = spread(base[5], y) - spread(stir_down, y) * draws[2]
            keep_y = spread(keep, y)
            centre[0, x, y] = keep_y
            centre[1, x, y] = keep_y - STEP * OXIDATION
        return 0

    lax.fori_loop(0, 4, coefficients, 0)

    def advance(k, c):
        base_weight, section_weight = WEIGHTS[k - 1]
        old = k - 1
        flat = out.reshape(8 * NS * 64, 128)

        def body(x, h):
            y0 = h * 8
            tiles, weights = [[], []], []
            columns = [[p[old, 2 * c + j, x + 1, y0 + i] for i in range(10)] for j in range(2)]
            means = [mean_row[j, x, pl.ds(y0, 8), :] for j in range(2)]
            for i in range(8):
                y = y0 + i
                factor = [coef[d, x, y] for d in range(6)]
                keep = centre[int(c > 0), x, y]
                here = [columns[j][i + 1] for j in range(2)]
                new = [
                    keep * here[j]
                    + spread(means[j], i)
                    + factor[0] * p[old, 2 * c + j, x + 2, y + 1]
                    + factor[1] * p[old, 2 * c + j, x, y + 1]
                    + factor[2] * columns[j][i + 2]
                    + factor[3] * columns[j][i]
                    + factor[4] * pltpu.roll(here[j], 127, 1)
                    + factor[5] * pltpu.roll(here[j], 1, 1)
                    for j in range(2)
                ]
                if c == 0:
                    square = here[0] * here[0]
                    w = square / (1.0 + square) / (1.0 + jnp.exp(-3.0 * here[1]))
                    weights.append(w)
                    new[1] = new[1] - (STEP * RADIATION) * w
                else:
                    w = weight[x, y]
                    before = [p[old, 3, x + 1, y + 1] if c == 2 else None, here[0]]
                    for j in range(2):
                        gain = STEP * NUCLEATION[2 * c - 2 + j]
                        if before[j] is not None:
                            gain = gain + (STEP * GROWTH) * before[j]
                        new[j] = new[j] + w * gain
                for j in range(2):
                    s = 2 * c + j
                    if base_weight:
                        new[j] = base_weight * p[0, s, x + 1, y + 1] + section_weight * new[j]
                    tiles[j].append(new[j])
            for i, w in enumerate(weights):
                weight[x, y0 + i] = w
            for j in range(2):
                s = 2 * c + j
                for i in range(8):
                    if k < 3:
                        p[k, s, x + 1, y0 + i + 1] = tiles[j][i]
                    else:
                        flat[pl.ds(s * 64 + x * 16 + y0 + i, 8, stride=NS * 64), :] = tiles[j][i]
            if k < 3:
                for j in range(2):
                    part[k, 2 * c + j, x, pl.ds(y0, 8), :] = sum_rows(tiles[j])

        return body

    for k in range(1, 4):
        for c in range(PAIRS):
            mean_term(k - 1, c)
            arrived(k - 1, c, NORTH)
            arrived(k - 1, c, SOUTH)
            planes(1, 1, 2, advance(k, c))
            if k < 3:
                scatter(k, c, 1)
                scatter(k, c, 2)
            arrived_x(k - 1, c)
            if k == 1:
                for way in (EAST, WEST):
                    pl.when(has[back[way]])(lambda way=way: turn_face(c, way))
            planes(0, 3, 2, advance(k, c))
            if k < 3:
                send_x(k, c)
                scatter(k, c, 0)
                scatter(k, c, 3)
                for way in (NORTH, SOUTH):
                    send(k, c, way)
            if c == 0:
                pass_on(k - 1, PAIRS - 1)
                second_exchange(k - 1, PAIRS - 1)
            elif k < 3:
                pass_on(k, c - 1)
                second_exchange(k, c - 1)

    for way in (EAST, WEST, NORTH, SOUTH):
        pl.when(has[way])(lambda way=way: speed_face(way).wait_send())
        pl.when(has[way])(lambda way=way: all_sent(way))
    all_passed_on()
    wait_bytes(part_in, send_sem.at[SUM1])
    wait_bytes(part_in, send_sem.at[SUM2])


def local(fields_state, velocity, diffusivity, wiener_draw):
    counts = tuple(lax.axis_size(name) for name in ("gx", "gy", "af"))
    held = fields_state.shape
    dma = pltpu.SemaphoreType.DMA
    vmem = lambda *shape: pltpu.VMEM(shape, F32)
    held_in_hbm = (fields_state.reshape(8, NS, 64, 128), velocity, diffusivity, wiener_draw.T)
    out = pl.pallas_call(
        functools.partial(kernel, counts),
        out_shape=pltpu.VMEM((8, NS, 64, 128), F32),
        in_specs=[pl.BlockSpec(memory_space=pltpu.HBM)] * 4,
        out_specs=pl.BlockSpec(memory_space=pltpu.VMEM),
        scratch_shapes=[
            vmem(NS, 8, 64, 128),
            vmem(3, NS, 6, 18, 8, 128),
            vmem(6, 4, 16, 8, 128),
            vmem(2, 4, 16, 8, 128),
            vmem(4, 16, 8, 128),
            vmem(2, 4, 16, 128),
            vmem(3, NS, 4, 16, 128),
            vmem(3, PAIRS, 3, 2, 16, 128),
            vmem(3, NS, 4, 16, 128),
            vmem(6, 16, 128),
            vmem(4, 32, 128),
            vmem(4, 16, 128),
            vmem(4, 16, 128),
            vmem(3, 8),
            vmem(2, PAIRS, 1, 16, 8, 128),
            vmem(2, PAIRS, 8, 2, 16, 128),
            vmem(PAIRS, 8, 1, 16, 128),
            dma((NS,)),
            dma((5,)),
            dma,
            dma((3, PAIRS)),
            dma((4,)),
            dma((4,)),
            dma((6,)),
            dma((3, PAIRS, 6)),
        ],
        compiler_params=pltpu.CompilerParams(
            collective_id=0, has_side_effects=True, vmem_limit_bytes=48 * 1024 * 1024
        ),
    )(*(pltpu.with_memory_space_constraint(x, pltpu.HBM) for x in held_in_hbm))
    return out.reshape(held)


def solution(mesh):
    return jax.shard_map(
        local,
        mesh=mesh,
        in_specs=(
            P("af", None, "gx", "gy", None),
            P(None, "gx", "gy", None),
            P("gx", "gy", None),
            P("af", None),
        ),
        out_specs=P("af", None, "gx", "gy", None),
        check_vma=False,
    )
```

```python
import functools

import jax
import jax.numpy as jnp
from jax import lax
from jax.experimental import pallas as pl
from jax.experimental.pallas import tpu as pltpu
from jax.sharding import PartitionSpec as P

MESH = pl.DeviceIdType.MESH
F32 = jnp.float32

FIELDS = 32
NS = 6
PAIRS = 3
STEP = 0.3
MIX = 4.0
RADIATION = 0.5
NUCLEATION = (1.0, 0.8, 0.6, 0.5)
GROWTH = 0.5
OXIDATION = 0.3
WEIGHTS = ((0.0, 1.0), (0.75, 0.25), (1.0 / 3.0, 2.0 / 3.0))
EAST, WEST, NORTH, SOUTH, SUM1, SUM2 = range(6)


def sum_rows(tiles):
    row = lax.broadcasted_iota(jnp.int32, (8, 128), 0)
    low = row < 4
    quads = [
        jnp.where(low, tiles[i], tiles[i + 4])
        + pltpu.roll(jnp.where(low, tiles[i + 4], tiles[i]), 4, 0)
        for i in range(4)
    ]
    even = (row & 2) == 0
    pairs = [
        jnp.where(even, quads[i], quads[i + 2])
        + jnp.where(even, pltpu.roll(quads[i], 6, 0), pltpu.roll(quads[i + 2], 2, 0))
        for i in range(2)
    ]
    first = (row & 1) == 0
    return jnp.where(first, pairs[0], pairs[1]) + jnp.where(
        first, pltpu.roll(pairs[0], 7, 0), pltpu.roll(pairs[1], 1, 0)
    )


def spread(rows, i):
    return jnp.broadcast_to(rows[i : i + 1, :], (8, 128))


def kernel(
    counts,
    fields_hbm,
    velocity_hbm,
    diffusivity_hbm,
    wiener_hbm,
    out,
    rows_in,
    p,
    coef,
    centre,
    weight,
    mean_row,
    part,
    part_in,
    total,
    speed_x,
    speed_y,
    speed_z,
    diffusion,
    wiener,
    relay,
    raw,
    raw_relay,
    in_sem,
    own_sem,
    relay_send,
    relay_recv,
    speed_send,
    speed_recv,
    send_sem,
    recv_sem,
):
    nx, ny, na = counts
    ax, ix, iy = lax.axis_index("af"), lax.axis_index("gx"), lax.axis_index("gy")
    has = {EAST: ix < nx - 1, WEST: ix > 0, NORTH: iy < ny - 1, SOUTH: iy > 0}
    back = {EAST: WEST, WEST: EAST, NORTH: SOUTH, SOUTH: NORTH}
    target = {
        EAST: (ax, ix + 1, iy),
        WEST: (ax, ix - 1, iy),
        NORTH: (ax, ix, iy + 1),
        SOUTH: (ax, ix, iy - 1),
    }
    members = [lax.rem(ax + step, na) for step in range(na)]
    member_ids = [(other, ix, iy) for other in members]

    mid, end = nx // 2, nx - 1
    to_relay = {EAST: ix == mid - 1, WEST: ix == mid}
    is_relay = {EAST: ix == end, WEST: ix == 0}
    relay_of = {EAST: (ax, end, iy), WEST: (ax, 0, iy)}
    relay_to = {EAST: (ax, mid, iy), WEST: (ax, mid - 1, iy)}
    is_mid, is_end = to_relay[EAST] | to_relay[WEST], is_relay[EAST] | is_relay[WEST]
    both = {EAST: has[EAST] & has[WEST], NORTH: has[NORTH] & has[SOUTH]}
    plain = {way: has[way] & jnp.logical_not(to_relay[way]) for way in (EAST, WEST)}

    def load_in(s):
        return pltpu.make_async_copy(fields_hbm.at[:, s], rows_in.at[s], in_sem.at[s])

    def two(c):
        return pl.ds(2 * c, 2)

    own = [
        pltpu.make_async_copy(velocity_hbm.at[0], speed_x.at[pl.ds(1, 4)], own_sem.at[0]),
        pltpu.make_async_copy(velocity_hbm.at[1], speed_y.at[:, pl.ds(8, 16)], own_sem.at[1]),
        pltpu.make_async_copy(velocity_hbm.at[2], speed_z, own_sem.at[2]),
        pltpu.make_async_copy(diffusivity_hbm, diffusion, own_sem.at[3]),
        pltpu.make_async_copy(wiener_hbm, wiener, own_sem.at[4]),
    ]

    def speed_face(way):
        src, dst = {
            EAST: (velocity_hbm.at[0, 3], speed_x.at[0]),
            WEST: (velocity_hbm.at[0, 0], speed_x.at[5]),
            NORTH: (velocity_hbm.at[1, :, pl.ds(8, 8)], speed_y.at[:, pl.ds(0, 8)]),
            SOUTH: (velocity_hbm.at[1, :, pl.ds(0, 8)], speed_y.at[:, pl.ds(24, 8)]),
        }[way]
        return pltpu.make_async_remote_copy(
            src_ref=src,
            dst_ref=dst,
            send_sem=speed_send.at[way],
            recv_sem=speed_recv.at[way],
            device_id=target[way],
            device_id_type=MESH,
        )

    def face(k, s, way, recv=None):
        src, dst = {
            NORTH: lambda: (p.at[k, s, pl.ds(1, 4), 16], p.at[k, s, pl.ds(1, 4), 0]),
            SOUTH: lambda: (p.at[k, s, pl.ds(1, 4), 1], p.at[k, s, pl.ds(1, 4), 17]),
        }[way]()
        return pltpu.make_async_remote_copy(
            src_ref=src,
            dst_ref=dst,
            send_sem=send_sem.at[way],
            recv_sem=recv,
            device_id=target[way],
            device_id_type=MESH,
        )

    def chunk(k, c, way):
        return face(k, two(c), way, recv_sem.at[k, c, NORTH])

    def wait_bytes(ref, sem):
        pltpu.make_async_copy(ref, ref, sem).wait()

    def all_sent(way):
        if way in to_relay:
            wait_bytes(p.at[:, :, 1, pl.ds(1, 16)], send_sem.at[way])
        else:
            wait_bytes(p.at[:, :, pl.ds(1, 4), 1], send_sem.at[way])

    def x_face(k, c, way, s=None):
        src, dst = {EAST: (4, 0), WEST: (1, 5)}[way]
        side = way
        which = pl.ds(2 * c, 2) if s is None else pl.ds(2 * c + s, 1)
        to = pl.ds(0, 2) if s is None else pl.ds(s, 1)
        if k == 0:
            refs = fields_hbm.at[:, which, pl.ds(16 * (src - 1), 16)], raw.at[side, c, :, to]
        else:
            refs = p.at[k, which, src, pl.ds(1, 16)], p.at[k, which, dst, pl.ds(1, 16)]
        return refs

    def copy_x(refs, way, recv, to):
        return pltpu.make_async_remote_copy(
            src_ref=refs[0],
            dst_ref=refs[1],
            send_sem=send_sem.at[way],
            recv_sem=recv,
            device_id=to,
            device_id_type=MESH,
        )

    def relay_at(k, c):
        return raw_relay.at[c] if k == 0 else relay.at[k - 1, c]

    def send_x(k, c):
        recv = recv_sem.at[k, c, EAST]
        for way in (EAST, WEST):

            @pl.when(plain[way])
            def _():
                copy_x(x_face(k, c, way), way, recv, target[way]).start()

        @pl.when(is_mid)
        def _():
            for way in (EAST, WEST):

                @pl.when(to_relay[way])
                def _():
                    src = x_face(k, c, way, 1)[0]
                    copy_x(
                        (src, relay_at(k, c)), way, relay_recv.at[k, c], relay_of[way]
                    ).start()
                    copy_x(x_face(k, c, way, 0), way, recv, target[way]).start()

    def send_y(k, c):
        for way in (NORTH, SOUTH):
            pl.when(has[way])(lambda: chunk(k, c, way).start())

    def arrived_y(k, c):
        sem = recv_sem.at[k, c, NORTH]
        two_faces = p.at[k, two(c), pl.ds(1, 4), pl.ds(0, 2)]
        one_face = p.at[k, two(c), pl.ds(1, 4), pl.ds(0, 1)]
        pl.when(both[NORTH])(lambda: wait_bytes(two_faces, sem))
        pl.when(jnp.logical_not(both[NORTH]))(lambda: wait_bytes(one_face, sem))

    def arrived_x(k, c):
        sem = recv_sem.at[k, c, EAST]
        if k == 0:
            two_faces, one_face = raw.at[:, c], raw.at[0, c]
        else:
            two_faces = p.at[k, two(c), pl.ds(0, 2), pl.ds(1, 16)]
            one_face = p.at[k, two(c), pl.ds(0, 1), pl.ds(1, 16)]
        pl.when(both[EAST])(lambda: wait_bytes(two_faces, sem))
        pl.when(jnp.logical_not(both[EAST]))(lambda: wait_bytes(one_face, sem))

    def pass_on(k, c):
        @pl.when(is_end)
        def _():
            here = relay_at(k, c)
            wait_bytes(here, relay_recv.at[k, c])
            for way in (EAST, WEST):

                @pl.when(is_relay[way])
                def _():
                    pltpu.make_async_remote_copy(
                        src_ref=here,
                        dst_ref=x_face(k, c, way, 1)[1],
                        send_sem=relay_send,
                        recv_sem=recv_sem.at[k, c, EAST],
                        device_id=relay_to[way],
                        device_id_type=MESH,
                    ).start()

    def all_passed_on():
        @pl.when(is_end)
        def _():
            wait_bytes(relay, relay_send)
            wait_bytes(raw_relay, relay_send)

    def planes(first, step, count, body):
        def at(i, _):
            for h in range(2):
                body(first + step * i, h)
            return 0

        lax.fori_loop(0, count, at, 0)

    load_in(0).start()
    for copy in own:
        copy.start()
    for s in range(1, NS):
        load_in(s).start()

    barrier = pltpu.get_barrier_semaphore()
    expected = na - 1
    for way in (EAST, WEST, NORTH, SOUTH):
        pl.when(has[way])(
            lambda way=way: pl.semaphore_signal(
                barrier, inc=1, device_id=target[way], device_id_type=MESH
            )
        )
        expected = expected + has[way].astype(jnp.int32)
    for way in (EAST, WEST):
        for near, partners in (
            (to_relay[way], ((ax, 0, iy), (ax, end, iy))),
            (is_relay[way], ((ax, mid - 1, iy), (ax, mid, iy))),
        ):
            expected = expected + 2 * near.astype(jnp.int32)

            @pl.when(near)
            def _(partners=partners):
                for partner in partners:
                    pl.semaphore_signal(barrier, inc=1, device_id=partner, device_id_type=MESH)

    for step in range(1, na):
        pl.semaphore_signal(
            barrier, inc=1, device_id=member_ids[step], device_id_type=MESH
        )

    zero = jnp.zeros((8, 128), F32)

    def clear_x(x, speed):
        def at(s, _):
            for k in range(3):
                for y in range(16):
                    p[k, s, x, 1 + y] = zero
            return 0

        lax.fori_loop(0, NS, at, 0)
        speed_x[speed] = jnp.zeros((16, 128), F32)

    def clear_y(y, speed):
        def at(s, _):
            for k in range(3):
                for x in range(4):
                    p[k, s, 1 + x, y] = zero
            return 0

        lax.fori_loop(0, NS, at, 0)
        for x in range(4):
            speed_y[x, speed : speed + 8] = zero

    pl.when(ix == 0)(lambda: clear_x(0, 0))
    pl.when(ix == nx - 1)(lambda: clear_x(5, 5))
    pl.when(iy == 0)(lambda: clear_y(0, 0))
    pl.when(iy == ny - 1)(lambda: clear_y(17, 24))

    pl.semaphore_wait(barrier, expected)
    send_x(0, 0)
    for way in (EAST, WEST, NORTH, SOUTH):
        pl.when(has[way])(lambda way=way: speed_face(way).start())
    for c in range(1, PAIRS):
        send_x(0, c)

    def scatter(k, c):
        for step in range(1, na):
            pltpu.make_async_remote_copy(
                src_ref=part.at[k, two(c), members[step]],
                dst_ref=part_in.at[k, c, step - 1],
                send_sem=send_sem.at[SUM1],
                recv_sem=recv_sem.at[k, c, SUM1],
                device_id=member_ids[step],
                device_id_type=MESH,
            ).start()

    def second_exchange(k, c):
        wait_bytes(part_in.at[k, c], recv_sem.at[k, c, SUM1])
        for i in range(2):
            total[k, 2 * c + i, ax] = (part[k, 2 * c + i, ax] + part_in[k, c, 0, i]) + (
                part_in[k, c, 1, i] + part_in[k, c, 2, i]
            )
        mine = total.at[k, two(c), ax]
        for step in range(1, na):
            pltpu.make_async_remote_copy(
                src_ref=mine,
                dst_ref=mine,
                send_sem=send_sem.at[SUM2],
                recv_sem=recv_sem.at[k, c, SUM2],
                device_id=member_ids[step],
                device_id_type=MESH,
            ).start()

    def mean_term(k, c):
        wait_bytes(total.at[k, two(c), pl.ds(0, na - 1)], recv_sem.at[k, c, SUM2])
        scale = (STEP * MIX / FIELDS) * diffusion[...]
        for i in range(2):
            mean_row[i] = scale * total[k, 2 * c + i]

    def turn(s):
        flat = rows_in.reshape(NS * 8 * 64, 128)

        def body(x, h):
            start = s * 512 + x * 16 + h * 8
            tiles = [flat[pl.ds(start + i, 8, stride=64), :] for i in range(8)]
            for i in range(8):
                p[0, s, x + 1, h * 8 + i + 1] = tiles[i]
            part[0, s, x, pl.ds(h * 8, 8), :] = sum_rows(tiles)

        return body

    raw_rows = raw.reshape(2 * PAIRS * 8 * 32, 128)

    def turn_face(c, way):
        for j in range(2):
            start = (way * PAIRS + c) * 256 + j * 16
            for y in range(16):
                tile = raw_rows[pl.ds(start + y, 8, stride=32), :]
                p[0, 2 * c + j, 0 if way == EAST else 5, y + 1] = tile

    for c in range(PAIRS):
        for s in (2 * c, 2 * c + 1):
            load_in(s).wait()
            planes(0, 1, 4, turn(s))
        scatter(0, c)
        send_y(0, c)
        if c > 0:
            pass_on(0, c - 1)
            second_exchange(0, c - 1)

    for copy in own:
        copy.wait()
    for way in (EAST, WEST, NORTH, SOUTH):
        pl.when(has[back[way]])(lambda way=way: speed_face(way).wait_recv())

    diagonal = lax.broadcasted_iota(jnp.int32, (8, 8), 0) == lax.broadcasted_iota(
        jnp.int32, (8, 8), 1
    )
    draws = []
    for d in range(3):
        row = jnp.broadcast_to(wiener[d : d + 1, :], (8, 8))
        draw = jnp.sum(jnp.where(diagonal, row, 0.0), axis=1, keepdims=True)
        draws.append(jnp.broadcast_to(draw, (8, 128)))

    def coefficients(x, _):
        g = diffusion[x]
        diffuse = STEP * g
        stir = (0.5 * STEP) * jnp.sqrt((2.0 / STEP) * g)
        lane = lax.broadcasted_iota(jnp.int32, (16, 128), 1)
        upper, lower = lane < 127, lane > 0
        half_step = 0.5 * STEP
        base = [
            diffuse - half_step * speed_x[x + 2],
            diffuse + half_step * speed_x[x],
            diffuse - half_step * speed_y[x, 9:25, :],
            diffuse + half_step * speed_y[x, 7:23, :],
            jnp.where(upper, diffuse - half_step * pltpu.roll(speed_z[x], 127, 1), 0.0),
            jnp.where(lower, diffuse + half_step * pltpu.roll(speed_z[x], 1, 1), 0.0),
        ]
        stir_up, stir_down = jnp.where(upper, stir, 0.0), jnp.where(lower, stir, 0.0)
        keep = 1.0 - (6.0 + MIX) * diffuse
        for y in range(16):
            stir_y = spread(stir, y)
            for d in range(2):
                move = stir_y * draws[d]
                coef[2 * d, x, y] = spread(base[2 * d], y) + move
                coef[2 * d + 1, x, y] = spread(base[2 * d + 1], y) - move
            coef[4, x, y] = spread(base[4], y) + spread(stir_up, y) * draws[2]
            coef[5, x, y] = spread(base[5], y) - spread(stir_down, y) * draws[2]
            keep_y = spread(keep, y)
            centre[0, x, y] = keep_y
            centre[1, x, y] = keep_y - STEP * OXIDATION
        return 0

    lax.fori_loop(0, 4, coefficients, 0)

    def advance(k, c):
        base_weight, section_weight = WEIGHTS[k - 1]
        old = k - 1
        flat = out.reshape(8 * NS * 64, 128)

        def body(x, h):
            y0 = h * 8
            tiles, weights = [[], []], []
            columns = [[p[old, 2 * c + j, x + 1, y0 + i] for i in range(10)] for j in range(2)]
            means = [mean_row[j, x, pl.ds(y0, 8), :] for j in range(2)]
            for i in range(8):
                y = y0 + i
                factor = [coef[d, x, y] for d in range(6)]
                keep = centre[int(c > 0), x, y]
                here = [columns[j][i + 1] for j in range(2)]
                new = [
                    keep * here[j]
                    + spread(means[j], i)
                    + factor[0] * p[old, 2 * c + j, x + 2, y + 1]
                    + factor[1] * p[old, 2 * c + j, x, y + 1]
                    + factor[2] * columns[j][i + 2]
                    + factor[3] * columns[j][i]
                    + factor[4] * pltpu.roll(here[j], 127, 1)
                    + factor[5] * pltpu.roll(here[j], 1, 1)
                    for j in range(2)
                ]
                if c == 0:
                    square = here[0] * here[0]
                    w = square / (1.0 + square) / (1.0 + jnp.exp(-3.0 * here[1]))
                    weights.append(w)
                    new[1] = new[1] - (STEP * RADIATION) * w
                else:
                    w = weight[x, y]
                    before = [p[old, 3, x + 1, y + 1] if c == 2 else None, here[0]]
                    for j in range(2):
                        gain = STEP * NUCLEATION[2 * c - 2 + j]
                        if before[j] is not None:
                            gain = gain + (STEP * GROWTH) * before[j]
                        new[j] = new[j] + w * gain
                for j in range(2):
                    s = 2 * c + j
                    if base_weight:
                        new[j] = base_weight * p[0, s, x + 1, y + 1] + section_weight * new[j]
                    tiles[j].append(new[j])
            for i, w in enumerate(weights):
                weight[x, y0 + i] = w
            for j in range(2):
                s = 2 * c + j
                for i in range(8):
                    if k < 3:
                        p[k, s, x + 1, y0 + i + 1] = tiles[j][i]
                    else:
                        flat[pl.ds(s * 64 + x * 16 + y0 + i, 8, stride=NS * 64), :] = tiles[j][i]
            if k < 3:
                for j in range(2):
                    part[k, 2 * c + j, x, pl.ds(y0, 8), :] = sum_rows(tiles[j])

        return body

    for k in range(1, 4):
        for c in range(PAIRS):
            mean_term(k - 1, c)
            arrived_y(k - 1, c)
            planes(1, 1, 2, advance(k, c))
            arrived_x(k - 1, c)
            if k == 1:
                for way in (EAST, WEST):
                    pl.when(has[back[way]])(lambda way=way: turn_face(c, way))
            planes(0, 3, 2, advance(k, c))
            if k < 3:
                send_x(k, c)
                scatter(k, c)
                send_y(k, c)
            if c == 0:
                pass_on(k - 1, PAIRS - 1)
                second_exchange(k - 1, PAIRS - 1)
            elif k < 3:
                pass_on(k, c - 1)
                second_exchange(k, c - 1)

    for way in (EAST, WEST, NORTH, SOUTH):
        pl.when(has[way])(lambda way=way: speed_face(way).wait_send())
        pl.when(has[way])(lambda way=way: all_sent(way))
    all_passed_on()
    wait_bytes(part_in, send_sem.at[SUM1])
    wait_bytes(part_in, send_sem.at[SUM2])


def local(fields_state, velocity, diffusivity, wiener_draw):
    counts = tuple(lax.axis_size(name) for name in ("gx", "gy", "af"))
    held = fields_state.shape
    dma = pltpu.SemaphoreType.DMA
    vmem = lambda *shape: pltpu.VMEM(shape, F32)
    held_in_hbm = (fields_state.reshape(8, NS, 64, 128), velocity, diffusivity, wiener_draw.T)
    out = pl.pallas_call(
        functools.partial(kernel, counts),
        out_shape=pltpu.VMEM((8, NS, 64, 128), F32),
        in_specs=[pl.BlockSpec(memory_space=pltpu.HBM)] * 4,
        out_specs=pl.BlockSpec(memory_space=pltpu.VMEM),
        scratch_shapes=[
            vmem(NS, 8, 64, 128),
            vmem(3, NS, 6, 18, 8, 128),
            vmem(6, 4, 16, 8, 128),
            vmem(2, 4, 16, 8, 128),
            vmem(4, 16, 8, 128),
            vmem(2, 4, 16, 128),
            vmem(3, NS, 4, 16, 128),
            vmem(3, PAIRS, 3, 2, 16, 128),
            vmem(3, NS, 4, 16, 128),
            vmem(6, 16, 128),
            vmem(4, 32, 128),
            vmem(4, 16, 128),
            vmem(4, 16, 128),
            vmem(3, 8),
            vmem(2, PAIRS, 1, 16, 8, 128),
            vmem(2, PAIRS, 8, 2, 16, 128),
            vmem(PAIRS, 8, 1, 16, 128),
            dma((NS,)),
            dma((5,)),
            dma,
            dma((3, PAIRS)),
            dma((4,)),
            dma((4,)),
            dma((6,)),
            dma((3, PAIRS, 6)),
        ],
        compiler_params=pltpu.CompilerParams(
            collective_id=0, has_side_effects=True, vmem_limit_bytes=48 * 1024 * 1024
        ),
    )(*(pltpu.with_memory_space_constraint(x, pltpu.HBM) for x in held_in_hbm))
    return out.reshape(held)


def solution(mesh):
    return jax.shard_map(
        local,
        mesh=mesh,
        in_specs=(
            P("af", None, "gx", "gy", None),
            P(None, "gx", "gy", None),
            P("gx", "gy", None),
            P("af", None),
        ),
        out_specs=P("af", None, "gx", "gy", None),
        check_vma=False,
    )
```

```python
import functools

import jax
import jax.numpy as jnp
from jax import lax
from jax.experimental import pallas as pl
from jax.experimental.pallas import tpu as pltpu
from jax.sharding import PartitionSpec as P

MESH = pl.DeviceIdType.MESH
F32 = jnp.float32

FIELDS = 32
NS = 6
PAIRS = 3
STEP = 0.3
MIX = 4.0
RADIATION = 0.5
NUCLEATION = (1.0, 0.8, 0.6, 0.5)
GROWTH = 0.5
OXIDATION = 0.3
WEIGHTS = ((0.0, 1.0), (0.75, 0.25), (1.0 / 3.0, 2.0 / 3.0))
EAST, WEST, NORTH, SOUTH, SUM1, SUM2 = range(6)


def sum_rows(tiles):
    row = lax.broadcasted_iota(jnp.int32, (8, 128), 0)
    low = row < 4
    quads = [
        jnp.where(low, tiles[i], tiles[i + 4])
        + pltpu.roll(jnp.where(low, tiles[i + 4], tiles[i]), 4, 0)
        for i in range(4)
    ]
    even = (row & 2) == 0
    pairs = [
        jnp.where(even, quads[i], quads[i + 2])
        + jnp.where(even, pltpu.roll(quads[i], 6, 0), pltpu.roll(quads[i + 2], 2, 0))
        for i in range(2)
    ]
    first = (row & 1) == 0
    return jnp.where(first, pairs[0], pairs[1]) + jnp.where(
        first, pltpu.roll(pairs[0], 7, 0), pltpu.roll(pairs[1], 1, 0)
    )


def spread(rows, i):
    return jnp.broadcast_to(rows[i : i + 1, :], (8, 128))


def kernel(
    counts,
    fields_hbm,
    velocity_hbm,
    diffusivity_hbm,
    wiener_hbm,
    out,
    rows_in,
    p,
    coef,
    centre,
    weight,
    mean_row,
    part,
    part_in,
    total,
    speed_x,
    speed_y,
    speed_z,
    diffusion,
    wiener,
    relay,
    raw,
    raw_relay,
    in_sem,
    own_sem,
    relay_send,
    relay_recv,
    speed_send,
    speed_recv,
    send_sem,
    recv_sem,
):
    nx, ny, na = counts
    ax, ix, iy = lax.axis_index("af"), lax.axis_index("gx"), lax.axis_index("gy")
    has = {EAST: ix < nx - 1, WEST: ix > 0, NORTH: iy < ny - 1, SOUTH: iy > 0}
    back = {EAST: WEST, WEST: EAST, NORTH: SOUTH, SOUTH: NORTH}
    target = {
        EAST: (ax, ix + 1, iy),
        WEST: (ax, ix - 1, iy),
        NORTH: (ax, ix, iy + 1),
        SOUTH: (ax, ix, iy - 1),
    }
    members = [lax.rem(ax + step, na) for step in range(na)]
    member_ids = [(other, ix, iy) for other in members]

    mid, end = nx // 2, nx - 1
    to_relay = {EAST: ix == mid - 1, WEST: ix == mid}
    is_relay = {EAST: ix == end, WEST: ix == 0}
    relay_of = {EAST: (ax, end, iy), WEST: (ax, 0, iy)}
    relay_to = {EAST: (ax, mid, iy), WEST: (ax, mid - 1, iy)}
    is_mid, is_end = to_relay[EAST] | to_relay[WEST], is_relay[EAST] | is_relay[WEST]
    both = {EAST: has[EAST] & has[WEST], NORTH: has[NORTH] & has[SOUTH]}
    plain = {way: has[way] & jnp.logical_not(to_relay[way]) for way in (EAST, WEST)}

    def load_in(s):
        return pltpu.make_async_copy(fields_hbm.at[:, s], rows_in.at[s], in_sem.at[s])

    def two(c):
        return pl.ds(2 * c, 2)

    own = [
        pltpu.make_async_copy(velocity_hbm.at[0], speed_x.at[pl.ds(1, 4)], own_sem.at[0]),
        pltpu.make_async_copy(velocity_hbm.at[1], speed_y.at[:, pl.ds(8, 16)], own_sem.at[1]),
        pltpu.make_async_copy(velocity_hbm.at[2], speed_z, own_sem.at[2]),
        pltpu.make_async_copy(diffusivity_hbm, diffusion, own_sem.at[3]),
        pltpu.make_async_copy(wiener_hbm, wiener, own_sem.at[4]),
    ]

    def speed_face(way):
        src, dst = {
            EAST: (velocity_hbm.at[0, 3], speed_x.at[0]),
            WEST: (velocity_hbm.at[0, 0], speed_x.at[5]),
            NORTH: (velocity_hbm.at[1, :, pl.ds(8, 8)], speed_y.at[:, pl.ds(0, 8)]),
            SOUTH: (velocity_hbm.at[1, :, pl.ds(0, 8)], speed_y.at[:, pl.ds(24, 8)]),
        }[way]
        return pltpu.make_async_remote_copy(
            src_ref=src,
            dst_ref=dst,
            send_sem=speed_send.at[way],
            recv_sem=speed_recv.at[way],
            device_id=target[way],
            device_id_type=MESH,
        )

    def face(k, s, way, recv=None):
        src, dst = {
            NORTH: lambda: (p.at[k, s, pl.ds(1, 4), 16], p.at[k, s, pl.ds(1, 4), 0]),
            SOUTH: lambda: (p.at[k, s, pl.ds(1, 4), 1], p.at[k, s, pl.ds(1, 4), 17]),
        }[way]()
        return pltpu.make_async_remote_copy(
            src_ref=src,
            dst_ref=dst,
            send_sem=send_sem.at[way],
            recv_sem=recv,
            device_id=target[way],
            device_id_type=MESH,
        )

    def chunk(k, c, way):
        return face(k, two(c), way, recv_sem.at[k, c, NORTH])

    def wait_bytes(ref, sem):
        pltpu.make_async_copy(ref, ref, sem).wait()

    def all_sent(way):
        if way in to_relay:
            wait_bytes(p.at[:, :, 1, pl.ds(1, 16)], send_sem.at[way])
        else:
            wait_bytes(p.at[:, :, pl.ds(1, 4), 1], send_sem.at[way])

    def x_face(k, c, way, s=None):
        src, dst = {EAST: (4, 0), WEST: (1, 5)}[way]
        side = way
        which = pl.ds(2 * c, 2) if s is None else pl.ds(2 * c + s, 1)
        to = pl.ds(0, 2) if s is None else pl.ds(s, 1)
        if k == 0:
            refs = fields_hbm.at[:, which, pl.ds(16 * (src - 1), 16)], raw.at[side, c, :, to]
        else:
            refs = p.at[k, which, src, pl.ds(1, 16)], p.at[k, which, dst, pl.ds(1, 16)]
        return refs

    def copy_x(refs, way, recv, to):
        return pltpu.make_async_remote_copy(
            src_ref=refs[0],
            dst_ref=refs[1],
            send_sem=send_sem.at[way],
            recv_sem=recv,
            device_id=to,
            device_id_type=MESH,
        )

    def relay_at(k, c):
        return raw_relay.at[c] if k == 0 else relay.at[k - 1, c]

    def send_x(k, c):
        recv = recv_sem.at[k, c, EAST]
        for way in (EAST, WEST):

            @pl.when(plain[way])
            def _():
                copy_x(x_face(k, c, way), way, recv, target[way]).start()

        @pl.when(is_mid)
        def _():
            for way in (EAST, WEST):

                @pl.when(to_relay[way])
                def _():
                    src = x_face(k, c, way, 1)[0]
                    copy_x(
                        (src, relay_at(k, c)), way, relay_recv.at[k, c], relay_of[way]
                    ).start()
                    copy_x(x_face(k, c, way, 0), way, recv, target[way]).start()

    def send_y(k, c):
        for way in (NORTH, SOUTH):
            pl.when(has[way])(lambda: chunk(k, c, way).start())

    def arrived_y(k, c):
        sem = recv_sem.at[k, c, NORTH]
        two_faces = p.at[k, two(c), pl.ds(1, 4), pl.ds(0, 2)]
        one_face = p.at[k, two(c), pl.ds(1, 4), pl.ds(0, 1)]
        pl.when(both[NORTH])(lambda: wait_bytes(two_faces, sem))
        pl.when(jnp.logical_not(both[NORTH]))(lambda: wait_bytes(one_face, sem))

    def arrived_x(k, c):
        sem = recv_sem.at[k, c, EAST]
        if k == 0:
            two_faces, one_face = raw.at[:, c], raw.at[0, c]
        else:
            two_faces = p.at[k, two(c), pl.ds(0, 2), pl.ds(1, 16)]
            one_face = p.at[k, two(c), pl.ds(0, 1), pl.ds(1, 16)]
        pl.when(both[EAST])(lambda: wait_bytes(two_faces, sem))
        pl.when(jnp.logical_not(both[EAST]))(lambda: wait_bytes(one_face, sem))

    def pass_on(k, c):
        @pl.when(is_end)
        def _():
            here = relay_at(k, c)
            wait_bytes(here, relay_recv.at[k, c])
            for way in (EAST, WEST):

                @pl.when(is_relay[way])
                def _():
                    pltpu.make_async_remote_copy(
                        src_ref=here,
                        dst_ref=x_face(k, c, way, 1)[1],
                        send_sem=relay_send,
                        recv_sem=recv_sem.at[k, c, EAST],
                        device_id=relay_to[way],
                        device_id_type=MESH,
                    ).start()

    def all_passed_on():
        @pl.when(is_end)
        def _():
            wait_bytes(relay, relay_send)
            wait_bytes(raw_relay, relay_send)

    def planes(first, step, count, body):
        def at(i, _):
            for h in range(2):
                body(first + step * i, h)
            return 0

        lax.fori_loop(0, count, at, 0)

    load_in(0).start()
    for copy in own:
        copy.start()
    for s in range(1, NS):
        load_in(s).start()

    barrier = pltpu.get_barrier_semaphore()
    expected = na - 1
    for way in (EAST, WEST, NORTH, SOUTH):
        pl.when(has[way])(
            lambda way=way: pl.semaphore_signal(
                barrier, inc=1, device_id=target[way], device_id_type=MESH
            )
        )
        expected = expected + has[way].astype(jnp.int32)
    for way in (EAST, WEST):
        for near, partners in (
            (to_relay[way], ((ax, 0, iy), (ax, end, iy))),
            (is_relay[way], ((ax, mid - 1, iy), (ax, mid, iy))),
        ):
            expected = expected + 2 * near.astype(jnp.int32)

            @pl.when(near)
            def _(partners=partners):
                for partner in partners:
                    pl.semaphore_signal(barrier, inc=1, device_id=partner, device_id_type=MESH)

    for step in range(1, na):
        pl.semaphore_signal(
            barrier, inc=1, device_id=member_ids[step], device_id_type=MESH
        )

    zero = jnp.zeros((8, 128), F32)

    def clear_x(x, speed):
        def at(s, _):
            for k in range(3):
                for y in range(16):
                    p[k, s, x, 1 + y] = zero
            return 0

        lax.fori_loop(0, NS, at, 0)
        speed_x[speed] = jnp.zeros((16, 128), F32)

    def clear_y(y, speed):
        def at(s, _):
            for k in range(3):
                for x in range(4):
                    p[k, s, 1 + x, y] = zero
            return 0

        lax.fori_loop(0, NS, at, 0)
        for x in range(4):
            speed_y[x, speed : speed + 8] = zero

    pl.when(ix == 0)(lambda: clear_x(0, 0))
    pl.when(ix == nx - 1)(lambda: clear_x(5, 5))
    pl.when(iy == 0)(lambda: clear_y(0, 0))
    pl.when(iy == ny - 1)(lambda: clear_y(17, 24))

    pl.semaphore_wait(barrier, expected)
    send_x(0, 0)
    for way in (EAST, WEST, NORTH, SOUTH):
        pl.when(has[way])(lambda way=way: speed_face(way).start())

    def scatter(k, c, owner):
        @pl.when(ax != owner)
        def _():
            pltpu.make_async_remote_copy(
                src_ref=part.at[k, two(c), owner],
                dst_ref=part_in.at[k, c, lax.rem(owner - ax + na, na) - 1],
                send_sem=send_sem.at[SUM1],
                recv_sem=recv_sem.at[k, c, SUM1],
                device_id=(owner, ix, iy),
                device_id_type=MESH,
            ).start()

    def second_exchange(k, c):
        wait_bytes(part_in.at[k, c], recv_sem.at[k, c, SUM1])
        for i in range(2):
            total[k, 2 * c + i, ax] = (part[k, 2 * c + i, ax] + part_in[k, c, 0, i]) + (
                part_in[k, c, 1, i] + part_in[k, c, 2, i]
            )
        mine = total.at[k, two(c), ax]
        for step in range(1, na):
            pltpu.make_async_remote_copy(
                src_ref=mine,
                dst_ref=mine,
                send_sem=send_sem.at[SUM2],
                recv_sem=recv_sem.at[k, c, SUM2],
                device_id=member_ids[step],
                device_id_type=MESH,
            ).start()

    def mean_term(k, c):
        wait_bytes(total.at[k, two(c), pl.ds(0, na - 1)], recv_sem.at[k, c, SUM2])
        scale = (STEP * MIX / FIELDS) * diffusion[...]
        for i in range(2):
            mean_row[i] = scale * total[k, 2 * c + i]

    def turn(s):
        flat = rows_in.reshape(NS * 8 * 64, 128)

        def body(x, h):
            start = s * 512 + x * 16 + h * 8
            tiles = [flat[pl.ds(start + i, 8, stride=64), :] for i in range(8)]
            for i in range(8):
                p[0, s, x + 1, h * 8 + i + 1] = tiles[i]
            part[0, s, x, pl.ds(h * 8, 8), :] = sum_rows(tiles)

        return body

    raw_rows = raw.reshape(2 * PAIRS * 8 * 32, 128)

    def turn_face(c, way):
        for j in range(2):
            start = (way * PAIRS + c) * 256 + j * 16
            for y in range(16):
                tile = raw_rows[pl.ds(start + y, 8, stride=32), :]
                p[0, 2 * c + j, 0 if way == EAST else 5, y + 1] = tile

    def coefficients(x, _):
        g = diffusion[x]
        diffuse = STEP * g
        stir = (0.5 * STEP) * jnp.sqrt((2.0 / STEP) * g)
        lane = lax.broadcasted_iota(jnp.int32, (16, 128), 1)
        upper, lower = lane < 127, lane > 0
        half_step = 0.5 * STEP
        base = [
            diffuse - half_step * speed_x[x + 2],
            diffuse + half_step * speed_x[x],
            diffuse - half_step * speed_y[x, 9:25, :],
            diffuse + half_step * speed_y[x, 7:23, :],
            jnp.where(upper, diffuse - half_step * pltpu.roll(speed_z[x], 127, 1), 0.0),
            jnp.where(lower, diffuse + half_step * pltpu.roll(speed_z[x], 1, 1), 0.0),
        ]
        stir_up, stir_down = jnp.where(upper, stir, 0.0), jnp.where(lower, stir, 0.0)
        keep = 1.0 - (6.0 + MIX) * diffuse
        for y in range(16):
            stir_y = spread(stir, y)
            for d in range(2):
                move = stir_y * draws[d]
                coef[2 * d, x, y] = spread(base[2 * d], y) + move
                coef[2 * d + 1, x, y] = spread(base[2 * d + 1], y) - move
            coef[4, x, y] = spread(base[4], y) + spread(stir_up, y) * draws[2]
            coef[5, x, y] = spread(base[5], y) - spread(stir_down, y) * draws[2]
            keep_y = spread(keep, y)
            centre[0, x, y] = keep_y
            centre[1, x, y] = keep_y - STEP * OXIDATION
        return 0

    def turn_pair(c):
        for s in (2 * c, 2 * c + 1):
            load_in(s).wait()
            planes(0, 1, 4, turn(s))
        if c + 1 < PAIRS:
            send_x(0, c + 1)
        for owner in range(na):
            scatter(0, c, owner)
        send_y(0, c)

    turn_pair(0)
    for copy in own:
        copy.wait()
    for way in (EAST, WEST, NORTH, SOUTH):
        pl.when(has[back[way]])(lambda way=way: speed_face(way).wait_recv())

    diagonal = lax.broadcasted_iota(jnp.int32, (8, 8), 0) == lax.broadcasted_iota(
        jnp.int32, (8, 8), 1
    )
    draws = []
    for d in range(3):
        row = jnp.broadcast_to(wiener[d : d + 1, :], (8, 8))
        draw = jnp.sum(jnp.where(diagonal, row, 0.0), axis=1, keepdims=True)
        draws.append(jnp.broadcast_to(draw, (8, 128)))

    lax.fori_loop(0, 4, coefficients, 0)
    turn_pair(1)
    pass_on(0, 0)
    second_exchange(0, 0)
    turn_pair(2)
    pass_on(0, 1)
    second_exchange(0, 1)

    def advance(k, c):
        base_weight, section_weight = WEIGHTS[k - 1]
        old = k - 1
        flat = out.reshape(8 * NS * 64, 128)

        def body(x, h):
            y0 = h * 8
            tiles, weights = [[], []], []
            columns = [[p[old, 2 * c + j, x + 1, y0 + i] for i in range(10)] for j in range(2)]
            means = [mean_row[j, x, pl.ds(y0, 8), :] for j in range(2)]
            for i in range(8):
                y = y0 + i
                factor = [coef[d, x, y] for d in range(6)]
                keep = centre[int(c > 0), x, y]
                here = [columns[j][i + 1] for j in range(2)]
                new = [
                    keep * here[j]
                    + spread(means[j], i)
                    + factor[0] * p[old, 2 * c + j, x + 2, y + 1]
                    + factor[1] * p[old, 2 * c + j, x, y + 1]
                    + factor[2] * columns[j][i + 2]
                    + factor[3] * columns[j][i]
                    + factor[4] * pltpu.roll(here[j], 127, 1)
                    + factor[5] * pltpu.roll(here[j], 1, 1)
                    for j in range(2)
                ]
                if c == 0:
                    square = here[0] * here[0]
                    w = square / (1.0 + square) / (1.0 + jnp.exp(-3.0 * here[1]))
                    weights.append(w)
                    new[1] = new[1] - (STEP * RADIATION) * w
                else:
                    w = weight[x, y]
                    before = [p[old, 3, x + 1, y + 1] if c == 2 else None, here[0]]
                    for j in range(2):
                        gain = STEP * NUCLEATION[2 * c - 2 + j]
                        if before[j] is not None:
                            gain = gain + (STEP * GROWTH) * before[j]
                        new[j] = new[j] + w * gain
                for j in range(2):
                    s = 2 * c + j
                    if base_weight:
                        new[j] = base_weight * p[0, s, x + 1, y + 1] + section_weight * new[j]
                    tiles[j].append(new[j])
            for i, w in enumerate(weights):
                weight[x, y0 + i] = w
            for j in range(2):
                s = 2 * c + j
                for i in range(8):
                    if k < 3:
                        p[k, s, x + 1, y0 + i + 1] = tiles[j][i]
                    else:
                        flat[pl.ds(s * 64 + x * 16 + y0 + i, 8, stride=NS * 64), :] = tiles[j][i]
            if k < 3:
                for j in range(2):
                    part[k, 2 * c + j, x, pl.ds(y0, 8), :] = sum_rows(tiles[j])

        return body

    for k in range(1, 4):
        for c in range(PAIRS):
            mean_term(k - 1, c)
            arrived_y(k - 1, c)
            planes(1, 1, 2, advance(k, c))
            if k < 3:
                scatter(k, c, 1)
                scatter(k, c, 2)
            arrived_x(k - 1, c)
            if c == 0:
                pass_on(k - 1, PAIRS - 1)
            elif k < 3:
                pass_on(k, c - 1)
            if k == 1:
                for way in (EAST, WEST):
                    pl.when(has[back[way]])(lambda way=way: turn_face(c, way))
            planes(0, 3, 2, advance(k, c))
            if k < 3:
                send_x(k, c)
                scatter(k, c, 0)
                scatter(k, c, 3)
                send_y(k, c)
            if c == 0:
                second_exchange(k - 1, PAIRS - 1)
            elif k < 3:
                second_exchange(k, c - 1)

    for way in (EAST, WEST, NORTH, SOUTH):
        pl.when(has[way])(lambda way=way: speed_face(way).wait_send())
        pl.when(has[way])(lambda way=way: all_sent(way))
    all_passed_on()
    wait_bytes(part_in, send_sem.at[SUM1])
    wait_bytes(part_in, send_sem.at[SUM2])


def local(fields_state, velocity, diffusivity, wiener_draw):
    counts = tuple(lax.axis_size(name) for name in ("gx", "gy", "af"))
    held = fields_state.shape
    dma = pltpu.SemaphoreType.DMA
    vmem = lambda *shape: pltpu.VMEM(shape, F32)
    held_in_hbm = (fields_state.reshape(8, NS, 64, 128), velocity, diffusivity, wiener_draw.T)
    out = pl.pallas_call(
        functools.partial(kernel, counts),
        out_shape=pltpu.VMEM((8, NS, 64, 128), F32),
        in_specs=[pl.BlockSpec(memory_space=pltpu.HBM)] * 4,
        out_specs=pl.BlockSpec(memory_space=pltpu.VMEM),
        scratch_shapes=[
            vmem(NS, 8, 64, 128),
            vmem(3, NS, 6, 18, 8, 128),
            vmem(6, 4, 16, 8, 128),
            vmem(2, 4, 16, 8, 128),
            vmem(4, 16, 8, 128),
            vmem(2, 4, 16, 128),
            vmem(3, NS, 4, 16, 128),
            vmem(3, PAIRS, 3, 2, 16, 128),
            vmem(3, NS, 4, 16, 128),
            vmem(6, 16, 128),
            vmem(4, 32, 128),
            vmem(4, 16, 128),
            vmem(4, 16, 128),
            vmem(3, 8),
            vmem(2, PAIRS, 1, 16, 8, 128),
            vmem(2, PAIRS, 8, 2, 16, 128),
            vmem(PAIRS, 8, 1, 16, 128),
            dma((NS,)),
            dma((5,)),
            dma,
            dma((3, PAIRS)),
            dma((4,)),
            dma((4,)),
            dma((6,)),
            dma((3, PAIRS, 6)),
        ],
        compiler_params=pltpu.CompilerParams(
            collective_id=0, has_side_effects=True, vmem_limit_bytes=48 * 1024 * 1024
        ),
    )(*(pltpu.with_memory_space_constraint(x, pltpu.HBM) for x in held_in_hbm))
    return out.reshape(held)


def solution(mesh):
    return jax.shard_map(
        local,
        mesh=mesh,
        in_specs=(
            P("af", None, "gx", "gy", None),
            P(None, "gx", "gy", None),
            P("gx", "gy", None),
            P("af", None),
        ),
        out_specs=P("af", None, "gx", "gy", None),
        check_vma=False,
    )
```

```python
import functools

import jax
import jax.numpy as jnp
from jax import lax
from jax.experimental import pallas as pl
from jax.experimental.pallas import tpu as pltpu
from jax.sharding import PartitionSpec as P

MESH = pl.DeviceIdType.MESH
F32 = jnp.float32

FIELDS = 32
NS = 6
PAIRS = 3
STEP = 0.3
MIX = 4.0
RADIATION = 0.5
NUCLEATION = (1.0, 0.8, 0.6, 0.5)
GROWTH = 0.5
OXIDATION = 0.3
WEIGHTS = ((0.0, 1.0), (0.75, 0.25), (1.0 / 3.0, 2.0 / 3.0))
EAST, WEST, NORTH, SOUTH, SUM1, SUM2 = range(6)


def sum_rows(tiles):
    row = lax.broadcasted_iota(jnp.int32, (8, 128), 0)
    low = row < 4
    quads = [
        jnp.where(low, tiles[i], tiles[i + 4])
        + pltpu.roll(jnp.where(low, tiles[i + 4], tiles[i]), 4, 0)
        for i in range(4)
    ]
    even = (row & 2) == 0
    pairs = [
        jnp.where(even, quads[i], quads[i + 2])
        + jnp.where(even, pltpu.roll(quads[i], 6, 0), pltpu.roll(quads[i + 2], 2, 0))
        for i in range(2)
    ]
    first = (row & 1) == 0
    return jnp.where(first, pairs[0], pairs[1]) + jnp.where(
        first, pltpu.roll(pairs[0], 7, 0), pltpu.roll(pairs[1], 1, 0)
    )


def spread(rows, i):
    return jnp.broadcast_to(rows[i : i + 1, :], (8, 128))


def kernel(
    counts,
    fields_hbm,
    velocity_hbm,
    diffusivity_hbm,
    wiener_hbm,
    out,
    rows_in,
    p,
    coef,
    centre,
    weight,
    mean_row,
    part,
    part_in,
    total,
    speed_x,
    speed_y,
    speed_z,
    diffusion,
    wiener,
    relay,
    raw,
    raw_relay,
    in_sem,
    own_sem,
    relay_send,
    relay_recv,
    speed_send,
    speed_recv,
    send_sem,
    recv_sem,
):
    nx, ny, na = counts
    ax, ix, iy = lax.axis_index("af"), lax.axis_index("gx"), lax.axis_index("gy")
    has = {EAST: ix < nx - 1, WEST: ix > 0, NORTH: iy < ny - 1, SOUTH: iy > 0}
    back = {EAST: WEST, WEST: EAST, NORTH: SOUTH, SOUTH: NORTH}
    target = {
        EAST: (ax, ix + 1, iy),
        WEST: (ax, ix - 1, iy),
        NORTH: (ax, ix, iy + 1),
        SOUTH: (ax, ix, iy - 1),
    }
    members = [lax.rem(ax + step, na) for step in range(na)]
    member_ids = [(other, ix, iy) for other in members]

    mid, end = nx // 2, nx - 1
    to_relay = {EAST: ix == mid - 1, WEST: ix == mid}
    is_relay = {EAST: ix == end, WEST: ix == 0}
    relay_of = {EAST: (ax, end, iy), WEST: (ax, 0, iy)}
    relay_to = {EAST: (ax, mid, iy), WEST: (ax, mid - 1, iy)}
    is_mid, is_end = to_relay[EAST] | to_relay[WEST], is_relay[EAST] | is_relay[WEST]
    both = {EAST: has[EAST] & has[WEST], NORTH: has[NORTH] & has[SOUTH]}
    plain = {way: has[way] & jnp.logical_not(to_relay[way]) for way in (EAST, WEST)}

    def load_in(s):
        return pltpu.make_async_copy(fields_hbm.at[:, s], rows_in.at[s], in_sem.at[s])

    def two(c):
        return pl.ds(2 * c, 2)

    own = [
        pltpu.make_async_copy(velocity_hbm.at[0], speed_x.at[pl.ds(1, 4)], own_sem.at[0]),
        pltpu.make_async_copy(velocity_hbm.at[1], speed_y.at[:, pl.ds(8, 16)], own_sem.at[1]),
        pltpu.make_async_copy(velocity_hbm.at[2], speed_z, own_sem.at[2]),
        pltpu.make_async_copy(diffusivity_hbm, diffusion, own_sem.at[3]),
        pltpu.make_async_copy(wiener_hbm, wiener, own_sem.at[4]),
    ]

    def speed_face(way):
        src, dst = {
            EAST: (velocity_hbm.at[0, 3], speed_x.at[0]),
            WEST: (velocity_hbm.at[0, 0], speed_x.at[5]),
            NORTH: (velocity_hbm.at[1, :, pl.ds(8, 8)], speed_y.at[:, pl.ds(0, 8)]),
            SOUTH: (velocity_hbm.at[1, :, pl.ds(0, 8)], speed_y.at[:, pl.ds(24, 8)]),
        }[way]
        return pltpu.make_async_remote_copy(
            src_ref=src,
            dst_ref=dst,
            send_sem=speed_send.at[way],
            recv_sem=speed_recv.at[way],
            device_id=target[way],
            device_id_type=MESH,
        )

    def face(k, s, way, recv=None):
        src, dst = {
            NORTH: lambda: (p.at[k, s, pl.ds(1, 4), 16], p.at[k, s, pl.ds(1, 4), 0]),
            SOUTH: lambda: (p.at[k, s, pl.ds(1, 4), 1], p.at[k, s, pl.ds(1, 4), 17]),
        }[way]()
        return pltpu.make_async_remote_copy(
            src_ref=src,
            dst_ref=dst,
            send_sem=send_sem.at[way],
            recv_sem=recv,
            device_id=target[way],
            device_id_type=MESH,
        )

    def chunk(k, c, way):
        return face(k, two(c), way, recv_sem.at[k, c, NORTH])

    def wait_bytes(ref, sem):
        pltpu.make_async_copy(ref, ref, sem).wait()

    def all_sent(way):
        if way in to_relay:
            wait_bytes(p.at[:, :, 1, pl.ds(1, 16)], send_sem.at[way])
        else:
            wait_bytes(p.at[:, :, pl.ds(1, 4), 1], send_sem.at[way])

    def x_face(k, c, way, s=None):
        src, dst = {EAST: (4, 0), WEST: (1, 5)}[way]
        side = way
        which = pl.ds(2 * c, 2) if s is None else pl.ds(2 * c + s, 1)
        to = pl.ds(0, 2) if s is None else pl.ds(s, 1)
        if k == 0:
            refs = fields_hbm.at[:, which, pl.ds(16 * (src - 1), 16)], raw.at[side, c, :, to]
        else:
            refs = p.at[k, which, src, pl.ds(1, 16)], p.at[k, which, dst, pl.ds(1, 16)]
        return refs

    def copy_x(refs, way, recv, to):
        return pltpu.make_async_remote_copy(
            src_ref=refs[0],
            dst_ref=refs[1],
            send_sem=send_sem.at[way],
            recv_sem=recv,
            device_id=to,
            device_id_type=MESH,
        )

    def relay_at(k, c):
        return raw_relay.at[c] if k == 0 else relay.at[k - 1, c]

    def send_x(k, c):
        recv = recv_sem.at[k, c, EAST]
        for way in (EAST, WEST):

            @pl.when(plain[way])
            def _():
                copy_x(x_face(k, c, way), way, recv, target[way]).start()

        @pl.when(is_mid)
        def _():
            for way in (EAST, WEST):

                @pl.when(to_relay[way])
                def _():
                    src = x_face(k, c, way, 1)[0]
                    copy_x(
                        (src, relay_at(k, c)), way, relay_recv.at[k, c], relay_of[way]
                    ).start()
                    copy_x(x_face(k, c, way, 0), way, recv, target[way]).start()

    def send_y(k, c):
        for way in (NORTH, SOUTH):
            pl.when(has[way])(lambda: chunk(k, c, way).start())

    def arrived_y(k, c):
        sem = recv_sem.at[k, c, NORTH]
        two_faces = p.at[k, two(c), pl.ds(1, 4), pl.ds(0, 2)]
        one_face = p.at[k, two(c), pl.ds(1, 4), pl.ds(0, 1)]
        pl.when(both[NORTH])(lambda: wait_bytes(two_faces, sem))
        pl.when(jnp.logical_not(both[NORTH]))(lambda: wait_bytes(one_face, sem))

    def arrived_x(k, c):
        sem = recv_sem.at[k, c, EAST]
        if k == 0:
            two_faces, one_face = raw.at[:, c], raw.at[0, c]
        else:
            two_faces = p.at[k, two(c), pl.ds(0, 2), pl.ds(1, 16)]
            one_face = p.at[k, two(c), pl.ds(0, 1), pl.ds(1, 16)]
        pl.when(both[EAST])(lambda: wait_bytes(two_faces, sem))
        pl.when(jnp.logical_not(both[EAST]))(lambda: wait_bytes(one_face, sem))

    def pass_on(k, c):
        @pl.when(is_end)
        def _():
            here = relay_at(k, c)
            wait_bytes(here, relay_recv.at[k, c])
            for way in (EAST, WEST):

                @pl.when(is_relay[way])
                def _():
                    pltpu.make_async_remote_copy(
                        src_ref=here,
                        dst_ref=x_face(k, c, way, 1)[1],
                        send_sem=relay_send,
                        recv_sem=recv_sem.at[k, c, EAST],
                        device_id=relay_to[way],
                        device_id_type=MESH,
                    ).start()

    def all_passed_on():
        @pl.when(is_end)
        def _():
            wait_bytes(relay, relay_send)
            wait_bytes(raw_relay, relay_send)

    def planes(first, step, count, body):
        def at(i, _):
            for h in range(2):
                body(first + step * i, h)
            return 0

        lax.fori_loop(0, count, at, 0)

    load_in(0).start()
    for copy in own:
        copy.start()
    for s in range(1, NS):
        load_in(s).start()

    barrier = pltpu.get_barrier_semaphore()
    expected = na - 1
    for way in (EAST, WEST, NORTH, SOUTH):
        pl.when(has[way])(
            lambda way=way: pl.semaphore_signal(
                barrier, inc=1, device_id=target[way], device_id_type=MESH
            )
        )
        expected = expected + has[way].astype(jnp.int32)
    for way in (EAST, WEST):
        for near, partners in (
            (to_relay[way], ((ax, 0, iy), (ax, end, iy))),
            (is_relay[way], ((ax, mid - 1, iy), (ax, mid, iy))),
        ):
            expected = expected + 2 * near.astype(jnp.int32)

            @pl.when(near)
            def _(partners=partners):
                for partner in partners:
                    pl.semaphore_signal(barrier, inc=1, device_id=partner, device_id_type=MESH)

    for step in range(1, na):
        pl.semaphore_signal(
            barrier, inc=1, device_id=member_ids[step], device_id_type=MESH
        )

    zero = jnp.zeros((8, 128), F32)

    def clear_x(x, speed):
        def at(s, _):
            for k in range(3):
                for y in range(16):
                    p[k, s, x, 1 + y] = zero
            return 0

        lax.fori_loop(0, NS, at, 0)
        speed_x[speed] = jnp.zeros((16, 128), F32)

    def clear_y(y, speed):
        def at(s, _):
            for k in range(3):
                for x in range(4):
                    p[k, s, 1 + x, y] = zero
            return 0

        lax.fori_loop(0, NS, at, 0)
        for x in range(4):
            speed_y[x, speed : speed + 8] = zero

    pl.when(ix == 0)(lambda: clear_x(0, 0))
    pl.when(ix == nx - 1)(lambda: clear_x(5, 5))
    pl.when(iy == 0)(lambda: clear_y(0, 0))
    pl.when(iy == ny - 1)(lambda: clear_y(17, 24))

    pl.semaphore_wait(barrier, expected)
    send_x(0, 0)
    for way in (EAST, WEST, NORTH, SOUTH):
        pl.when(has[way])(lambda way=way: speed_face(way).start())

    def scatter(k, c, owner):
        @pl.when(ax != owner)
        def _():
            pltpu.make_async_remote_copy(
                src_ref=part.at[k, two(c), owner],
                dst_ref=part_in.at[k, c, lax.rem(owner - ax + na, na) - 1],
                send_sem=send_sem.at[SUM1],
                recv_sem=recv_sem.at[k, c, SUM1],
                device_id=(owner, ix, iy),
                device_id_type=MESH,
            ).start()

    def second_exchange(k, c):
        wait_bytes(part_in.at[k, c], recv_sem.at[k, c, SUM1])
        for i in range(2):
            total[k, 2 * c + i, ax] = (part[k, 2 * c + i, ax] + part_in[k, c, 0, i]) + (
                part_in[k, c, 1, i] + part_in[k, c, 2, i]
            )
        mine = total.at[k, two(c), ax]
        for step in range(1, na):
            pltpu.make_async_remote_copy(
                src_ref=mine,
                dst_ref=mine,
                send_sem=send_sem.at[SUM2],
                recv_sem=recv_sem.at[k, c, SUM2],
                device_id=member_ids[step],
                device_id_type=MESH,
            ).start()

    def mean_term(k, c):
        wait_bytes(total.at[k, two(c), pl.ds(0, na - 1)], recv_sem.at[k, c, SUM2])
        scale = (STEP * MIX / FIELDS) * diffusion[...]
        for i in range(2):
            mean_row[i] = scale * total[k, 2 * c + i]

    def turn(s):
        flat = rows_in.reshape(NS * 8 * 64, 128)

        def body(x, h):
            start = s * 512 + x * 16 + h * 8
            tiles = [flat[pl.ds(start + i, 8, stride=64), :] for i in range(8)]
            for i in range(8):
                p[0, s, x + 1, h * 8 + i + 1] = tiles[i]
            part[0, s, x, pl.ds(h * 8, 8), :] = sum_rows(tiles)

        return body

    raw_rows = raw.reshape(2 * PAIRS * 8 * 32, 128)

    def turn_face(c, way):
        for j in range(2):
            start = (way * PAIRS + c) * 256 + j * 16
            for y in range(16):
                tile = raw_rows[pl.ds(start + y, 8, stride=32), :]
                p[0, 2 * c + j, 0 if way == EAST else 5, y + 1] = tile

    for c in range(PAIRS):
        for s in (2 * c, 2 * c + 1):
            load_in(s).wait()
            planes(0, 1, 4, turn(s))
        for owner in range(na):
            scatter(0, c, owner)
        send_y(0, c)
        if c > 0:
            second_exchange(0, c - 1)
            pass_on(0, c - 1)
        if c + 1 < PAIRS:
            send_x(0, c + 1)

    for copy in own:
        copy.wait()
    for way in (EAST, WEST, NORTH, SOUTH):
        pl.when(has[back[way]])(lambda way=way: speed_face(way).wait_recv())

    diagonal = lax.broadcasted_iota(jnp.int32, (8, 8), 0) == lax.broadcasted_iota(
        jnp.int32, (8, 8), 1
    )
    draws = []
    for d in range(3):
        row = jnp.broadcast_to(wiener[d : d + 1, :], (8, 8))
        draw = jnp.sum(jnp.where(diagonal, row, 0.0), axis=1, keepdims=True)
        draws.append(jnp.broadcast_to(draw, (8, 128)))

    def coefficients(x, _):
        g = diffusion[x]
        diffuse = STEP * g
        stir = (0.5 * STEP) * jnp.sqrt((2.0 / STEP) * g)
        lane = lax.broadcasted_iota(jnp.int32, (16, 128), 1)
        upper, lower = lane < 127, lane > 0
        half_step = 0.5 * STEP
        base = [
            diffuse - half_step * speed_x[x + 2],
            diffuse + half_step * speed_x[x],
            diffuse - half_step * speed_y[x, 9:25, :],
            diffuse + half_step * speed_y[x, 7:23, :],
            jnp.where(upper, diffuse - half_step * pltpu.roll(speed_z[x], 127, 1), 0.0),
            jnp.where(lower, diffuse + half_step * pltpu.roll(speed_z[x], 1, 1), 0.0),
        ]
        stir_up, stir_down = jnp.where(upper, stir, 0.0), jnp.where(lower, stir, 0.0)
        keep = 1.0 - (6.0 + MIX) * diffuse
        for y in range(16):
            stir_y = spread(stir, y)
            for d in range(2):
                move = stir_y * draws[d]
                coef[2 * d, x, y] = spread(base[2 * d], y) + move
                coef[2 * d + 1, x, y] = spread(base[2 * d + 1], y) - move
            coef[4, x, y] = spread(base[4], y) + spread(stir_up, y) * draws[2]
            coef[5, x, y] = spread(base[5], y) - spread(stir_down, y) * draws[2]
            keep_y = spread(keep, y)
            centre[0, x, y] = keep_y
            centre[1, x, y] = keep_y - STEP * OXIDATION
        return 0

    lax.fori_loop(0, 4, coefficients, 0)

    def advance(k, c):
        base_weight, section_weight = WEIGHTS[k - 1]
        old = k - 1
        flat = out.reshape(8 * NS * 64, 128)

        def body(x, h):
            y0 = h * 8
            tiles, weights = [[], []], []
            columns = [[p[old, 2 * c + j, x + 1, y0 + i] for i in range(10)] for j in range(2)]
            means = [mean_row[j, x, pl.ds(y0, 8), :] for j in range(2)]
            for i in range(8):
                y = y0 + i
                factor = [coef[d, x, y] for d in range(6)]
                keep = centre[int(c > 0), x, y]
                here = [columns[j][i + 1] for j in range(2)]
                new = [
                    keep * here[j]
                    + spread(means[j], i)
                    + factor[0] * p[old, 2 * c + j, x + 2, y + 1]
                    + factor[1] * p[old, 2 * c + j, x, y + 1]
                    + factor[2] * columns[j][i + 2]
                    + factor[3] * columns[j][i]
                    + factor[4] * pltpu.roll(here[j], 127, 1)
                    + factor[5] * pltpu.roll(here[j], 1, 1)
                    for j in range(2)
                ]
                if c == 0:
                    square = here[0] * here[0]
                    w = square / (1.0 + square) / (1.0 + jnp.exp(-3.0 * here[1]))
                    weights.append(w)
                    new[1] = new[1] - (STEP * RADIATION) * w
                else:
                    w = weight[x, y]
                    before = [p[old, 3, x + 1, y + 1] if c == 2 else None, here[0]]
                    for j in range(2):
                        gain = STEP * NUCLEATION[2 * c - 2 + j]
                        if before[j] is not None:
                            gain = gain + (STEP * GROWTH) * before[j]
                        new[j] = new[j] + w * gain
                for j in range(2):
                    s = 2 * c + j
                    if base_weight:
                        new[j] = base_weight * p[0, s, x + 1, y + 1] + section_weight * new[j]
                    tiles[j].append(new[j])
            for i, w in enumerate(weights):
                weight[x, y0 + i] = w
            for j in range(2):
                s = 2 * c + j
                for i in range(8):
                    if k < 3:
                        p[k, s, x + 1, y0 + i + 1] = tiles[j][i]
                    else:
                        flat[pl.ds(s * 64 + x * 16 + y0 + i, 8, stride=NS * 64), :] = tiles[j][i]
            if k < 3:
                for j in range(2):
                    part[k, 2 * c + j, x, pl.ds(y0, 8), :] = sum_rows(tiles[j])

        return body

    for k in range(1, 4):
        for c in range(PAIRS):
            mean_term(k - 1, c)
            arrived_y(k - 1, c)
            planes(1, 1, 2, advance(k, c))
            if k < 3:
                scatter(k, c, 1)
                scatter(k, c, 2)
            arrived_x(k - 1, c)
            if k == 1:
                for way in (EAST, WEST):
                    pl.when(has[back[way]])(lambda way=way: turn_face(c, way))
            planes(0, 3, 2, advance(k, c))
            if k < 3:
                scatter(k, c, 0)
                scatter(k, c, 3)
                send_y(k, c)
            if c == 0:
                second_exchange(k - 1, PAIRS - 1)
                pass_on(k - 1, PAIRS - 1)
            elif k < 3:
                second_exchange(k, c - 1)
                pass_on(k, c - 1)
            if k < 3:
                send_x(k, c)

    for way in (EAST, WEST, NORTH, SOUTH):
        pl.when(has[way])(lambda way=way: speed_face(way).wait_send())
        pl.when(has[way])(lambda way=way: all_sent(way))
    all_passed_on()
    wait_bytes(part_in, send_sem.at[SUM1])
    wait_bytes(part_in, send_sem.at[SUM2])


def local(fields_state, velocity, diffusivity, wiener_draw):
    counts = tuple(lax.axis_size(name) for name in ("gx", "gy", "af"))
    held = fields_state.shape
    dma = pltpu.SemaphoreType.DMA
    vmem = lambda *shape: pltpu.VMEM(shape, F32)
    held_in_hbm = (fields_state.reshape(8, NS, 64, 128), velocity, diffusivity, wiener_draw.T)
    out = pl.pallas_call(
        functools.partial(kernel, counts),
        out_shape=pltpu.VMEM((8, NS, 64, 128), F32),
        in_specs=[pl.BlockSpec(memory_space=pltpu.HBM)] * 4,
        out_specs=pl.BlockSpec(memory_space=pltpu.VMEM),
        scratch_shapes=[
            vmem(NS, 8, 64, 128),
            vmem(3, NS, 6, 18, 8, 128),
            vmem(6, 4, 16, 8, 128),
            vmem(2, 4, 16, 8, 128),
            vmem(4, 16, 8, 128),
            vmem(2, 4, 16, 128),
            vmem(3, NS, 4, 16, 128),
            vmem(3, PAIRS, 3, 2, 16, 128),
            vmem(3, NS, 4, 16, 128),
            vmem(6, 16, 128),
            vmem(4, 32, 128),
            vmem(4, 16, 128),
            vmem(4, 16, 128),
            vmem(3, 8),
            vmem(2, PAIRS, 1, 16, 8, 128),
            vmem(2, PAIRS, 8, 2, 16, 128),
            vmem(PAIRS, 8, 1, 16, 128),
            dma((NS,)),
            dma((5,)),
            dma,
            dma((3, PAIRS)),
            dma((4,)),
            dma((4,)),
            dma((6,)),
            dma((3, PAIRS, 6)),
        ],
        compiler_params=pltpu.CompilerParams(
            collective_id=0, has_side_effects=True, vmem_limit_bytes=48 * 1024 * 1024
        ),
    )(*(pltpu.with_memory_space_constraint(x, pltpu.HBM) for x in held_in_hbm))
    return out.reshape(held)


def solution(mesh):
    return jax.shard_map(
        local,
        mesh=mesh,
        in_specs=(
            P("af", None, "gx", "gy", None),
            P(None, "gx", "gy", None),
            P("gx", "gy", None),
            P("af", None),
        ),
        out_specs=P("af", None, "gx", "gy", None),
        check_vma=False,
    )
```

```python
import functools

import jax
import jax.numpy as jnp
from jax import lax
from jax.experimental import pallas as pl
from jax.experimental.pallas import tpu as pltpu
from jax.sharding import PartitionSpec as P

MESH = pl.DeviceIdType.MESH
F32 = jnp.float32

FIELDS = 32
NS = 6
PAIRS = 3
STEP = 0.3
MIX = 4.0
RADIATION = 0.5
NUCLEATION = (1.0, 0.8, 0.6, 0.5)
GROWTH = 0.5
OXIDATION = 0.3
WEIGHTS = ((0.0, 1.0), (0.75, 0.25), (1.0 / 3.0, 2.0 / 3.0))
EAST, WEST, NORTH, SOUTH, SUM1, SUM2 = range(6)


def sum_rows(tiles):
    row = lax.broadcasted_iota(jnp.int32, (8, 128), 0)
    low = row < 4
    quads = [
        jnp.where(low, tiles[i], tiles[i + 4])
        + pltpu.roll(jnp.where(low, tiles[i + 4], tiles[i]), 4, 0)
        for i in range(4)
    ]
    even = (row & 2) == 0
    pairs = [
        jnp.where(even, quads[i], quads[i + 2])
        + jnp.where(even, pltpu.roll(quads[i], 6, 0), pltpu.roll(quads[i + 2], 2, 0))
        for i in range(2)
    ]
    first = (row & 1) == 0
    return jnp.where(first, pairs[0], pairs[1]) + jnp.where(
        first, pltpu.roll(pairs[0], 7, 0), pltpu.roll(pairs[1], 1, 0)
    )


def spread(rows, i):
    return jnp.broadcast_to(rows[i : i + 1, :], (8, 128))


def kernel(
    counts,
    fields_hbm,
    velocity_hbm,
    diffusivity_hbm,
    wiener_hbm,
    out,
    rows_in,
    p,
    coef,
    centre,
    weight,
    mean_row,
    part,
    part_in,
    total,
    speed_x,
    speed_y,
    speed_z,
    diffusion,
    wiener,
    relay,
    raw,
    raw_relay,
    in_sem,
    own_sem,
    relay_send,
    relay_recv,
    speed_send,
    speed_recv,
    send_sem,
    recv_sem,
):
    nx, ny, na = counts
    ax, ix, iy = lax.axis_index("af"), lax.axis_index("gx"), lax.axis_index("gy")
    has = {EAST: ix < nx - 1, WEST: ix > 0, NORTH: iy < ny - 1, SOUTH: iy > 0}
    back = {EAST: WEST, WEST: EAST, NORTH: SOUTH, SOUTH: NORTH}
    target = {
        EAST: (ax, ix + 1, iy),
        WEST: (ax, ix - 1, iy),
        NORTH: (ax, ix, iy + 1),
        SOUTH: (ax, ix, iy - 1),
    }
    members = [lax.rem(ax + step, na) for step in range(na)]
    member_ids = [(other, ix, iy) for other in members]

    mid, end = nx // 2, nx - 1
    to_relay = {EAST: ix == mid - 1, WEST: ix == mid}
    is_relay = {EAST: ix == end, WEST: ix == 0}
    relay_of = {EAST: (ax, end, iy), WEST: (ax, 0, iy)}
    relay_to = {EAST: (ax, mid, iy), WEST: (ax, mid - 1, iy)}
    is_mid, is_end = to_relay[EAST] | to_relay[WEST], is_relay[EAST] | is_relay[WEST]
    yields = lax.rem(iy, 2) == 1
    both = {EAST: has[EAST] & has[WEST], NORTH: has[NORTH] & has[SOUTH]}
    plain = {way: has[way] & jnp.logical_not(to_relay[way]) for way in (EAST, WEST)}

    def load_in(s):
        return pltpu.make_async_copy(fields_hbm.at[:, s], rows_in.at[s], in_sem.at[s])

    def two(c):
        return pl.ds(2 * c, 2)

    own = [
        pltpu.make_async_copy(velocity_hbm.at[0], speed_x.at[pl.ds(1, 4)], own_sem.at[0]),
        pltpu.make_async_copy(velocity_hbm.at[1], speed_y.at[:, pl.ds(8, 16)], own_sem.at[1]),
        pltpu.make_async_copy(velocity_hbm.at[2], speed_z, own_sem.at[2]),
        pltpu.make_async_copy(diffusivity_hbm, diffusion, own_sem.at[3]),
        pltpu.make_async_copy(wiener_hbm, wiener, own_sem.at[4]),
    ]

    def speed_face(way):
        src, dst = {
            EAST: (velocity_hbm.at[0, 3], speed_x.at[0]),
            WEST: (velocity_hbm.at[0, 0], speed_x.at[5]),
            NORTH: (velocity_hbm.at[1, :, pl.ds(8, 8)], speed_y.at[:, pl.ds(0, 8)]),
            SOUTH: (velocity_hbm.at[1, :, pl.ds(0, 8)], speed_y.at[:, pl.ds(24, 8)]),
        }[way]
        return pltpu.make_async_remote_copy(
            src_ref=src,
            dst_ref=dst,
            send_sem=speed_send.at[way],
            recv_sem=speed_recv.at[way],
            device_id=target[way],
            device_id_type=MESH,
        )

    def face(k, s, way, recv=None):
        src, dst = {
            NORTH: lambda: (p.at[k, s, pl.ds(1, 4), 16], p.at[k, s, pl.ds(1, 4), 0]),
            SOUTH: lambda: (p.at[k, s, pl.ds(1, 4), 1], p.at[k, s, pl.ds(1, 4), 17]),
        }[way]()
        return pltpu.make_async_remote_copy(
            src_ref=src,
            dst_ref=dst,
            send_sem=send_sem.at[way],
            recv_sem=recv,
            device_id=target[way],
            device_id_type=MESH,
        )

    def chunk(k, c, way):
        return face(k, two(c), way, recv_sem.at[k, c, NORTH])

    def wait_bytes(ref, sem):
        pltpu.make_async_copy(ref, ref, sem).wait()

    def all_sent(way):
        if way in to_relay:
            pl.when(jnp.logical_not(yields))(
                lambda: wait_bytes(p.at[:, :, 1, pl.ds(1, 16)], send_sem.at[way])
            )
        else:
            wait_bytes(p.at[:, :, pl.ds(1, 4), 1], send_sem.at[way])

    def x_face(k, c, way, s=None, y=0, count=16):
        src, dst = {EAST: (4, 0), WEST: (1, 5)}[way]
        which = pl.ds(2 * c, 2) if s is None else pl.ds(2 * c + s, 1)
        to = pl.ds(0, 2) if s is None else pl.ds(s, 1)
        if k == 0:
            rows = pl.ds(16 * (src - 1) + y, count)
            return fields_hbm.at[:, which, rows], raw.at[way, c, :, to, pl.ds(y, count)]
        rows = pl.ds(1 + y, count)
        return p.at[k, which, src, rows], p.at[k, which, dst, rows]

    def copy_x(refs, way, recv, to):
        return pltpu.make_async_remote_copy(
            src_ref=refs[0],
            dst_ref=refs[1],
            send_sem=send_sem.at[way],
            recv_sem=recv,
            device_id=to,
            device_id_type=MESH,
        )

    def relay_at(k, c):
        return raw_relay.at[c] if k == 0 else relay.at[k - 1, c]

    def left_x():
        for way in (EAST, WEST):
            pl.when(has[way] & yields)(
                lambda: wait_bytes(p.at[1, two(0), 1, pl.ds(1, 16)], send_sem.at[way])
            )

    def send_x(k, c):
        if k or c:
            left_x()
        recv = recv_sem.at[k, c, EAST]
        for way in (EAST, WEST):

            @pl.when(plain[way])
            def _():
                copy_x(x_face(k, c, way), way, recv, target[way]).start()

        @pl.when(is_mid)
        def _():
            for way in (EAST, WEST):

                @pl.when(to_relay[way])
                def _():
                    src = x_face(k, c, way, 1, 8, 8)[0]
                    copy_x(
                        (src, relay_at(k, c)), way, relay_recv.at[k, c], relay_of[way]
                    ).start()
                    copy_x(x_face(k, c, way, 0), way, recv, target[way]).start()
                    copy_x(x_face(k, c, way, 1, 0, 8), way, recv, target[way]).start()

    def send_y(k, c):
        for way in (NORTH, SOUTH):
            pl.when(has[way])(lambda: chunk(k, c, way).start())

    def arrived_y(k, c):
        sem = recv_sem.at[k, c, NORTH]
        two_faces = p.at[k, two(c), pl.ds(1, 4), pl.ds(0, 2)]
        one_face = p.at[k, two(c), pl.ds(1, 4), pl.ds(0, 1)]
        pl.when(both[NORTH])(lambda: wait_bytes(two_faces, sem))
        pl.when(jnp.logical_not(both[NORTH]))(lambda: wait_bytes(one_face, sem))

    def arrived_x(k, c):
        sem = recv_sem.at[k, c, EAST]
        if k == 0:
            two_faces, one_face = raw.at[:, c], raw.at[0, c]
        else:
            two_faces = p.at[k, two(c), pl.ds(0, 2), pl.ds(1, 16)]
            one_face = p.at[k, two(c), pl.ds(0, 1), pl.ds(1, 16)]
        pl.when(both[EAST])(lambda: wait_bytes(two_faces, sem))
        pl.when(jnp.logical_not(both[EAST]))(lambda: wait_bytes(one_face, sem))

    def pass_on(k, c):
        @pl.when(is_end)
        def _():
            here = relay_at(k, c)
            wait_bytes(here, relay_recv.at[k, c])
            for way in (EAST, WEST):

                @pl.when(is_relay[way])
                def _():
                    pltpu.make_async_remote_copy(
                        src_ref=here,
                        dst_ref=x_face(k, c, way, 1, 8, 8)[1],
                        send_sem=relay_send,
                        recv_sem=recv_sem.at[k, c, EAST],
                        device_id=relay_to[way],
                        device_id_type=MESH,
                    ).start()

    def all_passed_on():
        @pl.when(is_end)
        def _():
            wait_bytes(relay, relay_send)
            wait_bytes(raw_relay, relay_send)

    def planes(first, step, count, body):
        def at(i, _):
            for h in range(2):
                body(first + step * i, h)
            return 0

        lax.fori_loop(0, count, at, 0)

    load_in(0).start()
    for copy in own:
        copy.start()
    for s in range(1, NS):
        load_in(s).start()

    barrier = pltpu.get_barrier_semaphore()
    expected = na - 1
    for way in (EAST, WEST, NORTH, SOUTH):
        pl.when(has[way])(
            lambda way=way: pl.semaphore_signal(
                barrier, inc=1, device_id=target[way], device_id_type=MESH
            )
        )
        expected = expected + has[way].astype(jnp.int32)
    for way in (EAST, WEST):
        for near, partners in (
            (to_relay[way], ((ax, 0, iy), (ax, end, iy))),
            (is_relay[way], ((ax, mid - 1, iy), (ax, mid, iy))),
        ):
            expected = expected + 2 * near.astype(jnp.int32)

            @pl.when(near)
            def _(partners=partners):
                for partner in partners:
                    pl.semaphore_signal(barrier, inc=1, device_id=partner, device_id_type=MESH)

    for step in range(1, na):
        pl.semaphore_signal(
            barrier, inc=1, device_id=member_ids[step], device_id_type=MESH
        )

    zero = jnp.zeros((8, 128), F32)

    def clear_x(x, speed):
        def at(s, _):
            for k in range(3):
                for y in range(16):
                    p[k, s, x, 1 + y] = zero
            return 0

        lax.fori_loop(0, NS, at, 0)
        speed_x[speed] = jnp.zeros((16, 128), F32)

    def clear_y(y, speed):
        def at(s, _):
            for k in range(3):
                for x in range(4):
                    p[k, s, 1 + x, y] = zero
            return 0

        lax.fori_loop(0, NS, at, 0)
        for x in range(4):
            speed_y[x, speed : speed + 8] = zero

    pl.when(ix == 0)(lambda: clear_x(0, 0))
    pl.when(ix == nx - 1)(lambda: clear_x(5, 5))
    pl.when(iy == 0)(lambda: clear_y(0, 0))
    pl.when(iy == ny - 1)(lambda: clear_y(17, 24))

    pl.semaphore_wait(barrier, expected)
    send_x(0, 0)
    for way in (EAST, WEST, NORTH, SOUTH):
        pl.when(has[way])(lambda way=way: speed_face(way).start())

    def scatter(k, c, owner):
        @pl.when(ax != owner)
        def _():
            pltpu.make_async_remote_copy(
                src_ref=part.at[k, two(c), owner],
                dst_ref=part_in.at[k, c, lax.rem(owner - ax + na, na) - 1],
                send_sem=send_sem.at[SUM1],
                recv_sem=recv_sem.at[k, c, SUM1],
                device_id=(owner, ix, iy),
                device_id_type=MESH,
            ).start()

    def second_exchange(k, c):
        wait_bytes(part_in.at[k, c], recv_sem.at[k, c, SUM1])
        for i in range(2):
            total[k, 2 * c + i, ax] = (part[k, 2 * c + i, ax] + part_in[k, c, 0, i]) + (
                part_in[k, c, 1, i] + part_in[k, c, 2, i]
            )
        mine = total.at[k, two(c), ax]
        for step in range(1, na):
            pltpu.make_async_remote_copy(
                src_ref=mine,
                dst_ref=mine,
                send_sem=send_sem.at[SUM2],
                recv_sem=recv_sem.at[k, c, SUM2],
                device_id=member_ids[step],
                device_id_type=MESH,
            ).start()

    def mean_term(k, c):
        wait_bytes(total.at[k, two(c), pl.ds(0, na - 1)], recv_sem.at[k, c, SUM2])
        scale = (STEP * MIX / FIELDS) * diffusion[...]
        for i in range(2):
            mean_row[i] = scale * total[k, 2 * c + i]

    def turn(s):
        flat = rows_in.reshape(NS * 8 * 64, 128)

        def body(x, h):
            start = s * 512 + x * 16 + h * 8
            tiles = [flat[pl.ds(start + i, 8, stride=64), :] for i in range(8)]
            for i in range(8):
                p[0, s, x + 1, h * 8 + i + 1] = tiles[i]
            part[0, s, x, pl.ds(h * 8, 8), :] = sum_rows(tiles)

        return body

    raw_rows = raw.reshape(2 * PAIRS * 8 * 32, 128)

    def turn_face(c, way):
        for j in range(2):
            start = (way * PAIRS + c) * 256 + j * 16
            for y in range(16):
                tile = raw_rows[pl.ds(start + y, 8, stride=32), :]
                p[0, 2 * c + j, 0 if way == EAST else 5, y + 1] = tile

    for c in range(PAIRS):
        for s in (2 * c, 2 * c + 1):
            load_in(s).wait()
            planes(0, 1, 4, turn(s))
        for owner in range(na):
            scatter(0, c, owner)
        send_y(0, c)
        if c > 0:
            second_exchange(0, c - 1)
            pass_on(0, c - 1)
        if c + 1 < PAIRS:
            send_x(0, c + 1)

    for copy in own:
        copy.wait()
    for way in (EAST, WEST, NORTH, SOUTH):
        pl.when(has[back[way]])(lambda way=way: speed_face(way).wait_recv())

    diagonal = lax.broadcasted_iota(jnp.int32, (8, 8), 0) == lax.broadcasted_iota(
        jnp.int32, (8, 8), 1
    )
    draws = []
    for d in range(3):
        row = jnp.broadcast_to(wiener[d : d + 1, :], (8, 8))
        draw = jnp.sum(jnp.where(diagonal, row, 0.0), axis=1, keepdims=True)
        draws.append(jnp.broadcast_to(draw, (8, 128)))

    def coefficients(x, _):
        g = diffusion[x]
        diffuse = STEP * g
        stir = (0.5 * STEP) * jnp.sqrt((2.0 / STEP) * g)
        lane = lax.broadcasted_iota(jnp.int32, (16, 128), 1)
        upper, lower = lane < 127, lane > 0
        half_step = 0.5 * STEP
        base = [
            diffuse - half_step * speed_x[x + 2],
            diffuse + half_step * speed_x[x],
            diffuse - half_step * speed_y[x, 9:25, :],
            diffuse + half_step * speed_y[x, 7:23, :],
            jnp.where(upper, diffuse - half_step * pltpu.roll(speed_z[x], 127, 1), 0.0),
            jnp.where(lower, diffuse + half_step * pltpu.roll(speed_z[x], 1, 1), 0.0),
        ]
        stir_up, stir_down = jnp.where(upper, stir, 0.0), jnp.where(lower, stir, 0.0)
        keep = 1.0 - (6.0 + MIX) * diffuse
        for y in range(16):
            stir_y = spread(stir, y)
            for d in range(2):
                move = stir_y * draws[d]
                coef[2 * d, x, y] = spread(base[2 * d], y) + move
                coef[2 * d + 1, x, y] = spread(base[2 * d + 1], y) - move
            coef[4, x, y] = spread(base[4], y) + spread(stir_up, y) * draws[2]
            coef[5, x, y] = spread(base[5], y) - spread(stir_down, y) * draws[2]
            keep_y = spread(keep, y)
            centre[0, x, y] = keep_y
            centre[1, x, y] = keep_y - STEP * OXIDATION
        return 0

    lax.fori_loop(0, 4, coefficients, 0)

    def advance(k, c):
        base_weight, section_weight = WEIGHTS[k - 1]
        old = k - 1
        flat = out.reshape(8 * NS * 64, 128)

        def body(x, h):
            y0 = h * 8
            tiles, weights = [[], []], []
            columns = [[p[old, 2 * c + j, x + 1, y0 + i] for i in range(10)] for j in range(2)]
            means = [mean_row[j, x, pl.ds(y0, 8), :] for j in range(2)]
            for i in range(8):
                y = y0 + i
                factor = [coef[d, x, y] for d in range(6)]
                keep = centre[int(c > 0), x, y]
                here = [columns[j][i + 1] for j in range(2)]
                new = [
                    keep * here[j]
                    + spread(means[j], i)
                    + factor[0] * p[old, 2 * c + j, x + 2, y + 1]
                    + factor[1] * p[old, 2 * c + j, x, y + 1]
                    + factor[2] * columns[j][i + 2]
                    + factor[3] * columns[j][i]
                    + factor[4] * pltpu.roll(here[j], 127, 1)
                    + factor[5] * pltpu.roll(here[j], 1, 1)
                    for j in range(2)
                ]
                if c == 0:
                    square = here[0] * here[0]
                    w = square / (1.0 + square) / (1.0 + jnp.exp(-3.0 * here[1]))
                    weights.append(w)
                    new[1] = new[1] - (STEP * RADIATION) * w
                else:
                    w = weight[x, y]
                    before = [p[old, 3, x + 1, y + 1] if c == 2 else None, here[0]]
                    for j in range(2):
                        gain = STEP * NUCLEATION[2 * c - 2 + j]
                        if before[j] is not None:
                            gain = gain + (STEP * GROWTH) * before[j]
                        new[j] = new[j] + w * gain
                for j in range(2):
                    s = 2 * c + j
                    if base_weight:
                        new[j] = base_weight * p[0, s, x + 1, y + 1] + section_weight * new[j]
                    tiles[j].append(new[j])
            for i, w in enumerate(weights):
                weight[x, y0 + i] = w
            for j in range(2):
                s = 2 * c + j
                for i in range(8):
                    if k < 3:
                        p[k, s, x + 1, y0 + i + 1] = tiles[j][i]
                    else:
                        flat[pl.ds(s * 64 + x * 16 + y0 + i, 8, stride=NS * 64), :] = tiles[j][i]
            if k < 3:
                for j in range(2):
                    part[k, 2 * c + j, x, pl.ds(y0, 8), :] = sum_rows(tiles[j])

        return body

    for k in range(1, 4):
        for c in range(PAIRS):
            mean_term(k - 1, c)
            arrived_y(k - 1, c)
            planes(1, 1, 2, advance(k, c))
            if k < 3:
                scatter(k, c, 1)
                scatter(k, c, 2)
            arrived_x(k - 1, c)
            if c == 0:
                pass_on(k - 1, PAIRS - 1)
            elif k < 3:
                pass_on(k, c - 1)
            if k == 1:
                for way in (EAST, WEST):
                    pl.when(has[back[way]])(lambda way=way: turn_face(c, way))
            planes(0, 3, 2, advance(k, c))
            if k < 3:
                scatter(k, c, 0)
                scatter(k, c, 3)
                send_y(k, c)
            if c == 0:
                second_exchange(k - 1, PAIRS - 1)
            elif k < 3:
                second_exchange(k, c - 1)
            if k < 3:
                send_x(k, c)

    for way in (EAST, WEST, NORTH, SOUTH):
        pl.when(has[way])(lambda way=way: speed_face(way).wait_send())
        pl.when(has[way])(lambda way=way: all_sent(way))
    left_x()
    all_passed_on()
    wait_bytes(part_in, send_sem.at[SUM1])
    wait_bytes(part_in, send_sem.at[SUM2])


def local(fields_state, velocity, diffusivity, wiener_draw):
    counts = tuple(lax.axis_size(name) for name in ("gx", "gy", "af"))
    held = fields_state.shape
    dma = pltpu.SemaphoreType.DMA
    vmem = lambda *shape: pltpu.VMEM(shape, F32)
    held_in_hbm = (fields_state.reshape(8, NS, 64, 128), velocity, diffusivity, wiener_draw.T)
    out = pl.pallas_call(
        functools.partial(kernel, counts),
        out_shape=pltpu.VMEM((8, NS, 64, 128), F32),
        in_specs=[pl.BlockSpec(memory_space=pltpu.HBM)] * 4,
        out_specs=pl.BlockSpec(memory_space=pltpu.VMEM),
        scratch_shapes=[
            vmem(NS, 8, 64, 128),
            vmem(3, NS, 6, 18, 8, 128),
            vmem(6, 4, 16, 8, 128),
            vmem(2, 4, 16, 8, 128),
            vmem(4, 16, 8, 128),
            vmem(2, 4, 16, 128),
            vmem(3, NS, 4, 16, 128),
            vmem(3, PAIRS, 3, 2, 16, 128),
            vmem(3, NS, 4, 16, 128),
            vmem(6, 16, 128),
            vmem(4, 32, 128),
            vmem(4, 16, 128),
            vmem(4, 16, 128),
            vmem(3, 8),
            vmem(2, PAIRS, 1, 8, 8, 128),
            vmem(2, PAIRS, 8, 2, 16, 128),
            vmem(PAIRS, 8, 1, 8, 128),
            dma((NS,)),
            dma((5,)),
            dma,
            dma((3, PAIRS)),
            dma((4,)),
            dma((4,)),
            dma((6,)),
            dma((3, PAIRS, 6)),
        ],
        compiler_params=pltpu.CompilerParams(
            collective_id=0, has_side_effects=True, vmem_limit_bytes=48 * 1024 * 1024
        ),
    )(*(pltpu.with_memory_space_constraint(x, pltpu.HBM) for x in held_in_hbm))
    return out.reshape(held)


def solution(mesh):
    return jax.shard_map(
        local,
        mesh=mesh,
        in_specs=(
            P("af", None, "gx", "gy", None),
            P(None, "gx", "gy", None),
            P("gx", "gy", None),
            P("af", None),
        ),
        out_specs=P("af", None, "gx", "gy", None),
        check_vma=False,
    )
```

```python
import functools

import jax
import jax.numpy as jnp
from jax import lax
from jax.experimental import pallas as pl
from jax.experimental.pallas import tpu as pltpu
from jax.sharding import PartitionSpec as P

MESH = pl.DeviceIdType.MESH
F32 = jnp.float32

FIELDS = 32
NS = 6
PAIRS = 3
STEP = 0.3
MIX = 4.0
RADIATION = 0.5
NUCLEATION = (1.0, 0.8, 0.6, 0.5)
GROWTH = 0.5
OXIDATION = 0.3
WEIGHTS = ((0.0, 1.0), (0.75, 0.25), (1.0 / 3.0, 2.0 / 3.0))
EAST, WEST, NORTH, SOUTH, SUM1, SUM2 = range(6)


def add_up(tiles):
    while len(tiles) > 1:
        tiles = [a + b for a, b in zip(tiles[::2], tiles[1::2])]
    return tiles[0]


def spread(rows, i):
    return jnp.broadcast_to(rows[i : i + 1, :], (8, 128))


def kernel(
    counts,
    fields_hbm,
    velocity_hbm,
    diffusivity_hbm,
    wiener_hbm,
    out,
    rows_in,
    p,
    coef,
    centre,
    weight,
    mean_row,
    part,
    part_in,
    total,
    speed_x,
    speed_y,
    speed_z,
    diffusion,
    wiener,
    relay,
    raw,
    raw_relay,
    in_sem,
    own_sem,
    relay_send,
    relay_recv,
    speed_send,
    speed_recv,
    send_sem,
    recv_sem,
):
    nx, ny, na = counts
    ax, ix, iy = lax.axis_index("af"), lax.axis_index("gx"), lax.axis_index("gy")
    has = {EAST: ix < nx - 1, WEST: ix > 0, NORTH: iy < ny - 1, SOUTH: iy > 0}
    back = {EAST: WEST, WEST: EAST, NORTH: SOUTH, SOUTH: NORTH}
    target = {
        EAST: (ax, ix + 1, iy),
        WEST: (ax, ix - 1, iy),
        NORTH: (ax, ix, iy + 1),
        SOUTH: (ax, ix, iy - 1),
    }
    members = [lax.rem(ax + step, na) for step in range(na)]
    member_ids = [(other, ix, iy) for other in members]

    mid, end = nx // 2, nx - 1
    to_relay = {EAST: ix == mid - 1, WEST: ix == mid}
    is_relay = {EAST: ix == end, WEST: ix == 0}
    relay_of = {EAST: (ax, end, iy), WEST: (ax, 0, iy)}
    relay_to = {EAST: (ax, mid, iy), WEST: (ax, mid - 1, iy)}
    is_mid, is_end = to_relay[EAST] | to_relay[WEST], is_relay[EAST] | is_relay[WEST]
    both = {EAST: has[EAST] & has[WEST], NORTH: has[NORTH] & has[SOUTH]}
    plain = {way: has[way] & jnp.logical_not(to_relay[way]) for way in (EAST, WEST)}

    def load_in(s):
        return pltpu.make_async_copy(fields_hbm.at[:, s], rows_in.at[s], in_sem.at[s])

    def two(c):
        return pl.ds(2 * c, 2)

    own = [
        pltpu.make_async_copy(velocity_hbm.at[0], speed_x.at[pl.ds(1, 4)], own_sem.at[0]),
        pltpu.make_async_copy(velocity_hbm.at[1], speed_y.at[:, pl.ds(8, 16)], own_sem.at[1]),
        pltpu.make_async_copy(velocity_hbm.at[2], speed_z, own_sem.at[2]),
        pltpu.make_async_copy(diffusivity_hbm, diffusion, own_sem.at[3]),
        pltpu.make_async_copy(wiener_hbm, wiener, own_sem.at[4]),
    ]

    def speed_face(way):
        src, dst = {
            EAST: (velocity_hbm.at[0, 3], speed_x.at[0]),
            WEST: (velocity_hbm.at[0, 0], speed_x.at[5]),
            NORTH: (velocity_hbm.at[1, :, pl.ds(8, 8)], speed_y.at[:, pl.ds(0, 8)]),
            SOUTH: (velocity_hbm.at[1, :, pl.ds(0, 8)], speed_y.at[:, pl.ds(24, 8)]),
        }[way]
        return pltpu.make_async_remote_copy(
            src_ref=src,
            dst_ref=dst,
            send_sem=speed_send.at[way],
            recv_sem=speed_recv.at[way],
            device_id=target[way],
            device_id_type=MESH,
        )

    def face(k, s, way, recv=None):
        src, dst = {
            NORTH: lambda: (p.at[k, s, pl.ds(1, 4), 16], p.at[k, s, pl.ds(1, 4), 0]),
            SOUTH: lambda: (p.at[k, s, pl.ds(1, 4), 1], p.at[k, s, pl.ds(1, 4), 17]),
        }[way]()
        return pltpu.make_async_remote_copy(
            src_ref=src,
            dst_ref=dst,
            send_sem=send_sem.at[way],
            recv_sem=recv,
            device_id=target[way],
            device_id_type=MESH,
        )

    def chunk(k, c, way):
        return face(k, two(c), way, recv_sem.at[k, c, NORTH])

    def wait_bytes(ref, sem):
        pltpu.make_async_copy(ref, ref, sem).wait()

    def all_sent(way):
        if way in to_relay:
            wait_bytes(p.at[:, :, 1, pl.ds(1, 16)], send_sem.at[way])
        else:
            wait_bytes(p.at[:, :, pl.ds(1, 4), 1], send_sem.at[way])

    def x_face(k, c, way, s=None):
        src, dst = {EAST: (4, 0), WEST: (1, 5)}[way]
        side = way
        which = pl.ds(2 * c, 2) if s is None else pl.ds(2 * c + s, 1)
        to = pl.ds(0, 2) if s is None else pl.ds(s, 1)
        if k == 0:
            refs = fields_hbm.at[:, which, pl.ds(16 * (src - 1), 16)], raw.at[side, c, :, to]
        else:
            refs = p.at[k, which, src, pl.ds(1, 16)], p.at[k, which, dst, pl.ds(1, 16)]
        return refs

    def copy_x(refs, way, recv, to):
        return pltpu.make_async_remote_copy(
            src_ref=refs[0],
            dst_ref=refs[1],
            send_sem=send_sem.at[way],
            recv_sem=recv,
            device_id=to,
            device_id_type=MESH,
        )

    def relay_at(k, c):
        return raw_relay.at[c] if k == 0 else relay.at[k - 1, c]

    def send_x(k, c):
        recv = recv_sem.at[k, c, EAST]
        for way in (EAST, WEST):

            @pl.when(plain[way])
            def _():
                copy_x(x_face(k, c, way), way, recv, target[way]).start()

        @pl.when(is_mid)
        def _():
            for way in (EAST, WEST):

                @pl.when(to_relay[way])
                def _():
                    src = x_face(k, c, way, 1)[0]
                    copy_x(
                        (src, relay_at(k, c)), way, relay_recv.at[k, c], relay_of[way]
                    ).start()
                    copy_x(x_face(k, c, way, 0), way, recv, target[way]).start()

    def send_y(k, c):
        for way in (NORTH, SOUTH):
            pl.when(has[way])(lambda: chunk(k, c, way).start())

    def arrived_y(k, c):
        sem = recv_sem.at[k, c, NORTH]
        two_faces = p.at[k, two(c), pl.ds(1, 4), pl.ds(0, 2)]
        one_face = p.at[k, two(c), pl.ds(1, 4), pl.ds(0, 1)]
        pl.when(both[NORTH])(lambda: wait_bytes(two_faces, sem))
        pl.when(jnp.logical_not(both[NORTH]))(lambda: wait_bytes(one_face, sem))

    def arrived_x(k, c):
        sem = recv_sem.at[k, c, EAST]
        if k == 0:
            two_faces, one_face = raw.at[:, c], raw.at[0, c]
        else:
            two_faces = p.at[k, two(c), pl.ds(0, 2), pl.ds(1, 16)]
            one_face = p.at[k, two(c), pl.ds(0, 1), pl.ds(1, 16)]
        pl.when(both[EAST])(lambda: wait_bytes(two_faces, sem))
        pl.when(jnp.logical_not(both[EAST]))(lambda: wait_bytes(one_face, sem))

    def pass_on(k, c):
        @pl.when(is_end)
        def _():
            here = relay_at(k, c)
            wait_bytes(here, relay_recv.at[k, c])
            for way in (EAST, WEST):

                @pl.when(is_relay[way])
                def _():
                    pltpu.make_async_remote_copy(
                        src_ref=here,
                        dst_ref=x_face(k, c, way, 1)[1],
                        send_sem=relay_send,
                        recv_sem=recv_sem.at[k, c, EAST],
                        device_id=relay_to[way],
                        device_id_type=MESH,
                    ).start()

    def all_passed_on():
        @pl.when(is_end)
        def _():
            wait_bytes(relay, relay_send)
            wait_bytes(raw_relay, relay_send)

    def planes(first, step, count, body):
        def at(i, _):
            for h in range(2):
                body(first + step * i, h)
            return 0

        lax.fori_loop(0, count, at, 0)

    load_in(0).start()
    for copy in own:
        copy.start()
    for s in range(1, NS):
        load_in(s).start()

    barrier = pltpu.get_barrier_semaphore()
    expected = na - 1
    for way in (EAST, WEST, NORTH, SOUTH):
        pl.when(has[way])(
            lambda way=way: pl.semaphore_signal(
                barrier, inc=1, device_id=target[way], device_id_type=MESH
            )
        )
        expected = expected + has[way].astype(jnp.int32)
    for way in (EAST, WEST):
        for near, partners in (
            (to_relay[way], ((ax, 0, iy), (ax, end, iy))),
            (is_relay[way], ((ax, mid - 1, iy), (ax, mid, iy))),
        ):
            expected = expected + 2 * near.astype(jnp.int32)

            @pl.when(near)
            def _(partners=partners):
                for partner in partners:
                    pl.semaphore_signal(barrier, inc=1, device_id=partner, device_id_type=MESH)

    for step in range(1, na):
        pl.semaphore_signal(
            barrier, inc=1, device_id=member_ids[step], device_id_type=MESH
        )

    zero = jnp.zeros((8, 128), F32)

    def clear_x(x, speed):
        def at(s, _):
            for k in range(3):
                for y in range(16):
                    p[k, s, x, 1 + y] = zero
            return 0

        lax.fori_loop(0, NS, at, 0)
        speed_x[speed] = jnp.zeros((16, 128), F32)

    def clear_y(y, speed):
        def at(s, _):
            for k in range(3):
                for x in range(4):
                    p[k, s, 1 + x, y] = zero
            return 0

        lax.fori_loop(0, NS, at, 0)
        for x in range(4):
            speed_y[x, speed : speed + 8] = zero

    pl.when(ix == 0)(lambda: clear_x(0, 0))
    pl.when(ix == nx - 1)(lambda: clear_x(5, 5))
    pl.when(iy == 0)(lambda: clear_y(0, 0))
    pl.when(iy == ny - 1)(lambda: clear_y(17, 24))

    pl.semaphore_wait(barrier, expected)
    send_x(0, 0)
    for way in (EAST, WEST, NORTH, SOUTH):
        pl.when(has[way])(lambda way=way: speed_face(way).start())

    def scatter(k, c, owner):
        @pl.when(ax != owner)
        def _():
            pltpu.make_async_remote_copy(
                src_ref=part.at[k, two(c), owner],
                dst_ref=part_in.at[k, c, lax.rem(owner - ax + na, na) - 1],
                send_sem=send_sem.at[SUM1],
                recv_sem=recv_sem.at[k, c, SUM1],
                device_id=(owner, ix, iy),
                device_id_type=MESH,
            ).start()

    def second_exchange(k, c):
        wait_bytes(part_in.at[k, c], recv_sem.at[k, c, SUM1])
        for i in range(2):
            total[k, 2 * c + i, ax] = (part[k, 2 * c + i, ax] + part_in[k, c, 0, i]) + (
                part_in[k, c, 1, i] + part_in[k, c, 2, i]
            )
        mine = total.at[k, two(c), ax]
        for step in range(1, na):
            pltpu.make_async_remote_copy(
                src_ref=mine,
                dst_ref=mine,
                send_sem=send_sem.at[SUM2],
                recv_sem=recv_sem.at[k, c, SUM2],
                device_id=member_ids[step],
                device_id_type=MESH,
            ).start()

    def mean_term(k, c):
        wait_bytes(total.at[k, two(c), pl.ds(0, na - 1)], recv_sem.at[k, c, SUM2])
        scale = (STEP * MIX / FIELDS) * diffusion[...]
        for i in range(2):
            mean_row[i] = scale * total[k, 2 * c + i]

    def turn(s):
        flat = rows_in.reshape(NS * 8 * 64, 128)

        def body(x, h):
            start = s * 512 + x * 16 + h * 8
            tiles = [flat[pl.ds(start + i, 8, stride=64), :] for i in range(8)]
            for i in range(8):
                p[0, s, x + 1, h * 8 + i + 1] = tiles[i]
            part[0, s, x, pl.ds(h * 8, 8), :] = add_up(
                [rows_in[s, f, pl.ds(x * 16 + h * 8, 8), :] for f in range(8)]
            )

        return body

    raw_rows = raw.reshape(2 * PAIRS * 8 * 32, 128)

    def turn_face(c, way):
        for j in range(2):
            start = (way * PAIRS + c) * 256 + j * 16
            for y in range(16):
                tile = raw_rows[pl.ds(start + y, 8, stride=32), :]
                p[0, 2 * c + j, 0 if way == EAST else 5, y + 1] = tile

    for c in range(PAIRS):
        for s in (2 * c, 2 * c + 1):
            load_in(s).wait()
            planes(0, 1, 4, turn(s))
        for owner in range(na):
            scatter(0, c, owner)
        send_y(0, c)
        if c > 0:
            second_exchange(0, c - 1)
            pass_on(0, c - 1)
        if c + 1 < PAIRS:
            send_x(0, c + 1)

    for copy in own:
        copy.wait()
    for way in (EAST, WEST, NORTH, SOUTH):
        pl.when(has[back[way]])(lambda way=way: speed_face(way).wait_recv())

    diagonal = lax.broadcasted_iota(jnp.int32, (8, 8), 0) == lax.broadcasted_iota(
        jnp.int32, (8, 8), 1
    )
    draws = []
    for d in range(3):
        row = jnp.broadcast_to(wiener[d : d + 1, :], (8, 8))
        draw = jnp.sum(jnp.where(diagonal, row, 0.0), axis=1, keepdims=True)
        draws.append(jnp.broadcast_to(draw, (8, 128)))

    def coefficients(x, _):
        g = diffusion[x]
        diffuse = STEP * g
        stir = (0.5 * STEP) * jnp.sqrt((2.0 / STEP) * g)
        lane = lax.broadcasted_iota(jnp.int32, (16, 128), 1)
        upper, lower = lane < 127, lane > 0
        half_step = 0.5 * STEP
        base = [
            diffuse - half_step * speed_x[x + 2],
            diffuse + half_step * speed_x[x],
            diffuse - half_step * speed_y[x, 9:25, :],
            diffuse + half_step * speed_y[x, 7:23, :],
            jnp.where(upper, diffuse - half_step * pltpu.roll(speed_z[x], 127, 1), 0.0),
            jnp.where(lower, diffuse + half_step * pltpu.roll(speed_z[x], 1, 1), 0.0),
        ]
        stir_up, stir_down = jnp.where(upper, stir, 0.0), jnp.where(lower, stir, 0.0)
        keep = 1.0 - (6.0 + MIX) * diffuse
        for y in range(16):
            stir_y = spread(stir, y)
            for d in range(2):
                move = stir_y * draws[d]
                coef[2 * d, x, y] = spread(base[2 * d], y) + move
                coef[2 * d + 1, x, y] = spread(base[2 * d + 1], y) - move
            coef[4, x, y] = spread(base[4], y) + spread(stir_up, y) * draws[2]
            coef[5, x, y] = spread(base[5], y) - spread(stir_down, y) * draws[2]
            keep_y = spread(keep, y)
            centre[0, x, y] = keep_y
            centre[1, x, y] = keep_y - STEP * OXIDATION
        return 0

    lax.fori_loop(0, 4, coefficients, 0)

    def advance(k, c):
        base_weight, section_weight = WEIGHTS[k - 1]
        old = k - 1
        flat = out.reshape(8 * NS * 64, 128)
        flat_p = p.reshape(3 * NS * 6 * 18 * 8, 128)

        def body(x, h):
            y0 = h * 8
            tiles, weights = [[], []], []
            columns = [[p[old, 2 * c + j, x + 1, y0 + i] for i in range(10)] for j in range(2)]
            for i in range(8):
                y = y0 + i
                factor = [coef[d, x, y] for d in range(6)]
                keep = centre[int(c > 0), x, y]
                here = [columns[j][i + 1] for j in range(2)]
                new = [
                    keep * here[j]
                    + jnp.broadcast_to(mean_row[j, x, pl.ds(y, 1), :], (8, 128))
                    + factor[0] * p[old, 2 * c + j, x + 2, y + 1]
                    + factor[1] * p[old, 2 * c + j, x, y + 1]
                    + factor[2] * columns[j][i + 2]
                    + factor[3] * columns[j][i]
                    + factor[4] * pltpu.roll(here[j], 127, 1)
                    + factor[5] * pltpu.roll(here[j], 1, 1)
                    for j in range(2)
                ]
                if c == 0:
                    square = here[0] * here[0]
                    w = square / (1.0 + square) / (1.0 + jnp.exp(-3.0 * here[1]))
                    weights.append(w)
                    new[1] = new[1] - (STEP * RADIATION) * w
                else:
                    w = weight[x, y]
                    before = [p[old, 3, x + 1, y + 1] if c == 2 else None, here[0]]
                    for j in range(2):
                        gain = STEP * NUCLEATION[2 * c - 2 + j]
                        if before[j] is not None:
                            gain = gain + (STEP * GROWTH) * before[j]
                        new[j] = new[j] + w * gain
                for j in range(2):
                    s = 2 * c + j
                    if base_weight:
                        new[j] = base_weight * p[0, s, x + 1, y + 1] + section_weight * new[j]
                    tiles[j].append(new[j])
            for i, w in enumerate(weights):
                weight[x, y0 + i] = w
            for j in range(2):
                s = 2 * c + j
                for i in range(8):
                    if k < 3:
                        p[k, s, x + 1, y0 + i + 1] = tiles[j][i]
                    else:
                        flat[pl.ds(s * 64 + x * 16 + y0 + i, 8, stride=NS * 64), :] = tiles[j][i]
            if k < 3:
                for j in range(2):
                    s = 2 * c + j
                    row = (((k * NS + s) * 6 + x + 1) * 18 + y0 + 1) * 8
                    part[k, s, x, pl.ds(y0, 8), :] = add_up(
                        [flat_p[pl.ds(row + f, 8, stride=8), :] for f in range(8)]
                    )

        return body

    for k in range(1, 4):
        for c in range(PAIRS):
            mean_term(k - 1, c)
            arrived_y(k - 1, c)
            planes(1, 1, 2, advance(k, c))
            if k < 3:
                scatter(k, c, 1)
                scatter(k, c, 2)
            arrived_x(k - 1, c)
            if k == 1:
                for way in (EAST, WEST):
                    pl.when(has[back[way]])(lambda way=way: turn_face(c, way))
            planes(0, 3, 2, advance(k, c))
            if k < 3:
                scatter(k, c, 0)
                scatter(k, c, 3)
                send_y(k, c)
            if c == 0:
                pass_on(k - 1, PAIRS - 1)
                second_exchange(k - 1, PAIRS - 1)
            elif k < 3:
                pass_on(k, c - 1)
                second_exchange(k, c - 1)
            if k < 3:
                send_x(k, c)

    for way in (EAST, WEST, NORTH, SOUTH):
        pl.when(has[way])(lambda way=way: speed_face(way).wait_send())
        pl.when(has[way])(lambda way=way: all_sent(way))
    all_passed_on()
    wait_bytes(part_in, send_sem.at[SUM1])
    wait_bytes(part_in, send_sem.at[SUM2])


def local(fields_state, velocity, diffusivity, wiener_draw):
    counts = tuple(lax.axis_size(name) for name in ("gx", "gy", "af"))
    held = fields_state.shape
    dma = pltpu.SemaphoreType.DMA
    vmem = lambda *shape: pltpu.VMEM(shape, F32)
    held_in_hbm = (fields_state.reshape(8, NS, 64, 128), velocity, diffusivity, wiener_draw.T)
    out = pl.pallas_call(
        functools.partial(kernel, counts),
        out_shape=pltpu.VMEM((8, NS, 64, 128), F32),
        in_specs=[pl.BlockSpec(memory_space=pltpu.HBM)] * 4,
        out_specs=pl.BlockSpec(memory_space=pltpu.VMEM),
        scratch_shapes=[
            vmem(NS, 8, 64, 128),
            vmem(3, NS, 6, 18, 8, 128),
            vmem(6, 4, 16, 8, 128),
            vmem(2, 4, 16, 8, 128),
            vmem(4, 16, 8, 128),
            vmem(2, 4, 16, 128),
            vmem(3, NS, 4, 16, 128),
            vmem(3, PAIRS, 3, 2, 16, 128),
            vmem(3, NS, 4, 16, 128),
            vmem(6, 16, 128),
            vmem(4, 32, 128),
            vmem(4, 16, 128),
            vmem(4, 16, 128),
            vmem(3, 8),
            vmem(2, PAIRS, 1, 16, 8, 128),
            vmem(2, PAIRS, 8, 2, 16, 128),
            vmem(PAIRS, 8, 1, 16, 128),
            dma((NS,)),
            dma((5,)),
            dma,
            dma((3, PAIRS)),
            dma((4,)),
            dma((4,)),
            dma((6,)),
            dma((3, PAIRS, 6)),
        ],
        compiler_params=pltpu.CompilerParams(
            collective_id=0, has_side_effects=True, vmem_limit_bytes=48 * 1024 * 1024
        ),
    )(*(pltpu.with_memory_space_constraint(x, pltpu.HBM) for x in held_in_hbm))
    return out.reshape(held)


def solution(mesh):
    return jax.shard_map(
        local,
        mesh=mesh,
        in_specs=(
            P("af", None, "gx", "gy", None),
            P(None, "gx", "gy", None),
            P("gx", "gy", None),
            P("af", None),
        ),
        out_specs=P("af", None, "gx", "gy", None),
        check_vma=False,
    )
```

```python
import functools

import jax
import jax.numpy as jnp
from jax import lax
from jax.experimental import pallas as pl
from jax.experimental.pallas import tpu as pltpu
from jax.sharding import PartitionSpec as P

MESH = pl.DeviceIdType.MESH
F32 = jnp.float32

FIELDS = 32
NS = 6
PAIRS = 3
STEP = 0.3
MIX = 4.0
RADIATION = 0.5
NUCLEATION = (1.0, 0.8, 0.6, 0.5)
GROWTH = 0.5
OXIDATION = 0.3
WEIGHTS = ((0.0, 1.0), (0.75, 0.25), (1.0 / 3.0, 2.0 / 3.0))
EAST, WEST, NORTH, SOUTH, SUM1, SUM2 = range(6)


def sum_rows(tiles):
    row = lax.broadcasted_iota(jnp.int32, (8, 128), 0)
    low = row < 4
    quads = [
        jnp.where(low, tiles[i], tiles[i + 4])
        + pltpu.roll(jnp.where(low, tiles[i + 4], tiles[i]), 4, 0)
        for i in range(4)
    ]
    even = (row & 2) == 0
    pairs = [
        jnp.where(even, quads[i], quads[i + 2])
        + jnp.where(even, pltpu.roll(quads[i], 6, 0), pltpu.roll(quads[i + 2], 2, 0))
        for i in range(2)
    ]
    first = (row & 1) == 0
    return jnp.where(first, pairs[0], pairs[1]) + jnp.where(
        first, pltpu.roll(pairs[0], 7, 0), pltpu.roll(pairs[1], 1, 0)
    )


def spread(rows, i):
    return jnp.broadcast_to(rows[i : i + 1, :], (8, 128))


def kernel(
    counts,
    fields_hbm,
    velocity_hbm,
    diffusivity_hbm,
    wiener_hbm,
    out,
    rows_in,
    p,
    coef,
    centre,
    weight,
    mean_row,
    part,
    part_in,
    total,
    speed_x,
    speed_y,
    speed_z,
    diffusion,
    wiener,
    relay,
    raw,
    raw_relay,
    in_sem,
    own_sem,
    relay_send,
    relay_recv,
    speed_send,
    speed_recv,
    send_sem,
    recv_sem,
):
    nx, ny, na = counts
    ax, ix, iy = lax.axis_index("af"), lax.axis_index("gx"), lax.axis_index("gy")
    has = {EAST: ix < nx - 1, WEST: ix > 0, NORTH: iy < ny - 1, SOUTH: iy > 0}
    back = {EAST: WEST, WEST: EAST, NORTH: SOUTH, SOUTH: NORTH}
    target = {
        EAST: (ax, ix + 1, iy),
        WEST: (ax, ix - 1, iy),
        NORTH: (ax, ix, iy + 1),
        SOUTH: (ax, ix, iy - 1),
    }
    members = [lax.rem(ax + step, na) for step in range(na)]
    member_ids = [(other, ix, iy) for other in members]

    mid, end = nx // 2, nx - 1
    to_relay = {EAST: ix == mid - 1, WEST: ix == mid}
    is_relay = {EAST: ix == end, WEST: ix == 0}
    relay_of = {EAST: (ax, end, iy), WEST: (ax, 0, iy)}
    relay_to = {EAST: (ax, mid, iy), WEST: (ax, mid - 1, iy)}
    is_mid, is_end = to_relay[EAST] | to_relay[WEST], is_relay[EAST] | is_relay[WEST]
    both = {EAST: has[EAST] & has[WEST], NORTH: has[NORTH] & has[SOUTH]}
    plain = {way: has[way] & jnp.logical_not(to_relay[way]) for way in (EAST, WEST)}

    def load_in(s):
        return pltpu.make_async_copy(fields_hbm.at[:, s], rows_in.at[s], in_sem.at[s])

    def two(c):
        return pl.ds(2 * c, 2)

    own = [
        pltpu.make_async_copy(velocity_hbm.at[0], speed_x.at[pl.ds(1, 4)], own_sem.at[0]),
        pltpu.make_async_copy(velocity_hbm.at[1], speed_y.at[:, pl.ds(8, 16)], own_sem.at[1]),
        pltpu.make_async_copy(velocity_hbm.at[2], speed_z, own_sem.at[2]),
        pltpu.make_async_copy(diffusivity_hbm, diffusion, own_sem.at[3]),
        pltpu.make_async_copy(wiener_hbm, wiener, own_sem.at[4]),
    ]

    def speed_face(way):
        src, dst = {
            EAST: (velocity_hbm.at[0, 3], speed_x.at[0]),
            WEST: (velocity_hbm.at[0, 0], speed_x.at[5]),
            NORTH: (velocity_hbm.at[1, :, pl.ds(8, 8)], speed_y.at[:, pl.ds(0, 8)]),
            SOUTH: (velocity_hbm.at[1, :, pl.ds(0, 8)], speed_y.at[:, pl.ds(24, 8)]),
        }[way]
        return pltpu.make_async_remote_copy(
            src_ref=src,
            dst_ref=dst,
            send_sem=speed_send.at[way],
            recv_sem=speed_recv.at[way],
            device_id=target[way],
            device_id_type=MESH,
        )

    def face(k, s, way, recv=None):
        src, dst = {
            NORTH: lambda: (p.at[k, s, pl.ds(1, 4), 16], p.at[k, s, pl.ds(1, 4), 0]),
            SOUTH: lambda: (p.at[k, s, pl.ds(1, 4), 1], p.at[k, s, pl.ds(1, 4), 17]),
        }[way]()
        return pltpu.make_async_remote_copy(
            src_ref=src,
            dst_ref=dst,
            send_sem=send_sem.at[way],
            recv_sem=recv,
            device_id=target[way],
            device_id_type=MESH,
        )

    def chunk(k, c, way):
        return face(k, two(c), way, recv_sem.at[k, c, NORTH])

    def wait_bytes(ref, sem):
        pltpu.make_async_copy(ref, ref, sem).wait()

    def all_sent(way):
        if way in to_relay:
            wait_bytes(p.at[:, :, 1, pl.ds(1, 16)], send_sem.at[way])
        else:
            wait_bytes(p.at[:, :, pl.ds(1, 4), 1], send_sem.at[way])

    halves = [(s, y) for s in range(2) for y in (0, 8)]

    def x_face(k, c, way, s, y):
        src, dst = {EAST: (4, 0), WEST: (1, 5)}[way]
        which, rows = pl.ds(2 * c + s, 1), pl.ds(1 + y, 8)
        if k == 0:
            return (
                fields_hbm.at[:, which, pl.ds(16 * (src - 1) + y, 8)],
                raw.at[way, c, :, pl.ds(s, 1), pl.ds(y, 8)],
            )
        return p.at[k, which, src, rows], p.at[k, which, dst, rows]

    def copy_x(refs, way, recv, to):
        return pltpu.make_async_remote_copy(
            src_ref=refs[0],
            dst_ref=refs[1],
            send_sem=send_sem.at[way],
            recv_sem=recv,
            device_id=to,
            device_id_type=MESH,
        )

    def relay_at(k, c, y):
        return raw_relay.at[c, y // 8] if k == 0 else relay.at[k - 1, c, y // 8]

    def send_x(k, c):
        recv = recv_sem.at[k, c, EAST]
        for way in (EAST, WEST):

            @pl.when(plain[way])
            def _():
                for s, y in halves:
                    copy_x(x_face(k, c, way, s, y), way, recv, target[way]).start()

        @pl.when(is_mid)
        def _():
            for way in (EAST, WEST):

                @pl.when(to_relay[way])
                def _():
                    for y in (0, 8):
                        refs = (x_face(k, c, way, 1, y)[0], relay_at(k, c, y))
                        copy_x(refs, way, relay_recv.at[k, c], relay_of[way]).start()
                    for y in (0, 8):
                        copy_x(x_face(k, c, way, 0, y), way, recv, target[way]).start()

    def send_y(k, c):
        for way in (NORTH, SOUTH):
            pl.when(has[way])(lambda: chunk(k, c, way).start())

    def arrived_y(k, c):
        sem = recv_sem.at[k, c, NORTH]
        two_faces = p.at[k, two(c), pl.ds(1, 4), pl.ds(0, 2)]
        one_face = p.at[k, two(c), pl.ds(1, 4), pl.ds(0, 1)]
        pl.when(both[NORTH])(lambda: wait_bytes(two_faces, sem))
        pl.when(jnp.logical_not(both[NORTH]))(lambda: wait_bytes(one_face, sem))

    def arrived_x(k, c):
        sem = recv_sem.at[k, c, EAST]
        if k == 0:
            two_faces, one_face = raw.at[:, c], raw.at[0, c]
        else:
            two_faces = p.at[k, two(c), pl.ds(0, 2), pl.ds(1, 16)]
            one_face = p.at[k, two(c), pl.ds(0, 1), pl.ds(1, 16)]
        pl.when(both[EAST])(lambda: wait_bytes(two_faces, sem))
        pl.when(jnp.logical_not(both[EAST]))(lambda: wait_bytes(one_face, sem))

    def pass_on(k, c):
        @pl.when(is_end)
        def _():
            wait_bytes(raw_relay.at[c] if k == 0 else relay.at[k - 1, c], relay_recv.at[k, c])
            for way in (EAST, WEST):

                @pl.when(is_relay[way])
                def _():
                    for y in (0, 8):
                        pltpu.make_async_remote_copy(
                            src_ref=relay_at(k, c, y),
                            dst_ref=x_face(k, c, way, 1, y)[1],
                            send_sem=relay_send,
                            recv_sem=recv_sem.at[k, c, EAST],
                            device_id=relay_to[way],
                            device_id_type=MESH,
                        ).start()

    def all_passed_on():
        @pl.when(is_end)
        def _():
            wait_bytes(relay, relay_send)
            wait_bytes(raw_relay, relay_send)

    def planes(first, step, count, body):
        def at(i, _):
            for h in range(2):
                body(first + step * i, h)
            return 0

        lax.fori_loop(0, count, at, 0)

    load_in(0).start()
    for copy in own:
        copy.start()
    for s in range(1, NS):
        load_in(s).start()

    barrier = pltpu.get_barrier_semaphore()
    expected = na - 1
    for way in (EAST, WEST, NORTH, SOUTH):
        pl.when(has[way])(
            lambda way=way: pl.semaphore_signal(
                barrier, inc=1, device_id=target[way], device_id_type=MESH
            )
        )
        expected = expected + has[way].astype(jnp.int32)
    for way in (EAST, WEST):
        for near, partners in (
            (to_relay[way], ((ax, 0, iy), (ax, end, iy))),
            (is_relay[way], ((ax, mid - 1, iy), (ax, mid, iy))),
        ):
            expected = expected + 2 * near.astype(jnp.int32)

            @pl.when(near)
            def _(partners=partners):
                for partner in partners:
                    pl.semaphore_signal(barrier, inc=1, device_id=partner, device_id_type=MESH)

    for step in range(1, na):
        pl.semaphore_signal(
            barrier, inc=1, device_id=member_ids[step], device_id_type=MESH
        )

    zero = jnp.zeros((8, 128), F32)

    def clear_x(x, speed):
        def at(s, _):
            for k in range(3):
                for y in range(16):
                    p[k, s, x, 1 + y] = zero
            return 0

        lax.fori_loop(0, NS, at, 0)
        speed_x[speed] = jnp.zeros((16, 128), F32)

    def clear_y(y, speed):
        def at(s, _):
            for k in range(3):
                for x in range(4):
                    p[k, s, 1 + x, y] = zero
            return 0

        lax.fori_loop(0, NS, at, 0)
        for x in range(4):
            speed_y[x, speed : speed + 8] = zero

    pl.when(ix == 0)(lambda: clear_x(0, 0))
    pl.when(ix == nx - 1)(lambda: clear_x(5, 5))
    pl.when(iy == 0)(lambda: clear_y(0, 0))
    pl.when(iy == ny - 1)(lambda: clear_y(17, 24))

    pl.semaphore_wait(barrier, expected)
    send_x(0, 0)
    for way in (EAST, WEST, NORTH, SOUTH):
        pl.when(has[way])(lambda way=way: speed_face(way).start())
    for c in range(1, PAIRS):
        send_x(0, c)

    def scatter(k, c, owner):
        @pl.when(ax != owner)
        def _():
            pltpu.make_async_remote_copy(
                src_ref=part.at[k, two(c), owner],
                dst_ref=part_in.at[k, c, lax.rem(owner - ax + na, na) - 1],
                send_sem=send_sem.at[SUM1],
                recv_sem=recv_sem.at[k, c, SUM1],
                device_id=(owner, ix, iy),
                device_id_type=MESH,
            ).start()

    def second_exchange(k, c):
        wait_bytes(part_in.at[k, c], recv_sem.at[k, c, SUM1])
        for i in range(2):
            total[k, 2 * c + i, ax] = (part[k, 2 * c + i, ax] + part_in[k, c, 0, i]) + (
                part_in[k, c, 1, i] + part_in[k, c, 2, i]
            )
        mine = total.at[k, two(c), ax]
        for step in range(1, na):
            pltpu.make_async_remote_copy(
                src_ref=mine,
                dst_ref=mine,
                send_sem=send_sem.at[SUM2],
                recv_sem=recv_sem.at[k, c, SUM2],
                device_id=member_ids[step],
                device_id_type=MESH,
            ).start()

    def mean_term(k, c):
        wait_bytes(total.at[k, two(c), pl.ds(0, na - 1)], recv_sem.at[k, c, SUM2])
        scale = (STEP * MIX / FIELDS) * diffusion[...]
        for i in range(2):
            mean_row[i] = scale * total[k, 2 * c + i]

    def turn(s):
        flat = rows_in.reshape(NS * 8 * 64, 128)

        def body(x, h):
            start = s * 512 + x * 16 + h * 8
            tiles = [flat[pl.ds(start + i, 8, stride=64), :] for i in range(8)]
            for i in range(8):
                p[0, s, x + 1, h * 8 + i + 1] = tiles[i]
            part[0, s, x, pl.ds(h * 8, 8), :] = sum_rows(tiles)

        return body

    raw_rows = raw.reshape(2 * PAIRS * 8 * 32, 128)

    def turn_face(c, way):
        for j in range(2):
            start = (way * PAIRS + c) * 256 + j * 16
            for y in range(16):
                tile = raw_rows[pl.ds(start + y, 8, stride=32), :]
                p[0, 2 * c + j, 0 if way == EAST else 5, y + 1] = tile

    for c in range(PAIRS):
        for s in (2 * c, 2 * c + 1):
            load_in(s).wait()
            planes(0, 1, 4, turn(s))
        for owner in range(na):
            scatter(0, c, owner)
        send_y(0, c)
        if c > 0:
            pass_on(0, c - 1)
            second_exchange(0, c - 1)

    for copy in own:
        copy.wait()
    for way in (EAST, WEST, NORTH, SOUTH):
        pl.when(has[back[way]])(lambda way=way: speed_face(way).wait_recv())

    diagonal = lax.broadcasted_iota(jnp.int32, (8, 8), 0) == lax.broadcasted_iota(
        jnp.int32, (8, 8), 1
    )
    draws = []
    for d in range(3):
        row = jnp.broadcast_to(wiener[d : d + 1, :], (8, 8))
        draw = jnp.sum(jnp.where(diagonal, row, 0.0), axis=1, keepdims=True)
        draws.append(jnp.broadcast_to(draw, (8, 128)))

    def coefficients(x, _):
        g = diffusion[x]
        diffuse = STEP * g
        stir = (0.5 * STEP) * jnp.sqrt((2.0 / STEP) * g)
        lane = lax.broadcasted_iota(jnp.int32, (16, 128), 1)
        upper, lower = lane < 127, lane > 0
        half_step = 0.5 * STEP
        base = [
            diffuse - half_step * speed_x[x + 2],
            diffuse + half_step * speed_x[x],
            diffuse - half_step * speed_y[x, 9:25, :],
            diffuse + half_step * speed_y[x, 7:23, :],
            jnp.where(upper, diffuse - half_step * pltpu.roll(speed_z[x], 127, 1), 0.0),
            jnp.where(lower, diffuse + half_step * pltpu.roll(speed_z[x], 1, 1), 0.0),
        ]
        stir_up, stir_down = jnp.where(upper, stir, 0.0), jnp.where(lower, stir, 0.0)
        keep = 1.0 - (6.0 + MIX) * diffuse
        for y in range(16):
            stir_y = spread(stir, y)
            for d in range(2):
                move = stir_y * draws[d]
                coef[2 * d, x, y] = spread(base[2 * d], y) + move
                coef[2 * d + 1, x, y] = spread(base[2 * d + 1], y) - move
            coef[4, x, y] = spread(base[4], y) + spread(stir_up, y) * draws[2]
            coef[5, x, y] = spread(base[5], y) - spread(stir_down, y) * draws[2]
            keep_y = spread(keep, y)
            centre[0, x, y] = keep_y
            centre[1, x, y] = keep_y - STEP * OXIDATION
        return 0

    lax.fori_loop(0, 4, coefficients, 0)

    def advance(k, c):
        base_weight, section_weight = WEIGHTS[k - 1]
        old = k - 1
        flat = out.reshape(8 * NS * 64, 128)

        def body(x, h):
            y0 = h * 8
            tiles, weights = [[], []], []
            columns = [[p[old, 2 * c + j, x + 1, y0 + i] for i in range(10)] for j in range(2)]
            means = [mean_row[j, x, pl.ds(y0, 8), :] for j in range(2)]
            for i in range(8):
                y = y0 + i
                factor = [coef[d, x, y] for d in range(6)]
                keep = centre[int(c > 0), x, y]
                here = [columns[j][i + 1] for j in range(2)]
                new = [
                    keep * here[j]
                    + spread(means[j], i)
                    + factor[0] * p[old, 2 * c + j, x + 2, y + 1]
                    + factor[1] * p[old, 2 * c + j, x, y + 1]
                    + factor[2] * columns[j][i + 2]
                    + factor[3] * columns[j][i]
                    + factor[4] * pltpu.roll(here[j], 127, 1)
                    + factor[5] * pltpu.roll(here[j], 1, 1)
                    for j in range(2)
                ]
                if c == 0:
                    square = here[0] * here[0]
                    w = square / (1.0 + square) / (1.0 + jnp.exp(-3.0 * here[1]))
                    weights.append(w)
                    new[1] = new[1] - (STEP * RADIATION) * w
                else:
                    w = weight[x, y]
                    before = [p[old, 3, x + 1, y + 1] if c == 2 else None, here[0]]
                    for j in range(2):
                        gain = STEP * NUCLEATION[2 * c - 2 + j]
                        if before[j] is not None:
                            gain = gain + (STEP * GROWTH) * before[j]
                        new[j] = new[j] + w * gain
                for j in range(2):
                    s = 2 * c + j
                    if base_weight:
                        new[j] = base_weight * p[0, s, x + 1, y + 1] + section_weight * new[j]
                    tiles[j].append(new[j])
            for i, w in enumerate(weights):
                weight[x, y0 + i] = w
            for j in range(2):
                s = 2 * c + j
                for i in range(8):
                    if k < 3:
                        p[k, s, x + 1, y0 + i + 1] = tiles[j][i]
                    else:
                        flat[pl.ds(s * 64 + x * 16 + y0 + i, 8, stride=NS * 64), :] = tiles[j][i]
            if k < 3:
                for j in range(2):
                    part[k, 2 * c + j, x, pl.ds(y0, 8), :] = sum_rows(tiles[j])

        return body

    for k in range(1, 4):
        for c in range(PAIRS):
            mean_term(k - 1, c)
            arrived_y(k - 1, c)
            planes(1, 1, 2, advance(k, c))
            if k < 3:
                scatter(k, c, 1)
                scatter(k, c, 2)
            arrived_x(k - 1, c)
            if k == 1:
                for way in (EAST, WEST):
                    pl.when(has[back[way]])(lambda way=way: turn_face(c, way))
            planes(0, 3, 2, advance(k, c))
            if k < 3:
                send_x(k, c)
                scatter(k, c, 0)
                scatter(k, c, 3)
                send_y(k, c)
            if c == 0:
                pass_on(k - 1, PAIRS - 1)
                second_exchange(k - 1, PAIRS - 1)
            elif k < 3:
                pass_on(k, c - 1)
                second_exchange(k, c - 1)

    for way in (EAST, WEST, NORTH, SOUTH):
        pl.when(has[way])(lambda way=way: speed_face(way).wait_send())
        pl.when(has[way])(lambda way=way: all_sent(way))
    all_passed_on()
    wait_bytes(part_in, send_sem.at[SUM1])
    wait_bytes(part_in, send_sem.at[SUM2])


def local(fields_state, velocity, diffusivity, wiener_draw):
    counts = tuple(lax.axis_size(name) for name in ("gx", "gy", "af"))
    held = fields_state.shape
    dma = pltpu.SemaphoreType.DMA
    vmem = lambda *shape: pltpu.VMEM(shape, F32)
    held_in_hbm = (fields_state.reshape(8, NS, 64, 128), velocity, diffusivity, wiener_draw.T)
    out = pl.pallas_call(
        functools.partial(kernel, counts),
        out_shape=pltpu.VMEM((8, NS, 64, 128), F32),
        in_specs=[pl.BlockSpec(memory_space=pltpu.HBM)] * 4,
        out_specs=pl.BlockSpec(memory_space=pltpu.VMEM),
        scratch_shapes=[
            vmem(NS, 8, 64, 128),
            vmem(3, NS, 6, 18, 8, 128),
            vmem(6, 4, 16, 8, 128),
            vmem(2, 4, 16, 8, 128),
            vmem(4, 16, 8, 128),
            vmem(2, 4, 16, 128),
            vmem(3, NS, 4, 16, 128),
            vmem(3, PAIRS, 3, 2, 16, 128),
            vmem(3, NS, 4, 16, 128),
            vmem(6, 16, 128),
            vmem(4, 32, 128),
            vmem(4, 16, 128),
            vmem(4, 16, 128),
            vmem(3, 8),
            vmem(2, PAIRS, 2, 1, 8, 8, 128),
            vmem(2, PAIRS, 8, 2, 16, 128),
            vmem(PAIRS, 2, 8, 1, 8, 128),
            dma((NS,)),
            dma((5,)),
            dma,
            dma((3, PAIRS)),
            dma((4,)),
            dma((4,)),
            dma((6,)),
            dma((3, PAIRS, 6)),
        ],
        compiler_params=pltpu.CompilerParams(
            collective_id=0, has_side_effects=True, vmem_limit_bytes=48 * 1024 * 1024
        ),
    )(*(pltpu.with_memory_space_constraint(x, pltpu.HBM) for x in held_in_hbm))
    return out.reshape(held)


def solution(mesh):
    return jax.shard_map(
        local,
        mesh=mesh,
        in_specs=(
            P("af", None, "gx", "gy", None),
            P(None, "gx", "gy", None),
            P("gx", "gy", None),
            P("af", None),
        ),
        out_specs=P("af", None, "gx", "gy", None),
        check_vma=False,
    )
```

```python
import functools

import jax
import jax.numpy as jnp
from jax import lax
from jax.experimental import pallas as pl
from jax.experimental.pallas import tpu as pltpu
from jax.sharding import PartitionSpec as P

MESH = pl.DeviceIdType.MESH
F32 = jnp.float32

FIELDS = 32
NS = 6
PAIRS = 3
STEP = 0.3
MIX = 4.0
RADIATION = 0.5
NUCLEATION = (1.0, 0.8, 0.6, 0.5)
GROWTH = 0.5
OXIDATION = 0.3
WEIGHTS = ((0.0, 1.0), (0.75, 0.25), (1.0 / 3.0, 2.0 / 3.0))
EAST, WEST, NORTH, SOUTH, SUM1, SUM2 = range(6)


def sum_rows(tiles):
    row = lax.broadcasted_iota(jnp.int32, (8, 128), 0)
    low = row < 4
    quads = [
        jnp.where(low, tiles[i], tiles[i + 4])
        + pltpu.roll(jnp.where(low, tiles[i + 4], tiles[i]), 4, 0)
        for i in range(4)
    ]
    even = (row & 2) == 0
    pairs = [
        jnp.where(even, quads[i], quads[i + 2])
        + jnp.where(even, pltpu.roll(quads[i], 6, 0), pltpu.roll(quads[i + 2], 2, 0))
        for i in range(2)
    ]
    first = (row & 1) == 0
    return jnp.where(first, pairs[0], pairs[1]) + jnp.where(
        first, pltpu.roll(pairs[0], 7, 0), pltpu.roll(pairs[1], 1, 0)
    )


def spread(rows, i):
    return jnp.broadcast_to(rows[i : i + 1, :], (8, 128))


def kernel(
    counts,
    fields_hbm,
    velocity_hbm,
    diffusivity_hbm,
    wiener_hbm,
    out,
    rows_in,
    p,
    coef,
    centre,
    weight,
    mean_row,
    part,
    part_in,
    total,
    speed_x,
    speed_y,
    speed_z,
    diffusion,
    wiener,
    relay,
    raw,
    raw_relay,
    in_sem,
    own_sem,
    relay_send,
    relay_recv,
    speed_send,
    speed_recv,
    send_sem,
    recv_sem,
):
    nx, ny, na = counts
    ax, ix, iy = lax.axis_index("af"), lax.axis_index("gx"), lax.axis_index("gy")
    has = {EAST: ix < nx - 1, WEST: ix > 0, NORTH: iy < ny - 1, SOUTH: iy > 0}
    back = {EAST: WEST, WEST: EAST, NORTH: SOUTH, SOUTH: NORTH}
    target = {
        EAST: (ax, ix + 1, iy),
        WEST: (ax, ix - 1, iy),
        NORTH: (ax, ix, iy + 1),
        SOUTH: (ax, ix, iy - 1),
    }
    members = [lax.rem(ax + step, na) for step in range(na)]
    member_ids = [(other, ix, iy) for other in members]

    mid, end = nx // 2, nx - 1
    to_relay = {EAST: ix == mid - 1, WEST: ix == mid}
    is_relay = {EAST: ix == end, WEST: ix == 0}
    relay_of = {EAST: (ax, end, iy), WEST: (ax, 0, iy)}
    relay_to = {EAST: (ax, mid, iy), WEST: (ax, mid - 1, iy)}
    is_mid, is_end = to_relay[EAST] | to_relay[WEST], is_relay[EAST] | is_relay[WEST]
    both = {EAST: has[EAST] & has[WEST], NORTH: has[NORTH] & has[SOUTH]}
    plain = {way: has[way] & jnp.logical_not(to_relay[way]) for way in (EAST, WEST)}

    def load_in(s):
        return pltpu.make_async_copy(fields_hbm.at[:, s], rows_in.at[s], in_sem.at[s])

    def two(c):
        return pl.ds(2 * c, 2)

    own = [
        pltpu.make_async_copy(velocity_hbm.at[0], speed_x.at[pl.ds(1, 4)], own_sem.at[0]),
        pltpu.make_async_copy(velocity_hbm.at[1], speed_y.at[:, pl.ds(8, 16)], own_sem.at[1]),
        pltpu.make_async_copy(velocity_hbm.at[2], speed_z, own_sem.at[2]),
        pltpu.make_async_copy(diffusivity_hbm, diffusion, own_sem.at[3]),
        pltpu.make_async_copy(wiener_hbm, wiener, own_sem.at[4]),
    ]

    def speed_face(way):
        src, dst = {
            EAST: (velocity_hbm.at[0, 3], speed_x.at[0]),
            WEST: (velocity_hbm.at[0, 0], speed_x.at[5]),
            NORTH: (velocity_hbm.at[1, :, pl.ds(8, 8)], speed_y.at[:, pl.ds(0, 8)]),
            SOUTH: (velocity_hbm.at[1, :, pl.ds(0, 8)], speed_y.at[:, pl.ds(24, 8)]),
        }[way]
        return pltpu.make_async_remote_copy(
            src_ref=src,
            dst_ref=dst,
            send_sem=speed_send.at[way],
            recv_sem=speed_recv.at[way],
            device_id=target[way],
            device_id_type=MESH,
        )

    def face(k, s, way, recv=None):
        src, dst = {
            NORTH: lambda: (p.at[k, s, pl.ds(1, 4), 16], p.at[k, s, pl.ds(1, 4), 0]),
            SOUTH: lambda: (p.at[k, s, pl.ds(1, 4), 1], p.at[k, s, pl.ds(1, 4), 17]),
        }[way]()
        return pltpu.make_async_remote_copy(
            src_ref=src,
            dst_ref=dst,
            send_sem=send_sem.at[way],
            recv_sem=recv,
            device_id=target[way],
            device_id_type=MESH,
        )

    def chunk(k, c, way):
        return face(k, two(c), way, recv_sem.at[k, c, NORTH])

    def wait_bytes(ref, sem):
        pltpu.make_async_copy(ref, ref, sem).wait()

    def all_sent(way):
        if way in to_relay:
            wait_bytes(p.at[:, :, 1, pl.ds(1, 16)], send_sem.at[way])
        else:
            wait_bytes(p.at[:, :, pl.ds(1, 4), 1], send_sem.at[way])

    def x_face(k, c, way, s=None):
        src, dst = {EAST: (4, 0), WEST: (1, 5)}[way]
        side = way
        which = pl.ds(2 * c, 2) if s is None else pl.ds(2 * c + s, 1)
        to = pl.ds(0, 2) if s is None else pl.ds(s, 1)
        if k == 0:
            refs = fields_hbm.at[:, which, pl.ds(16 * (src - 1), 16)], raw.at[side, c, :, to]
        else:
            refs = p.at[k, which, src, pl.ds(1, 16)], p.at[k, which, dst, pl.ds(1, 16)]
        return refs

    def copy_x(refs, way, recv, to):
        return pltpu.make_async_remote_copy(
            src_ref=refs[0],
            dst_ref=refs[1],
            send_sem=send_sem.at[way],
            recv_sem=recv,
            device_id=to,
            device_id_type=MESH,
        )

    def relay_at(k, c):
        return raw_relay.at[c] if k == 0 else relay.at[k - 1, c]

    def send_x(k, c):
        recv = recv_sem.at[k, c, EAST]
        for way in (EAST, WEST):

            @pl.when(plain[way])
            def _():
                copy_x(x_face(k, c, way), way, recv, target[way]).start()

        @pl.when(is_mid)
        def _():
            for way in (EAST, WEST):

                @pl.when(to_relay[way])
                def _():
                    src = x_face(k, c, way, 1)[0]
                    copy_x(
                        (src, relay_at(k, c)), way, relay_recv.at[k, c], relay_of[way]
                    ).start()
                    copy_x(x_face(k, c, way, 0), way, recv, target[way]).start()

    def send_y(k, c):
        for way in (NORTH, SOUTH):
            pl.when(has[way])(lambda: chunk(k, c, way).start())

    def arrived_y(k, c):
        sem = recv_sem.at[k, c, NORTH]
        two_faces = p.at[k, two(c), pl.ds(1, 4), pl.ds(0, 2)]
        one_face = p.at[k, two(c), pl.ds(1, 4), pl.ds(0, 1)]
        pl.when(both[NORTH])(lambda: wait_bytes(two_faces, sem))
        pl.when(jnp.logical_not(both[NORTH]))(lambda: wait_bytes(one_face, sem))

    def arrived_x(k, c):
        sem = recv_sem.at[k, c, EAST]
        if k == 0:
            two_faces, one_face = raw.at[:, c], raw.at[0, c]
        else:
            two_faces = p.at[k, two(c), pl.ds(0, 2), pl.ds(1, 16)]
            one_face = p.at[k, two(c), pl.ds(0, 1), pl.ds(1, 16)]
        pl.when(both[EAST])(lambda: wait_bytes(two_faces, sem))
        pl.when(jnp.logical_not(both[EAST]))(lambda: wait_bytes(one_face, sem))

    def pass_on(n, way):
        if not 0 <= n < 3 * PAIRS:
            return
        k, c = divmod(n, PAIRS)

        @pl.when(is_relay[way])
        def _():
            here = relay_at(k, c)
            wait_bytes(here, relay_recv.at[k, c])
            pltpu.make_async_remote_copy(
                src_ref=here,
                dst_ref=x_face(k, c, way, 1)[1],
                send_sem=relay_send,
                recv_sem=recv_sem.at[k, c, EAST],
                device_id=relay_to[way],
                device_id_type=MESH,
            ).start()

    def all_passed_on():
        @pl.when(is_end)
        def _():
            wait_bytes(relay, relay_send)
            wait_bytes(raw_relay, relay_send)

    def planes(first, step, count, body):
        def at(i, _):
            for h in range(2):
                body(first + step * i, h)
            return 0

        lax.fori_loop(0, count, at, 0)

    load_in(0).start()
    for copy in own:
        copy.start()
    for s in range(1, NS):
        load_in(s).start()

    barrier = pltpu.get_barrier_semaphore()
    expected = na - 1
    for way in (EAST, WEST, NORTH, SOUTH):
        pl.when(has[way])(
            lambda way=way: pl.semaphore_signal(
                barrier, inc=1, device_id=target[way], device_id_type=MESH
            )
        )
        expected = expected + has[way].astype(jnp.int32)
    for way in (EAST, WEST):
        for near, partners in (
            (to_relay[way], ((ax, 0, iy), (ax, end, iy))),
            (is_relay[way], ((ax, mid - 1, iy), (ax, mid, iy))),
        ):
            expected = expected + 2 * near.astype(jnp.int32)

            @pl.when(near)
            def _(partners=partners):
                for partner in partners:
                    pl.semaphore_signal(barrier, inc=1, device_id=partner, device_id_type=MESH)

    for step in range(1, na):
        pl.semaphore_signal(
            barrier, inc=1, device_id=member_ids[step], device_id_type=MESH
        )

    zero = jnp.zeros((8, 128), F32)

    def clear_x(x, speed):
        def at(s, _):
            for k in range(3):
                for y in range(16):
                    p[k, s, x, 1 + y] = zero
            return 0

        lax.fori_loop(0, NS, at, 0)
        speed_x[speed] = jnp.zeros((16, 128), F32)

    def clear_y(y, speed):
        def at(s, _):
            for k in range(3):
                for x in range(4):
                    p[k, s, 1 + x, y] = zero
            return 0

        lax.fori_loop(0, NS, at, 0)
        for x in range(4):
            speed_y[x, speed : speed + 8] = zero

    pl.when(ix == 0)(lambda: clear_x(0, 0))
    pl.when(ix == nx - 1)(lambda: clear_x(5, 5))
    pl.when(iy == 0)(lambda: clear_y(0, 0))
    pl.when(iy == ny - 1)(lambda: clear_y(17, 24))

    pl.semaphore_wait(barrier, expected)
    send_x(0, 0)
    for way in (EAST, WEST, NORTH, SOUTH):
        pl.when(has[way])(lambda way=way: speed_face(way).start())
    for c in range(1, PAIRS):
        send_x(0, c)

    def scatter(k, c, owner):
        @pl.when(ax != owner)
        def _():
            pltpu.make_async_remote_copy(
                src_ref=part.at[k, two(c), owner],
                dst_ref=part_in.at[k, c, lax.rem(owner - ax + na, na) - 1],
                send_sem=send_sem.at[SUM1],
                recv_sem=recv_sem.at[k, c, SUM1],
                device_id=(owner, ix, iy),
                device_id_type=MESH,
            ).start()

    def second_exchange(k, c):
        wait_bytes(part_in.at[k, c], recv_sem.at[k, c, SUM1])
        for i in range(2):
            total[k, 2 * c + i, ax] = (part[k, 2 * c + i, ax] + part_in[k, c, 0, i]) + (
                part_in[k, c, 1, i] + part_in[k, c, 2, i]
            )
        mine = total.at[k, two(c), ax]
        for step in range(1, na):
            pltpu.make_async_remote_copy(
                src_ref=mine,
                dst_ref=mine,
                send_sem=send_sem.at[SUM2],
                recv_sem=recv_sem.at[k, c, SUM2],
                device_id=member_ids[step],
                device_id_type=MESH,
            ).start()

    def mean_term(k, c):
        wait_bytes(total.at[k, two(c), pl.ds(0, na - 1)], recv_sem.at[k, c, SUM2])
        scale = (STEP * MIX / FIELDS) * diffusion[...]
        for i in range(2):
            mean_row[i] = scale * total[k, 2 * c + i]

    def turn(s):
        flat = rows_in.reshape(NS * 8 * 64, 128)

        def body(x, h):
            start = s * 512 + x * 16 + h * 8
            tiles = [flat[pl.ds(start + i, 8, stride=64), :] for i in range(8)]
            for i in range(8):
                p[0, s, x + 1, h * 8 + i + 1] = tiles[i]
            part[0, s, x, pl.ds(h * 8, 8), :] = sum_rows(tiles)

        return body

    raw_rows = raw.reshape(2 * PAIRS * 8 * 32, 128)

    def turn_face(c, way):
        for j in range(2):
            start = (way * PAIRS + c) * 256 + j * 16
            for y in range(16):
                tile = raw_rows[pl.ds(start + y, 8, stride=32), :]
                p[0, 2 * c + j, 0 if way == EAST else 5, y + 1] = tile

    for c in range(PAIRS):
        for s in (2 * c, 2 * c + 1):
            load_in(s).wait()
            planes(0, 1, 4, turn(s))
        for owner in range(na):
            scatter(0, c, owner)
        send_y(0, c)
        pass_on(c - 1, EAST)
        pass_on(c - 2, WEST)
        if c > 0:
            second_exchange(0, c - 1)

    for copy in own:
        copy.wait()
    for way in (EAST, WEST, NORTH, SOUTH):
        pl.when(has[back[way]])(lambda way=way: speed_face(way).wait_recv())

    diagonal = lax.broadcasted_iota(jnp.int32, (8, 8), 0) == lax.broadcasted_iota(
        jnp.int32, (8, 8), 1
    )
    draws = []
    for d in range(3):
        row = jnp.broadcast_to(wiener[d : d + 1, :], (8, 8))
        draw = jnp.sum(jnp.where(diagonal, row, 0.0), axis=1, keepdims=True)
        draws.append(jnp.broadcast_to(draw, (8, 128)))

    def coefficients(x, _):
        g = diffusion[x]
        diffuse = STEP * g
        stir = (0.5 * STEP) * jnp.sqrt((2.0 / STEP) * g)
        lane = lax.broadcasted_iota(jnp.int32, (16, 128), 1)
        upper, lower = lane < 127, lane > 0
        half_step = 0.5 * STEP
        base = [
            diffuse - half_step * speed_x[x + 2],
            diffuse + half_step * speed_x[x],
            diffuse - half_step * speed_y[x, 9:25, :],
            diffuse + half_step * speed_y[x, 7:23, :],
            jnp.where(upper, diffuse - half_step * pltpu.roll(speed_z[x], 127, 1), 0.0),
            jnp.where(lower, diffuse + half_step * pltpu.roll(speed_z[x], 1, 1), 0.0),
        ]
        stir_up, stir_down = jnp.where(upper, stir, 0.0), jnp.where(lower, stir, 0.0)
        keep = 1.0 - (6.0 + MIX) * diffuse
        for y in range(16):
            stir_y = spread(stir, y)
            for d in range(2):
                move = stir_y * draws[d]
                coef[2 * d, x, y] = spread(base[2 * d], y) + move
                coef[2 * d + 1, x, y] = spread(base[2 * d + 1], y) - move
            coef[4, x, y] = spread(base[4], y) + spread(stir_up, y) * draws[2]
            coef[5, x, y] = spread(base[5], y) - spread(stir_down, y) * draws[2]
            keep_y = spread(keep, y)
            centre[0, x, y] = keep_y
            centre[1, x, y] = keep_y - STEP * OXIDATION
        return 0

    lax.fori_loop(0, 4, coefficients, 0)

    def advance(k, c):
        base_weight, section_weight = WEIGHTS[k - 1]
        old = k - 1
        flat = out.reshape(8 * NS * 64, 128)

        def body(x, h):
            y0 = h * 8
            tiles, weights = [[], []], []
            columns = [[p[old, 2 * c + j, x + 1, y0 + i] for i in range(10)] for j in range(2)]
            means = [mean_row[j, x, pl.ds(y0, 8), :] for j in range(2)]
            for i in range(8):
                y = y0 + i
                factor = [coef[d, x, y] for d in range(6)]
                keep = centre[int(c > 0), x, y]
                here = [columns[j][i + 1] for j in range(2)]
                new = [
                    keep * here[j]
                    + spread(means[j], i)
                    + factor[0] * p[old, 2 * c + j, x + 2, y + 1]
                    + factor[1] * p[old, 2 * c + j, x, y + 1]
                    + factor[2] * columns[j][i + 2]
                    + factor[3] * columns[j][i]
                    + factor[4] * pltpu.roll(here[j], 127, 1)
                    + factor[5] * pltpu.roll(here[j], 1, 1)
                    for j in range(2)
                ]
                if c == 0:
                    square = here[0] * here[0]
                    w = square / (1.0 + square) / (1.0 + jnp.exp(-3.0 * here[1]))
                    weights.append(w)
                    new[1] = new[1] - (STEP * RADIATION) * w
                else:
                    w = weight[x, y]
                    before = [p[old, 3, x + 1, y + 1] if c == 2 else None, here[0]]
                    for j in range(2):
                        gain = STEP * NUCLEATION[2 * c - 2 + j]
                        if before[j] is not None:
                            gain = gain + (STEP * GROWTH) * before[j]
                        new[j] = new[j] + w * gain
                for j in range(2):
                    s = 2 * c + j
                    if base_weight:
                        new[j] = base_weight * p[0, s, x + 1, y + 1] + section_weight * new[j]
                    tiles[j].append(new[j])
            for i, w in enumerate(weights):
                weight[x, y0 + i] = w
            for j in range(2):
                s = 2 * c + j
                for i in range(8):
                    if k < 3:
                        p[k, s, x + 1, y0 + i + 1] = tiles[j][i]
                    else:
                        flat[pl.ds(s * 64 + x * 16 + y0 + i, 8, stride=NS * 64), :] = tiles[j][i]
            if k < 3:
                for j in range(2):
                    part[k, 2 * c + j, x, pl.ds(y0, 8), :] = sum_rows(tiles[j])

        return body

    for k in range(1, 4):
        for c in range(PAIRS):
            mean_term(k - 1, c)
            arrived_y(k - 1, c)
            planes(1, 1, 2, advance(k, c))
            if k < 3:
                scatter(k, c, 1)
                scatter(k, c, 2)
            arrived_x(k - 1, c)
            pass_on(3 * k + c - 1, EAST)
            if k == 1:
                for way in (EAST, WEST):
                    pl.when(has[back[way]])(lambda way=way: turn_face(c, way))
            planes(0, 3, 2, advance(k, c))
            if k < 3:
                send_x(k, c)
                scatter(k, c, 0)
                scatter(k, c, 3)
                send_y(k, c)
            pass_on(3 * k + c - 2, WEST)
            if c == 0:
                second_exchange(k - 1, PAIRS - 1)
            elif k < 3:
                second_exchange(k, c - 1)

    for way in (EAST, WEST, NORTH, SOUTH):
        pl.when(has[way])(lambda way=way: speed_face(way).wait_send())
        pl.when(has[way])(lambda way=way: all_sent(way))
    all_passed_on()
    wait_bytes(part_in, send_sem.at[SUM1])
    wait_bytes(part_in, send_sem.at[SUM2])


def local(fields_state, velocity, diffusivity, wiener_draw):
    counts = tuple(lax.axis_size(name) for name in ("gx", "gy", "af"))
    held = fields_state.shape
    dma = pltpu.SemaphoreType.DMA
    vmem = lambda *shape: pltpu.VMEM(shape, F32)
    held_in_hbm = (fields_state.reshape(8, NS, 64, 128), velocity, diffusivity, wiener_draw.T)
    out = pl.pallas_call(
        functools.partial(kernel, counts),
        out_shape=pltpu.VMEM((8, NS, 64, 128), F32),
        in_specs=[pl.BlockSpec(memory_space=pltpu.HBM)] * 4,
        out_specs=pl.BlockSpec(memory_space=pltpu.VMEM),
        scratch_shapes=[
            vmem(NS, 8, 64, 128),
            vmem(3, NS, 6, 18, 8, 128),
            vmem(6, 4, 16, 8, 128),
            vmem(2, 4, 16, 8, 128),
            vmem(4, 16, 8, 128),
            vmem(2, 4, 16, 128),
            vmem(3, NS, 4, 16, 128),
            vmem(3, PAIRS, 3, 2, 16, 128),
            vmem(3, NS, 4, 16, 128),
            vmem(6, 16, 128),
            vmem(4, 32, 128),
            vmem(4, 16, 128),
            vmem(4, 16, 128),
            vmem(3, 8),
            vmem(2, PAIRS, 1, 16, 8, 128),
            vmem(2, PAIRS, 8, 2, 16, 128),
            vmem(PAIRS, 8, 1, 16, 128),
            dma((NS,)),
            dma((5,)),
            dma,
            dma((3, PAIRS)),
            dma((4,)),
            dma((4,)),
            dma((6,)),
            dma((3, PAIRS, 6)),
        ],
        compiler_params=pltpu.CompilerParams(
            collective_id=0, has_side_effects=True, vmem_limit_bytes=48 * 1024 * 1024
        ),
    )(*(pltpu.with_memory_space_constraint(x, pltpu.HBM) for x in held_in_hbm))
    return out.reshape(held)


def solution(mesh):
    return jax.shard_map(
        local,
        mesh=mesh,
        in_specs=(
            P("af", None, "gx", "gy", None),
            P(None, "gx", "gy", None),
            P("gx", "gy", None),
            P("af", None),
        ),
        out_specs=P("af", None, "gx", "gy", None),
        check_vma=False,
    )
```

```python
import functools

import jax
import jax.numpy as jnp
from jax import lax
from jax.experimental import pallas as pl
from jax.experimental.pallas import tpu as pltpu
from jax.sharding import PartitionSpec as P

MESH = pl.DeviceIdType.MESH
F32 = jnp.float32

FIELDS = 32
NS = 6
PAIRS = 3
SPLIT = 7
STEP = 0.3
MIX = 4.0
RADIATION = 0.5
NUCLEATION = (1.0, 0.8, 0.6, 0.5)
GROWTH = 0.5
OXIDATION = 0.3
WEIGHTS = ((0.0, 1.0), (0.75, 0.25), (1.0 / 3.0, 2.0 / 3.0))
EAST, WEST, NORTH, SOUTH, SUM1, SUM2 = range(6)


def sum_rows(tiles):
    row = lax.broadcasted_iota(jnp.int32, (8, 128), 0)
    low = row < 4
    quads = [
        jnp.where(low, tiles[i], tiles[i + 4])
        + pltpu.roll(jnp.where(low, tiles[i + 4], tiles[i]), 4, 0)
        for i in range(4)
    ]
    even = (row & 2) == 0
    pairs = [
        jnp.where(even, quads[i], quads[i + 2])
        + jnp.where(even, pltpu.roll(quads[i], 6, 0), pltpu.roll(quads[i + 2], 2, 0))
        for i in range(2)
    ]
    first = (row & 1) == 0
    return jnp.where(first, pairs[0], pairs[1]) + jnp.where(
        first, pltpu.roll(pairs[0], 7, 0), pltpu.roll(pairs[1], 1, 0)
    )


def spread(rows, i):
    return jnp.broadcast_to(rows[i : i + 1, :], (8, 128))


def kernel(
    counts,
    fields_hbm,
    velocity_hbm,
    diffusivity_hbm,
    wiener_hbm,
    out,
    rows_in,
    p,
    coef,
    centre,
    weight,
    mean_row,
    part,
    part_in,
    total,
    speed_x,
    speed_y,
    speed_z,
    diffusion,
    wiener,
    relay,
    raw,
    raw_relay,
    in_sem,
    own_sem,
    relay_send,
    relay_recv,
    speed_send,
    speed_recv,
    send_sem,
    recv_sem,
):
    nx, ny, na = counts
    ax, ix, iy = lax.axis_index("af"), lax.axis_index("gx"), lax.axis_index("gy")
    has = {EAST: ix < nx - 1, WEST: ix > 0, NORTH: iy < ny - 1, SOUTH: iy > 0}
    back = {EAST: WEST, WEST: EAST, NORTH: SOUTH, SOUTH: NORTH}
    target = {
        EAST: (ax, ix + 1, iy),
        WEST: (ax, ix - 1, iy),
        NORTH: (ax, ix, iy + 1),
        SOUTH: (ax, ix, iy - 1),
    }
    members = [lax.rem(ax + step, na) for step in range(na)]
    member_ids = [(other, ix, iy) for other in members]

    mid, end = nx // 2, nx - 1
    to_relay = {EAST: ix == mid - 1, WEST: ix == mid}
    is_relay = {EAST: ix == end, WEST: ix == 0}
    relay_of = {EAST: (ax, end, iy), WEST: (ax, 0, iy)}
    relay_to = {EAST: (ax, mid, iy), WEST: (ax, mid - 1, iy)}
    is_mid, is_end = to_relay[EAST] | to_relay[WEST], is_relay[EAST] | is_relay[WEST]
    both = {EAST: has[EAST] & has[WEST], NORTH: has[NORTH] & has[SOUTH]}
    plain = {way: has[way] & jnp.logical_not(to_relay[way]) for way in (EAST, WEST)}

    def load_in(s):
        return pltpu.make_async_copy(fields_hbm.at[:, s], rows_in.at[s], in_sem.at[s])

    def two(c):
        return pl.ds(2 * c, 2)

    own = [
        pltpu.make_async_copy(velocity_hbm.at[0], speed_x.at[pl.ds(1, 4)], own_sem.at[0]),
        pltpu.make_async_copy(velocity_hbm.at[1], speed_y.at[:, pl.ds(8, 16)], own_sem.at[1]),
        pltpu.make_async_copy(velocity_hbm.at[2], speed_z, own_sem.at[2]),
        pltpu.make_async_copy(diffusivity_hbm, diffusion, own_sem.at[3]),
        pltpu.make_async_copy(wiener_hbm, wiener, own_sem.at[4]),
    ]

    def speed_face(way):
        src, dst = {
            EAST: (velocity_hbm.at[0, 3], speed_x.at[0]),
            WEST: (velocity_hbm.at[0, 0], speed_x.at[5]),
            NORTH: (velocity_hbm.at[1, :, pl.ds(8, 8)], speed_y.at[:, pl.ds(0, 8)]),
            SOUTH: (velocity_hbm.at[1, :, pl.ds(0, 8)], speed_y.at[:, pl.ds(24, 8)]),
        }[way]
        return pltpu.make_async_remote_copy(
            src_ref=src,
            dst_ref=dst,
            send_sem=speed_send.at[way],
            recv_sem=speed_recv.at[way],
            device_id=target[way],
            device_id_type=MESH,
        )

    def face(k, s, way, recv=None):
        src, dst = {
            NORTH: lambda: (p.at[k, s, pl.ds(1, 4), 16], p.at[k, s, pl.ds(1, 4), 0]),
            SOUTH: lambda: (p.at[k, s, pl.ds(1, 4), 1], p.at[k, s, pl.ds(1, 4), 17]),
        }[way]()
        return pltpu.make_async_remote_copy(
            src_ref=src,
            dst_ref=dst,
            send_sem=send_sem.at[way],
            recv_sem=recv,
            device_id=target[way],
            device_id_type=MESH,
        )

    def chunk(k, c, way):
        return face(k, two(c), way, recv_sem.at[k, c, NORTH])

    def wait_bytes(ref, sem):
        pltpu.make_async_copy(ref, ref, sem).wait()

    def all_sent(way):
        if way in to_relay:
            wait_bytes(p.at[:, :, 1, pl.ds(1, 16)], send_sem.at[way])
        else:
            wait_bytes(p.at[:, :, pl.ds(1, 4), 1], send_sem.at[way])

    def x_face(k, c, way, s=None):
        src, dst = {EAST: (4, 0), WEST: (1, 5)}[way]
        side = way
        which = pl.ds(2 * c, 2) if s is None else pl.ds(2 * c + s, 1)
        to = pl.ds(0, 2) if s is None else pl.ds(s, 1)
        if k == 0:
            refs = fields_hbm.at[:, which, pl.ds(16 * (src - 1), 16)], raw.at[side, c, :, to]
        else:
            refs = p.at[k, which, src, pl.ds(1, 16)], p.at[k, which, dst, pl.ds(1, 16)]
        return refs

    def copy_x(refs, way, recv, to):
        return pltpu.make_async_remote_copy(
            src_ref=refs[0],
            dst_ref=refs[1],
            send_sem=send_sem.at[way],
            recv_sem=recv,
            device_id=to,
            device_id_type=MESH,
        )

    def relay_at(k, c):
        return raw_relay.at[c] if k == 0 else relay.at[k - 1, c]

    def send_x(k, c):
        recv = recv_sem.at[k, c, EAST]
        for way in (EAST, WEST):

            @pl.when(plain[way] if 3 * k + c < SPLIT else has[way])
            def _():
                copy_x(x_face(k, c, way), way, recv, target[way]).start()

        if 3 * k + c >= SPLIT:
            return

        @pl.when(is_mid)
        def _():
            for way in (EAST, WEST):

                @pl.when(to_relay[way])
                def _():
                    src = x_face(k, c, way, 1)[0]
                    copy_x(
                        (src, relay_at(k, c)), way, relay_recv.at[k, c], relay_of[way]
                    ).start()
                    copy_x(x_face(k, c, way, 0), way, recv, target[way]).start()

    def send_y(k, c):
        for way in (NORTH, SOUTH):
            pl.when(has[way])(lambda: chunk(k, c, way).start())

    def arrived_y(k, c):
        sem = recv_sem.at[k, c, NORTH]
        two_faces = p.at[k, two(c), pl.ds(1, 4), pl.ds(0, 2)]
        one_face = p.at[k, two(c), pl.ds(1, 4), pl.ds(0, 1)]
        pl.when(both[NORTH])(lambda: wait_bytes(two_faces, sem))
        pl.when(jnp.logical_not(both[NORTH]))(lambda: wait_bytes(one_face, sem))

    def arrived_x(k, c):
        sem = recv_sem.at[k, c, EAST]
        if k == 0:
            two_faces, one_face = raw.at[:, c], raw.at[0, c]
        else:
            two_faces = p.at[k, two(c), pl.ds(0, 2), pl.ds(1, 16)]
            one_face = p.at[k, two(c), pl.ds(0, 1), pl.ds(1, 16)]
        pl.when(both[EAST])(lambda: wait_bytes(two_faces, sem))
        pl.when(jnp.logical_not(both[EAST]))(lambda: wait_bytes(one_face, sem))

    def pass_on(n, way):
        if not 0 <= n < SPLIT:
            return
        k, c = divmod(n, PAIRS)

        @pl.when(is_relay[way])
        def _():
            here = relay_at(k, c)
            wait_bytes(here, relay_recv.at[k, c])
            pltpu.make_async_remote_copy(
                src_ref=here,
                dst_ref=x_face(k, c, way, 1)[1],
                send_sem=relay_send,
                recv_sem=recv_sem.at[k, c, EAST],
                device_id=relay_to[way],
                device_id_type=MESH,
            ).start()

    def all_passed_on():
        @pl.when(is_end)
        def _():
            wait_bytes(relay.at[0], relay_send)
            wait_bytes(relay.at[1, pl.ds(0, SPLIT - 2 * PAIRS)], relay_send)
            wait_bytes(raw_relay, relay_send)

    def planes(first, step, count, body):
        def at(i, _):
            for h in range(2):
                body(first + step * i, h)
            return 0

        lax.fori_loop(0, count, at, 0)

    load_in(0).start()
    for copy in own:
        copy.start()
    for s in range(1, NS):
        load_in(s).start()

    barrier = pltpu.get_barrier_semaphore()
    expected = na - 1
    for way in (EAST, WEST, NORTH, SOUTH):
        pl.when(has[way])(
            lambda way=way: pl.semaphore_signal(
                barrier, inc=1, device_id=target[way], device_id_type=MESH
            )
        )
        expected = expected + has[way].astype(jnp.int32)
    for way in (EAST, WEST):
        for near, partners in (
            (to_relay[way], ((ax, 0, iy), (ax, end, iy))),
            (is_relay[way], ((ax, mid - 1, iy), (ax, mid, iy))),
        ):
            expected = expected + 2 * near.astype(jnp.int32)

            @pl.when(near)
            def _(partners=partners):
                for partner in partners:
                    pl.semaphore_signal(barrier, inc=1, device_id=partner, device_id_type=MESH)

    for step in range(1, na):
        pl.semaphore_signal(
            barrier, inc=1, device_id=member_ids[step], device_id_type=MESH
        )

    zero = jnp.zeros((8, 128), F32)

    def clear_x(x, speed):
        def at(s, _):
            for k in range(3):
                for y in range(16):
                    p[k, s, x, 1 + y] = zero
            return 0

        lax.fori_loop(0, NS, at, 0)
        speed_x[speed] = jnp.zeros((16, 128), F32)

    def clear_y(y, speed):
        def at(s, _):
            for k in range(3):
                for x in range(4):
                    p[k, s, 1 + x, y] = zero
            return 0

        lax.fori_loop(0, NS, at, 0)
        for x in range(4):
            speed_y[x, speed : speed + 8] = zero

    pl.when(ix == 0)(lambda: clear_x(0, 0))
    pl.when(ix == nx - 1)(lambda: clear_x(5, 5))
    pl.when(iy == 0)(lambda: clear_y(0, 0))
    pl.when(iy == ny - 1)(lambda: clear_y(17, 24))

    pl.semaphore_wait(barrier, expected)
    send_x(0, 0)
    for way in (EAST, WEST, NORTH, SOUTH):
        pl.when(has[way])(lambda way=way: speed_face(way).start())
    for c in range(1, PAIRS):
        send_x(0, c)

    def scatter(k, c, owner):
        @pl.when(ax != owner)
        def _():
            pltpu.make_async_remote_copy(
                src_ref=part.at[k, two(c), owner],
                dst_ref=part_in.at[k, c, lax.rem(owner - ax + na, na) - 1],
                send_sem=send_sem.at[SUM1],
                recv_sem=recv_sem.at[k, c, SUM1],
                device_id=(owner, ix, iy),
                device_id_type=MESH,
            ).start()

    def second_exchange(k, c):
        wait_bytes(part_in.at[k, c], recv_sem.at[k, c, SUM1])
        for i in range(2):
            total[k, 2 * c + i, ax] = (part[k, 2 * c + i, ax] + part_in[k, c, 0, i]) + (
                part_in[k, c, 1, i] + part_in[k, c, 2, i]
            )
        mine = total.at[k, two(c), ax]
        for step in range(1, na):
            pltpu.make_async_remote_copy(
                src_ref=mine,
                dst_ref=mine,
                send_sem=send_sem.at[SUM2],
                recv_sem=recv_sem.at[k, c, SUM2],
                device_id=member_ids[step],
                device_id_type=MESH,
            ).start()

    def mean_term(k, c):
        wait_bytes(total.at[k, two(c), pl.ds(0, na - 1)], recv_sem.at[k, c, SUM2])
        scale = (STEP * MIX / FIELDS) * diffusion[...]
        for i in range(2):
            mean_row[i] = scale * total[k, 2 * c + i]

    def turn(s):
        flat = rows_in.reshape(NS * 8 * 64, 128)

        def body(x, h):
            start = s * 512 + x * 16 + h * 8
            tiles = [flat[pl.ds(start + i, 8, stride=64), :] for i in range(8)]
            for i in range(8):
                p[0, s, x + 1, h * 8 + i + 1] = tiles[i]
            part[0, s, x, pl.ds(h * 8, 8), :] = sum_rows(tiles)

        return body

    raw_rows = raw.reshape(2 * PAIRS * 8 * 32, 128)

    def turn_face(c, way):
        for j in range(2):
            start = (way * PAIRS + c) * 256 + j * 16
            for y in range(16):
                tile = raw_rows[pl.ds(start + y, 8, stride=32), :]
                p[0, 2 * c + j, 0 if way == EAST else 5, y + 1] = tile

    for c in range(PAIRS):
        for s in (2 * c, 2 * c + 1):
            load_in(s).wait()
            planes(0, 1, 4, turn(s))
        for owner in range(na):
            scatter(0, c, owner)
        send_y(0, c)
        pass_on(c - 1, EAST)
        pass_on(c - 2, WEST)
        if c > 0:
            second_exchange(0, c - 1)

    for copy in own:
        copy.wait()
    for way in (EAST, WEST, NORTH, SOUTH):
        pl.when(has[back[way]])(lambda way=way: speed_face(way).wait_recv())

    diagonal = lax.broadcasted_iota(jnp.int32, (8, 8), 0) == lax.broadcasted_iota(
        jnp.int32, (8, 8), 1
    )
    draws = []
    for d in range(3):
        row = jnp.broadcast_to(wiener[d : d + 1, :], (8, 8))
        draw = jnp.sum(jnp.where(diagonal, row, 0.0), axis=1, keepdims=True)
        draws.append(jnp.broadcast_to(draw, (8, 128)))

    def coefficients(x, _):
        g = diffusion[x]
        diffuse = STEP * g
        stir = (0.5 * STEP) * jnp.sqrt((2.0 / STEP) * g)
        lane = lax.broadcasted_iota(jnp.int32, (16, 128), 1)
        upper, lower = lane < 127, lane > 0
        half_step = 0.5 * STEP
        base = [
            diffuse - half_step * speed_x[x + 2],
            diffuse + half_step * speed_x[x],
            diffuse - half_step * speed_y[x, 9:25, :],
            diffuse + half_step * speed_y[x, 7:23, :],
            jnp.where(upper, diffuse - half_step * pltpu.roll(speed_z[x], 127, 1), 0.0),
            jnp.where(lower, diffuse + half_step * pltpu.roll(speed_z[x], 1, 1), 0.0),
        ]
        stir_up, stir_down = jnp.where(upper, stir, 0.0), jnp.where(lower, stir, 0.0)
        keep = 1.0 - (6.0 + MIX) * diffuse
        for y in range(16):
            stir_y = spread(stir, y)
            for d in range(2):
                move = stir_y * draws[d]
                coef[2 * d, x, y] = spread(base[2 * d], y) + move
                coef[2 * d + 1, x, y] = spread(base[2 * d + 1], y) - move
            coef[4, x, y] = spread(base[4], y) + spread(stir_up, y) * draws[2]
            coef[5, x, y] = spread(base[5], y) - spread(stir_down, y) * draws[2]
            keep_y = spread(keep, y)
            centre[0, x, y] = keep_y
            centre[1, x, y] = keep_y - STEP * OXIDATION
        return 0

    lax.fori_loop(0, 4, coefficients, 0)

    def advance(k, c):
        base_weight, section_weight = WEIGHTS[k - 1]
        old = k - 1
        flat = out.reshape(8 * NS * 64, 128)

        def body(x, h):
            y0 = h * 8
            tiles, weights = [[], []], []
            columns = [[p[old, 2 * c + j, x + 1, y0 + i] for i in range(10)] for j in range(2)]
            means = [mean_row[j, x, pl.ds(y0, 8), :] for j in range(2)]
            for i in range(8):
                y = y0 + i
                factor = [coef[d, x, y] for d in range(6)]
                keep = centre[int(c > 0), x, y]
                here = [columns[j][i + 1] for j in range(2)]
                new = [
                    keep * here[j]
                    + spread(means[j], i)
                    + factor[0] * p[old, 2 * c + j, x + 2, y + 1]
                    + factor[1] * p[old, 2 * c + j, x, y + 1]
                    + factor[2] * columns[j][i + 2]
                    + factor[3] * columns[j][i]
                    + factor[4] * pltpu.roll(here[j], 127, 1)
                    + factor[5] * pltpu.roll(here[j], 1, 1)
                    for j in range(2)
                ]
                if c == 0:
                    square = here[0] * here[0]
                    w = square / (1.0 + square) / (1.0 + jnp.exp(-3.0 * here[1]))
                    weights.append(w)
                    new[1] = new[1] - (STEP * RADIATION) * w
                else:
                    w = weight[x, y]
                    before = [p[old, 3, x + 1, y + 1] if c == 2 else None, here[0]]
                    for j in range(2):
                        gain = STEP * NUCLEATION[2 * c - 2 + j]
                        if before[j] is not None:
                            gain = gain + (STEP * GROWTH) * before[j]
                        new[j] = new[j] + w * gain
                for j in range(2):
                    s = 2 * c + j
                    if base_weight:
                        new[j] = base_weight * p[0, s, x + 1, y + 1] + section_weight * new[j]
                    tiles[j].append(new[j])
            for i, w in enumerate(weights):
                weight[x, y0 + i] = w
            for j in range(2):
                s = 2 * c + j
                for i in range(8):
                    if k < 3:
                        p[k, s, x + 1, y0 + i + 1] = tiles[j][i]
                    else:
                        flat[pl.ds(s * 64 + x * 16 + y0 + i, 8, stride=NS * 64), :] = tiles[j][i]
            if k < 3:
                for j in range(2):
                    part[k, 2 * c + j, x, pl.ds(y0, 8), :] = sum_rows(tiles[j])

        return body

    for k in range(1, 4):
        for c in range(PAIRS):
            mean_term(k - 1, c)
            arrived_y(k - 1, c)
            planes(1, 1, 2, advance(k, c))
            if k < 3:
                scatter(k, c, 1)
                scatter(k, c, 2)
            arrived_x(k - 1, c)
            if k == 1:
                for way in (EAST, WEST):
                    pl.when(has[back[way]])(lambda way=way: turn_face(c, way))
            planes(0, 3, 2, advance(k, c))
            if k < 3:
                send_x(k, c)
                scatter(k, c, 0)
                scatter(k, c, 3)
                send_y(k, c)
            pass_on(3 * k + c - 1, EAST)
            pass_on(3 * k + c - 2, WEST)
            if c == 0:
                second_exchange(k - 1, PAIRS - 1)
            elif k < 3:
                second_exchange(k, c - 1)

    for way in (EAST, WEST, NORTH, SOUTH):
        pl.when(has[way])(lambda way=way: speed_face(way).wait_send())
        pl.when(has[way])(lambda way=way: all_sent(way))
    all_passed_on()
    wait_bytes(part_in, send_sem.at[SUM1])
    wait_bytes(part_in, send_sem.at[SUM2])


def local(fields_state, velocity, diffusivity, wiener_draw):
    counts = tuple(lax.axis_size(name) for name in ("gx", "gy", "af"))
    held = fields_state.shape
    dma = pltpu.SemaphoreType.DMA
    vmem = lambda *shape: pltpu.VMEM(shape, F32)
    held_in_hbm = (fields_state.reshape(8, NS, 64, 128), velocity, diffusivity, wiener_draw.T)
    out = pl.pallas_call(
        functools.partial(kernel, counts),
        out_shape=pltpu.VMEM((8, NS, 64, 128), F32),
        in_specs=[pl.BlockSpec(memory_space=pltpu.HBM)] * 4,
        out_specs=pl.BlockSpec(memory_space=pltpu.VMEM),
        scratch_shapes=[
            vmem(NS, 8, 64, 128),
            vmem(3, NS, 6, 18, 8, 128),
            vmem(6, 4, 16, 8, 128),
            vmem(2, 4, 16, 8, 128),
            vmem(4, 16, 8, 128),
            vmem(2, 4, 16, 128),
            vmem(3, NS, 4, 16, 128),
            vmem(3, PAIRS, 3, 2, 16, 128),
            vmem(3, NS, 4, 16, 128),
            vmem(6, 16, 128),
            vmem(4, 32, 128),
            vmem(4, 16, 128),
            vmem(4, 16, 128),
            vmem(3, 8),
            vmem(2, PAIRS, 1, 16, 8, 128),
            vmem(2, PAIRS, 8, 2, 16, 128),
            vmem(PAIRS, 8, 1, 16, 128),
            dma((NS,)),
            dma((5,)),
            dma,
            dma((3, PAIRS)),
            dma((4,)),
            dma((4,)),
            dma((6,)),
            dma((3, PAIRS, 6)),
        ],
        compiler_params=pltpu.CompilerParams(
            collective_id=0, has_side_effects=True, vmem_limit_bytes=48 * 1024 * 1024
        ),
    )(*(pltpu.with_memory_space_constraint(x, pltpu.HBM) for x in held_in_hbm))
    return out.reshape(held)


def solution(mesh):
    return jax.shard_map(
        local,
        mesh=mesh,
        in_specs=(
            P("af", None, "gx", "gy", None),
            P(None, "gx", "gy", None),
            P("gx", "gy", None),
            P("af", None),
        ),
        out_specs=P("af", None, "gx", "gy", None),
        check_vma=False,
    )
```

```python
import functools

import jax
import jax.numpy as jnp
from jax import lax
from jax.experimental import pallas as pl
from jax.experimental.pallas import tpu as pltpu
from jax.sharding import PartitionSpec as P

MESH = pl.DeviceIdType.MESH
F32 = jnp.float32

FIELDS = 32
NS = 6
PAIRS = 3
STEP = 0.3
MIX = 4.0
RADIATION = 0.5
NUCLEATION = (1.0, 0.8, 0.6, 0.5)
GROWTH = 0.5
OXIDATION = 0.3
WEIGHTS = ((0.0, 1.0), (0.75, 0.25), (1.0 / 3.0, 2.0 / 3.0))
EAST, WEST, NORTH, SOUTH, SUM1, SUM2 = range(6)


def sum_rows(tiles):
    row = lax.broadcasted_iota(jnp.int32, (8, 128), 0)
    low = row < 4
    quads = [
        jnp.where(low, tiles[i], tiles[i + 4])
        + pltpu.roll(jnp.where(low, tiles[i + 4], tiles[i]), 4, 0)
        for i in range(4)
    ]
    even = (row & 2) == 0
    pairs = [
        jnp.where(even, quads[i], quads[i + 2])
        + jnp.where(even, pltpu.roll(quads[i], 6, 0), pltpu.roll(quads[i + 2], 2, 0))
        for i in range(2)
    ]
    first = (row & 1) == 0
    return jnp.where(first, pairs[0], pairs[1]) + jnp.where(
        first, pltpu.roll(pairs[0], 7, 0), pltpu.roll(pairs[1], 1, 0)
    )


def spread(rows, i):
    return jnp.broadcast_to(rows[i : i + 1, :], (8, 128))


def kernel(
    counts,
    fields_hbm,
    velocity_hbm,
    diffusivity_hbm,
    wiener_hbm,
    out,
    rows_in,
    p,
    coef,
    centre,
    weight,
    mean_row,
    part,
    part_in,
    total,
    speed_x,
    speed_y,
    speed_z,
    diffusion,
    wiener,
    relay,
    raw,
    raw_relay,
    in_sem,
    own_sem,
    relay_send,
    relay_recv,
    speed_send,
    speed_recv,
    send_sem,
    recv_sem,
):
    nx, ny, na = counts
    ax, ix, iy = lax.axis_index("af"), lax.axis_index("gx"), lax.axis_index("gy")
    has = {EAST: ix < nx - 1, WEST: ix > 0, NORTH: iy < ny - 1, SOUTH: iy > 0}
    back = {EAST: WEST, WEST: EAST, NORTH: SOUTH, SOUTH: NORTH}
    target = {
        EAST: {"gx": ix + 1},
        WEST: {"gx": ix - 1},
        NORTH: {"gy": iy + 1},
        SOUTH: {"gy": iy - 1},
    }

    mid, end = nx // 2, nx - 1
    to_relay = {EAST: ix == mid - 1, WEST: ix == mid}
    is_relay = {EAST: ix == end, WEST: ix == 0}
    relay_of = {EAST: {"gx": end}, WEST: {"gx": 0}}
    relay_to = {EAST: {"gx": mid}, WEST: {"gx": mid - 1}}

    def load_in(s):
        return pltpu.make_async_copy(fields_hbm.at[:, s], rows_in.at[s], in_sem.at[s])

    def two(c):
        return pl.ds(2 * c, 2)

    own = [
        pltpu.make_async_copy(velocity_hbm.at[0], speed_x.at[pl.ds(1, 4)], own_sem.at[0]),
        pltpu.make_async_copy(velocity_hbm.at[1], speed_y.at[:, pl.ds(8, 16)], own_sem.at[1]),
        pltpu.make_async_copy(velocity_hbm.at[2], speed_z, own_sem.at[2]),
        pltpu.make_async_copy(diffusivity_hbm, diffusion, own_sem.at[3]),
        pltpu.make_async_copy(wiener_hbm, wiener, own_sem.at[4]),
    ]

    def speed_face(way):
        src, dst = {
            EAST: (velocity_hbm.at[0, 3], speed_x.at[0]),
            WEST: (velocity_hbm.at[0, 0], speed_x.at[5]),
            NORTH: (velocity_hbm.at[1, :, pl.ds(8, 8)], speed_y.at[:, pl.ds(0, 8)]),
            SOUTH: (velocity_hbm.at[1, :, pl.ds(0, 8)], speed_y.at[:, pl.ds(24, 8)]),
        }[way]
        return pltpu.make_async_remote_copy(
            src_ref=src,
            dst_ref=dst,
            send_sem=speed_send.at[way],
            recv_sem=speed_recv.at[way],
            device_id=target[way],
            device_id_type=MESH,
        )

    def face(k, s, way, recv=None):
        src, dst = {
            NORTH: lambda: (p.at[k, s, pl.ds(1, 4), 16], p.at[k, s, pl.ds(1, 4), 0]),
            SOUTH: lambda: (p.at[k, s, pl.ds(1, 4), 1], p.at[k, s, pl.ds(1, 4), 17]),
        }[way]()
        return pltpu.make_async_remote_copy(
            src_ref=src,
            dst_ref=dst,
            send_sem=send_sem.at[way],
            recv_sem=recv,
            device_id=target[way],
            device_id_type=MESH,
        )

    def chunk(k, c, way):
        return face(k, two(c), way, recv_sem.at[k, c, way])

    def all_sent(way):
        if way in to_relay:
            all_x = p.at[:, :, 1, pl.ds(1, 16)]
            copy_x((all_x, all_x), way, recv_sem.at[0, 0, way], target[way]).wait_send()
        else:
            face(pl.ds(0, 3), pl.ds(0, NS), way, recv_sem.at[0, 0, way]).wait_send()

    def x_face(k, c, way, s=None):
        src, dst = {EAST: (4, 0), WEST: (1, 5)}[way]
        side = way
        which = pl.ds(2 * c, 2) if s is None else pl.ds(2 * c + s, 1)
        to = pl.ds(0, 2) if s is None else pl.ds(s, 1)
        if k == 0:
            refs = fields_hbm.at[:, which, pl.ds(16 * (src - 1), 16)], raw.at[side, c, :, to]
        else:
            refs = p.at[k, which, src, pl.ds(1, 16)], p.at[k, which, dst, pl.ds(1, 16)]
        return refs

    def copy_x(refs, way, recv, to):
        return pltpu.make_async_remote_copy(
            src_ref=refs[0],
            dst_ref=refs[1],
            send_sem=send_sem.at[way],
            recv_sem=recv,
            device_id=to,
            device_id_type=MESH,
        )

    def relay_at(k, c):
        return raw_relay.at[c] if k == 0 else relay.at[k - 1, c]

    def send_x(k, c):
        for way in (EAST, WEST):
            recv = recv_sem.at[k, c, way]

            @pl.when(has[way] & jnp.logical_not(to_relay[way]))
            def _():
                copy_x(x_face(k, c, way), way, recv, target[way]).start()

            @pl.when(to_relay[way])
            def _():
                src = x_face(k, c, way, 1)[0]
                copy_x(
                    (src, relay_at(k, c)), way, relay_recv.at[k, c], relay_of[way]
                ).start()
                copy_x(x_face(k, c, way, 0), way, recv, target[way]).start()

    def send(k, c, way):
        pl.when(has[way])(lambda: chunk(k, c, way).start())

    def arrived_x(k, c):
        for way in (EAST, WEST):

            @pl.when(has[back[way]])
            def _():
                copy_x(x_face(k, c, way), way, recv_sem.at[k, c, way], target[way]).wait_recv()

    def pass_on(n, way):
        if not 0 <= n < 3 * PAIRS:
            return
        k, c = divmod(n, PAIRS)

        @pl.when(is_relay[way])
        def _():
            here = relay_at(k, c)
            pltpu.make_async_copy(here, here, relay_recv.at[k, c]).wait()
            pltpu.make_async_remote_copy(
                src_ref=here,
                dst_ref=x_face(k, c, way, 1)[1],
                send_sem=relay_send,
                recv_sem=recv_sem.at[k, c, way],
                device_id=relay_to[way],
                device_id_type=MESH,
            ).start()

    def all_passed_on():
        for way in (EAST, WEST):

            @pl.when(is_relay[way])
            def _():
                pltpu.make_async_copy(relay, relay, relay_send).wait()
                pltpu.make_async_copy(raw_relay, raw_relay, relay_send).wait()

    def arrived(k, c, way):
        pl.when(has[back[way]])(lambda: chunk(k, c, way).wait_recv())

    def planes(first, step, count, body):
        def at(i, _):
            for h in range(2):
                body(first + step * i, h)
            return 0

        lax.fori_loop(0, count, at, 0)

    load_in(0).start()
    for copy in own:
        copy.start()
    for s in range(1, NS):
        load_in(s).start()

    barrier = pltpu.get_barrier_semaphore()
    expected = na - 1
    for way in (EAST, WEST, NORTH, SOUTH):
        pl.when(has[way])(
            lambda way=way: pl.semaphore_signal(
                barrier, inc=1, device_id=target[way], device_id_type=MESH
            )
        )
        expected = expected + has[way].astype(jnp.int32)
    for way in (EAST, WEST):
        for near, partners in (
            (to_relay[way], ({"gx": 0}, {"gx": end})),
            (is_relay[way], ({"gx": mid - 1}, {"gx": mid})),
        ):
            expected = expected + 2 * near.astype(jnp.int32)

            @pl.when(near)
            def _(partners=partners):
                for partner in partners:
                    pl.semaphore_signal(barrier, inc=1, device_id=partner, device_id_type=MESH)

    for step in range(1, na):
        other = {"af": lax.rem(ax + step, na)}
        pl.semaphore_signal(barrier, inc=1, device_id=other, device_id_type=MESH)

    zero = jnp.zeros((8, 128), F32)

    def clear_x(x, speed):
        def at(s, _):
            for k in range(3):
                for y in range(16):
                    p[k, s, x, 1 + y] = zero
            return 0

        lax.fori_loop(0, NS, at, 0)
        speed_x[speed] = jnp.zeros((16, 128), F32)

    def clear_y(y, speed):
        def at(s, _):
            for k in range(3):
                for x in range(4):
                    p[k, s, 1 + x, y] = zero
            return 0

        lax.fori_loop(0, NS, at, 0)
        for x in range(4):
            speed_y[x, speed : speed + 8] = zero

    pl.when(ix == 0)(lambda: clear_x(0, 0))
    pl.when(ix == nx - 1)(lambda: clear_x(5, 5))
    pl.when(iy == 0)(lambda: clear_y(0, 0))
    pl.when(iy == ny - 1)(lambda: clear_y(17, 24))

    pl.semaphore_wait(barrier, expected)
    send_x(0, 0)
    for way in (EAST, WEST, NORTH, SOUTH):
        pl.when(has[way])(lambda way=way: speed_face(way).start())
    for c in range(1, PAIRS):
        send_x(0, c)

    def scatter(k, c, owner):
        @pl.when(ax != owner)
        def _():
            pltpu.make_async_remote_copy(
                src_ref=part.at[k, two(c), owner],
                dst_ref=part_in.at[k, c, lax.rem(owner - ax + na, na) - 1],
                send_sem=send_sem.at[SUM1],
                recv_sem=recv_sem.at[k, c, SUM1],
                device_id={"af": owner},
                device_id_type=MESH,
            ).start()

    def wait_bytes(ref, sem):
        pltpu.make_async_copy(ref, ref, sem).wait()

    def second_exchange(k, c):
        wait_bytes(part_in.at[k, c], recv_sem.at[k, c, SUM1])
        for i in range(2):
            total[k, 2 * c + i, ax] = (part[k, 2 * c + i, ax] + part_in[k, c, 0, i]) + (
                part_in[k, c, 1, i] + part_in[k, c, 2, i]
            )
        for member in range(na):

            @pl.when(ax != member)
            def _():
                mine = total.at[k, two(c), ax]
                pltpu.make_async_remote_copy(
                    src_ref=mine,
                    dst_ref=mine,
                    send_sem=send_sem.at[SUM2],
                    recv_sem=recv_sem.at[k, c, SUM2],
                    device_id={"af": member},
                    device_id_type=MESH,
                ).start()

    def mean_term(k, c):
        wait_bytes(total.at[k, two(c), pl.ds(0, na - 1)], recv_sem.at[k, c, SUM2])
        scale = (STEP * MIX / FIELDS) * diffusion[...]
        for i in range(2):
            mean_row[i] = scale * total[k, 2 * c + i]

    def turn(s):
        flat = rows_in.reshape(NS * 8 * 64, 128)

        def body(x, h):
            start = s * 512 + x * 16 + h * 8
            tiles = [flat[pl.ds(start + i, 8, stride=64), :] for i in range(8)]
            for i in range(8):
                p[0, s, x + 1, h * 8 + i + 1] = tiles[i]
            part[0, s, x, pl.ds(h * 8, 8), :] = sum_rows(tiles)

        return body

    raw_rows = raw.reshape(2 * PAIRS * 8 * 32, 128)

    def turn_face(c, way):
        for j in range(2):
            start = (way * PAIRS + c) * 256 + j * 16
            for y in range(16):
                tile = raw_rows[pl.ds(start + y, 8, stride=32), :]
                p[0, 2 * c + j, 0 if way == EAST else 5, y + 1] = tile

    for c in range(PAIRS):
        for s in (2 * c, 2 * c + 1):
            load_in(s).wait()
            planes(0, 1, 4, turn(s))
        send(0, c, NORTH)
        send(0, c, SOUTH)
        for owner in range(na):
            scatter(0, c, owner)
        pass_on(c - 1, EAST)
        pass_on(c - 2, WEST)
        if c > 0:
            second_exchange(0, c - 1)

    for copy in own:
        copy.wait()
    for way in (EAST, WEST, NORTH, SOUTH):
        pl.when(has[back[way]])(lambda way=way: speed_face(way).wait_recv())

    diagonal = lax.broadcasted_iota(jnp.int32, (8, 8), 0) == lax.broadcasted_iota(
        jnp.int32, (8, 8), 1
    )
    draws = []
    for d in range(3):
        row = jnp.broadcast_to(wiener[d : d + 1, :], (8, 8))
        column = jnp.sum(jnp.where(diagonal, row, 0.0), axis=1, keepdims=True)
        draws.append(jnp.broadcast_to(column, (8, 128)))

    def coefficients(x, _):
        g = diffusion[x]
        diffuse = STEP * g
        stir = (0.5 * STEP) * jnp.sqrt((2.0 / STEP) * g)
        lane = lax.broadcasted_iota(jnp.int32, (16, 128), 1)
        upper, lower = lane < 127, lane > 0
        half_step = 0.5 * STEP
        base = [
            diffuse - half_step * speed_x[x + 2],
            diffuse + half_step * speed_x[x],
            diffuse - half_step * speed_y[x, 9:25, :],
            diffuse + half_step * speed_y[x, 7:23, :],
            jnp.where(upper, diffuse - half_step * pltpu.roll(speed_z[x], 127, 1), 0.0),
            jnp.where(lower, diffuse + half_step * pltpu.roll(speed_z[x], 1, 1), 0.0),
        ]
        stir_up, stir_down = jnp.where(upper, stir, 0.0), jnp.where(lower, stir, 0.0)
        keep = 1.0 - (6.0 + MIX) * diffuse
        for y in range(16):
            stir_y = spread(stir, y)
            for d in range(2):
                move = stir_y * draws[d]
                coef[2 * d, x, y] = spread(base[2 * d], y) + move
                coef[2 * d + 1, x, y] = spread(base[2 * d + 1], y) - move
            coef[4, x, y] = spread(base[4], y) + spread(stir_up, y) * draws[2]
            coef[5, x, y] = spread(base[5], y) - spread(stir_down, y) * draws[2]
            keep_y = spread(keep, y)
            centre[0, x, y] = keep_y
            centre[1, x, y] = keep_y - STEP * OXIDATION
        return 0

    lax.fori_loop(0, 4, coefficients, 0)

    def advance(k, c):
        base_weight, section_weight = WEIGHTS[k - 1]
        old = k - 1
        flat = out.reshape(8 * NS * 64, 128)

        def body(x, h):
            y0 = h * 8
            tiles, weights = [[], []], []
            columns = [[p[old, 2 * c + j, x + 1, y0 + i] for i in range(10)] for j in range(2)]
            means = [mean_row[j, x, pl.ds(y0, 8), :] for j in range(2)]
            for i in range(8):
                y = y0 + i
                factor = [coef[d, x, y] for d in range(6)]
                keep = centre[int(c > 0), x, y]
                here = [columns[j][i + 1] for j in range(2)]
                new = [
                    keep * here[j]
                    + spread(means[j], i)
                    + factor[0] * p[old, 2 * c + j, x + 2, y + 1]
                    + factor[1] * p[old, 2 * c + j, x, y + 1]
                    + factor[2] * columns[j][i + 2]
                    + factor[3] * columns[j][i]
                    + factor[4] * pltpu.roll(here[j], 127, 1)
                    + factor[5] * pltpu.roll(here[j], 1, 1)
                    for j in range(2)
                ]
                if c == 0:
                    square = here[0] * here[0]
                    w = square / (1.0 + square) / (1.0 + jnp.exp(-3.0 * here[1]))
                    weights.append(w)
                    new[1] = new[1] - (STEP * RADIATION) * w
                else:
                    w = weight[x, y]
                    before = [p[old, 3, x + 1, y + 1] if c == 2 else None, here[0]]
                    for j in range(2):
                        gain = STEP * NUCLEATION[2 * c - 2 + j]
                        if before[j] is not None:
                            gain = gain + (STEP * GROWTH) * before[j]
                        new[j] = new[j] + w * gain
                for j in range(2):
                    s = 2 * c + j
                    if base_weight:
                        new[j] = base_weight * p[0, s, x + 1, y + 1] + section_weight * new[j]
                    tiles[j].append(new[j])
            for i, w in enumerate(weights):
                weight[x, y0 + i] = w
            for j in range(2):
                s = 2 * c + j
                for i in range(8):
                    if k < 3:
                        p[k, s, x + 1, y0 + i + 1] = tiles[j][i]
                    else:
                        flat[pl.ds(s * 64 + x * 16 + y0 + i, 8, stride=NS * 64), :] = tiles[j][i]
            if k < 3:
                for j in range(2):
                    part[k, 2 * c + j, x, pl.ds(y0, 8), :] = sum_rows(tiles[j])

        return body

    for k in range(1, 4):
        for c in range(PAIRS):
            mean_term(k - 1, c)
            arrived(k - 1, c, NORTH)
            arrived(k - 1, c, SOUTH)
            planes(1, 1, 2, advance(k, c))
            if k < 3:
                scatter(k, c, 1)
                scatter(k, c, 2)
            arrived_x(k - 1, c)
            if k == 1:
                for way in (EAST, WEST):
                    pl.when(has[back[way]])(lambda way=way: turn_face(c, way))
            planes(0, 3, 2, advance(k, c))
            pass_on(3 * k + c - 1, EAST)
            if k < 3:
                send_x(k, c)
                scatter(k, c, 0)
                scatter(k, c, 3)
                for way in (NORTH, SOUTH):
                    send(k, c, way)
            pass_on(3 * k + c - 2, WEST)
            if c == 0:
                second_exchange(k - 1, PAIRS - 1)
            elif k < 3:
                second_exchange(k, c - 1)

    for way in (EAST, WEST, NORTH, SOUTH):
        pl.when(has[way])(lambda way=way: speed_face(way).wait_send())
        pl.when(has[way])(lambda way=way: all_sent(way))
    all_passed_on()
    wait_bytes(part_in, send_sem.at[SUM1])
    wait_bytes(part_in, send_sem.at[SUM2])


def local(fields_state, velocity, diffusivity, wiener_draw):
    counts = tuple(lax.axis_size(name) for name in ("gx", "gy", "af"))
    held = fields_state.shape
    dma = pltpu.SemaphoreType.DMA
    vmem = lambda *shape: pltpu.VMEM(shape, F32)
    held_in_hbm = (fields_state.reshape(8, NS, 64, 128), velocity, diffusivity, wiener_draw.T)
    out = pl.pallas_call(
        functools.partial(kernel, counts),
        out_shape=pltpu.VMEM((8, NS, 64, 128), F32),
        in_specs=[pl.BlockSpec(memory_space=pltpu.HBM)] * 4,
        out_specs=pl.BlockSpec(memory_space=pltpu.VMEM),
        scratch_shapes=[
            vmem(NS, 8, 64, 128),
            vmem(3, NS, 6, 18, 8, 128),
            vmem(6, 4, 16, 8, 128),
            vmem(2, 4, 16, 8, 128),
            vmem(4, 16, 8, 128),
            vmem(2, 4, 16, 128),
            vmem(3, NS, 4, 16, 128),
            vmem(3, PAIRS, 3, 2, 16, 128),
            vmem(3, NS, 4, 16, 128),
            vmem(6, 16, 128),
            vmem(4, 32, 128),
            vmem(4, 16, 128),
            vmem(4, 16, 128),
            vmem(3, 8),
            vmem(2, PAIRS, 1, 16, 8, 128),
            vmem(2, PAIRS, 8, 2, 16, 128),
            vmem(PAIRS, 8, 1, 16, 128),
            dma((NS,)),
            dma((5,)),
            dma,
            dma((3, PAIRS)),
            dma((4,)),
            dma((4,)),
            dma((6,)),
            dma((3, PAIRS, 6)),
        ],
        compiler_params=pltpu.CompilerParams(
            collective_id=0, has_side_effects=True, vmem_limit_bytes=48 * 1024 * 1024
        ),
    )(*(pltpu.with_memory_space_constraint(x, pltpu.HBM) for x in held_in_hbm))
    return out.reshape(held)


def solution(mesh):
    return jax.shard_map(
        local,
        mesh=mesh,
        in_specs=(
            P("af", None, "gx", "gy", None),
            P(None, "gx", "gy", None),
            P("gx", "gy", None),
            P("af", None),
        ),
        out_specs=P("af", None, "gx", "gy", None),
        check_vma=False,
    )
```

```python
import functools

import jax
import jax.numpy as jnp
from jax import lax
from jax.experimental import pallas as pl
from jax.experimental.pallas import tpu as pltpu
from jax.sharding import PartitionSpec as P

MESH = pl.DeviceIdType.MESH
F32 = jnp.float32

FIELDS = 32
NS = 6
PAIRS = 3
STEP = 0.3
MIX = 4.0
RADIATION = 0.5
NUCLEATION = (1.0, 0.8, 0.6, 0.5)
GROWTH = 0.5
OXIDATION = 0.3
WEIGHTS = ((0.0, 1.0), (0.75, 0.25), (1.0 / 3.0, 2.0 / 3.0))
EAST, WEST, NORTH, SOUTH, SUM1, SUM2 = range(6)


def sum_rows(tiles):
    row = lax.broadcasted_iota(jnp.int32, (8, 128), 0)
    low = row < 4
    quads = [
        jnp.where(low, tiles[i], tiles[i + 4])
        + pltpu.roll(jnp.where(low, tiles[i + 4], tiles[i]), 4, 0)
        for i in range(4)
    ]
    even = (row & 2) == 0
    pairs = [
        jnp.where(even, quads[i], quads[i + 2])
        + jnp.where(even, pltpu.roll(quads[i], 6, 0), pltpu.roll(quads[i + 2], 2, 0))
        for i in range(2)
    ]
    first = (row & 1) == 0
    return jnp.where(first, pairs[0], pairs[1]) + jnp.where(
        first, pltpu.roll(pairs[0], 7, 0), pltpu.roll(pairs[1], 1, 0)
    )


def spread(rows, i):
    return jnp.broadcast_to(rows[i : i + 1, :], (8, 128))


def kernel(
    counts,
    fields_hbm,
    velocity_hbm,
    diffusivity_hbm,
    wiener_hbm,
    out,
    rows_in,
    p,
    coef,
    centre,
    weight,
    mean_row,
    part,
    part_in,
    total,
    speed_x,
    speed_y,
    speed_z,
    diffusion,
    wiener,
    relay,
    raw,
    raw_relay,
    in_sem,
    own_sem,
    relay_send,
    relay_recv,
    speed_send,
    speed_recv,
    send_sem,
    recv_sem,
):
    nx, ny, na = counts
    ax, ix, iy = lax.axis_index("af"), lax.axis_index("gx"), lax.axis_index("gy")
    has = {EAST: ix < nx - 1, WEST: ix > 0, NORTH: iy < ny - 1, SOUTH: iy > 0}
    back = {EAST: WEST, WEST: EAST, NORTH: SOUTH, SOUTH: NORTH}
    target = {
        EAST: {"gx": ix + 1},
        WEST: {"gx": ix - 1},
        NORTH: {"gy": iy + 1},
        SOUTH: {"gy": iy - 1},
    }

    mid, end = nx // 2, nx - 1
    to_relay = {EAST: ix == mid - 1, WEST: ix == mid}
    is_relay = {EAST: ix == end, WEST: ix == 0}
    relay_of = {EAST: {"gx": end}, WEST: {"gx": 0}}
    relay_to = {EAST: {"gx": mid}, WEST: {"gx": mid - 1}}

    def load_in(s):
        return pltpu.make_async_copy(fields_hbm.at[:, s], rows_in.at[s], in_sem.at[s])

    def two(c):
        return pl.ds(2 * c, 2)

    own = [
        pltpu.make_async_copy(velocity_hbm.at[0], speed_x.at[pl.ds(1, 4)], own_sem.at[0]),
        pltpu.make_async_copy(velocity_hbm.at[1], speed_y.at[:, pl.ds(8, 16)], own_sem.at[1]),
        pltpu.make_async_copy(velocity_hbm.at[2], speed_z, own_sem.at[2]),
        pltpu.make_async_copy(diffusivity_hbm, diffusion, own_sem.at[3]),
        pltpu.make_async_copy(wiener_hbm, wiener, own_sem.at[4]),
    ]

    def speed_face(way):
        src, dst = {
            EAST: (velocity_hbm.at[0, 3], speed_x.at[0]),
            WEST: (velocity_hbm.at[0, 0], speed_x.at[5]),
            NORTH: (velocity_hbm.at[1, :, pl.ds(8, 8)], speed_y.at[:, pl.ds(0, 8)]),
            SOUTH: (velocity_hbm.at[1, :, pl.ds(0, 8)], speed_y.at[:, pl.ds(24, 8)]),
        }[way]
        return pltpu.make_async_remote_copy(
            src_ref=src,
            dst_ref=dst,
            send_sem=speed_send.at[way],
            recv_sem=speed_recv.at[way],
            device_id=target[way],
            device_id_type=MESH,
        )

    def face(k, s, way, recv=None):
        src, dst = {
            NORTH: lambda: (p.at[k, s, pl.ds(1, 4), 16], p.at[k, s, pl.ds(1, 4), 0]),
            SOUTH: lambda: (p.at[k, s, pl.ds(1, 4), 1], p.at[k, s, pl.ds(1, 4), 17]),
        }[way]()
        return pltpu.make_async_remote_copy(
            src_ref=src,
            dst_ref=dst,
            send_sem=send_sem.at[way],
            recv_sem=recv,
            device_id=target[way],
            device_id_type=MESH,
        )

    def chunk(k, c, way):
        return face(k, two(c), way, recv_sem.at[k, c, way])

    def all_sent(way):
        if way in to_relay:
            all_x = p.at[:, :, 1, pl.ds(1, 16)]
            copy_x((all_x, all_x), way, recv_sem.at[0, 0, way], target[way]).wait_send()
        else:
            face(pl.ds(0, 3), pl.ds(0, NS), way, recv_sem.at[0, 0, way]).wait_send()

    def x_face(k, c, way, s=None):
        src, dst = {EAST: (4, 0), WEST: (1, 5)}[way]
        side = way
        which = pl.ds(2 * c, 2) if s is None else pl.ds(2 * c + s, 1)
        to = pl.ds(0, 2) if s is None else pl.ds(s, 1)
        if k == 0:
            refs = fields_hbm.at[:, which, pl.ds(16 * (src - 1), 16)], raw.at[side, c, :, to]
        else:
            refs = p.at[k, which, src, pl.ds(1, 16)], p.at[k, which, dst, pl.ds(1, 16)]
        return refs

    def copy_x(refs, way, recv, to):
        return pltpu.make_async_remote_copy(
            src_ref=refs[0],
            dst_ref=refs[1],
            send_sem=send_sem.at[way],
            recv_sem=recv,
            device_id=to,
            device_id_type=MESH,
        )

    def relay_at(k, c):
        return raw_relay.at[c] if k == 0 else relay.at[k - 1, c]

    def send_x(k, c):
        for way in (EAST, WEST):
            recv = recv_sem.at[k, c, way]

            @pl.when(has[way] & jnp.logical_not(to_relay[way]))
            def _():
                copy_x(x_face(k, c, way), way, recv, target[way]).start()

            @pl.when(to_relay[way])
            def _():
                src = x_face(k, c, way, 1)[0]
                copy_x(
                    (src, relay_at(k, c)), way, relay_recv.at[k, c], relay_of[way]
                ).start()
                copy_x(x_face(k, c, way, 0), way, recv, target[way]).start()

    def send(k, c, way):
        pl.when(has[way])(lambda: chunk(k, c, way).start())

    def arrived_x(k, c):
        for way in (EAST, WEST):

            @pl.when(has[back[way]])
            def _():
                copy_x(x_face(k, c, way), way, recv_sem.at[k, c, way], target[way]).wait_recv()

    def pass_on(k, c):
        for way in (EAST, WEST):

            @pl.when(is_relay[way])
            def _():
                here = relay_at(k, c)
                pltpu.make_async_copy(here, here, relay_recv.at[k, c]).wait()
                pltpu.make_async_remote_copy(
                    src_ref=here,
                    dst_ref=x_face(k, c, way, 1)[1],
                    send_sem=relay_send,
                    recv_sem=recv_sem.at[k, c, way],
                    device_id=relay_to[way],
                    device_id_type=MESH,
                ).start()

    def all_passed_on():
        for way in (EAST, WEST):

            @pl.when(is_relay[way])
            def _():
                pltpu.make_async_copy(relay, relay, relay_send).wait()
                pltpu.make_async_copy(raw_relay, raw_relay, relay_send).wait()

    def arrived(k, c, way):
        pl.when(has[back[way]])(lambda: chunk(k, c, way).wait_recv())

    def planes(first, step, count, body):
        def at(i, _):
            for h in range(2):
                body(first + step * i, h)
            return 0

        lax.fori_loop(0, count, at, 0)

    load_in(0).start()
    for copy in own:
        copy.start()
    for s in range(1, NS):
        load_in(s).start()

    barrier = pltpu.get_barrier_semaphore()
    expected = na - 1
    for way in (EAST, WEST, NORTH, SOUTH):
        pl.when(has[way])(
            lambda way=way: pl.semaphore_signal(
                barrier, inc=1, device_id=target[way], device_id_type=MESH
            )
        )
        expected = expected + has[way].astype(jnp.int32)
    for way in (EAST, WEST):
        for near, partners in (
            (to_relay[way], ({"gx": 0}, {"gx": end})),
            (is_relay[way], ({"gx": mid - 1}, {"gx": mid})),
        ):
            expected = expected + 2 * near.astype(jnp.int32)

            @pl.when(near)
            def _(partners=partners):
                for partner in partners:
                    pl.semaphore_signal(barrier, inc=1, device_id=partner, device_id_type=MESH)

    for step in range(1, na):
        other = {"af": lax.rem(ax + step, na)}
        pl.semaphore_signal(barrier, inc=1, device_id=other, device_id_type=MESH)

    zero = jnp.zeros((8, 128), F32)

    def clear_x(x, speed):
        def at(s, _):
            for k in range(3):
                for y in range(16):
                    p[k, s, x, 1 + y] = zero
            return 0

        lax.fori_loop(0, NS, at, 0)
        speed_x[speed] = jnp.zeros((16, 128), F32)

    def clear_y(y, speed):
        def at(s, _):
            for k in range(3):
                for x in range(4):
                    p[k, s, 1 + x, y] = zero
            return 0

        lax.fori_loop(0, NS, at, 0)
        for x in range(4):
            speed_y[x, speed : speed + 8] = zero

    pl.when(ix == 0)(lambda: clear_x(0, 0))
    pl.when(ix == nx - 1)(lambda: clear_x(5, 5))
    pl.when(iy == 0)(lambda: clear_y(0, 0))
    pl.when(iy == ny - 1)(lambda: clear_y(17, 24))

    pl.semaphore_wait(barrier, expected)
    send_x(0, 0)
    for way in (EAST, WEST, NORTH, SOUTH):
        pl.when(has[way])(lambda way=way: speed_face(way).start())
    for c in range(1, PAIRS):
        send_x(0, c)

    def scatter(k, c, owner):
        @pl.when(ax != owner)
        def _():
            pltpu.make_async_remote_copy(
                src_ref=part.at[k, two(c), owner],
                dst_ref=part_in.at[k, c, lax.rem(owner - ax + na, na) - 1],
                send_sem=send_sem.at[SUM1],
                recv_sem=recv_sem.at[k, c, SUM1],
                device_id={"af": owner},
                device_id_type=MESH,
            ).start()

    def wait_bytes(ref, sem):
        pltpu.make_async_copy(ref, ref, sem).wait()

    def second_exchange(k, c):
        wait_bytes(part_in.at[k, c], recv_sem.at[k, c, SUM1])
        for i in range(2):
            total[k, 2 * c + i, ax] = (part[k, 2 * c + i, ax] + part_in[k, c, 0, i]) + (
                part_in[k, c, 1, i] + part_in[k, c, 2, i]
            )
        for member in range(na):

            @pl.when(ax != member)
            def _():
                mine = total.at[k, two(c), ax]
                pltpu.make_async_remote_copy(
                    src_ref=mine,
                    dst_ref=mine,
                    send_sem=send_sem.at[SUM2],
                    recv_sem=recv_sem.at[k, c, SUM2],
                    device_id={"af": member},
                    device_id_type=MESH,
                ).start()

    def mean_term(k, c):
        wait_bytes(total.at[k, two(c), pl.ds(0, na - 1)], recv_sem.at[k, c, SUM2])
        scale = (STEP * MIX / FIELDS) * diffusion[...]
        for i in range(2):
            mean_row[i] = scale * total[k, 2 * c + i]

    def turn(s):
        flat = rows_in.reshape(NS * 8 * 64, 128)

        def body(x, h):
            start = s * 512 + x * 16 + h * 8
            tiles = [flat[pl.ds(start + i, 8, stride=64), :] for i in range(8)]
            for i in range(8):
                p[0, s, x + 1, h * 8 + i + 1] = tiles[i]
            fields = [rows_in[s, f, pl.ds(x * 16 + h * 8, 8), :] for f in range(8)]
            while len(fields) > 1:
                fields = [a + b for a, b in zip(fields[::2], fields[1::2])]
            part[0, s, x, pl.ds(h * 8, 8), :] = fields[0]

        return body

    raw_rows = raw.reshape(2 * PAIRS * 8 * 32, 128)

    def turn_face(c, way):
        for j in range(2):
            start = (way * PAIRS + c) * 256 + j * 16
            for y in range(16):
                tile = raw_rows[pl.ds(start + y, 8, stride=32), :]
                p[0, 2 * c + j, 0 if way == EAST else 5, y + 1] = tile

    for c in range(PAIRS):
        for s in (2 * c, 2 * c + 1):
            load_in(s).wait()
            planes(0, 1, 4, turn(s))
        send(0, c, NORTH)
        send(0, c, SOUTH)
        for owner in range(na):
            scatter(0, c, owner)
        if c > 0:
            pass_on(0, c - 1)
            second_exchange(0, c - 1)

    for copy in own:
        copy.wait()
    for way in (EAST, WEST, NORTH, SOUTH):
        pl.when(has[back[way]])(lambda way=way: speed_face(way).wait_recv())

    diagonal = lax.broadcasted_iota(jnp.int32, (8, 8), 0) == lax.broadcasted_iota(
        jnp.int32, (8, 8), 1
    )
    draws = []
    for d in range(3):
        row = jnp.broadcast_to(wiener[d : d + 1, :], (8, 8))
        column = jnp.sum(jnp.where(diagonal, row, 0.0), axis=1, keepdims=True)
        draws.append(jnp.broadcast_to(column, (8, 128)))

    def coefficients(x, _):
        g = diffusion[x]
        diffuse = STEP * g
        stir = (0.5 * STEP) * jnp.sqrt((2.0 / STEP) * g)
        lane = lax.broadcasted_iota(jnp.int32, (16, 128), 1)
        upper, lower = lane < 127, lane > 0
        half_step = 0.5 * STEP
        base = [
            diffuse - half_step * speed_x[x + 2],
            diffuse + half_step * speed_x[x],
            diffuse - half_step * speed_y[x, 9:25, :],
            diffuse + half_step * speed_y[x, 7:23, :],
            jnp.where(upper, diffuse - half_step * pltpu.roll(speed_z[x], 127, 1), 0.0),
            jnp.where(lower, diffuse + half_step * pltpu.roll(speed_z[x], 1, 1), 0.0),
        ]
        stir_up, stir_down = jnp.where(upper, stir, 0.0), jnp.where(lower, stir, 0.0)
        keep = 1.0 - (6.0 + MIX) * diffuse
        for y in range(16):
            stir_y = spread(stir, y)
            for d in range(2):
                move = stir_y * draws[d]
                coef[2 * d, x, y] = spread(base[2 * d], y) + move
                coef[2 * d + 1, x, y] = spread(base[2 * d + 1], y) - move
            coef[4, x, y] = spread(base[4], y) + spread(stir_up, y) * draws[2]
            coef[5, x, y] = spread(base[5], y) - spread(stir_down, y) * draws[2]
            keep_y = spread(keep, y)
            centre[0, x, y] = keep_y
            centre[1, x, y] = keep_y - STEP * OXIDATION
        return 0

    lax.fori_loop(0, 4, coefficients, 0)

    def advance(k, c):
        base_weight, section_weight = WEIGHTS[k - 1]
        old = k - 1
        flat = out.reshape(8 * NS * 64, 128)

        def body(x, h):
            y0 = h * 8
            tiles, weights = [[], []], []
            columns = [[p[old, 2 * c + j, x + 1, y0 + i] for i in range(10)] for j in range(2)]
            means = [mean_row[j, x, pl.ds(y0, 8), :] for j in range(2)]
            for i in range(8):
                y = y0 + i
                factor = [coef[d, x, y] for d in range(6)]
                keep = centre[int(c > 0), x, y]
                here = [columns[j][i + 1] for j in range(2)]
                new = [
                    keep * here[j]
                    + spread(means[j], i)
                    + factor[0] * p[old, 2 * c + j, x + 2, y + 1]
                    + factor[1] * p[old, 2 * c + j, x, y + 1]
                    + factor[2] * columns[j][i + 2]
                    + factor[3] * columns[j][i]
                    + factor[4] * pltpu.roll(here[j], 127, 1)
                    + factor[5] * pltpu.roll(here[j], 1, 1)
                    for j in range(2)
                ]
                if c == 0:
                    square = here[0] * here[0]
                    w = square / (1.0 + square) / (1.0 + jnp.exp(-3.0 * here[1]))
                    weights.append(w)
                    new[1] = new[1] - (STEP * RADIATION) * w
                else:
                    w = weight[x, y]
                    before = [p[old, 3, x + 1, y + 1] if c == 2 else None, here[0]]
                    for j in range(2):
                        gain = STEP * NUCLEATION[2 * c - 2 + j]
                        if before[j] is not None:
                            gain = gain + (STEP * GROWTH) * before[j]
                        new[j] = new[j] + w * gain
                for j in range(2):
                    s = 2 * c + j
                    if base_weight:
                        new[j] = base_weight * p[0, s, x + 1, y + 1] + section_weight * new[j]
                    tiles[j].append(new[j])
            for i, w in enumerate(weights):
                weight[x, y0 + i] = w
            for j in range(2):
                s = 2 * c + j
                for i in range(8):
                    if k < 3:
                        p[k, s, x + 1, y0 + i + 1] = tiles[j][i]
                    else:
                        flat[pl.ds(s * 64 + x * 16 + y0 + i, 8, stride=NS * 64), :] = tiles[j][i]
            if k < 3:
                for j in range(2):
                    part[k, 2 * c + j, x, pl.ds(y0, 8), :] = sum_rows(tiles[j])

        return body

    for k in range(1, 4):
        for c in range(PAIRS):
            mean_term(k - 1, c)
            arrived(k - 1, c, NORTH)
            arrived(k - 1, c, SOUTH)
            planes(1, 1, 2, advance(k, c))
            if k < 3:
                scatter(k, c, 1)
                scatter(k, c, 2)
            arrived_x(k - 1, c)
            if k == 1:
                for way in (EAST, WEST):
                    pl.when(has[back[way]])(lambda way=way: turn_face(c, way))
            planes(0, 3, 2, advance(k, c))
            if k < 3:
                send_x(k, c)
                scatter(k, c, 0)
                scatter(k, c, 3)
                for way in (NORTH, SOUTH):
                    send(k, c, way)
            if c == 0:
                pass_on(k - 1, PAIRS - 1)
                second_exchange(k - 1, PAIRS - 1)
            elif k < 3:
                pass_on(k, c - 1)
                second_exchange(k, c - 1)

    for way in (EAST, WEST, NORTH, SOUTH):
        pl.when(has[way])(lambda way=way: speed_face(way).wait_send())
        pl.when(has[way])(lambda way=way: all_sent(way))
    all_passed_on()
    wait_bytes(part_in, send_sem.at[SUM1])
    wait_bytes(part_in, send_sem.at[SUM2])


def local(fields_state, velocity, diffusivity, wiener_draw):
    counts = tuple(lax.axis_size(name) for name in ("gx", "gy", "af"))
    held = fields_state.shape
    dma = pltpu.SemaphoreType.DMA
    vmem = lambda *shape: pltpu.VMEM(shape, F32)
    held_in_hbm = (fields_state.reshape(8, NS, 64, 128), velocity, diffusivity, wiener_draw.T)
    out = pl.pallas_call(
        functools.partial(kernel, counts),
        out_shape=pltpu.VMEM((8, NS, 64, 128), F32),
        in_specs=[pl.BlockSpec(memory_space=pltpu.HBM)] * 4,
        out_specs=pl.BlockSpec(memory_space=pltpu.VMEM),
        scratch_shapes=[
            vmem(NS, 8, 64, 128),
            vmem(3, NS, 6, 18, 8, 128),
            vmem(6, 4, 16, 8, 128),
            vmem(2, 4, 16, 8, 128),
            vmem(4, 16, 8, 128),
            vmem(2, 4, 16, 128),
            vmem(3, NS, 4, 16, 128),
            vmem(3, PAIRS, 3, 2, 16, 128),
            vmem(3, NS, 4, 16, 128),
            vmem(6, 16, 128),
            vmem(4, 32, 128),
            vmem(4, 16, 128),
            vmem(4, 16, 128),
            vmem(3, 8),
            vmem(2, PAIRS, 1, 16, 8, 128),
            vmem(2, PAIRS, 8, 2, 16, 128),
            vmem(PAIRS, 8, 1, 16, 128),
            dma((NS,)),
            dma((5,)),
            dma,
            dma((3, PAIRS)),
            dma((4,)),
            dma((4,)),
            dma((6,)),
            dma((3, PAIRS, 6)),
        ],
        compiler_params=pltpu.CompilerParams(
            collective_id=0, has_side_effects=True, vmem_limit_bytes=48 * 1024 * 1024
        ),
    )(*(pltpu.with_memory_space_constraint(x, pltpu.HBM) for x in held_in_hbm))
    return out.reshape(held)


def solution(mesh):
    return jax.shard_map(
        local,
        mesh=mesh,
        in_specs=(
            P("af", None, "gx", "gy", None),
            P(None, "gx", "gy", None),
            P("gx", "gy", None),
            P("af", None),
        ),
        out_specs=P("af", None, "gx", "gy", None),
        check_vma=False,
    )
```
